32 devices in a mesh: dp: 8 (over y, x, core), head: 4 (over z).
Axes of the slice: x: 2, y: 2, z: 4, core: 2. Of those that a mesh axis runs over, the one named last changes fastest.
Arguments:
- tokens: bfloat16 [12288, 1024], P(('dp', 'head')), may hold values from -6 to 6
- cotangent: bfloat16 [12288, 1024], P(('dp', 'head')), may hold values from -6 to 6
- class_table: bfloat16 [1000, 1024], replicated, may hold values from -5 to 5
- ada_weight: bfloat16 [1024, 6144], replicated, may hold values from -0.1875 to 0.1875
- ada_bias: bfloat16 [6144], replicated, may hold values from -2 to 2
- qkv_weight: bfloat16 [3, 1024, 1024], replicated, may hold values from -0.1875 to 0.1875
- q_bias: bfloat16 [1024], replicated, may hold values from -3 to 3
- v_bias: bfloat16 [1024], replicated, may hold values from -3 to 3
- log_scale: float32 [16], replicated, may hold values from 2.3 to 3
- proj_weight: bfloat16 [1024, 1024], replicated, may hold values from -1 to 1
- proj_bias: bfloat16 [1024], replicated, may hold values from -3 to 3
- fc1_weight: bfloat16 [1024, 4096], P(None, 'head'), may hold values from -0.1875 to 0.1875
- fc1_bias: bfloat16 [4096], P('head'), may hold values from -3 to 3
- fc2_weight: bfloat16 [4096, 1024], P('head'), may hold values from -0.09375 to 0.09375
- fc2_bias: bfloat16 [1024], replicated, may hold values from -3 to 3
- item_lens: int32 [8, 4], replicated, may hold values from 1 to 680, as said below
- class_ids: int32 [8, 4], replicated, may hold values from 0 to 999
- section_ids: int32 [8, 1536], P('dp'), may hold values from 0 to 39, never falling along the last dimension, each value on 1 to 256 neighbouring positions
- destination: int32 [12288], P(('dp', 'head')), may hold values from 0 to 12287, as said below
Outputs:
- output: bfloat16 [12288, 1024], P(('dp', 'head'))
- tokens_grad: float32 [12288, 1024], P(('dp', 'head'))
- ada_weight_grad: float32 [1024, 6144], P(None, ('dp', 'head'))
- ada_bias_grad: float32 [6144], P(('dp', 'head'))
- qkv_weight_grad: float32 [3, 1024, 1024], P(None, 'head', 'dp')
- q_bias_grad: float32 [1024], replicated
- v_bias_grad: float32 [1024], replicated
- log_scale_grad: float32 [16], replicated
- proj_weight_grad: float32 [1024, 1024], P('head', 'dp')
- proj_bias_grad: float32 [1024], replicated
- fc1_weight_grad: float32 [1024, 4096], P('dp', 'head')
- fc1_bias_grad: float32 [4096], P('head')
- fc2_weight_grad: float32 [4096, 1024], P('head', 'dp')
- fc2_bias_grad: float32 [1024], replicated
The draws below stay inside these ranges and needn't reach their ends.
Inputs may be any that keep to these rules, and one draw needn't show every extreme that they name: destination is a permutation of 0 to 12287; row r of the data layout goes to pack destination[r] // 1536, and the 384 rows of each device of the data layout (devices along dp+head, dp slowest) send exactly 48 rows to each pack. Within a pack, the positions are ranked by the class of their item, then item, then position, and device d takes the d-th run of 48 of that order, so that a device's rows come from items of nearby classes; a device's rows stand in order of class, then pack, then position. `item_lens`: each row sums to 1536, and each pack has an item of exactly 680 positions.
All inputs are finite; a program needn't handle non-finite values.
Results may differ from the reference program's by a relative error of at most 0.018.
Values may be sent and summed in bfloat16 or wider, within the bound.
No kernel may reach another device: no remote copies, remote signals or barrier semaphores. Data moves between devices by JAX's collectives and lax.ppermute only.
A program may use at most 192 MiB of HBM per device.

```python
import math
import jax
import jax.numpy as jnp
import numpy as np
from jax import lax

D = 1024
HEADS = 16
HEAD_DIM = 64
FF = 4096
CLASSES = 1000
TOK_DEV = 384
SECTION_MAX = 256
PACK = 1536
PACKS = 8
TOKENS = 12288
ITEMS_PACK = 4
ITEM_MAX = 680
SECTIONS = 40
QBLOCK = 512


def shared_items(key):
    class_key = jax.random.fold_in(key, 101)
    length_key = jax.random.fold_in(key, 102)
    classes = jax.random.randint(class_key, (PACKS, ITEMS_PACK), 0, CLASSES, dtype=jnp.int32)
    others = ITEMS_PACK - 1
    remainder = PACK - ITEM_MAX
    base_len = remainder // others
    extra_count = remainder % others
    even_lens = base_len + (jnp.arange(others, dtype=jnp.int32) < extra_count).astype(jnp.int32)
    jitter_width = max(0, min(base_len - 1, ITEM_MAX - base_len - 1) // 2)
    shifts = jax.random.randint(jax.random.fold_in(length_key, 1), (PACKS, others), 0, jitter_width + 1, dtype=jnp.int32)
    jitter = shifts - jnp.roll(shifts, 1, axis=1)
    rest_lens = even_lens[None, :] + jitter
    longest = jnp.full((PACKS, 1), ITEM_MAX, jnp.int32)
    full_lens = jnp.concatenate([longest, rest_lens], axis=1).astype(jnp.int32)
    order_keys = jax.random.split(jax.random.fold_in(length_key, 2), PACKS)
    orders = jax.vmap(lambda order_key: jax.random.permutation(order_key, ITEMS_PACK))(order_keys).astype(jnp.int32)
    lengths = jnp.take_along_axis(full_lens, orders, axis=1).astype(jnp.int32)
    return (classes, lengths)


def draw_class_ids(key, part):
    classes, lengths = shared_items(key)
    return classes


def draw_item_lens(key, part):
    classes, lengths = shared_items(key)
    return lengths


def draw_destination(key, part):
    classes, lengths = shared_items(key)
    per_pack = TOK_DEV // PACKS
    sources = TOKENS // TOK_DEV
    item_ends = jnp.cumsum(lengths, axis=1).astype(jnp.int32)
    positions = jnp.arange(PACK, dtype=jnp.int32)
    item_of = jnp.sum((positions[None, :, None] >= item_ends[:, None, :]).astype(jnp.int32), axis=2).astype(jnp.int32)
    class_of = jnp.take_along_axis(classes, item_of, axis=1)
    score = class_of * (ITEMS_PACK * PACK) + item_of * PACK + positions[None, :]
    ranked = jnp.argsort(score, axis=1).astype(jnp.int32)
    ranked_class = jnp.take_along_axis(class_of, ranked, axis=1)
    chosen_pos = ranked.reshape(PACKS, sources, per_pack).transpose(1, 0, 2).reshape(sources, TOK_DEV)
    chosen_class = ranked_class.reshape(PACKS, sources, per_pack).transpose(1, 0, 2).reshape(sources, TOK_DEV)
    pack_of = jnp.broadcast_to(jnp.arange(PACKS, dtype=jnp.int32)[None, :, None], (sources, PACKS, per_pack)).reshape(sources, TOK_DEV)
    device_score = chosen_class * (PACKS * PACK) + pack_of * PACK + chosen_pos
    device_order = jnp.argsort(device_score, axis=1).astype(jnp.int32)
    targets = pack_of * PACK + chosen_pos
    return jnp.take_along_axis(targets, device_order, axis=1).reshape(-1).astype(jnp.int32)


def with_spikes(drawn, stream_key, source, target, shards_of, factor):
    owner, partner = [(jnp.arange(drawn.shape[dim]) // (drawn.shape[dim] // shards_of)).reshape([-1 if axis == dim else 1 for axis in range(drawn.ndim)]) for dim in (source, target)]
    chosen = jax.random.permutation(stream_key, shards_of)[partner]
    strong = (owner == chosen) | (owner == (partner + shards_of // 2) % shards_of)
    return jnp.where(strong, factor * drawn, drawn)


def level_of(own_key, dims, pieces, low, high):
    loudness = 1.0
    for position, shards_of in pieces:
        heights = jax.random.uniform(jax.random.fold_in(jax.random.fold_in(own_key, 6), position), (shards_of,), jnp.float32, low / len(pieces), high / len(pieces))
        loudness = loudness * jnp.repeat(jnp.exp(heights), dims[position] // shards_of).reshape((-1,) + (1,) * (len(dims) - 1 - position))
    return loudness


def profile(count, total, limit, skew):
    portions = [(1 << 20) // math.isqrt(rank ** skew) + 1 for rank in range(2, count + 1)]
    spare, counts = total - limit - (count - 1), [1] * (count - 1)
    while spare > 0:
        movable = [i for i in range(count - 1) if counts[i] < limit]
        mass, remaining = sum([portions[i] for i in movable]), spare
        for i in movable:
            more = min(limit - counts[i], max(1, remaining * portions[i] // mass), spare)
            counts[i] = counts[i] + more
            spare = spare - more
    return np.array([limit] + counts)


def uneven_parts(stream_key, number_of, total, limit, slope):
    if number_of == 2:
        one = jax.random.randint(stream_key, (), max(1, total - limit), min(limit, total - 1) + 1)
        return jnp.stack([one, total - one])
    tallies = jnp.asarray(profile(number_of, total, limit, slope), jnp.int32)
    couples = (number_of - 1) // 2
    donor, taker = tallies[1:1 + 2 * couples:2], tallies[2:2 + 2 * couples:2]
    margin = jnp.minimum(donor - 1, limit - taker)
    moved = jax.random.randint(jax.random.fold_in(stream_key, 1), (couples,), 0, 1 << 20) % (margin + 1)
    tallies = tallies.at[1:1 + 2 * couples:2].set(donor - moved).at[2:2 + 2 * couples:2].set(taker + moved)
    return tallies[jax.random.permutation(jax.random.fold_in(stream_key, 2), number_of)]


def bell_draw(key, dims, spread, bound, shards=(), kind=jnp.bfloat16):
    entries = spread * jax.random.normal(key, dims, jnp.float32)
    if shards:
        entries = entries * level_of(key, dims, shards, -0.22, 0.18)
    return jnp.clip(entries, -bound, bound).astype(kind)


def heavy_noise(stream_key, extent, width, limit, pieces, heavy, held_as=jnp.bfloat16):
    drawn = width * jax.random.normal(stream_key, extent, jnp.float32)
    if pieces:
        drawn = drawn * level_of(stream_key, extent, pieces, -0.22, 0.18)
    return jnp.clip(with_spikes(drawn, jax.random.fold_in(stream_key, 3), *heavy), -limit, limit).astype(held_as)


def setup_inputs(seed: int = 0) -> dict:
    keys = jax.random.split(jax.random.key(seed), 20)
    return {
        "tokens": bell_draw(keys[0], (TOKENS, D), 1.0, 6.0, ((0, 32),)),
        "cotangent": heavy_noise(keys[1], (TOKENS, D), 1.0, 6.0, ((0, 32),), (0, 1, 32, 2.75)),
        "class_table": bell_draw(keys[2], (CLASSES, D), 1.0, 5.0),
        "ada_weight": bell_draw(keys[3], (D, 6 * D), D ** -0.5, 0.1875),
        "ada_bias": bell_draw(keys[4], (6 * D,), 0.3, 2.0),
        "qkv_weight": bell_draw(keys[5], (3, D, D), D ** -0.5, 0.1875),
        "q_bias": bell_draw(keys[6], (D,), 0.5, 3.0),
        "v_bias": bell_draw(keys[7], (D,), 0.5, 3.0),
        "log_scale": jnp.clip(jax.random.uniform(keys[8], (HEADS,), jnp.float32, 2.3, 3.0), 2.3, 3.0),
        "proj_weight": bell_draw(keys[9], (D, D), (D // 32) ** -0.5, 1.0),
        "proj_bias": bell_draw(keys[10], (D,), 0.5, 3.0),
        "fc1_weight": bell_draw(keys[11], (D, FF), D ** -0.5, 0.1875, ((1, 4),)),
        "fc1_bias": bell_draw(keys[12], (FF,), 0.5, 3.0, ((0, 4),)),
        "fc2_weight": bell_draw(keys[13], (FF, D), FF ** -0.5, 0.09375, ((0, 4),)),
        "fc2_bias": bell_draw(keys[14], (D,), 0.5, 3.0),
        "item_lens": draw_item_lens(jax.random.fold_in(keys[19], 71), 0),
        "class_ids": draw_class_ids(jax.random.fold_in(keys[19], 71), 0),
        "section_ids": jax.vmap(lambda own: jnp.searchsorted(jnp.cumsum(uneven_parts(own, SECTIONS, PACK, SECTION_MAX, 1)), jnp.arange(PACK), side="right"))(jax.random.split(keys[17], PACKS)).reshape((PACKS, PACK)).astype(jnp.int32),
        "destination": draw_destination(jax.random.fold_in(keys[19], 71), 0),
    }


@jax.custom_vjp
def low(v):
    return lax.optimization_barrier(v.astype(jnp.bfloat16)).astype(jnp.float32)

@jax.custom_vjp
def low_back(v):
    return v

def low_keep(v):
    return (low(v), None)

def low_pass(kept, grad):
    return (grad,)

def back_keep(v):
    return (v, None)

def back_low(kept, grad):
    return (low(grad),)
low.defvjp(low_keep, low_pass)
low_back.defvjp(back_keep, back_low)

def layer_norm(values):
    centre = values - lax.optimization_barrier(jnp.mean(values, axis=-1, keepdims=True))
    return centre * lax.rsqrt(lax.optimization_barrier(jnp.mean(centre * centre, axis=-1, keepdims=True)) + 1e-06)

def unit_rows(values):
    return values * lax.rsqrt(lax.optimization_barrier(jnp.sum(values * values, axis=-1, keepdims=True)) + 1e-06)

def product(left_side, right_side):
    return jnp.dot(left_side, right_side, precision=lax.Precision.HIGHEST)

def pack_forward(params, rows_pack, mod_rows, pack_item, pack_section):
    qkv_weight, q_bias, v_bias, log_scale, proj_weight, proj_bias, fc1_weight, fc1_bias, fc2_weight, fc2_bias = params
    gamma_one, gamma_two, scale_one, scale_two, shift_one, shift_two = jnp.split(mod_rows, 6, axis=1)
    attn_in = low(layer_norm(rows_pack) * (1.0 + scale_one) + shift_one)
    query_pre = low_back(product(attn_in, qkv_weight[0]) + q_bias)
    key_pre = low_back(product(attn_in, qkv_weight[1]))
    value_rows = low_back(low(product(attn_in, qkv_weight[2]) + v_bias))
    temper = jnp.exp(log_scale)[None, :, None]
    query_heads = low_back(low(unit_rows(query_pre.reshape(PACK, HEADS, HEAD_DIM)) * temper))
    key_heads = low_back(low(unit_rows(key_pre.reshape(PACK, HEADS, HEAD_DIM))))
    value_heads = value_rows.reshape(PACK, HEADS, HEAD_DIM)

    def attend(block_index):
        first_row = block_index * QBLOCK
        query_part = lax.dynamic_slice_in_dim(query_heads, first_row, QBLOCK, 0)
        item_part = lax.dynamic_slice_in_dim(pack_item, first_row, QBLOCK, 0)
        section_part = lax.dynamic_slice_in_dim(pack_section, first_row, QBLOCK, 0)
        scores = low_back(jnp.einsum('qhd,khd->hqk', query_part, key_heads, precision=lax.Precision.HIGHEST))
        allowed = (item_part[:, None] == pack_item[None, :]) & (pack_section[None, :] <= section_part[:, None])
        scores = jnp.where(allowed[None], scores, -1e+30)
        weights_p = low(jax.nn.softmax(scores, axis=-1))
        return jnp.einsum('hqk,khd->qhd', weights_p, value_heads, precision=lax.Precision.HIGHEST)
    mixed_heads = lax.map(jax.checkpoint(attend), jnp.arange(PACK // QBLOCK))
    attn_out = low_back(low(mixed_heads.reshape(PACK, D)))
    branch = low_back(product(attn_out, proj_weight) + proj_bias)
    middle = rows_pack + gamma_one * branch
    mlp_in = low(layer_norm(middle) * (1.0 + scale_two) + shift_two)
    hidden_pre = low_back(product(mlp_in, fc1_weight) + fc1_bias)
    hidden_act = low(jax.nn.gelu(hidden_pre, approximate=True))
    mlp_out = low_back(product(hidden_act, fc2_weight) + fc2_bias)
    return middle + gamma_two * mlp_out

def reference(tokens, cotangent, class_table, ada_weight, ada_bias, qkv_weight, q_bias, v_bias, log_scale, proj_weight, proj_bias, fc1_weight, fc1_bias, fc2_weight, fc2_bias, item_lens, class_ids, section_ids, destination):
    packed = jnp.zeros((TOKENS, D), jnp.float32).at[destination].set(tokens.astype(jnp.float32)).reshape(PACKS, PACK, D)
    upstream = jnp.zeros((TOKENS, D), jnp.float32).at[destination].set(cotangent.astype(jnp.float32)).reshape(PACKS, PACK, D)
    item_ends = jnp.cumsum(item_lens, axis=1).astype(jnp.int32)
    positions = jnp.arange(PACK, dtype=jnp.int32)
    local_item = lax.optimization_barrier(jnp.sum((positions[None, :, None] >= item_ends[:, None, :]).astype(jnp.int32), axis=2))
    pack_items = (local_item + ITEMS_PACK * jnp.arange(PACKS, dtype=jnp.int32)[:, None]).astype(jnp.int32)
    class_rows = jax.nn.silu(class_table.astype(jnp.float32)[class_ids.reshape(-1)])
    block_params = (qkv_weight.astype(jnp.float32), q_bias.astype(jnp.float32), v_bias.astype(jnp.float32), log_scale.astype(jnp.float32), proj_weight.astype(jnp.float32), proj_bias.astype(jnp.float32), fc1_weight.astype(jnp.float32), fc1_bias.astype(jnp.float32), fc2_weight.astype(jnp.float32), fc2_bias.astype(jnp.float32))

    def forward(ada_matrix, ada_offset, params, packed_rows):
        modulation = low_back(product(low(class_rows), ada_matrix) + ada_offset)

        def one_pack(pack_inputs):
            rows_pack, items_here, sections_here = pack_inputs
            return pack_forward(params, rows_pack, modulation[items_here], items_here, sections_here)
        return lax.map(jax.checkpoint(one_pack), (packed_rows, pack_items, section_ids))
    result, pullback = jax.vjp(forward, ada_weight.astype(jnp.float32), ada_bias.astype(jnp.float32), block_params, packed)
    ada_grad, ada_bias_grad, block_grads, input_grad = pullback(upstream)
    output = result.reshape(TOKENS, D)[destination].astype(jnp.bfloat16)
    tokens_grad = input_grad.reshape(TOKENS, D)[destination]
    return (output, tokens_grad, ada_grad, ada_bias_grad, block_grads[0], block_grads[1], block_grads[2], block_grads[3], block_grads[4], block_grads[5], block_grads[6], block_grads[7], block_grads[8], block_grads[9])
```

```python
import functools

import jax
import jax.numpy as jnp
from jax import lax
from jax.experimental import pallas as pl
from jax.experimental.pallas import tpu as pltpu
from jax.sharding import Mesh, PartitionSpec as P

BF = jnp.bfloat16
F32 = jnp.float32


def layer_norm(values):
    centre = values - jnp.mean(values, axis=-1, keepdims=True)
    inverse = lax.rsqrt(jnp.mean(centre * centre, axis=-1, keepdims=True) + 1e-06)
    return (centre * inverse, inverse)


def norm_back(gradient, normed, inverse):
    return inverse * (
        gradient
        - jnp.mean(gradient, axis=-1, keepdims=True)
        - normed * jnp.mean(gradient * normed, axis=-1, keepdims=True)
    )


def unit_rows(values):
    inverse = lax.rsqrt(jnp.sum(values * values, axis=-1, keepdims=True) + 1e-06)
    return (values * inverse, inverse)


def unit_back(gradient, unit_vec, inverse):
    return inverse * (gradient - unit_vec * jnp.sum(gradient * unit_vec, axis=-1, keepdims=True))


def smooth_gate(hidden_val):
    return jax.nn.gelu(hidden_val, approximate=True)


def gelu_back(pre_act, gradient):
    return jax.vjp(smooth_gate, pre_act)[1](gradient)[0]


def dot(left, right, dims):
    return lax.dot_general(left, right, (dims, ((), ())), preferred_element_type=F32)


def head_lanes(width, head_dim):
    return lax.broadcasted_iota(jnp.int32, (1, width), 1) // head_dim


def attend_kernel(
    heads, head_dim, block, first_ref, last_ref, lo_ref, hi_ref, q_ref, k_ref, v_ref,
    out_ref, out_t_ref, lse_ref, v_t, acc, total,
):
    pack_len, width = q_ref.shape
    lanes = head_lanes(width, head_dim)
    v_t[...] = v_ref[...].T

    @pl.loop(0, pack_len // block)
    def _(q_block):
        q_rows = pl.ds(pl.multiple_of(q_block * block, block), block)
        q_t = q_ref[q_rows, :].T
        low, high = lo_ref[:, q_rows], hi_ref[:, q_rows]
        acc[...] = jnp.zeros_like(acc)
        total[...] = jnp.zeros_like(total)

        @pl.loop(first_ref[q_block], last_ref[q_block])
        def _(k_block):
            k_rows = pl.ds(pl.multiple_of(k_block * block, block), block)
            keys = k_ref[k_rows, :]
            index = k_block * block + lax.broadcasted_iota(jnp.int32, (block, block), 0)
            seen = (index >= low) & (index < high)
            for h in range(heads):
                own = pl.ds(h * head_dim, head_dim)
                scores = dot(jnp.where(lanes == h, keys, jnp.zeros_like(keys)), q_t, ((1,), (0,)))
                raised = jnp.where(seen, jnp.exp(scores), 0.0)
                total[h : h + 1, :] += jnp.sum(raised, axis=0, keepdims=True)
                acc[own, :] += dot(v_t[own, k_rows], raised.astype(BF), ((1,), (0,)))

        for h in range(heads):
            own = pl.ds(h * head_dim, head_dim)
            acc[own, :] = acc[own, :] / total[h : h + 1, :]
            lse_ref[h : h + 1, q_rows] = jnp.log(total[h : h + 1, :])
        out_t_ref[:, q_rows] = acc[...]
        out_ref[q_rows, :] = acc[...].T.astype(BF)


def attend(first, last, low, high, queries, keys, values, heads, head_dim, block):
    pack_len, width = queries.shape
    smem = pl.BlockSpec(memory_space=pltpu.SMEM)
    vmem = pl.BlockSpec(memory_space=pltpu.VMEM)
    pairs = heads * pack_len * pack_len // 2
    return pl.pallas_call(
        functools.partial(attend_kernel, heads, head_dim, block),
        out_shape=(
            jax.ShapeDtypeStruct((pack_len, width), BF),
            jax.ShapeDtypeStruct((width, pack_len), F32),
            jax.ShapeDtypeStruct((8, pack_len), F32),
        ),
        in_specs=[smem, smem] + [vmem] * 5,
        out_specs=(vmem, vmem, vmem),
        scratch_shapes=[
            pltpu.VMEM((width, pack_len), BF),
            pltpu.VMEM((width, block), F32),
            pltpu.VMEM((8, block), F32),
        ],
        compiler_params=pltpu.CompilerParams(vmem_limit_bytes=40 * 1024 * 1024),
        cost_estimate=pl.CostEstimate(
            flops=4 * pairs * head_dim, bytes_accessed=8 * pack_len * width, transcendentals=pairs
        ),
    )(first, last, low, high, queries, keys, values)


def attend_back_kernel(
    heads, head_dim, block, first_ref, last_ref, lo_ref, hi_ref, q_ref, k_ref, v_ref, g_ref,
    out_t_ref, lse_ref, dq_ref, dk_ref, dv_ref, k_t, dk_acc, dv_acc, acc, sums,
):
    pack_len, width = q_ref.shape
    lanes = head_lanes(width, head_dim)
    k_t[...] = k_ref[...].T
    dk_acc[...] = jnp.zeros_like(dk_acc)
    dv_acc[...] = jnp.zeros_like(dv_acc)

    @pl.loop(0, pack_len // block)
    def _(q_block):
        q_rows = pl.ds(pl.multiple_of(q_block * block, block), block)
        queries, grads = q_ref[q_rows, :], g_ref[q_rows, :]
        q_t, g_t = queries.T, grads.T
        low, high = lo_ref[:, q_rows], hi_ref[:, q_rows]
        weighted = g_t.astype(F32) * out_t_ref[:, q_rows]
        for h in range(heads):
            sums[h : h + 1, :] = jnp.sum(
                weighted[h * head_dim : (h + 1) * head_dim, :], axis=0, keepdims=True
            )
        acc[...] = jnp.zeros_like(acc)

        @pl.loop(first_ref[q_block], last_ref[q_block])
        def _(k_block):
            k_rows = pl.ds(pl.multiple_of(k_block * block, block), block)
            keys, values = k_ref[k_rows, :], v_ref[k_rows, :]
            index = k_block * block + lax.broadcasted_iota(jnp.int32, (block, block), 0)
            seen = (index >= low) & (index < high)
            for h in range(heads):
                own = pl.ds(h * head_dim, head_dim)
                mine = lanes == h
                scores = dot(jnp.where(mine, keys, jnp.zeros_like(keys)), q_t, ((1,), (0,)))
                probs = jnp.where(seen, jnp.exp(scores - lse_ref[h : h + 1, q_rows]), 0.0)
                grad_probs = dot(jnp.where(mine, values, jnp.zeros_like(values)), g_t, ((1,), (0,)))
                grad_scores = (probs * (grad_probs - sums[h : h + 1, :])).astype(BF)
                acc[own, :] += dot(k_t[own, k_rows], grad_scores, ((1,), (0,)))
                dk_acc[k_rows, :] += dot(
                    grad_scores, jnp.where(mine, queries, jnp.zeros_like(queries)), ((1,), (0,))
                )
                dv_acc[k_rows, :] += dot(
                    probs.astype(BF), jnp.where(mine, grads, jnp.zeros_like(grads)), ((1,), (0,))
                )

        dq_ref[q_rows, :] = acc[...].T.astype(BF)

    dk_ref[...] = dk_acc[...].astype(BF)
    dv_ref[...] = dv_acc[...].astype(BF)


def attend_back(
    first, last, low, high, queries, keys, values, grads, out_t, lse, heads, head_dim, block
):
    pack_len, width = queries.shape
    smem = pl.BlockSpec(memory_space=pltpu.SMEM)
    vmem = pl.BlockSpec(memory_space=pltpu.VMEM)
    pairs = heads * pack_len * pack_len // 2
    return pl.pallas_call(
        functools.partial(attend_back_kernel, heads, head_dim, block),
        out_shape=(jax.ShapeDtypeStruct((pack_len, width), BF),) * 3,
        in_specs=[smem, smem] + [vmem] * 8,
        out_specs=(vmem,) * 3,
        scratch_shapes=[
            pltpu.VMEM((width, pack_len), BF),
            pltpu.VMEM((pack_len, width), F32),
            pltpu.VMEM((pack_len, width), F32),
            pltpu.VMEM((width, block), F32),
            pltpu.VMEM((8, block), F32),
        ],
        compiler_params=pltpu.CompilerParams(vmem_limit_bytes=40 * 1024 * 1024),
        cost_estimate=pl.CostEstimate(
            flops=10 * pairs * head_dim, bytes_accessed=16 * pack_len * width, transcendentals=pairs
        ),
    )(first, last, low, high, queries, keys, values, grads, out_t, lse)


def to_packs(rows):
    return lax.all_to_all(rows, ("yy", "head"), split_axis=0, concat_axis=0, tiled=True)


def bits(count):
    steps = []
    while count > 1:
        count //= 2
        steps.append(count)
    return steps


def xor_swap(values, axis, step):
    size = lax.axis_size(axis)
    return lax.ppermute(values, axis, [(i, i ^ step) for i in range(size)])


def xor_gather(block, axis):
    blocks = {0: block}
    for step in bits(lax.axis_size(axis)):
        for k in list(blocks):
            blocks[k ^ step] = xor_swap(blocks[k], axis, step)
    return [blocks[k] for k in range(len(blocks))]


def xor_scatter(blocks, axis):
    blocks = list(blocks)
    for step in reversed(bits(lax.axis_size(axis))):
        blocks = {k: b for k, b in enumerate(blocks)} if isinstance(blocks, list) else blocks
        kept = {}
        for k in blocks:
            if not k & step:
                arrived = xor_swap(blocks[k ^ step], axis, step)
                kept[k] = (blocks[k].astype(F32) + arrived.astype(F32)).astype(blocks[k].dtype)
        blocks = kept
    return blocks[0]


def butterfly(values, axes):
    for axis in axes:
        for step in reversed(bits(lax.axis_size(axis))):
            values = values + xor_swap(values, axis, step)
    return values


def pick(values, index, axis):
    return lax.dynamic_index_in_dim(values, index, axis, keepdims=False)


def xor_blocks(values, axis, dim):
    me = lax.axis_index(axis)
    return [pick(values, me ^ k, dim) for k in range(lax.axis_size(axis))]


def sum_packs(parts):
    half = xor_scatter(xor_blocks(parts, "yy", 0), "yy")
    arrived = lax.all_to_all(half, "head", split_axis=0, concat_axis=0, tiled=True)
    return jnp.sum(arrived.astype(F32), axis=0)


def shards(
    tokens,
    cotangent,
    class_table,
    ada_weight,
    ada_bias,
    qkv_weight,
    q_bias,
    v_bias,
    log_scale,
    proj_weight,
    proj_bias,
    fc1_weight,
    fc1_bias,
    fc2_weight,
    fc2_bias,
    item_lens,
    class_ids,
    section_ids,
    destination,
):
    yy_size = lax.axis_size("yy")
    g_size = lax.axis_size("g")
    head_size = lax.axis_size("head")
    yy, g, z = lax.axis_index("yy"), lax.axis_index("g"), lax.axis_index("head")
    pack = yy * head_size + z
    row_count, model_width = tokens.shape
    heads_all = log_scale.shape[0]
    head_dim = model_width // heads_all
    heads_here = heads_all // g_size
    width = model_width // g_size
    dp_size = yy_size * g_size
    pack_len = row_count * head_size
    seg = row_count // yy_size
    items_pack = item_lens.shape[1]
    block = min(256, pack_len)
    col = model_width // dp_size
    parts = yy_size if col % head_dim == 0 else 1
    sub = width // parts

    def own_cols(values):
        shape = values.shape[:-1]
        return pick(values.reshape(*shape, parts, g_size, sub), g, len(shape) + 1).reshape(
            *shape, width
        )

    row_pack = destination // pack_len
    index = jnp.arange(row_count, dtype=jnp.int32)
    before = (row_pack[None, :] < row_pack[:, None]) | (
        (row_pack[None, :] == row_pack[:, None]) & (index[None, :] < index[:, None])
    )
    slot = jnp.sum(before.astype(jnp.int32), axis=1)
    to_slot = (slot[None, :] == index[:, None]).astype(BF)
    sorted_tokens = dot(to_slot, tokens, ((1,), (0,))).astype(BF)
    sorted_cotangent = dot(to_slot, cotangent, ((1,), (0,))).astype(BF)
    inputs = to_packs(sorted_tokens).astype(F32)
    upstream = to_packs(sorted_cotangent).astype(F32)

    hidden = fc1_weight.shape[1] // g_size
    half = model_width // yy_size
    fc1_own = lax.dynamic_slice(fc1_weight, (yy * half, g * hidden), (half, hidden))
    fc1_bias_own = lax.dynamic_slice(fc1_bias, (g * hidden,), (hidden,))
    fc1_sent = jnp.concatenate(
        [fc1_own, jnp.broadcast_to(fc1_bias_own[None, :], (16, hidden))], axis=0
    )
    fc1_all = lax.all_gather(fc1_sent, ("yy", "head"), axis=0)
    fc1_all = fc1_all.reshape(yy_size, head_size, half + 16, hidden)
    fc1_here = (
        fc1_all[:, :, :half].transpose(0, 2, 1, 3).reshape(model_width, head_size * hidden)
    )
    fc1_bias_here = fc1_all[0, :, half].reshape(head_size * hidden)
    fc2_own = lax.dynamic_slice(fc2_weight, (g * hidden, yy * half), (hidden, half))
    fc2_all = lax.all_gather(fc2_own, ("yy", "head"), axis=0)
    fc2_here = (
        fc2_all.reshape(yy_size, head_size, hidden, half)
        .transpose(1, 2, 0, 3)
        .reshape(head_size * hidden, model_width)
    )

    lens_here = pick(item_lens, pack, 0)
    class_here = pick(class_ids, pack, 0)
    item_index = jnp.arange(items_pack, dtype=jnp.int32)
    order_key = class_here * items_pack + item_index
    item_rank = jnp.sum(
        jnp.where(order_key[None, :] < order_key[:, None], lens_here[None, :], 0), axis=1
    )
    item_pos = jnp.cumsum(lens_here) - lens_here
    item_end = item_rank + lens_here

    def items_of(rank):
        return (rank[:, None] >= item_rank[None, :]) & (rank[:, None] < item_end[None, :])

    rank_all = jnp.arange(pack_len, dtype=jnp.int32)
    member = items_of(rank_all)

    def of_item(values):
        return jnp.sum(jnp.where(member, values[None, :], 0), axis=1)

    section_here = lax.ppermute(
        section_ids[0],
        ("g", "head"),
        [(a * head_size + b, b * head_size + a) for a in range(g_size) for b in range(head_size)],
    )
    position = rank_all - of_item(item_rank - item_pos)
    section_rank = jnp.sum(
        jnp.where(rank_all[None, :] == position[:, None], section_here[None, :], 0), axis=1
    )
    up_to = jnp.sum((section_here[None, :] <= section_rank[:, None]).astype(jnp.int32), axis=1)
    low = of_item(item_rank)
    high = jnp.minimum(up_to + of_item(item_rank - item_pos), of_item(item_end))
    first = low[::block] // block
    last = (high[block - 1 :: block] + block - 1) // block
    low, high = low[None, :], high[None, :]

    row_rank = (
        (jnp.arange(yy_size, dtype=jnp.int32)[:, None] * g_size + g) * seg
        + jnp.arange(seg, dtype=jnp.int32)[None, :]
    ).reshape(row_count)
    row_member = items_of(row_rank)

    class_rows = jnp.take(class_table, class_ids.reshape(-1), axis=0).astype(F32)
    silu_cond = jax.nn.silu(class_rows).astype(BF)
    silu_here = lax.dynamic_slice_in_dim(silu_cond, pack * items_pack, items_pack, 0)
    modulation = jnp.dot(silu_here, ada_weight, preferred_element_type=F32) + ada_bias.astype(F32)

    def mod_part(part):
        values = modulation[:, part * model_width : (part + 1) * model_width]
        rows = jnp.zeros((row_count, model_width), F32)
        for item in range(items_pack):
            rows = jnp.where(row_member[:, item : item + 1], values[item : item + 1], rows)
        return rows

    gamma_one, gamma_two, scale_one, scale_two, shift_one, shift_two = (
        mod_part(part) for part in range(6)
    )

    def rank_order(blocks):
        stacked = jnp.stack(blocks).reshape(g_size, yy_size, seg, -1)
        ordered = jnp.stack([pick(stacked, g ^ k, 0) for k in range(g_size)], axis=1)
        return ordered.reshape(pack_len, -1)

    def xor_order(values):
        by_g = values.reshape(yy_size, g_size, seg, -1)
        ordered = jnp.stack([pick(by_g, g ^ k, 1) for k in range(g_size)])
        return ordered.reshape(pack_len, -1)

    def split_blocks(values):
        return [values[k * row_count : (k + 1) * row_count] for k in range(g_size)]

    normed_one, inverse_one = layer_norm(inputs)
    attn_in = (normed_one * (1.0 + scale_one) + shift_one).astype(BF)
    attn_in_all = jnp.concatenate(xor_gather(attn_in, "g"), axis=0)
    qkv_own = own_cols(qkv_weight)
    query_pre = dot(attn_in_all, qkv_own[0], ((1,), (0,))) + own_cols(q_bias).astype(F32)
    key_pre = dot(attn_in_all, qkv_own[1], ((1,), (0,)))
    value_all = (dot(attn_in_all, qkv_own[2], ((1,), (0,))) + own_cols(v_bias).astype(F32)).astype(BF)

    def by_head(values):
        return values.reshape(pack_len, heads_here, head_dim)

    query_unit, query_inv = unit_rows(by_head(query_pre))
    key_unit, key_inv = unit_rows(by_head(key_pre))
    heads_part = sub // head_dim
    scale_here = pick(log_scale.reshape(parts, g_size, heads_part), g, 1).reshape(heads_here)
    temper = jnp.exp(scale_here)[None, :, None]
    query_all = (query_unit * temper).reshape(pack_len, width).astype(BF)
    key_all = key_unit.reshape(pack_len, width).astype(BF)

    def ranked(values):
        return rank_order(split_blocks(values))

    pack_query, pack_key, pack_value = ranked(query_all), ranked(key_all), ranked(value_all)
    out_rank, out_t, lse = attend(
        first, last, low, high, pack_query, pack_key, pack_value, heads_here, head_dim, block
    )
    leaving = out_rank.reshape(yy_size, g_size, seg, width).transpose(1, 0, 2, 3)
    returned = lax.all_to_all(
        leaving.reshape(g_size, row_count, width), "g", split_axis=0, concat_axis=0, tiled=True
    )
    attn_rows = (
        returned.reshape(g_size, row_count, parts, sub)
        .transpose(1, 2, 0, 3)
        .reshape(row_count, model_width)
    )
    branch = jnp.dot(attn_rows, proj_weight, preferred_element_type=F32) + proj_bias.astype(F32)
    middle = inputs + gamma_one * branch
    normed_two, inverse_two = layer_norm(middle)
    mlp_in = (normed_two * (1.0 + scale_two) + shift_two).astype(BF)

    grad_mlp = (upstream * gamma_two).astype(BF)
    grad_mlp_all = jnp.concatenate(xor_gather(grad_mlp, "g"), axis=0)
    mlp_all = jnp.concatenate(xor_gather(mlp_in, "g"), axis=0)
    hidden_pre = dot(mlp_all, fc1_here, ((1,), (0,))) + fc1_bias_here.astype(F32)
    hidden_act = smooth_gate(hidden_pre).astype(BF)
    grad_act = dot(grad_mlp_all, fc2_here, ((1,), (1,)))
    grad_hidden = gelu_back(hidden_pre, grad_act).astype(BF)
    grad_in_part = dot(grad_hidden, fc1_here, ((1,), (1,))).astype(BF)
    out_part = dot(hidden_act, fc2_here, ((1,), (0,))).astype(BF)
    grad_mlp_in = xor_scatter(split_blocks(grad_in_part), "g").astype(F32)
    mlp_out = xor_scatter(split_blocks(out_part), "g").astype(F32) + fc2_bias.astype(F32)
    output_rows = (middle + gamma_two * mlp_out).astype(BF)
    grad_gamma_two = upstream * mlp_out
    up_grad = dot(mlp_all, grad_hidden, ((0,), (0,))).astype(BF)
    down_grad = dot(hidden_act, grad_mlp_all, ((0,), (0,))).astype(BF)
    up_sum = sum_packs(up_grad.reshape(yy_size, half, head_size, hidden).transpose(0, 2, 1, 3))
    down_sum = sum_packs(down_grad.reshape(head_size, hidden, yy_size, half).transpose(2, 0, 1, 3))
    up_part = lax.all_to_all(
        up_sum.astype(BF).reshape(g_size, half // g_size, hidden), "g", 0, 0, tiled=True
    )
    up_part = up_part.transpose(1, 0, 2).reshape(half // g_size, g_size * hidden).astype(F32)
    down_part = lax.all_to_all(
        down_sum.astype(BF).reshape(hidden, g_size, half // g_size).transpose(1, 0, 2),
        "g",
        0,
        0,
        tiled=True,
    )
    down_part = down_part.reshape(g_size * hidden, half // g_size).astype(F32)

    grad_middle = upstream + norm_back(grad_mlp_in * (1.0 + scale_two), normed_two, inverse_two)
    grad_branch = (grad_middle * gamma_one).astype(BF)
    grad_attn = dot(grad_branch, proj_weight, ((1,), (1,))).astype(BF)
    outbound = (
        grad_attn.reshape(row_count, parts, g_size, sub)
        .transpose(2, 0, 1, 3)
        .reshape(g_size, row_count, width)
    )
    inbound = lax.all_to_all(outbound, "g", split_axis=0, concat_axis=0, tiled=True)
    pack_grad = (
        inbound.reshape(g_size, yy_size, seg, width).transpose(1, 0, 2, 3).reshape(pack_len, width)
    )
    proj_grad = dot(attn_rows, grad_branch, ((0,), (0,))).astype(BF)
    grad_query, grad_key, grad_value = attend_back(
        first, last, low, high, pack_query, pack_key, pack_value, pack_grad, out_t, lse,
        heads_here, head_dim, block,
    )
    grad_query = by_head(xor_order(grad_query)).astype(F32)
    grad_key = by_head(xor_order(grad_key)).astype(F32)
    grad_value = xor_order(grad_value)
    grad_log = jnp.sum(grad_query * query_unit * temper, axis=(0, 2))
    grad_query_pre = (
        unit_back(grad_query * temper, query_unit, query_inv).reshape(pack_len, width).astype(BF)
    )
    grad_key_pre = unit_back(grad_key, key_unit, key_inv).reshape(pack_len, width).astype(BF)
    grad_qkv = jnp.concatenate([grad_query_pre, grad_key_pre, grad_value], axis=1)
    weights_here = jnp.concatenate([qkv_own[0], qkv_own[1], qkv_own[2]], axis=1)
    grad_in_part = dot(grad_qkv, weights_here, ((1,), (1,))).astype(BF)
    grad_attn_in = xor_scatter(split_blocks(grad_in_part), "g").astype(F32)
    qkv_grad = dot(attn_in_all, grad_qkv, ((0,), (0,))).astype(BF)
    tokens_grad_rows = grad_middle + norm_back(
        grad_attn_in * (1.0 + scale_one), normed_one, inverse_one
    )

    def to_data(rows):
        return dot(to_slot, to_packs(rows), ((0,), (0,)))

    output = to_data(output_rows).astype(BF)
    tokens_grad = to_data(tokens_grad_rows.astype(BF))

    grad_mod = jnp.concatenate(
        [
            grad_middle * branch,
            grad_gamma_two,
            grad_attn_in * normed_one,
            grad_mlp_in * normed_two,
            grad_attn_in,
            grad_mlp_in,
        ],
        axis=1,
    )
    item_part = lax.dot_general(
        row_member.astype(F32), grad_mod, (((0,), (0,)), ((), ())), precision=lax.Precision.HIGHEST
    )
    ada_cols = 6 * model_width // (dp_size * head_size)
    item_part = item_part.reshape(items_pack, yy_size, g_size, head_size, ada_cols)
    item_own = xor_scatter(xor_blocks(item_part, "g", 2), "g")
    item_all = lax.all_to_all(
        item_own.reshape(items_pack, yy_size * head_size, ada_cols).transpose(1, 0, 2),
        ("yy", "head"),
        0,
        0,
        tiled=True,
    )
    item_low = item_all.reshape(-1, ada_cols).astype(BF)
    ada_grad = dot(silu_cond, item_low, ((0,), (0,)))
    ada_bias_grad = jnp.sum(item_low.astype(F32), axis=0)

    proj_own = xor_scatter(
        [
            block_cols.reshape(model_width, width)
            for block_cols in xor_blocks(
                proj_grad.reshape(model_width, parts, g_size, sub), "g", 2
            )
        ],
        "g",
    )
    rows_z = model_width // head_size
    if parts == yy_size:
        both = jnp.concatenate(
            [
                proj_own.reshape(1, head_size, rows_z, yy_size, col),
                qkv_grad.reshape(head_size, rows_z, 3, yy_size, col).transpose(2, 0, 1, 3, 4),
            ],
            axis=0,
        )
        summed = sum_packs(both.transpose(3, 1, 0, 2, 4))
        proj_part, qkv_part = summed[0], summed[1:]
    else:
        both = jnp.concatenate(
            [
                proj_own.reshape(1, model_width, width),
                qkv_grad.reshape(model_width, 3, width).transpose(1, 0, 2),
            ],
            axis=0,
        )
        full = lax.dynamic_update_slice(
            jnp.zeros((4, model_width, model_width), BF), both, (0, 0, g * width)
        )
        summed = lax.psum_scatter(full, ("yy", "g"), scatter_dimension=2, tiled=True)
        summed = lax.psum_scatter(summed, "head", scatter_dimension=1, tiled=True).astype(F32)
        proj_part, qkv_part = summed[0], summed[1:]

    def spread(values):
        zero = jnp.zeros((parts, g_size, values.shape[0] // parts), F32)
        return lax.dynamic_update_slice(
            zero, values.reshape(parts, 1, values.shape[0] // parts), (0, g, 0)
        ).reshape(-1)

    def spread_hidden(values):
        zero = jnp.zeros((head_size, g_size, hidden), F32)
        return lax.dynamic_update_slice(
            zero, values.reshape(head_size, 1, hidden), (0, g, 0)
        ).reshape(-1)

    vectors = [
        spread(jnp.sum(grad_query_pre.astype(F32), axis=0)),
        spread(jnp.sum(grad_value.astype(F32), axis=0)),
        spread(grad_log),
        jnp.sum(grad_branch.astype(F32), axis=0),
        spread_hidden(jnp.sum(grad_hidden.astype(F32), axis=0)),
        jnp.sum(grad_mlp.astype(F32), axis=0),
    ]
    joined = jnp.concatenate(vectors)
    filler = -joined.shape[0] % 1024
    joined = jnp.pad(joined, (0, filler)).reshape(-1, 128)
    joined = butterfly(joined, ("yy", "g", "head")).reshape(-1)
    totals, start = [], 0
    for vector in vectors:
        totals.append(joined[start : start + vector.shape[0]])
        start += vector.shape[0]
    fc1_bias_grad = pick(totals[4].reshape(head_size, -1), z, 0)
    return (
        output,
        tokens_grad,
        ada_grad,
        ada_bias_grad,
        qkv_part,
        totals[0],
        totals[1],
        totals[2],
        proj_part,
        totals[3],
        up_part,
        fc1_bias_grad,
        down_part,
        totals[5],
    )


def solution(mesh):
    head_size = mesh.shape["head"]
    dp_size = mesh.shape["dp"]
    inner = Mesh(
        mesh.devices.reshape(dp_size // head_size, head_size, head_size), ("yy", "g", "head")
    )
    dp = ("yy", "g")
    everything = ("yy", "g", "head")
    in_specs = (
        P(everything, None),
        P(everything, None),
        P(),
        P(),
        P(),
        P(),
        P(),
        P(),
        P(),
        P(),
        P(),
        P(None, "head"),
        P("head"),
        P("head", None),
        P(),
        P(),
        P(),
        P(dp, None),
        P(everything),
    )
    out_specs = (
        P(everything, None),
        P(everything, None),
        P(None, everything),
        P(everything),
        P(None, "head", dp),
        P(),
        P(),
        P(),
        P("head", dp),
        P(),
        P(dp, "head"),
        P("head"),
        P("head", dp),
        P(),
    )
    return jax.shard_map(
        shards, mesh=inner, in_specs=in_specs, out_specs=out_specs, check_vma=False
    )
```

```python
import functools

import jax
import jax.numpy as jnp
from jax import lax
from jax.experimental import pallas as pl
from jax.experimental.pallas import tpu as pltpu
from jax.sharding import Mesh, PartitionSpec as P

BF = jnp.bfloat16
F32 = jnp.float32
SMEM = pl.BlockSpec(memory_space=pltpu.SMEM)
VMEM = pl.BlockSpec(memory_space=pltpu.VMEM)
ANY = pl.BlockSpec(memory_space=pl.ANY)
PLAIN = ((1,), (0,))
BY_ROW = ((1,), (1,))


def shape_of(shape, dtype):
    return jax.ShapeDtypeStruct(shape, dtype)


def dot(left, right, dims=PLAIN):
    return lax.dot_general(left, right, (dims, ((), ())), preferred_element_type=F32)


def call(name, kernel, operands, specs, outs, scratch=(), flops=0, exps=0):
    size = sum(a.size * a.dtype.itemsize for a, s in zip(operands, specs) if s is VMEM)
    size += sum(o.size * o.dtype.itemsize for o in outs)
    return pl.pallas_call(
        kernel,
        name=name,
        out_shape=tuple(outs),
        in_specs=list(specs),
        out_specs=(VMEM,) * len(outs),
        scratch_shapes=list(scratch),
        compiler_params=pltpu.CompilerParams(vmem_limit_bytes=48 * 1024 * 1024),
        cost_estimate=pl.CostEstimate(flops=flops, bytes_accessed=size, transcendentals=exps),
    )(*operands)


def row_norm(values):
    centre = values - jnp.mean(values, axis=-1, keepdims=True)
    inverse = lax.rsqrt(jnp.mean(centre * centre, axis=-1, keepdims=True) + 1e-06)
    return (centre * inverse, inverse)


def norm_back(gradient, normed, inverse):
    return inverse * (
        gradient
        - jnp.mean(gradient, axis=-1, keepdims=True)
        - normed * jnp.mean(gradient * normed, axis=-1, keepdims=True)
    )


def mod_rows(mod_ref, part, item, width):
    cols = slice(part * width, (part + 1) * width)
    rows = jnp.broadcast_to(mod_ref[0:1, cols], (item.shape[0], width))
    for index in range(1, mod_ref.shape[0]):
        rows = jnp.where(item == index, mod_ref[index : index + 1, cols], rows)
    return rows


def add_item_sums(sums_ref, part, item, values, count):
    width = values.shape[1]
    cols = slice(part * width, (part + 1) * width)
    for index in range(count):
        kept = jnp.where(item == index, values, 0.0)
        sums_ref[index : index + 1, cols] += jnp.sum(kept, axis=0, keepdims=True)


def same_head(width, head_dim):
    row = lax.broadcasted_iota(jnp.int32, (width, width), 0) // head_dim
    col = lax.broadcasted_iota(jnp.int32, (width, width), 1) // head_dim
    return (row == col).astype(BF)


def head_sums(values, same):
    high = values.astype(BF)
    low = (values - high.astype(F32)).astype(BF)
    return dot(high, same) + dot(low, same)


def chunks(rows, size):
    return pl.loop(0, rows // size)


def at(index, size):
    return pl.ds(pl.multiple_of(index * size, size), size)


def first_norm_kernel(x_ref, mod_ref, item_ref, out_ref):
    rows, width = x_ref.shape

    @chunks(rows, 64)
    def _(i):
        r = at(i, 64)
        item = item_ref[r, :]
        normed, _ = row_norm(x_ref[r, :].astype(F32))
        scale, shift = mod_rows(mod_ref, 2, item, width), mod_rows(mod_ref, 4, item, width)
        out_ref[r, :] = (normed * (1.0 + scale) + shift).astype(BF)


def grad_mlp_kernel(up_ref, mod_ref, item_ref, out_ref, sum_ref):
    rows, width = up_ref.shape
    sum_ref[...] = jnp.zeros_like(sum_ref)

    @chunks(rows, 64)
    def _(i):
        r = at(i, 64)
        gamma = mod_rows(mod_ref, 1, item_ref[r, :], width)
        grad = (up_ref[r, :].astype(F32) * gamma).astype(BF)
        out_ref[r, :] = grad
        sum_ref[0:1, :] += jnp.sum(grad.astype(F32), axis=0, keepdims=True)


def load_columns(weight_ref, held, sems, offset_of, parts, sub):
    copies = []
    for t in range(3):
        for p in range(parts):
            copies.append(
                pltpu.make_async_copy(
                    weight_ref.at[t, :, pl.ds(pl.multiple_of(offset_of(p), sub), sub)],
                    held.at[:, pl.ds((t * parts + p) * sub, sub)],
                    sems.at[t * parts + p],
                )
            )
    for copy in copies:
        copy.start()
    return copies


def attend_kernel(dims, *refs):
    group, segs, heads, head_dim, parts, block = dims
    me_ref, first_ref, last_ref, lo_ref, hi_ref, temper_ref, qb_ref, vb_ref, w_ref = refs[:9]
    blocks = refs[9 : 9 + group]
    outs = refs[9 + group :]
    out_ref, out_t_ref, lse_ref, q_ref, k_ref, v_ref, qp_ref, kp_ref = outs[:8]
    held, v_t, out_s, acc, total, sems = outs[8:]
    pack_len, width = q_ref.shape
    rows = blocks[0].shape[0]
    seg, sub = rows // segs, width // parts
    me = me_ref[0]
    copies = load_columns(w_ref, held, sems, lambda p: (p * group + me) * sub, parts, sub)
    same = same_head(width, head_dim)
    for copy in copies:
        copy.wait()
    for k in range(group):
        for y in range(segs):
            ranks = pl.ds(pl.multiple_of((y * group + (me ^ k)) * seg, 16), seg)
            made = dot(blocks[k][y * seg : (y + 1) * seg, :], held[...])
            query = made[:, :width] + qb_ref[...]
            key = made[:, width : 2 * width]
            qp_ref[ranks, :] = query
            kp_ref[ranks, :] = key
            inverse = lax.rsqrt(head_sums(query * query, same) + 1e-06)
            q_ref[ranks, :] = (query * inverse * temper_ref[...]).astype(BF)
            inverse = lax.rsqrt(head_sums(key * key, same) + 1e-06)
            k_ref[ranks, :] = (key * inverse).astype(BF)
            v_ref[ranks, :] = (made[:, 2 * width :] + vb_ref[...]).astype(BF)
    v_t[...] = v_ref[...].T
    lanes = lax.broadcasted_iota(jnp.int32, (1, width), 1) // head_dim

    @pl.loop(0, pack_len // block)
    def _(q_block):
        q_rows = at(q_block, block)
        q_t = q_ref[q_rows, :].T
        low, high = lo_ref[:, q_rows], hi_ref[:, q_rows]
        acc[...] = jnp.zeros_like(acc)
        total[...] = jnp.zeros_like(total)

        @pl.loop(first_ref[q_block], last_ref[q_block])
        def _(k_block):
            k_rows = at(k_block, block)
            keys = k_ref[k_rows, :]
            index = k_block * block + lax.broadcasted_iota(jnp.int32, (block, block), 0)
            seen = (index >= low) & (index < high)
            for h in range(heads):
                own = pl.ds(h * head_dim, head_dim)
                scores = dot(jnp.where(lanes == h, keys, jnp.zeros_like(keys)), q_t)
                raised = jnp.where(seen, jnp.exp(scores), 0.0)
                total[h : h + 1, :] += jnp.sum(raised, axis=0, keepdims=True)
                acc[own, :] += dot(v_t[own, k_rows], raised.astype(BF))

        for h in range(heads):
            own = pl.ds(h * head_dim, head_dim)
            acc[own, :] = acc[own, :] / total[h : h + 1, :]
            lse_ref[h : h + 1, q_rows] = jnp.log(total[h : h + 1, :])
        out_t_ref[:, q_rows] = acc[...]
        out_s[q_rows, :] = acc[...].T.astype(BF)

    for y in range(segs):
        for g in range(group):
            start = (y * group + g) * seg
            out_ref[g, y * seg : (y + 1) * seg, :] = out_s[start : start + seg, :]


def attend_back_kernel(dims, *refs):
    group, segs, heads, head_dim, parts, block = dims
    me_ref, first_ref, last_ref, lo_ref, hi_ref, temper_ref, w_ref, in_ref = refs[:8]
    q_ref, k_ref, v_ref, qp_ref, kp_ref, out_t_ref, lse_ref = refs[8:15]
    sent = refs[15 : 15 + group]
    dqkv_ref, sums_ref = refs[15 + group : 17 + group]
    held, g_s, k_t, dq_s, dk_acc, dv_acc, acc, sums, sems = refs[17 + group :]
    pack_len, width = q_ref.shape
    rows = in_ref.shape[1]
    seg, sub = rows // segs, width // parts
    me = me_ref[0]
    copies = load_columns(w_ref, held, sems, lambda p: (p * group + me) * sub, parts, sub)
    for y in range(segs):
        for g in range(group):
            start = (y * group + g) * seg
            g_s[start : start + seg, :] = in_ref[g, y * seg : (y + 1) * seg, :]
    lanes = lax.broadcasted_iota(jnp.int32, (1, width), 1) // head_dim
    k_t[...] = k_ref[...].T
    dk_acc[...] = jnp.zeros_like(dk_acc)
    dv_acc[...] = jnp.zeros_like(dv_acc)

    @pl.loop(0, pack_len // block)
    def _(q_block):
        q_rows = at(q_block, block)
        queries, grads = q_ref[q_rows, :], g_s[q_rows, :]
        q_t, g_t = queries.T, grads.T
        low, high = lo_ref[:, q_rows], hi_ref[:, q_rows]
        weighted = g_t.astype(F32) * out_t_ref[:, q_rows]
        for h in range(heads):
            sums[h : h + 1, :] = jnp.sum(
                weighted[h * head_dim : (h + 1) * head_dim, :], axis=0, keepdims=True
            )
        acc[...] = jnp.zeros_like(acc)

        @pl.loop(first_ref[q_block], last_ref[q_block])
        def _(k_block):
            k_rows = at(k_block, block)
            keys, values = k_ref[k_rows, :], v_ref[k_rows, :]
            index = k_block * block + lax.broadcasted_iota(jnp.int32, (block, block), 0)
            seen = (index >= low) & (index < high)
            for h in range(heads):
                own = pl.ds(h * head_dim, head_dim)
                mine = lanes == h
                scores = dot(jnp.where(mine, keys, jnp.zeros_like(keys)), q_t)
                probs = jnp.where(seen, jnp.exp(scores - lse_ref[h : h + 1, q_rows]), 0.0)
                grad_probs = dot(jnp.where(mine, values, jnp.zeros_like(values)), g_t)
                grad_scores = (probs * (grad_probs - sums[h : h + 1, :])).astype(BF)
                acc[own, :] += dot(k_t[own, k_rows], grad_scores)
                dk_acc[k_rows, :] += dot(
                    grad_scores, jnp.where(mine, queries, jnp.zeros_like(queries))
                )
                dv_acc[k_rows, :] += dot(
                    probs.astype(BF), jnp.where(mine, grads, jnp.zeros_like(grads))
                )

        dq_s[q_rows, :] = acc[...].T

    for copy in copies:
        copy.wait()
    same = same_head(width, head_dim)
    sums_ref[...] = jnp.zeros_like(sums_ref)

    def back(gradient, pre):
        inverse = lax.rsqrt(head_sums(pre * pre, same) + 1e-06)
        unit = pre * inverse
        return inverse * (gradient - unit * head_sums(gradient * unit, same)), unit

    for k in range(group):
        for y in range(segs):
            ranks = pl.ds(pl.multiple_of((y * group + (me ^ k)) * seg, 16), seg)
            own = slice(k * rows + y * seg, k * rows + (y + 1) * seg)
            grad = dq_s[ranks, :].astype(BF).astype(F32) * temper_ref[...]
            grad_query, unit = back(grad, qp_ref[ranks, :])
            grad_query = grad_query.astype(BF)
            grad_key, _ = back(dk_acc[ranks, :].astype(BF).astype(F32), kp_ref[ranks, :])
            grad_value = dv_acc[ranks, :].astype(BF)
            dqkv_ref[own, :width] = grad_query
            dqkv_ref[own, width : 2 * width] = grad_key.astype(BF)
            dqkv_ref[own, 2 * width :] = grad_value
            for index, values in enumerate((grad_query, grad_value, grad * unit)):
                sums_ref[index : index + 1, :] += jnp.sum(
                    values.astype(F32), axis=0, keepdims=True
                )
        sent[k][...] = dot(
            dqkv_ref[k * rows : (k + 1) * rows, :], held[...], BY_ROW
        ).astype(BF)


def project_kernel(
    parts, ret_ref, wp_ref, pb_ref, x_ref, mod_ref, item_ref, attn_ref, branch_ref, middle_ref, out_ref
):
    group, rows, width = ret_ref.shape
    model = x_ref.shape[1]
    sub = width // parts
    for g in range(group):
        for p in range(parts):
            start = (p * group + g) * sub
            attn_ref[:, start : start + sub] = ret_ref[g, :, p * sub : (p + 1) * sub]
    branch_ref[...] = dot(attn_ref[...], wp_ref[...]) + pb_ref[...].astype(F32)

    @chunks(rows, 64)
    def _(i):
        r = at(i, 64)
        item = item_ref[r, :]
        middle = x_ref[r, :].astype(F32) + mod_rows(mod_ref, 0, item, model) * branch_ref[r, :]
        middle_ref[r, :] = middle
        normed, _ = row_norm(middle)
        scale, shift = mod_rows(mod_ref, 3, item, model), mod_rows(mod_ref, 5, item, model)
        out_ref[r, :] = (normed * (1.0 + scale) + shift).astype(BF)


def load_tiles(tiles_ref, held, sems, first, depth):
    count_a, count_b = tiles_ref.shape[:2]
    tall = held.shape[0] // (count_a if depth == 0 else count_b)
    wide = held.shape[1] // (count_b if depth == 0 else count_a)
    copies = []
    for a in range(count_a):
        for b in range(count_b):
            r, c = (a, b) if depth == 0 else (b, a)
            copies.append(
                pltpu.make_async_copy(
                    tiles_ref.at[a, b, pl.ds(0, tall), :],
                    held.at[pl.ds(r * tall, tall), pl.ds(c * wide, wide)],
                    sems.at[first + a * count_b + b],
                )
            )
    for copy in copies:
        copy.start()
    return copies


def feed_kernel(count, *refs):
    fc1_ref, fc2_ref, b1_ref = refs[:3]
    ins = refs[3 : 3 + count]
    grads = refs[3 + count : 3 + 2 * count]
    rest = refs[3 + 2 * count :]
    back, outs = rest[:count], rest[count : 2 * count]
    act_ref, gh_ref, sum_ref, w1, w2, pre, grad, sems = rest[2 * count :]
    tiles = fc1_ref.shape[0] * fc1_ref.shape[1]
    first = load_tiles(fc1_ref, w1, sems, 0, 0)
    second = load_tiles(fc2_ref, w2, sems, tiles, 1)
    rows = ins[0].shape[0]
    sum_ref[...] = jnp.zeros_like(sum_ref)
    for copy in first:
        copy.wait()
    for k in range(count):
        pre[...] = dot(ins[k][...], w1[...]) + b1_ref[...]
        if k == 0:
            for copy in second:
                copy.wait()
        grad[...] = dot(grads[k][...], w2[...], BY_ROW)

        @chunks(rows, 32)
        def _(i):
            r = at(i, 32)
            to = pl.ds(pl.multiple_of(k * rows + i * 32, 32), 32)
            value = pre[r, :]
            square = value * value
            gate = jnp.tanh(value * (0.7978845608028654 + 0.035677408136300125 * square))
            half = 0.5 + 0.5 * gate
            act = value * half
            slope = half + act * (1.0 - gate) * (0.7978845608028654 + 0.10703222440890037 * square)
            back_grad = (slope * grad[r, :]).astype(BF)
            act_ref[to, :] = act.astype(BF)
            gh_ref[to, :] = back_grad
            sum_ref[0:1, :] += jnp.sum(back_grad.astype(F32), axis=0, keepdims=True)

        own = slice(k * rows, (k + 1) * rows)
        back[k][...] = dot(gh_ref[own, :], w1[...], BY_ROW).astype(BF)
        outs[k][...] = dot(act_ref[own, :], w2[...]).astype(BF)


def feed_weights_kernel(dims, *refs):
    count, group, split = dims
    me_ref, act_ref, gh_ref = refs[:3]
    ins = refs[3 : 3 + count]
    grads = refs[3 + count : 3 + 2 * count]
    up_ref, down_ref, left_t, right, act_t = refs[3 + 2 * count :]
    rows, model = ins[0].shape
    for k in range(count):
        own = slice(k * rows, (k + 1) * rows)
        left_t[:, own] = ins[k][...].T
        right[own, :] = grads[k][...]
    act_t[...] = act_ref[...].T
    part = model // split
    fine = part // group
    head_size = up_ref.shape[2]
    hidden = up_ref.shape[4]
    for y in range(split):
        start = pl.multiple_of((me_ref[1] ^ y) * part, part) if split > 1 else 0
        for z in range(head_size):
            cols = slice(z * hidden, (z + 1) * hidden)
            made = dot(left_t[pl.ds(start, part), :], gh_ref[:, cols]).astype(BF)
            for g in range(group):
                up_ref[y, g, z] = made[g * fine : (g + 1) * fine, :]
            made = dot(act_t[cols, :], right[:, pl.ds(start, part)]).astype(BF)
            for g in range(group):
                down_ref[y, g, z] = made[:, g * fine : (g + 1) * fine]


def middle_back_kernel(
    dims, kept_ref, came_ref, middle_ref, branch_ref, up_ref, mod_ref, item_ref, wp_ref,
    out_ref, gb_ref, gm_ref, sums_ref, col_ref, attn,
):
    parts, items = dims
    rows, model = middle_ref.shape
    group, _, width = out_ref.shape
    sub = width // parts
    sums_ref[...] = jnp.zeros_like(sums_ref)
    col_ref[...] = jnp.zeros_like(col_ref)

    @chunks(rows, 64)
    def _(i):
        r = at(i, 64)
        item = item_ref[r, :]
        grad_in = kept_ref[r, :].astype(F32) + came_ref[r, :].astype(F32)
        normed, inverse = row_norm(middle_ref[r, :])
        scale = mod_rows(mod_ref, 3, item, model)
        grad_middle = up_ref[r, :].astype(F32) + norm_back(grad_in * (1.0 + scale), normed, inverse)
        gm_ref[r, :] = grad_middle
        grad_branch = (grad_middle * mod_rows(mod_ref, 0, item, model)).astype(BF)
        gb_ref[r, :] = grad_branch
        col_ref[0:1, :] += jnp.sum(grad_branch.astype(F32), axis=0, keepdims=True)
        add_item_sums(sums_ref, 0, item, grad_middle * branch_ref[r, :], items)
        add_item_sums(sums_ref, 1, item, grad_in * normed, items)
        add_item_sums(sums_ref, 2, item, grad_in, items)

    attn[...] = dot(gb_ref[...], wp_ref[...], BY_ROW).astype(BF)
    for g in range(group):
        for p in range(parts):
            start = (p * group + g) * sub
            out_ref[g, :, p * sub : (p + 1) * sub] = attn[:, start : start + sub]


def output_kernel(
    items, kept_ref, came_ref, middle_ref, up_ref, mod_ref, item_ref, bias_ref, out_ref, sums_ref
):
    rows, model = middle_ref.shape
    sums_ref[...] = jnp.zeros_like(sums_ref)

    @chunks(rows, 64)
    def _(i):
        r = at(i, 64)
        item = item_ref[r, :]
        made = kept_ref[r, :].astype(F32) + came_ref[r, :].astype(F32) + bias_ref[...].astype(F32)
        gamma = mod_rows(mod_ref, 1, item, model)
        out_ref[r, :] = (middle_ref[r, :] + gamma * made).astype(BF)
        add_item_sums(sums_ref, 0, item, up_ref[r, :].astype(F32) * made, items)


def tokens_back_kernel(
    items, kept_ref, came_ref, x_ref, gm_ref, mod_ref, item_ref, out_ref, sums_ref
):
    rows, model = x_ref.shape
    sums_ref[...] = jnp.zeros_like(sums_ref)

    @chunks(rows, 64)
    def _(i):
        r = at(i, 64)
        item = item_ref[r, :]
        grad_in = kept_ref[r, :].astype(F32) + came_ref[r, :].astype(F32)
        normed, inverse = row_norm(x_ref[r, :].astype(F32))
        scale = mod_rows(mod_ref, 2, item, model)
        out_ref[r, :] = (
            gm_ref[r, :] + norm_back(grad_in * (1.0 + scale), normed, inverse)
        ).astype(BF)
        add_item_sums(sums_ref, 0, item, grad_in * normed, items)
        add_item_sums(sums_ref, 1, item, grad_in, items)


def proj_weights_kernel(dims, me_ref, attn_ref, gb_ref, *refs):
    group, parts, split = dims
    outs, left_t, right = refs[:group], refs[group], refs[group + 1]
    left_t[...] = attn_ref[...].T
    chunk, head_size, tall, wide = outs[0].shape
    for k in range(group):
        for y in range(chunk):
            part = (me_ref[1] ^ y) if split else y
            start = pl.multiple_of((part * group + (me_ref[0] ^ k)) * wide, wide)
            right[:, y * wide : (y + 1) * wide] = gb_ref[:, pl.ds(start, wide)]
        made = dot(left_t[...], right[...]).astype(BF)
        for y in range(chunk):
            for z in range(head_size):
                outs[k][y, z] = made[z * tall : (z + 1) * tall, y * wide : (y + 1) * wide]


def qkv_weights_kernel(dims, me_ref, dqkv_ref, *refs):
    count, parts, split = dims
    ins, (out_ref, left_t, right) = refs[:count], refs[count:]
    rows = ins[0].shape[0]
    for k in range(count):
        left_t[:, k * rows : (k + 1) * rows] = ins[k][...].T
    chunk, head_size, _, tall, wide = out_ref.shape
    for y in range(chunk):
        part = (me_ref[1] ^ y) if split else y
        for t in range(3):
            start = pl.multiple_of((t * parts + part) * wide, wide)
            right[:, t * wide : (t + 1) * wide] = dqkv_ref[:, pl.ds(start, wide)]
        made = dot(left_t[...], right[...]).astype(BF)
        for z in range(head_size):
            for t in range(3):
                out_ref[y, z, t] = made[z * tall : (z + 1) * tall, t * wide : (t + 1) * wide]


def to_packs(rows):
    return lax.all_to_all(rows, ("yy", "head"), split_axis=0, concat_axis=0, tiled=True)


def over_group(blocks):
    return lax.all_to_all(blocks, "g", split_axis=0, concat_axis=0, tiled=True)


def bits(count):
    steps = []
    while count > 1:
        count //= 2
        steps.append(count)
    return steps


def xor_swap(values, axis, step):
    size = lax.axis_size(axis)
    return lax.ppermute(values, axis, [(i, i ^ step) for i in range(size)])


def xor_gather(block, axis):
    blocks = {0: block}
    for step in bits(lax.axis_size(axis)):
        for k in list(blocks):
            blocks[k ^ step] = xor_swap(blocks[k], axis, step)
    return [blocks[k] for k in range(len(blocks))]


def xor_scatter(blocks, axis):
    blocks = dict(enumerate(blocks))
    for step in reversed(bits(lax.axis_size(axis))):
        kept = {}
        for k in blocks:
            if not k & step:
                kept[k] = (blocks[k], xor_swap(blocks[k ^ step], axis, step))
        if len(kept) == 1:
            return kept[0]
        blocks = {k: add_low(*pair) for k, pair in kept.items()}


def add_low(left, right):
    return (left.astype(F32) + right.astype(F32)).astype(left.dtype)


def butterfly(values, axes):
    for axis in axes:
        for step in reversed(bits(lax.axis_size(axis))):
            values = values + xor_swap(values, axis, step)
    return values


def pick(values, index, axis):
    return lax.dynamic_index_in_dim(values, index, axis, keepdims=False)


def xor_blocks(values, axis, dim):
    me = lax.axis_index(axis)
    return [pick(values, me ^ k, dim) for k in range(lax.axis_size(axis))]


def tie(*values):
    return lax.optimization_barrier(values)


def shards(
    tokens,
    cotangent,
    class_table,
    ada_weight,
    ada_bias,
    qkv_weight,
    q_bias,
    v_bias,
    log_scale,
    proj_weight,
    proj_bias,
    fc1_weight,
    fc1_bias,
    fc2_weight,
    fc2_bias,
    item_lens,
    class_ids,
    section_ids,
    destination,
):
    segs = lax.axis_size("yy")
    group = lax.axis_size("g")
    head_size = lax.axis_size("head")
    yy, g, z = lax.axis_index("yy"), lax.axis_index("g"), lax.axis_index("head")
    me = jnp.stack([g, yy]).astype(jnp.int32)
    pack = yy * head_size + z
    rows, model = tokens.shape
    heads_all = log_scale.shape[0]
    head_dim = model // heads_all
    heads = heads_all // group
    width = model // group
    dp_size = segs * group
    pack_len = rows * head_size
    seg = rows // segs
    items = item_lens.shape[1]
    block = min(256, pack_len)
    col = model // dp_size
    parts = segs if col % 128 == 0 else 1
    sub = width // parts

    def own_cols(values):
        return pick(values.reshape(parts, group, sub), g, 1).reshape(1, width)

    row_pack = destination // pack_len
    index = jnp.arange(rows, dtype=jnp.int32)
    before = (row_pack[None, :] < row_pack[:, None]) | (
        (row_pack[None, :] == row_pack[:, None]) & (index[None, :] < index[:, None])
    )
    slot = jnp.sum(before.astype(jnp.int32), axis=1)
    to_slot = (slot[None, :] == index[:, None]).astype(BF)
    sorted_tokens = dot(to_slot, tokens).astype(BF)
    sorted_cotangent = dot(to_slot, cotangent).astype(BF)
    inputs = to_packs(sorted_tokens)

    hidden = fc1_weight.shape[1] // group
    units = head_size * hidden
    half = model // segs
    fc1_own = lax.dynamic_slice(fc1_weight, (yy * half, g * hidden), (half, hidden))
    fc1_bias_own = lax.dynamic_slice(fc1_bias, (g * hidden,), (hidden,))
    fc1_sent = jnp.concatenate(
        [fc1_own, jnp.broadcast_to(fc1_bias_own[None, :], (16, hidden))], axis=0
    )
    fc1_all = lax.all_gather(fc1_sent, ("yy", "head"), axis=0)
    fc1_all = fc1_all.reshape(segs, head_size, half + 16, hidden)
    fc2_own = lax.dynamic_slice(fc2_weight, (g * hidden, yy * half), (hidden, half))
    fc2_all = lax.all_gather(fc2_own, ("yy", "head"), axis=0)
    fc2_all = fc2_all.reshape(segs, head_size, hidden, half)
    fc1_bias_here = fc1_all[0, :, half].reshape(1, units).astype(F32)
    tiled = hidden % 128 == 0
    if not tiled:
        fc1_all = fc1_all[:, :, :half].transpose(0, 2, 1, 3).reshape(1, 1, model, units)
        fc2_all = fc2_all.transpose(1, 2, 0, 3).reshape(1, 1, units, model)

    lens_here = pick(item_lens, pack, 0)
    class_here = pick(class_ids, pack, 0)
    order_key = class_here * items + jnp.arange(items, dtype=jnp.int32)
    item_rank = jnp.sum(
        jnp.where(order_key[None, :] < order_key[:, None], lens_here[None, :], 0), axis=1
    )
    item_pos = jnp.cumsum(lens_here) - lens_here
    item_end = item_rank + lens_here

    def items_of(rank):
        return (rank[:, None] >= item_rank[None, :]) & (rank[:, None] < item_end[None, :])

    rank_all = jnp.arange(pack_len, dtype=jnp.int32)
    member = items_of(rank_all)

    def of_item(values):
        return jnp.sum(jnp.where(member, values[None, :], 0), axis=1)

    section_here = lax.ppermute(
        section_ids[0],
        ("g", "head"),
        [(a * head_size + b, b * head_size + a) for a in range(group) for b in range(head_size)],
    )
    position = rank_all - of_item(item_rank - item_pos)
    section_rank = jnp.sum(
        jnp.where(rank_all[None, :] == position[:, None], section_here[None, :], 0), axis=1
    )
    up_to = jnp.sum((section_here[None, :] <= section_rank[:, None]).astype(jnp.int32), axis=1)
    low = of_item(item_rank)
    high = jnp.minimum(up_to + of_item(item_rank - item_pos), of_item(item_end))
    first = low[::block] // block
    last = (high[block - 1 :: block] + block - 1) // block
    low, high = low[None, :], high[None, :]

    row_rank = (
        (jnp.arange(segs, dtype=jnp.int32)[:, None] * group + g) * seg
        + jnp.arange(seg, dtype=jnp.int32)[None, :]
    ).reshape(rows)
    row_item = jnp.sum(
        jnp.where(items_of(row_rank), jnp.arange(items, dtype=jnp.int32)[None, :], 0), axis=1
    )[:, None]

    class_rows = jnp.take(class_table, class_ids.reshape(-1), axis=0).astype(F32)
    silu_cond = jax.nn.silu(class_rows).astype(BF)
    silu_here = lax.dynamic_slice_in_dim(silu_cond, pack * items, items, 0)
    mod = jnp.dot(silu_here, ada_weight, preferred_element_type=F32) + ada_bias.astype(F32)

    (attn_in,) = call("first_norm",
        first_norm_kernel, (inputs, mod, row_item), (VMEM,) * 3, (shape_of((rows, model), BF),)
    )
    attn_blocks = xor_gather(attn_in, "g")
    sorted_cotangent, _ = tie(sorted_cotangent, inputs)
    upstream = to_packs(sorted_cotangent)
    grad_mlp, grad_mlp_sum = call("grad_mlp",
        grad_mlp_kernel,
        (upstream, mod, row_item),
        (VMEM,) * 3,
        (shape_of((rows, model), BF), shape_of((8, model), F32)),
    )
    grad_blocks = xor_gather(grad_mlp, "g")
    per_part = sub // head_dim
    scale_here = pick(log_scale.reshape(parts, group, per_part), g, 1).reshape(heads)
    temper = jnp.repeat(jnp.exp(scale_here), head_dim)[None, :]
    dims = (group, segs, heads, head_dim, parts, block)
    pairs = heads * pack_len * pack_len // 2
    wide = shape_of((pack_len, width), BF)
    wide_f32 = shape_of((pack_len, width), F32)
    out_blocks, out_t, lse, queries, keys, values, query_pre, key_pre = call("attend",
        functools.partial(attend_kernel, dims),
        (me, first, last, low, high, temper, own_cols(q_bias).astype(F32),
         own_cols(v_bias).astype(F32), qkv_weight, *attn_blocks),
        (SMEM, SMEM, SMEM) + (VMEM,) * 5 + (ANY,) + (VMEM,) * group,
        (shape_of((group, rows, width), BF), shape_of((width, pack_len), F32),
         shape_of((8, pack_len), F32), wide, wide, wide, wide_f32, wide_f32),
        [
            pltpu.VMEM((model, 3 * width), BF),
            pltpu.VMEM((width, pack_len), BF),
            pltpu.VMEM((pack_len, width), BF),
            pltpu.VMEM((width, block), F32),
            pltpu.VMEM((8, block), F32),
            pltpu.SemaphoreType.DMA((3 * parts,)),
        ],
        flops=4 * pairs * head_dim + 6 * pack_len * model * width,
        exps=pairs,
    )
    returned = over_group(out_blocks)
    rows_bf, rows_f32 = shape_of((rows, model), BF), shape_of((rows, model), F32)
    attn_rows, branch, middle, mlp_in = call("project",
        functools.partial(project_kernel, parts),
        (returned, proj_weight, proj_bias[None, :], inputs, mod, row_item),
        (VMEM,) * 6,
        (rows_bf, rows_f32, rows_f32, rows_bf),
        flops=2 * rows * model * model,
    )

    mlp_blocks = xor_gather(mlp_in, "g")
    tiles = fc1_all.shape[0] * fc1_all.shape[1]
    made = call("feed",
        functools.partial(feed_kernel, group),
        (fc1_all, fc2_all, fc1_bias_here, *mlp_blocks, *grad_blocks),
        (ANY, ANY) + (VMEM,) * (1 + 2 * group),
        (rows_bf,) * (2 * group)
        + (shape_of((pack_len, units), BF),) * 2
        + (shape_of((8, units), F32),),
        [
            pltpu.VMEM((model, units), BF),
            pltpu.VMEM((units, model), BF),
            pltpu.VMEM((rows, units), F32),
            pltpu.VMEM((rows, units), F32),
            pltpu.SemaphoreType.DMA((2 * tiles,)),
        ],
        flops=8 * pack_len * model * units,
        exps=pack_len * units,
    )
    back_parts, out_parts = made[:group], made[group : 2 * group]
    act, grad_hidden, grad_hidden_sum = made[2 * group :]
    grad_in_pair = xor_scatter(back_parts, "g")
    out_pair = xor_scatter(out_parts, "g")
    if tiled:
        up_shape = (segs, group, head_size, half // group, hidden)
        down_shape = (segs, group, head_size, hidden, half // group)
        feed_dims = (group, group, segs)
    else:
        up_shape, down_shape = (1, 1, 1, model, units), (1, 1, 1, units, model)
        feed_dims = (group, 1, 1)
    up_grad, down_grad = call("feed_weights",
        functools.partial(feed_weights_kernel, feed_dims),
        (me, act, grad_hidden, *mlp_blocks, *grad_blocks),
        (SMEM,) + (VMEM,) * (2 + 2 * group),
        (shape_of(up_shape, BF), shape_of(down_shape, BF)),
        [
            pltpu.VMEM((model, pack_len), BF),
            pltpu.VMEM((pack_len, model), BF),
            pltpu.VMEM((units, pack_len), BF),
        ],
        flops=4 * pack_len * model * units,
    )
    if not tiled:
        fine = half // group
        up_grad = up_grad.reshape(segs, group, fine, head_size, hidden).transpose(0, 1, 3, 2, 4)
        down_grad = down_grad.reshape(head_size, hidden, segs, group, fine)
        down_grad = down_grad.transpose(2, 3, 0, 1, 4)
        up_grad = jnp.stack(xor_blocks(up_grad, "yy", 0))
        down_grad = jnp.stack(xor_blocks(down_grad, "yy", 0))

    def sum_tiles(tiles):
        half_sum = add_low(*xor_scatter([tiles[y] for y in range(segs)], "yy"))
        shape = half_sum.shape[2:]
        came = lax.all_to_all(
            half_sum.reshape(group * head_size, *shape), ("g", "head"), 0, 0, tiled=True
        )
        return jnp.sum(came.reshape(group, head_size, *shape).astype(F32), axis=1)

    up_sum, down_sum = sum_tiles(up_grad), sum_tiles(down_grad)
    up_part = up_sum.transpose(1, 0, 2).reshape(half // group, group * hidden)
    down_part = down_sum.reshape(group * hidden, half // group)

    outbound, grad_branch, grad_middle, middle_sums, branch_sum = call("middle_back",
        functools.partial(middle_back_kernel, (parts, items)),
        (*grad_in_pair, middle, branch, upstream, mod, row_item, proj_weight),
        (VMEM,) * 8,
        (shape_of((group, rows, width), BF), rows_bf, rows_f32, shape_of((8, 3 * model), F32),
         shape_of((8, model), F32)),
        [pltpu.VMEM((rows, model), BF)],
        flops=2 * rows * model * model,
    )
    inbound = over_group(outbound)
    output_rows, output_sums = call("output",
        functools.partial(output_kernel, items),
        (*out_pair, middle, upstream, mod, row_item, fc2_bias[None, :]),
        (VMEM,) * 7,
        (rows_bf, shape_of((8, model), F32)),
    )
    proj_parts = call("proj_weights",
        functools.partial(proj_weights_kernel, (group, parts, parts == segs)),
        (me, attn_rows, grad_branch),
        (SMEM, VMEM, VMEM),
        (shape_of((parts, head_size, model // head_size, sub), BF),) * group,
        [pltpu.VMEM((model, rows), BF), pltpu.VMEM((rows, width), BF)],
        flops=2 * rows * model * model,
    )
    proj_own = add_low(*xor_scatter(proj_parts, "g"))
    made = call("attend_back",
        functools.partial(attend_back_kernel, dims),
        (me, first, last, low, high, temper, qkv_weight, inbound, queries, keys, values,
         query_pre, key_pre, out_t, lse),
        (SMEM, SMEM, SMEM, VMEM, VMEM, VMEM, ANY) + (VMEM,) * 8,
        (rows_bf,) * group + (shape_of((pack_len, 3 * width), BF), shape_of((8, width), F32)),
        [
            pltpu.VMEM((model, 3 * width), BF),
            pltpu.VMEM((pack_len, width), BF),
            pltpu.VMEM((width, pack_len), BF),
            pltpu.VMEM((pack_len, width), F32),
            pltpu.VMEM((pack_len, width), F32),
            pltpu.VMEM((pack_len, width), F32),
            pltpu.VMEM((width, block), F32),
            pltpu.VMEM((8, block), F32),
            pltpu.SemaphoreType.DMA((3 * parts,)),
        ],
        flops=10 * pairs * head_dim + 6 * pack_len * model * width,
        exps=pairs,
    )
    grad_qkv, qkv_sums = made[group:]
    attn_pair = xor_scatter(made[:group], "g")
    (qkv_grad,) = call("qkv_weights",
        functools.partial(qkv_weights_kernel, (group, parts, parts == segs)),
        (me, grad_qkv, *attn_blocks),
        (SMEM,) + (VMEM,) * (1 + group),
        (shape_of((parts, head_size, 3, model // head_size, sub), BF),),
        [pltpu.VMEM((model, pack_len), BF), pltpu.VMEM((pack_len, 3 * sub), BF)],
        flops=6 * pack_len * model * width,
    )
    tokens_grad_rows, tokens_sums = call("tokens_back",
        functools.partial(tokens_back_kernel, items),
        (*attn_pair, inputs, grad_middle, mod, row_item),
        (VMEM,) * 6,
        (rows_bf, shape_of((8, 2 * model), F32)),
    )

    def to_data(values):
        return dot(to_slot, to_packs(values), ((0,), (0,)))

    output = to_data(output_rows).astype(BF)
    tokens_grad = to_data(tokens_grad_rows)

    item_part = jnp.concatenate(
        [
            middle_sums[:items, :model],
            output_sums[:items],
            tokens_sums[:items, :model],
            middle_sums[:items, model : 2 * model],
            tokens_sums[:items, model:],
            middle_sums[:items, 2 * model :],
        ],
        axis=1,
    )
    ada_cols = 6 * model // (dp_size * head_size)
    item_part = item_part.reshape(items, segs, group, head_size, ada_cols)
    item_own = add_low(*xor_scatter(xor_blocks(item_part, "g", 2), "g"))
    item_all = to_packs(
        item_own.reshape(items, segs * head_size, ada_cols).transpose(1, 0, 2)
    )
    item_low = item_all.reshape(-1, ada_cols).astype(BF)
    ada_grad = dot(silu_cond, item_low, ((0,), (0,)))
    ada_bias_grad = jnp.sum(item_low.astype(F32), axis=0)

    both = jnp.concatenate([proj_own[:, :, None], qkv_grad], axis=2)
    if parts == segs:
        half_sum = add_low(*xor_scatter([both[y] for y in range(segs)], "yy"))
        came = lax.all_to_all(half_sum, "head", 0, 0, tiled=True)
        summed = jnp.sum(came.astype(F32), axis=0)
    else:
        both = both.transpose(2, 1, 3, 0, 4).reshape(4, model, width)
        full = lax.dynamic_update_slice(
            jnp.zeros((4, model, model), BF), both, (0, 0, g * width)
        )
        summed = lax.psum_scatter(full, ("yy", "g"), scatter_dimension=2, tiled=True)
        summed = lax.psum_scatter(summed, "head", scatter_dimension=1, tiled=True).astype(F32)
    proj_part, qkv_part = summed[0], summed[1:]

    def spread(values, count, size):
        zero = jnp.zeros((count, group, size), F32)
        return lax.dynamic_update_slice(zero, values.reshape(count, 1, size), (0, g, 0)).reshape(-1)

    log_sums = jnp.sum(qkv_sums[2].reshape(heads, head_dim), axis=1)
    vectors = [
        spread(qkv_sums[0], parts, sub),
        spread(qkv_sums[1], parts, sub),
        spread(log_sums, parts, per_part),
        branch_sum[0],
        spread(grad_hidden_sum[0], head_size, hidden),
        grad_mlp_sum[0],
    ]
    joined = jnp.concatenate(vectors)
    filler = -joined.shape[0] % 1024
    joined = jnp.pad(joined, (0, filler)).reshape(-1, 128)
    joined = butterfly(joined, ("yy", "g", "head")).reshape(-1)
    totals, start = [], 0
    for vector in vectors:
        totals.append(joined[start : start + vector.shape[0]])
        start += vector.shape[0]
    fc1_bias_grad = pick(totals[4].reshape(head_size, -1), z, 0)
    return (
        output,
        tokens_grad,
        ada_grad,
        ada_bias_grad,
        qkv_part,
        totals[0],
        totals[1],
        totals[2],
        proj_part,
        totals[3],
        up_part,
        fc1_bias_grad,
        down_part,
        totals[5],
    )


def solution(mesh):
    head_size = mesh.shape["head"]
    dp_size = mesh.shape["dp"]
    inner = Mesh(
        mesh.devices.reshape(dp_size // head_size, head_size, head_size), ("yy", "g", "head")
    )
    dp = ("yy", "g")
    everything = ("yy", "g", "head")
    in_specs = (
        P(everything, None),
        P(everything, None),
        P(),
        P(),
        P(),
        P(),
        P(),
        P(),
        P(),
        P(),
        P(),
        P(None, "head"),
        P("head"),
        P("head", None),
        P(),
        P(),
        P(),
        P(dp, None),
        P(everything),
    )
    out_specs = (
        P(everything, None),
        P(everything, None),
        P(None, everything),
        P(everything),
        P(None, "head", dp),
        P(),
        P(),
        P(),
        P("head", dp),
        P(),
        P(dp, "head"),
        P("head"),
        P("head", dp),
        P(),
    )
    return jax.shard_map(
        shards, mesh=inner, in_specs=in_specs, out_specs=out_specs, check_vma=False
    )
```

```python
import functools

import jax
import jax.numpy as jnp
from jax import lax
from jax.experimental import pallas as pl
from jax.experimental.pallas import tpu as pltpu
from jax.sharding import Mesh, PartitionSpec as P

BF = jnp.bfloat16
F32 = jnp.float32
SMEM = pl.BlockSpec(memory_space=pltpu.SMEM)
VMEM = pl.BlockSpec(memory_space=pltpu.VMEM)
ANY = pl.BlockSpec(memory_space=pl.ANY)
HBM = "hbm"
LIMIT = 40
PLAIN = ((1,), (0,))
BY_ROW = ((1,), (1,))


def shape_of(shape, dtype):
    return jax.ShapeDtypeStruct(shape, dtype)


def dot(left, right, dims=PLAIN):
    return lax.dot_general(left, right, (dims, ((), ())), preferred_element_type=F32)


def call(name, kernel, operands, specs, outs, scratch=(), limit=LIMIT, out_specs=None):
    out_specs = out_specs or tuple(HBM if o.size >= 65536 else VMEM for o in outs)
    n_in, n_out, n_scratch = len(specs), len(outs), len(scratch)
    staged_in = [i for i, spec in enumerate(specs) if spec is HBM]
    staged_out = [i for i, spec in enumerate(out_specs) if spec is HBM]
    staged = [pltpu.VMEM(operands[i].shape, operands[i].dtype) for i in staged_in]
    staged += [pltpu.VMEM(outs[i].shape, outs[i].dtype) for i in staged_out]
    sems = [pltpu.SemaphoreType.DMA((len(staged),))] if staged else []

    def body(*refs):
        given, made = list(refs[:n_in]), list(refs[n_in : n_in + n_out])
        own = refs[n_in + n_out : n_in + n_out + n_scratch]
        held = refs[n_in + n_out + n_scratch :]
        copies = []
        for place, i in enumerate(staged_in):
            copies.append(pltpu.make_async_copy(given[i], held[place], held[-1].at[place]))
            copies[-1].start()
            given[i] = held[place]
        backs = []
        for place, i in enumerate(staged_out, len(staged_in)):
            backs.append(pltpu.make_async_copy(held[place], made[i], held[-1].at[place]))
            made[i] = held[place]
        for copy in copies:
            copy.wait()
        kernel(*given, *made, *own)
        for copy in backs:
            copy.start()
        for copy in backs:
            copy.wait()

    return pl.pallas_call(
        body,
        name=name,
        out_shape=tuple(outs),
        in_specs=[ANY if spec is HBM else spec for spec in specs],
        out_specs=tuple(ANY if spec is HBM else spec for spec in out_specs),
        scratch_shapes=list(scratch) + staged + sems,
        compiler_params=pltpu.CompilerParams(vmem_limit_bytes=limit * 1024 * 1024),
        cost_estimate=pl.CostEstimate(flops=1, bytes_accessed=1, transcendentals=0),
    )(*operands)


def row_norm(values):
    centre = values - jnp.mean(values, axis=-1, keepdims=True)
    inverse = lax.rsqrt(jnp.mean(centre * centre, axis=-1, keepdims=True) + 1e-06)
    return (centre * inverse, inverse)


def norm_back(gradient, normed, inverse):
    return inverse * (
        gradient
        - jnp.mean(gradient, axis=-1, keepdims=True)
        - normed * jnp.mean(gradient * normed, axis=-1, keepdims=True)
    )


def mod_rows(mod_ref, part, item, width):
    cols = slice(part * width, (part + 1) * width)
    rows = jnp.broadcast_to(mod_ref[0:1, cols], (item.shape[0], width))
    for index in range(1, mod_ref.shape[0]):
        rows = jnp.where(item == index, mod_ref[index : index + 1, cols], rows)
    return rows


def add_item_sums(sums_ref, part, item, values, count):
    width = values.shape[1]
    cols = slice(part * width, (part + 1) * width)
    for index in range(count):
        kept = jnp.where(item == index, values, 0.0)
        sums_ref[index : index + 1, cols] += jnp.sum(kept, axis=0, keepdims=True)


def same_head(width, head_dim):
    row = lax.broadcasted_iota(jnp.int32, (width, width), 0) // head_dim
    col = lax.broadcasted_iota(jnp.int32, (width, width), 1) // head_dim
    return (row == col).astype(BF)


def head_sums(values, same):
    high = values.astype(BF)
    low = (values - high.astype(F32)).astype(BF)
    return dot(high, same) + dot(low, same)


def chunks(rows, size):
    return pl.loop(0, rows // size)


def at(index, size):
    return pl.ds(pl.multiple_of(index * size, size), size)


def first_norm_kernel(x_ref, mod_ref, item_ref, out_ref):
    rows, width = x_ref.shape

    @chunks(rows, 64)
    def _(i):
        r = at(i, 64)
        item = item_ref[r, :]
        normed, _ = row_norm(x_ref[r, :].astype(F32))
        scale, shift = mod_rows(mod_ref, 2, item, width), mod_rows(mod_ref, 4, item, width)
        out_ref[r, :] = (normed * (1.0 + scale) + shift).astype(BF)


def grad_mlp_kernel(up_ref, mod_ref, item_ref, out_ref, sum_ref):
    rows, width = up_ref.shape
    sum_ref[...] = jnp.zeros_like(sum_ref)

    @chunks(rows, 64)
    def _(i):
        r = at(i, 64)
        gamma = mod_rows(mod_ref, 1, item_ref[r, :], width)
        grad = (up_ref[r, :].astype(F32) * gamma).astype(BF)
        out_ref[r, :] = grad
        sum_ref[0:1, :] += jnp.sum(grad.astype(F32), axis=0, keepdims=True)


def load_columns(weight_ref, held, sems, offset_of, parts, sub):
    copies = []
    for t in range(3):
        for p in range(parts):
            copies.append(
                pltpu.make_async_copy(
                    weight_ref.at[t, :, pl.ds(pl.multiple_of(offset_of(p), sub), sub)],
                    held.at[:, pl.ds((t * parts + p) * sub, sub)],
                    sems.at[t * parts + p],
                )
            )
    for copy in copies:
        copy.start()
    return copies


def qkv_kernel(dims, *refs):
    group, segs, head_dim, parts = dims
    me_ref, temper_ref, qb_ref, vb_ref, w_ref = refs[:5]
    blocks = refs[5 : 5 + group]
    q_ref, k_ref, v_ref, qp_ref, kp_ref, held, sems = refs[5 + group :]
    width = q_ref.shape[1]
    rows = blocks[0].shape[0]
    seg, sub = rows // segs, width // parts
    me = me_ref[0]
    copies = load_columns(w_ref, held, sems, lambda p: (p * group + me) * sub, parts, sub)
    same = same_head(width, head_dim)
    for copy in copies:
        copy.wait()
    for k in range(group):
        for y in range(segs):
            ranks = pl.ds(pl.multiple_of((y * group + (me ^ k)) * seg, 16), seg)
            made = dot(blocks[k][y * seg : (y + 1) * seg, :], held[...])
            query = made[:, :width] + qb_ref[...]
            key = made[:, width : 2 * width]
            qp_ref[ranks, :] = query
            kp_ref[ranks, :] = key
            inverse = lax.rsqrt(head_sums(query * query, same) + 1e-06)
            q_ref[ranks, :] = (query * inverse * temper_ref[...]).astype(BF)
            inverse = lax.rsqrt(head_sums(key * key, same) + 1e-06)
            k_ref[ranks, :] = (key * inverse).astype(BF)
            v_ref[ranks, :] = (made[:, 2 * width :] + vb_ref[...]).astype(BF)


def attend_kernel(
    dims, first_ref, last_ref, lo_ref, hi_ref, q_ref, k_ref, v_ref,
    out_ref, out_t_ref, lse_ref, v_t, out_s, acc, total,
):
    group, segs, head_dim, block = dims
    pack_len, width = q_ref.shape
    rows = out_ref.shape[1]
    seg = rows // segs
    pair = 128 // head_dim
    heads = width // head_dim
    lanes = lax.broadcasted_iota(jnp.int32, (1, 128), 1) // head_dim
    v_t[...] = v_ref[...].T

    @pl.loop(0, pack_len // block)
    def _(q_block):
        q_rows = at(q_block, block)
        q_t = q_ref[q_rows, :].T
        low, high = lo_ref[:, q_rows], hi_ref[:, q_rows]
        acc[...] = jnp.zeros_like(acc)
        total[...] = jnp.zeros_like(total)

        @pl.loop(first_ref[q_block], last_ref[q_block])
        def _(k_block):
            k_rows = at(k_block, block)
            index = k_block * block + lax.broadcasted_iota(jnp.int32, (block, block), 0)
            seen = (index >= low) & (index < high)
            for h in range(heads):
                own = pl.ds(h * head_dim, head_dim)
                near = slice(h // pair * 128, (h // pair + 1) * 128)
                keys = k_ref[k_rows, near]
                scores = dot(jnp.where(lanes == h % pair, keys, jnp.zeros_like(keys)), q_t[near, :])
                raised = jnp.where(seen, jnp.exp(scores), 0.0)
                total[h : h + 1, :] += jnp.sum(raised, axis=0, keepdims=True)
                acc[own, :] += dot(v_t[own, k_rows], raised.astype(BF))

        for h in range(heads):
            own = pl.ds(h * head_dim, head_dim)
            acc[own, :] = acc[own, :] / total[h : h + 1, :]
            lse_ref[h : h + 1, q_rows] = jnp.log(total[h : h + 1, :])
        out_t_ref[:, q_rows] = acc[...]
        out_s[q_rows, :] = acc[...].T.astype(BF)

    for y in range(segs):
        for g in range(group):
            start = (y * group + g) * seg
            out_ref[g, y * seg : (y + 1) * seg, :] = out_s[start : start + seg, :]


def attend_back_heads(dims, refs, scratch, outs):
    group, segs, head_dim, block, near = dims
    first_ref, last_ref, lo_ref, hi_ref, in_ref, q_ref, k_ref, v_ref, out_t_ref, lse_ref = refs
    g_s, k_t, dk_acc, dv_acc, acc, sums = scratch
    dq_ref, dk_ref, dv_ref = outs
    pack_len = q_ref.shape[0]
    seg = in_ref.shape[1] // segs
    pair = 128 // head_dim
    cols = slice(near * 128, (near + 1) * 128)
    lanes = lax.broadcasted_iota(jnp.int32, (1, 128), 1) // head_dim
    for y in range(segs):
        for g in range(group):
            start = (y * group + g) * seg
            g_s[start : start + seg, :] = in_ref[g, y * seg : (y + 1) * seg, cols]
    k_t[...] = k_ref[:, cols].T
    dk_acc[...] = jnp.zeros_like(dk_acc)
    dv_acc[...] = jnp.zeros_like(dv_acc)

    @pl.loop(0, pack_len // block)
    def _(q_block):
        q_rows = at(q_block, block)
        queries, grads = q_ref[q_rows, cols], g_s[q_rows, :]
        q_t, g_t = queries.T, grads.T
        low, high = lo_ref[:, q_rows], hi_ref[:, q_rows]
        weighted = g_t.astype(F32) * out_t_ref[cols, q_rows]
        for h in range(pair):
            sums[h : h + 1, :] = jnp.sum(
                weighted[h * head_dim : (h + 1) * head_dim, :], axis=0, keepdims=True
            )
        acc[...] = jnp.zeros_like(acc)

        @pl.loop(first_ref[q_block], last_ref[q_block])
        def _(k_block):
            k_rows = at(k_block, block)
            keys, values = k_ref[k_rows, cols], v_ref[k_rows, cols]
            index = k_block * block + lax.broadcasted_iota(jnp.int32, (block, block), 0)
            seen = (index >= low) & (index < high)
            for h in range(pair):
                own = pl.ds(h * head_dim, head_dim)
                row = near * pair + h
                mine = lanes == h
                scores = dot(jnp.where(mine, keys, jnp.zeros_like(keys)), q_t)
                probs = jnp.where(seen, jnp.exp(scores - lse_ref[row : row + 1, q_rows]), 0.0)
                grad_probs = dot(jnp.where(mine, values, jnp.zeros_like(values)), g_t)
                grad_scores = (probs * (grad_probs - sums[h : h + 1, :])).astype(BF)
                acc[own, :] += dot(k_t[own, k_rows], grad_scores)
                dk_acc[k_rows, :] += dot(
                    grad_scores, jnp.where(mine, queries, jnp.zeros_like(queries))
                )
                dv_acc[k_rows, :] += dot(
                    probs.astype(BF), jnp.where(mine, grads, jnp.zeros_like(grads))
                )

        dq_ref[q_rows, :] = acc[...].T.astype(BF)

    dk_ref[...] = dk_acc[...].astype(BF)
    dv_ref[...] = dv_acc[...].astype(BF)


def attend_back_kernel(dims, *refs):
    attend_back_heads(dims, refs[:10], refs[13:], refs[10:13])


def qkv_back_kernel(dims, *refs):
    group, segs, head_dim, parts, pairs, tile_count = dims
    add_blocks(refs[:tile_count], refs[-4:-2])
    refs = refs[tile_count:-4] + refs[-2:]
    me_ref, temper_ref, w_ref, qp_ref, kp_ref = refs[:5]
    grads = [refs[5 + 3 * p : 8 + 3 * p] for p in range(pairs)]
    rest = refs[5 + 3 * pairs :]
    sent = rest[:group]
    dqkv_ref, sums_ref, held, sems = rest[group:]
    width = qp_ref.shape[1]
    rows = sent[0].shape[0]
    seg, sub = rows // segs, width // parts
    me = me_ref[0]
    copies = load_columns(w_ref, held, sems, lambda p: (p * group + me) * sub, parts, sub)
    same = same_head(width, head_dim)
    sums_ref[...] = jnp.zeros_like(sums_ref)

    def back(gradient, pre):
        inverse = lax.rsqrt(head_sums(pre * pre, same) + 1e-06)
        unit = pre * inverse
        return inverse * (gradient - unit * head_sums(gradient * unit, same)), unit

    def joined(which, ranks):
        return jnp.concatenate([grads[p][which][ranks, :] for p in range(pairs)], axis=1)

    for copy in copies:
        copy.wait()
    for k in reversed(range(group)):
        for y in range(segs):
            ranks = pl.ds(pl.multiple_of((y * group + (me ^ k)) * seg, 16), seg)
            own = slice(k * rows + y * seg, k * rows + (y + 1) * seg)
            grad = joined(0, ranks).astype(F32) * temper_ref[...]
            grad_query, unit = back(grad, qp_ref[ranks, :])
            grad_query = grad_query.astype(BF)
            grad_key, _ = back(joined(1, ranks).astype(F32), kp_ref[ranks, :])
            grad_value = joined(2, ranks)
            dqkv_ref[own, :width] = grad_query
            dqkv_ref[own, width : 2 * width] = grad_key.astype(BF)
            dqkv_ref[own, 2 * width :] = grad_value
            for index, values in enumerate((grad_query, grad_value, grad * unit)):
                sums_ref[index : index + 1, :] += jnp.sum(
                    values.astype(F32), axis=0, keepdims=True
                )
        sent[k][...] = dot(
            dqkv_ref[k * rows : (k + 1) * rows, :], held[...], BY_ROW
        ).astype(BF)


def project_kernel(
    parts, ret_ref, wp_ref, pb_ref, x_ref, mod_ref, item_ref, attn_ref, branch_ref, middle_ref, out_ref
):
    group, rows, width = ret_ref.shape
    model = x_ref.shape[1]
    sub = width // parts
    for g in range(group):
        for p in range(parts):
            start = (p * group + g) * sub
            attn_ref[:, start : start + sub] = ret_ref[g, :, p * sub : (p + 1) * sub]
    branch_ref[...] = dot(attn_ref[...], wp_ref[...]) + pb_ref[...].astype(F32)

    @chunks(rows, 64)
    def _(i):
        r = at(i, 64)
        item = item_ref[r, :]
        middle = x_ref[r, :].astype(F32) + mod_rows(mod_ref, 0, item, model) * branch_ref[r, :]
        middle_ref[r, :] = middle
        normed, _ = row_norm(middle)
        scale, shift = mod_rows(mod_ref, 3, item, model), mod_rows(mod_ref, 5, item, model)
        out_ref[r, :] = (normed * (1.0 + scale) + shift).astype(BF)


def add_blocks(terms, outs):
    count = outs[0].shape[0]
    for j in range(terms[0].shape[0]):
        made = sum(term[j].astype(F32) for term in terms).astype(BF)
        outs[j // count][j % count] = made


def weights_kernel(fc1_ref, fc2_ref, w1_ref, w2_ref, sems):
    segs, head_size, _, hidden = fc1_ref.shape
    half = fc2_ref.shape[3]
    copies = []
    for y in range(segs):
        for z in range(head_size):
            own = pl.ds(z * hidden, hidden)
            rows = pl.ds(y * half, half)
            for source, target in (
                (fc1_ref.at[y, z, pl.ds(0, half), :], w1_ref.at[rows, own]),
                (fc2_ref.at[y, z], w2_ref.at[own, rows]),
            ):
                copies.append(pltpu.make_async_copy(source, target, sems.at[len(copies)]))
                copies[-1].start()
    for copy in copies:
        copy.wait()


def feed_kernel(count, *refs):
    w1, w2, b1_ref = refs[:3]
    ins, grads = refs[3 : 3 + count], refs[3 + count : 3 + 2 * count]
    rest = refs[3 + 2 * count :]
    back, outs = rest[:count], rest[count : 2 * count]
    act_ref, gh_ref, sum_ref = rest[2 * count : 2 * count + 3]
    in_s, grad_s, back_s, out_s, act_s, gh_s, pre, grad, in_sems, out_sems = rest[2 * count + 3 :]
    rows = ins[0].shape[0]
    loads, stores = [], []
    for k in range(count):
        pair = (
            pltpu.make_async_copy(ins[k], in_s.at[k], in_sems.at[2 * k]),
            pltpu.make_async_copy(grads[k], grad_s.at[k], in_sems.at[2 * k + 1]),
        )
        pair[0].start()
        pair[1].start()
        loads.append(pair)
    sum_ref[...] = jnp.zeros_like(sum_ref)

    def store(source, target, index):
        stores.append(pltpu.make_async_copy(source, target, out_sems.at[index]))
        stores[-1].start()

    def front(k):
        loads[k][0].wait()
        pre[k % 2] = dot(in_s[k], w1[...]) + b1_ref[...]
        loads[k][1].wait()
        grad[k % 2] = dot(grad_s[k], w2[...], BY_ROW)

    def middle(k):
        total = 0.0
        for start in range(0, rows, 32):
            r = slice(start, start + 32)
            value = pre[k % 2, r, :]
            square = value * value
            gate = jnp.tanh(value * (0.7978845608028654 + 0.035677408136300125 * square))
            half = 0.5 + 0.5 * gate
            act = value * half
            slope = half + act * (1.0 - gate) * (0.7978845608028654 + 0.10703222440890037 * square)
            back_grad = (slope * grad[k % 2, r, :]).astype(BF)
            act_s[k, r, :] = act.astype(BF)
            gh_s[k, r, :] = back_grad
            total = total + jnp.sum(back_grad.astype(F32), axis=0, keepdims=True)
        sum_ref[0:1, :] += total
        own = pl.ds(k * rows, rows)
        store(act_s.at[k], act_ref.at[own, :], 4 * k)
        store(gh_s.at[k], gh_ref.at[own, :], 4 * k + 1)

    def end(k):
        back_s[k] = dot(gh_s[k], w1[...], BY_ROW).astype(BF)
        store(back_s.at[k], back[k], 4 * k + 2)
        out_s[k] = dot(act_s[k], w2[...]).astype(BF)
        store(out_s.at[k], outs[k], 4 * k + 3)

    order = list(reversed(range(count)))
    front(order[0])
    for place, k in enumerate(order):
        if place + 1 < count:
            front(order[place + 1])
        middle(k)
        end(k)
    for started in stores:
        started.wait()


def turned(index, count):
    made = 0
    while count > 1:
        made, index, count = made * 2 + index % 2, index // 2, count // 2
    return made


def feed_weights_kernel(dims, *refs):
    count, group, split, halves = dims
    me_ref, acts, ghs = refs[0], refs[1 : 1 + halves], refs[1 + halves : 1 + 2 * halves]
    refs = refs[1 + 2 * halves :]
    ins, grads, rest = refs[:count], refs[count : 2 * count], refs[2 * count :]
    outs, (in_t, grad_t, act_s, gh_s) = rest[:split], rest[split:]
    rows, model = ins[0].shape
    for k in range(count):
        own = slice(k * rows, (k + 1) * rows)
        in_t[:, own] = ins[k][...].T
        grad_t[:, own] = grads[k][...].T
    for k in range(halves):
        own = slice(k * acts[k].shape[0], (k + 1) * acts[k].shape[0])
        act_s[own, :] = acts[k][...]
        gh_s[own, :] = ghs[k][...]
    part = model // split
    fine = part // group
    head_size, _, _, _, hidden = outs[0].shape
    for y in reversed(range(split)):
        for which, left, right in ((0, in_t, gh_s), (1, grad_t, act_s)):
            start = pl.multiple_of((me_ref[1] ^ y) * part, part) if split > 1 else 0
            for j in range(head_size):
                z = me_ref[2] ^ turned(j, head_size)
                cols = slice(None)
                if split > 1:
                    cols = pl.ds(pl.multiple_of(z * hidden, hidden), hidden)
                made = dot(left[pl.ds(start, part), :], right[:, cols]).astype(BF)
                for g in range(group):
                    to = (me_ref[0] ^ g) if group > 1 else 0
                    outs[y][j, to, which] = made[g * fine : (g + 1) * fine, :]


def middle_back_kernel(
    dims, middle_ref, branch_ref, up_ref, mod_ref, item_ref, wp_ref, *refs
):
    parts, items, count = dims
    terms, (out_ref, gb_ref, gm_ref, sums_ref, col_ref, attn) = refs[:count], refs[count:]
    rows, model = middle_ref.shape
    group, _, width = out_ref.shape
    sub = width // parts
    sums_ref[...] = jnp.zeros_like(sums_ref)
    col_ref[...] = jnp.zeros_like(col_ref)

    @chunks(rows, 64)
    def _(i):
        r = at(i, 64)
        item = item_ref[r, :]
        grad_in = sum(term[r, :].astype(F32) for term in terms)
        normed, inverse = row_norm(middle_ref[r, :])
        scale = mod_rows(mod_ref, 3, item, model)
        grad_middle = up_ref[r, :].astype(F32) + norm_back(grad_in * (1.0 + scale), normed, inverse)
        gm_ref[r, :] = grad_middle
        grad_branch = (grad_middle * mod_rows(mod_ref, 0, item, model)).astype(BF)
        gb_ref[r, :] = grad_branch
        col_ref[0:1, :] += jnp.sum(grad_branch.astype(F32), axis=0, keepdims=True)
        add_item_sums(sums_ref, 0, item, grad_middle * branch_ref[r, :], items)
        add_item_sums(sums_ref, 1, item, grad_in * normed, items)
        add_item_sums(sums_ref, 2, item, grad_in, items)

    attn[...] = dot(gb_ref[...], wp_ref[...], BY_ROW).astype(BF)
    for g in range(group):
        for p in range(parts):
            start = (p * group + g) * sub
            out_ref[g, :, p * sub : (p + 1) * sub] = attn[:, start : start + sub]


def output_kernel(dims, middle_ref, up_ref, mod_ref, item_ref, bias_ref, *refs):
    items, count, proj_count = dims
    terms, refs = refs[:count], refs[count:]
    projs, (out_ref, sums_ref, proj_ref) = refs[:proj_count], refs[proj_count:]
    proj_ref[...] = sum(proj[...].astype(F32) for proj in projs).astype(BF)
    rows, model = middle_ref.shape
    sums_ref[...] = jnp.zeros_like(sums_ref)

    @chunks(rows, 64)
    def _(i):
        r = at(i, 64)
        item = item_ref[r, :]
        made = sum(term[r, :].astype(F32) for term in terms) + bias_ref[...].astype(F32)
        gamma = mod_rows(mod_ref, 1, item, model)
        out_ref[r, :] = (middle_ref[r, :] + gamma * made).astype(BF)
        add_item_sums(sums_ref, 0, item, up_ref[r, :].astype(F32) * made, items)


def tokens_back_kernel(dims, x_ref, gm_ref, mod_ref, item_ref, *refs):
    items, count, tile_count = dims
    terms, refs = refs[:count], refs[count:]
    tiles, (out_ref, sums_ref, kept_ref, sent_ref) = refs[:tile_count], refs[tile_count:]
    add_blocks(tiles, (kept_ref, sent_ref))
    rows, model = x_ref.shape
    sums_ref[...] = jnp.zeros_like(sums_ref)

    @chunks(rows, 64)
    def _(i):
        r = at(i, 64)
        item = item_ref[r, :]
        grad_in = sum(term[r, :].astype(F32) for term in terms)
        normed, inverse = row_norm(x_ref[r, :].astype(F32))
        scale = mod_rows(mod_ref, 2, item, model)
        out_ref[r, :] = (
            gm_ref[r, :] + norm_back(grad_in * (1.0 + scale), normed, inverse)
        ).astype(BF)
        add_item_sums(sums_ref, 0, item, grad_in * normed, items)
        add_item_sums(sums_ref, 1, item, grad_in, items)


def proj_weights_kernel(dims, me_ref, attn_ref, gb_ref, *refs):
    group, split, count = dims
    terms, refs = refs[:count], refs[count:]
    outs, (sum_ref, left_t, right) = refs[:group], refs[group:]
    sum_ref[...] = sum(term[...].astype(F32) for term in terms).astype(BF)
    left_t[...] = attn_ref[...].T
    chunk, head_size, tall, wide = outs[0].shape
    for k in range(group):
        for y in range(chunk):
            part = (me_ref[1] ^ y) if split else y
            start = pl.multiple_of((part * group + (me_ref[0] ^ k)) * wide, wide)
            right[:, y * wide : (y + 1) * wide] = gb_ref[:, pl.ds(start, wide)]
        for j in range(head_size):
            z = (me_ref[2] ^ turned(j, head_size)) if split else j
            made = dot(left_t[pl.ds(pl.multiple_of(z * tall, tall), tall), :], right[...])
            for y in range(chunk):
                outs[k][y, j] = made[:, y * wide : (y + 1) * wide].astype(BF)


def qkv_weights_kernel(dims, me_ref, dqkv_ref, *refs):
    count, chunk, split, proj_count = dims
    ins, refs = refs[:count], refs[count:]
    projs, refs = refs[:proj_count], refs[proj_count:]
    outs, (left_t, right) = refs[:chunk], refs[chunk:]
    rows = ins[0].shape[0]
    for k in range(count):
        left_t[:, k * rows : (k + 1) * rows] = ins[k][...].T
    head_size, _, tall, wide = outs[0].shape
    for y in reversed(range(chunk)):
        part = (me_ref[1] ^ y) if split else y
        for t in range(3):
            start = pl.multiple_of((t * chunk + part) * wide, wide)
            right[:, t * wide : (t + 1) * wide] = dqkv_ref[:, pl.ds(start, wide)]
        for j in range(head_size):
            z = (me_ref[2] ^ turned(j, head_size)) if split else j
            made = dot(left_t[pl.ds(pl.multiple_of(z * tall, tall), tall), :], right[...])
            outs[y][j, 0] = sum(proj[y, j].astype(F32) for proj in projs).astype(BF)
            for t in range(3):
                outs[y][j, 1 + t] = made[:, t * wide : (t + 1) * wide].astype(BF)


def sort_kernel(pack_len, dest_ref, tokens_ref, cot_ref, to_slot_ref, tokens_out, cot_out):
    rows = tokens_ref.shape[0]
    pack = dest_ref[...] // pack_len
    other = jnp.broadcast_to(pack, (8, rows)).astype(F32).T[:, 0:1].astype(jnp.int32)
    this = lax.broadcasted_iota(jnp.int32, (rows, rows), 1)
    that = lax.broadcasted_iota(jnp.int32, (rows, rows), 0)
    before = (other < pack) | ((other == pack) & (that < this))
    slot = jnp.sum(before.astype(jnp.int32), axis=0, keepdims=True)
    to_slot_ref[...] = (slot == that).astype(F32).astype(BF)
    tokens_out[...] = dot(to_slot_ref[...], tokens_ref[...]).astype(BF)
    cot_out[...] = dot(to_slot_ref[...], cot_ref[...]).astype(BF)


def item_blocks_kernel(dims, me_ref, middle_ref, output_ref, tokens_ref, out_ref, joined):
    group, segs, head_size, size = dims
    model = output_ref.shape[1]
    parts = (
        (middle_ref, 0), (output_ref, 0), (tokens_ref, 0),
        (middle_ref, 1), (tokens_ref, 1), (middle_ref, 2),
    )
    for part, (ref, start) in enumerate(parts):
        joined[:, part * model : (part + 1) * model] = ref[:, start * model : (start + 1) * model]
    place = me_ref[1] * head_size + me_ref[2]
    for g in range(group):
        for y in range(segs):
            for z in range(head_size):
                start = ((y * group + g) * head_size + z) * size
                block = place ^ (y * head_size + z)
                rows = pl.ds(pl.multiple_of(block * 8, 8), 8)
                out_ref[me_ref[0] ^ g, rows, 0:size] = joined[:, start : start + size]


def group_sums_kernel(count, bit, kept_ref, came_ref, vector_ref, own_ref, sent_ref, sum_ref):
    rows = kept_ref.shape[1]
    vectors = vector_ref[...] + came_ref[pl.ds(came_ref.shape[0] - 64, 64), :]
    sum_ref[...] = vectors
    last = count == 2
    place = 0
    for k in range(0, count, 2):
        made = kept_ref[k] + came_ref[pl.ds(k // 2 * rows, rows), :]
        if last:
            half = rows // 2
            own_ref[...] = made[:half]
            sent_ref[0:half, :] = made[half:]
        elif k // 2 % 2 == 0:
            own_ref[k // 2] = made
        else:
            own_ref[k // 2] = made
            sent_ref[place * rows : (place + 1) * rows, :] = made
            place += 1
    sent_ref[pl.ds(sent_ref.shape[0] - 64, 64), :] = vectors


def pack_sums_kernel(kept_ref, came_ref, vector_ref, own_ref, *refs):
    blocks, senders = own_ref.shape[0] * (2 if len(refs) == 2 else 1), kept_ref.shape[1]
    vectors = vector_ref[...] + came_ref[pl.ds(came_ref.shape[0] - 64, 64), :]
    refs[-1][...] = vectors
    for c in range(blocks):
        for t in range(2 * senders):
            if t < senders:
                value = kept_ref[c, t]
            else:
                value = came_ref[pl.ds((c * senders + t - senders) * 8, 8), :]
            if len(refs) == 1 or c < blocks // 2:
                own_ref[c, t] = value
            else:
                refs[0][pl.ds(((c - blocks // 2) * 2 * senders + t) * 8, 8), :] = value
    if len(refs) == 2:
        refs[0][pl.ds(refs[0].shape[0] - 64, 64), :] = vectors


def ada_kernel(me_ref, silu_ref, blocks_ref, grad_ref, bias_ref, held):
    head_size = me_ref[3]
    place = me_ref[1] * head_size + me_ref[2]
    for c in range(blocks_ref.shape[0]):
        sender = place ^ turned(c, blocks_ref.shape[0])
        held[pl.ds(pl.multiple_of(sender * 8, 8), 8), :] = blocks_ref[c]
    low = held[:, 0 : grad_ref.shape[1]].astype(BF)
    bias_ref[...] = jnp.broadcast_to(
        jnp.sum(low.astype(F32), axis=0, keepdims=True), bias_ref.shape
    )
    grad_ref[...] = lax.dot_general(
        silu_ref[...], low, (((0,), (0,)), ((), ())), preferred_element_type=F32
    )


def own_tiles_kernel(count, *refs):
    terms, outs = refs[:count], refs[count:]
    for i, out in enumerate(outs):
        out[...] = sum(term[0, i].astype(F32) for term in terms).astype(BF)


def place_kernel(group, me_ref, *refs):
    blocks, (up_ref, down_ref) = refs[:group], refs[group:]
    hidden = blocks[0].shape[2]
    for i in range(group):
        own = pl.ds(pl.multiple_of((me_ref[0] ^ i) * hidden, hidden), hidden)
        up_ref[:, own] = blocks[i][0].astype(F32)
        down_ref[own, :] = blocks[i][1].astype(F32).T


def vector_parts_kernel(dims, me_ref, qkv_ref, branch_ref, mlp_ref, *refs):
    group, parts, head_size = dims
    hidden_refs, (flat_ref, out_ref) = refs[:-2], refs[-2:]
    sub = qkv_ref.shape[1] // parts
    hidden = hidden_refs[0].shape[1] // head_size
    out_ref[...] = jnp.zeros_like(out_ref)
    for p in range(parts):
        own = pl.ds(pl.multiple_of((p * group + me_ref[0]) * sub, sub), sub)
        for row in range(3):
            out_ref[row : row + 1, own] = qkv_ref[row : row + 1, p * sub : (p + 1) * sub]
    out_ref[3:4, :] = branch_ref[0:1, :]
    out_ref[4:5, :] = mlp_ref[0:1, :]
    if hidden % 128 == 0:
        own = pl.ds(pl.multiple_of(me_ref[0] * hidden, hidden), hidden)
        for z in range(head_size):
            cols = slice(z * hidden, (z + 1) * hidden)
            out_ref[8 + z : 9 + z, own] = sum(ref[0:1, cols] for ref in hidden_refs)
    for c in range(out_ref.shape[1] // 256):
        flat_ref[c * 16 : (c + 1) * 16, :] = out_ref[:, c * 256 : (c + 1) * 256]


def to_packs(rows):
    return lax.all_to_all(rows, ("yy", "head"), split_axis=0, concat_axis=0, tiled=True)


def over_group(blocks):
    return lax.all_to_all(blocks, "g", split_axis=0, concat_axis=0, tiled=True)


def bits(count):
    steps = []
    while count > 1:
        count //= 2
        steps.append(count)
    return steps


def xor_swap(values, axis, step):
    size = lax.axis_size(axis)
    return lax.ppermute(values, axis, [(i, i ^ step) for i in range(size)])


def xor_gather(block, axis):
    blocks = {0: block}
    for step in bits(lax.axis_size(axis)):
        for k in list(blocks):
            blocks[k ^ step] = xor_swap(blocks[k], axis, step)
    return [blocks[k] for k in range(len(blocks))]


def xor_scatter(blocks, axis):
    terms = {k: [block] for k, block in enumerate(blocks)}
    for step in reversed(bits(lax.axis_size(axis))):
        for k in reversed([k for k in terms if k & step]):
            terms[k ^ step].append(xor_swap(add_low(*terms.pop(k)), axis, step))
    return terms[0]


def halves_over_head(values):
    count = lax.axis_size("head")
    step = count // values.shape[0]
    half = values.shape[0] // 2
    return values[:half], xor_swap(values[half:], "head", step)


def add_low(*terms):
    if len(terms) == 1:
        return terms[0]
    return sum(term.astype(F32) for term in terms).astype(terms[0].dtype)


def butterfly(values, axis):
    for step in bits(lax.axis_size(axis)):
        values = values + xor_swap(values, axis, step)
    return values


def pick(values, index, axis):
    return lax.dynamic_index_in_dim(values, index, axis, keepdims=False)


def xor_blocks(values, axis, dim):
    me = lax.axis_index(axis)
    return [pick(values, me ^ k, dim) for k in range(lax.axis_size(axis))]


def tie(*values):
    return lax.optimization_barrier(values)


def shards(
    tokens,
    cotangent,
    class_table,
    ada_weight,
    ada_bias,
    qkv_weight,
    q_bias,
    v_bias,
    log_scale,
    proj_weight,
    proj_bias,
    fc1_weight,
    fc1_bias,
    fc2_weight,
    fc2_bias,
    item_lens,
    class_ids,
    section_ids,
    destination,
):
    segs = lax.axis_size("yy")
    group = lax.axis_size("g")
    head_size = lax.axis_size("head")
    yy, g, z = lax.axis_index("yy"), lax.axis_index("g"), lax.axis_index("head")
    me = jnp.stack([g, yy, z, jnp.int32(head_size)]).astype(jnp.int32)
    pack = yy * head_size + z
    rows, model = tokens.shape
    heads_all = log_scale.shape[0]
    head_dim = model // heads_all
    heads = heads_all // group
    width = model // group
    dp_size = segs * group
    pack_len = rows * head_size
    seg = rows // segs
    items = item_lens.shape[1]
    block = min(256, pack_len)
    col = model // dp_size
    parts = segs if col % 128 == 0 else 1
    sub = width // parts

    def own_cols(values):
        return pick(values.reshape(parts, group, sub), g, 1).reshape(1, width)

    rows_bf, rows_f32 = shape_of((rows, model), BF), shape_of((rows, model), F32)
    to_slot, sorted_tokens, sorted_cotangent = call(
        "sort",
        functools.partial(sort_kernel, pack_len),
        (destination[None, :], tokens, cotangent),
        (VMEM, HBM, HBM),
        (shape_of((rows, rows), BF), rows_bf, rows_bf),
    )
    inputs = to_packs(sorted_tokens)

    hidden = fc1_weight.shape[1] // group
    units = head_size * hidden
    half = model // segs
    fc1_own = lax.dynamic_slice(fc1_weight, (yy * half, g * hidden), (half, hidden))
    fc1_bias_own = lax.dynamic_slice(fc1_bias, (g * hidden,), (hidden,))
    fc2_own = lax.dynamic_slice(fc2_weight, (g * hidden, yy * half), (hidden, half))
    fc1_sent = jnp.concatenate(
        [fc1_own, jnp.broadcast_to(fc1_bias_own[None, :], (16, hidden))], axis=0
    )
    fc1_all = lax.all_gather(fc1_sent, ("yy", "head"), axis=0)
    fc1_all = fc1_all.reshape(segs, head_size, half + 16, hidden)
    fc2_all = lax.all_gather(fc2_own, ("yy", "head"), axis=0)
    fc2_all = fc2_all.reshape(segs, head_size, hidden, half)
    fc1_bias_here = fc1_all[0, :, half].reshape(1, units).astype(F32)
    tiled = hidden % 128 == 0
    if tiled:
        fc1_here, fc2_here = call(
            "weights",
            weights_kernel,
            (fc1_all, fc2_all),
            (ANY, ANY),
            (shape_of((model, units), BF), shape_of((units, model), BF)),
            [pltpu.SemaphoreType.DMA((2 * segs * head_size,))],
            out_specs=(VMEM, VMEM),
        )
    else:
        fc1_here = fc1_all[:, :, :half].transpose(0, 2, 1, 3).reshape(model, units)
        fc2_here = fc2_all.transpose(1, 2, 0, 3).reshape(units, model)

    lens_here = pick(item_lens, pack, 0)
    class_here = pick(class_ids, pack, 0)
    order_key = class_here * items + jnp.arange(items, dtype=jnp.int32)
    item_rank = jnp.sum(
        jnp.where(order_key[None, :] < order_key[:, None], lens_here[None, :], 0), axis=1
    )
    item_pos = jnp.cumsum(lens_here) - lens_here
    item_end = item_rank + lens_here

    def items_of(rank):
        return (rank[:, None] >= item_rank[None, :]) & (rank[:, None] < item_end[None, :])

    rank_all = jnp.arange(pack_len, dtype=jnp.int32)
    member = items_of(rank_all)

    def of_item(values):
        return jnp.sum(jnp.where(member, values[None, :], 0), axis=1)

    section_here = lax.ppermute(
        section_ids[0],
        ("g", "head"),
        [(a * head_size + b, b * head_size + a) for a in range(group) for b in range(head_size)],
    )
    position = rank_all - of_item(item_rank - item_pos)
    section_rank = jnp.sum(
        jnp.where(rank_all[None, :] == position[:, None], section_here[None, :], 0), axis=1
    )
    up_to = jnp.sum((section_here[None, :] <= section_rank[:, None]).astype(jnp.int32), axis=1)
    low = of_item(item_rank)
    high = jnp.minimum(up_to + of_item(item_rank - item_pos), of_item(item_end))
    first = low[::block] // block
    last = (high[block - 1 :: block] + block - 1) // block
    low, high = low[None, :], high[None, :]

    row_rank = (
        (jnp.arange(segs, dtype=jnp.int32)[:, None] * group + g) * seg
        + jnp.arange(seg, dtype=jnp.int32)[None, :]
    ).reshape(rows)
    row_item = jnp.sum(
        jnp.where(items_of(row_rank), jnp.arange(items, dtype=jnp.int32)[None, :], 0), axis=1
    )[:, None]

    class_rows = jnp.take(class_table, class_ids.reshape(-1), axis=0).astype(F32)
    silu_cond = jax.nn.silu(class_rows).astype(BF)
    silu_here = lax.dynamic_slice_in_dim(silu_cond, pack * items, items, 0)
    mod = jnp.dot(silu_here, ada_weight, preferred_element_type=F32) + ada_bias.astype(F32)

    (attn_in,) = call("first_norm",
        first_norm_kernel, (inputs, mod, row_item), (HBM, VMEM, VMEM), (shape_of((rows, model), BF),)
    )
    attn_blocks = xor_gather(attn_in, "g")
    per_part = sub // head_dim
    scale_here = pick(log_scale.reshape(parts, group, per_part), g, 1).reshape(heads)
    temper = jnp.repeat(jnp.exp(scale_here), head_dim)[None, :]
    wide = shape_of((pack_len, width), BF)
    wide_f32 = shape_of((pack_len, width), F32)
    weights_held = [
        pltpu.VMEM((model, 3 * width), BF),
        pltpu.SemaphoreType.DMA((3 * parts,)),
    ]
    queries, keys, values, query_pre, key_pre = call(
        "qkv",
        functools.partial(qkv_kernel, (group, segs, head_dim, parts)),
        (me, temper, own_cols(q_bias).astype(F32), own_cols(v_bias).astype(F32), qkv_weight,
         *attn_blocks),
        (SMEM, VMEM, VMEM, VMEM, ANY) + (HBM,) * group,
        (wide, wide, wide, wide_f32, wide_f32),
        weights_held,
    )
    sorted_cotangent, _ = tie(sorted_cotangent, inputs)
    upstream = to_packs(sorted_cotangent)
    def near_blocks(own):
        blocks = {0: own}
        for step in bits(group)[1:]:
            for k in list(blocks):
                blocks[k ^ step] = xor_swap(blocks[k], "g", step)
        return [blocks[k] for k in range(len(blocks))]

    near = group // 2
    out_blocks, out_t, lse = call(
        "attend",
        functools.partial(attend_kernel, (group, segs, head_dim, block)),
        (first, last, low, high, queries, keys, values),
        (SMEM, SMEM, VMEM, VMEM, HBM, HBM, HBM),
        (shape_of((group, rows, width), BF), shape_of((width, pack_len), F32),
         shape_of((8, pack_len), F32)),
        [
            pltpu.VMEM((width, pack_len), BF),
            pltpu.VMEM((pack_len, width), BF),
            pltpu.VMEM((width, block), F32),
            pltpu.VMEM((8, block), F32),
        ],
    )
    returned = over_group(out_blocks)
    upstream, _ = tie(upstream, out_blocks)
    grad_mlp, grad_mlp_sum = call(
        "grad_mlp",
        grad_mlp_kernel,
        (upstream, mod, row_item),
        (HBM, VMEM, VMEM),
        (rows_bf, shape_of((8, model), F32)),
    )
    grad_far = xor_swap(grad_mlp, "g", near)
    grad_blocks = near_blocks(grad_mlp)
    returned, grad_mlp_sum = tie(returned, grad_mlp_sum)
    attn_rows, branch, middle, mlp_in = call(
        "project",
        functools.partial(project_kernel, parts),
        (returned, proj_weight, proj_bias[None, :], inputs, mod, row_item),
        (HBM, HBM, VMEM, HBM, VMEM, VMEM),
        (rows_bf, rows_f32, rows_f32, rows_bf),
    )

    mlp_blocks = near_blocks(mlp_in)
    mlp_far = xor_swap(mlp_in, "g", near)
    grad_blocks += near_blocks(tie(grad_far, mlp_in)[0])
    back_parts, out_parts, acts, ghs, hidden_sums = [], [], [], [], []
    for start in (0, near):
        if start:
            mlp_blocks += near_blocks(tie(mlp_far, acts[0])[0])
        made = call(
            "feed",
            functools.partial(feed_kernel, near),
            (fc1_here, fc2_here, fc1_bias_here, *mlp_blocks[start : start + near],
             *grad_blocks[start : start + near]),
            (VMEM,) * 3 + (ANY,) * (2 * near),
            (rows_bf,) * (2 * near)
            + (shape_of((near * rows, units), BF),) * 2
            + (shape_of((8, units), F32),),
            [pltpu.VMEM((near, rows, model), BF)] * 4
            + [pltpu.VMEM((near, rows, units), BF)] * 2
            + [pltpu.VMEM((2, rows, units), F32)] * 2
            + [pltpu.SemaphoreType.DMA((2 * near,)), pltpu.SemaphoreType.DMA((4 * near,))],
            out_specs=(ANY,) * (2 * near + 2) + (VMEM,),
        )
        back_parts += made[:near]
        out_parts += made[near : 2 * near]
        acts.append(made[2 * near])
        ghs.append(made[2 * near + 1])
        hidden_sums.append(made[2 * near + 2])
    far_terms = {k: back_parts[k] for k in range(near, group)}
    for step in reversed(bits(group)[1:]):
        for k in reversed([k for k in far_terms if k & step]):
            came = xor_swap(far_terms.pop(k), "g", step)
            far_terms[k ^ step] = add_low(far_terms[k ^ step], came)
    far_sum = far_terms[near]
    back_parts = list(tie(*back_parts[:near], far_sum)[:near])
    in_terms = {k: [back_parts[k]] for k in range(near)}
    for step in reversed(bits(group)[1:]):
        for k in reversed([k for k in in_terms if k & step]):
            in_terms[k ^ step].append(xor_swap(add_low(*in_terms.pop(k)), "g", step))
    in_terms = in_terms[0] + [xor_swap(far_sum, "g", near)]
    acts[0], _ = tie(acts[0], far_sum)
    split = segs if tiled else 1
    if tiled:
        fine = half // group
        tile_shape = (head_size, group, 2, fine, hidden)
        feed_dims = (group, group, segs, 2)
    else:
        tile_shape = (1, 1, 2, model, units)
        feed_dims = (group, 1, 1, 2)
    tile_parts = call(
        "feed_weights",
        functools.partial(feed_weights_kernel, feed_dims),
        (me, *acts, *ghs, *mlp_blocks, *grad_blocks),
        (SMEM,) + (HBM,) * (4 + 2 * group),
        (shape_of(tile_shape, BF),) * split,
        [
            pltpu.VMEM((model, pack_len), BF),
            pltpu.VMEM((model, pack_len), BF),
            pltpu.VMEM((pack_len, units), BF),
            pltpu.VMEM((pack_len, units), BF),
        ],
    )
    if not tiled:
        fine = half // group
        order = jnp.array([turned(j, head_size) for j in range(head_size)]) ^ z
        near_g = jnp.arange(group) ^ g
        near_y = jnp.arange(segs) ^ yy

        full = tile_parts[0].reshape(2, segs, group, fine, head_size, hidden)
        full = full.transpose(1, 4, 2, 0, 3, 5)
        tile_parts = list(full[near_y][:, order][:, :, near_g])

    middle_in, _ = tie(middle, tile_parts[0])
    outbound, grad_branch, grad_middle, middle_sums, branch_sum = call(
        "middle_back",
        functools.partial(middle_back_kernel, (parts, items, len(in_terms))),
        (middle_in, branch, upstream, mod, row_item, proj_weight, *in_terms),
        (HBM, HBM, HBM, VMEM, VMEM, HBM) + (HBM,) * len(in_terms),
        (shape_of((group, rows, width), BF), rows_bf, rows_f32, shape_of((8, 3 * model), F32),
         shape_of((8, model), F32)),
        [pltpu.VMEM((rows, model), BF)],
    )
    inbound = over_group(outbound)
    tile_terms = xor_scatter(tile_parts, "yy")
    def to_last(blocks):
        terms = {k: [block] for k, block in enumerate(blocks)}
        for step in reversed(bits(group)[1:]):
            for k in reversed([k for k in terms if k & step]):
                terms[k ^ step].append(xor_swap(add_low(*terms.pop(k)), "g", step))
        return terms[0], terms[near]

    out_terms, out_last = to_last(tie(*out_parts, tile_parts[0])[:group])
    made = call(
        "proj_weights",
        functools.partial(proj_weights_kernel, (group, parts == segs, len(out_last))),
        (me, attn_rows, grad_branch, *out_last),
        (SMEM,) + (HBM,) * (2 + len(out_last)),
        (shape_of((parts, head_size, model // head_size, sub), BF),) * group + (rows_bf,),
        [pltpu.VMEM((model, rows), BF), pltpu.VMEM((rows, width), BF)],
    )
    out_sent = made[group]
    proj_terms, proj_last = to_last(made[:group])
    inbound, out_sent = tie(inbound, out_sent)
    out_terms.append(xor_swap(out_sent, "g", near))

    def heads_back(index, given):
        return call(
            "attend_back",
            functools.partial(attend_back_kernel, (group, segs, head_dim, block, index)),
            (first, last, low, high, given, queries, keys, values, out_t, lse),
            (SMEM, SMEM, VMEM, VMEM) + (HBM,) * 5 + (VMEM,),
            (shape_of((pack_len, 128), BF),) * 3,
            [
                pltpu.VMEM((pack_len, 128), BF),
                pltpu.VMEM((128, pack_len), BF),
                pltpu.VMEM((pack_len, 128), F32),
                pltpu.VMEM((pack_len, 128), F32),
                pltpu.VMEM((128, block), F32),
                pltpu.VMEM((8, block), F32),
            ],
        )

    head_grads = list(heads_back(0, inbound))
    tied = tie(*out_terms, *proj_last, head_grads[0])[:-1]
    output_rows, output_sums, proj_sent = call(
        "output",
        functools.partial(output_kernel, (items, len(out_terms), len(proj_last))),
        (middle, upstream, mod, row_item, fc2_bias[None, :], *tied),
        (HBM, HBM, VMEM, VMEM, VMEM) + (HBM,) * len(tied),
        (rows_bf, shape_of((8, model), F32), shape_of(proj_last[0].shape, BF)),
    )
    output_back = to_packs(output_rows)
    inbound, output_rows = tie(inbound, output_rows)
    proj_terms.append(xor_swap(proj_sent, "g", near))
    for index in range(1, width // 128):
        head_grads += heads_back(index, inbound)
    tied = tie(*head_grads, output_back, proj_terms[-1])
    head_grads, output_back, proj_terms[-1] = tied[:-2], tied[-2], tied[-1]
    half_tiles = shape_of((head_size // 2, group, 2, fine, hidden), BF)
    quarter_tiles = shape_of((head_size // 4, group, 2, fine, hidden), BF)
    made = call(
        "qkv_back",
        functools.partial(
            qkv_back_kernel, (group, segs, head_dim, parts, width // 128, len(tile_terms))
        ),
        (*tile_terms, me, temper, qkv_weight, query_pre, key_pre, *head_grads),
        (HBM,) * len(tile_terms) + (SMEM, VMEM, ANY) + (HBM,) * (2 + len(head_grads)),
        (rows_bf,) * group
        + (shape_of((pack_len, 3 * width), BF), shape_of((8, width), F32), half_tiles, half_tiles),
        weights_held,
    )
    grad_qkv, qkv_sums, tiles_kept, tiles_sent = made[group:]
    tile_terms = (tiles_kept, xor_swap(tiles_sent, "head", 1))

    (vectors,) = call(
        "vector_parts",
        functools.partial(vector_parts_kernel, (group, parts, head_size)),
        (me, qkv_sums, branch_sum, grad_mlp_sum, *hidden_sums),
        (SMEM,) + (VMEM,) * (3 + len(hidden_sums)),
        (shape_of((64, 256), F32),),
        [pltpu.VMEM((16, model), F32)],
    )
    if not tiled:
        hidden_row = (hidden_sums[0] + hidden_sums[1])[0].reshape(head_size, hidden)
        hidden_row = lax.dynamic_update_slice(
            jnp.zeros((16, model), F32), hidden_row, (8, g * hidden)
        )
        vectors = vectors + hidden_row.reshape(16, 4, 256).transpose(1, 0, 2).reshape(64, 256)

    in_terms, last_terms = to_last(made[:group])
    sent = add_low(*last_terms)
    in_terms.append(xor_swap(sent, "g", near))
    grad_qkv, _ = tie(grad_qkv, sent)
    qkv_parts = call(
        "qkv_weights",
        functools.partial(
            qkv_weights_kernel, (group, parts, parts == segs, len(proj_terms))
        ),
        (me, grad_qkv, *attn_blocks, *proj_terms),
        (SMEM,) + (HBM,) * (1 + group + len(proj_terms)),
        (shape_of((head_size, 4, model // head_size, sub), BF),) * parts,
        [pltpu.VMEM((model, pack_len), BF), pltpu.VMEM((pack_len, 3 * sub), BF)],
    )
    inputs_back, _ = tie(inputs, qkv_parts[0])
    tokens_grad_rows, tokens_sums, tiles_kept, tiles_sent = call(
        "tokens_back",
        functools.partial(tokens_back_kernel, (items, len(in_terms), 2)),
        (inputs_back, grad_middle, mod, row_item, *in_terms, *tile_terms),
        (HBM, HBM, VMEM, VMEM) + (HBM,) * (len(in_terms) + 2),
        (rows_bf, shape_of((8, 2 * model), F32), quarter_tiles, quarter_tiles),
    )
    tile_terms = (tiles_kept, xor_swap(tiles_sent, "head", 2))

    def to_data(values):
        return dot(to_slot, values, ((0,), (0,)))

    output = to_data(output_back).astype(BF)
    tokens_came = to_packs(tokens_grad_rows)
    tokens_grad = to_data(tokens_came)

    def over_head(terms):
        while terms[0].shape[0] > 1:
            terms = halves_over_head(add_low(*terms))
        return terms

    tile_terms = tie(*tile_terms, tokens_came)[:-1]
    tied = over_head(tile_terms)
    own_tiles = call(
        "own_tiles",
        functools.partial(own_tiles_kernel, len(tied)),
        tied,
        (HBM,) * len(tied),
        (shape_of((2, fine, hidden), BF),) * group,
    )
    both_all = [own_tiles[0]]
    for i in range(1, group):
        both_all.append(lax.ppermute(own_tiles[i], "g", [(k, k ^ i) for k in range(group)]))
    if tiled:
        up_part, down_part = call(
            "place",
            functools.partial(place_kernel, group),
            (me, *both_all),
            (SMEM,) + (HBM,) * group,
            (shape_of((fine, group * hidden), F32), shape_of((group * hidden, fine), F32)),
        )
    else:
        placed = jnp.stack(both_all)[jnp.arange(group) ^ g].astype(F32)
        up_part = placed[:, 0].transpose(1, 0, 2).reshape(fine, group * hidden)
        down_part = placed[:, 1].transpose(0, 2, 1).reshape(group * hidden, fine)


    ada_cols = 6 * model // (dp_size * head_size)
    packs = segs * head_size
    (kept,) = call(
        "item_blocks",
        functools.partial(item_blocks_kernel, (group, segs, head_size, ada_cols)),
        (me, middle_sums, output_sums, tokens_sums),
        (SMEM, VMEM, VMEM, VMEM),
        (shape_of((group, packs * 8, 256), F32),),
        [pltpu.VMEM((8, 6 * model), F32)],
        out_specs=(VMEM,),
    )
    sent = jnp.concatenate([kept[k] for k in range(1, group, 2)] + [vectors], axis=0)
    count = group
    for step in reversed(bits(group)):
        came = xor_swap(sent, "g", step)
        left = count // 2
        own = (left, packs * 8, 256) if left > 1 else (packs * 4, 256)
        rows_sent = (left // 2 * packs * 8 if left > 1 else packs * 4) + 64
        kept, sent, vectors = call(
            "group_sums",
            functools.partial(group_sums_kernel, count, step),
            (kept, came, vectors),
            (VMEM,) * 3,
            (shape_of(own, F32), shape_of((rows_sent, 256), F32), shape_of((64, 256), F32)),
            out_specs=(VMEM,) * 3,
        )
        count = left
    kept = kept.reshape(packs // 2, 1, 8, 256)
    sent, _ = tie(sent, tokens_came)
    steps = [("yy", step) for step in bits(segs)] + [("head", step) for step in bits(head_size)]
    for place, (axis, step) in enumerate(steps):
        came = xor_swap(sent, axis, step)
        blocks, senders = kept.shape[0], kept.shape[1]
        end = place + 1 == len(steps)
        own = (blocks if end else blocks // 2, 2 * senders, 8, 256)
        outs = [shape_of(own, F32)]
        if not end:
            outs.append(shape_of((blocks // 2 * 2 * senders * 8 + 64, 256), F32))
        outs.append(shape_of((64, 256), F32))
        made = call(
            "pack_sums", pack_sums_kernel, (kept, came, vectors), (VMEM,) * 3, outs,
            out_specs=(VMEM,) * len(outs),
        )
        kept, vectors = made[0], made[-1]
        sent = made[1] if not end else None
    item_came = kept[0]
    vectors = vectors.reshape(4, 16, 256).transpose(1, 0, 2).reshape(16, model)
    silu_rows = jnp.pad(silu_cond.reshape(packs, items, model), ((0, 0), (0, 8 - items), (0, 0)))
    ada_grad, ada_bias_grad = call(
        "ada",
        ada_kernel,
        (me, silu_rows.reshape(packs * 8, model), item_came),
        (SMEM, VMEM, VMEM),
        (shape_of((model, ada_cols), F32), shape_of((8, ada_cols), F32)),
        [pltpu.VMEM((packs * 8, 256), F32)],
    )
    ada_bias_grad = ada_bias_grad[0]

    if parts == segs:
        terms = tie(*xor_scatter(qkv_parts, "yy"), tokens_came)[:-1]
        terms = over_head(terms)
        summed = sum(term[0].astype(F32) for term in terms)
        proj_part, qkv_part = summed[0], summed[1:]
    else:
        both = qkv_parts[0].transpose(1, 0, 2, 3).reshape(4, model, width)
        full = lax.dynamic_update_slice(
            jnp.zeros((4, model, model), BF), both, (0, 0, g * width)
        )
        summed = lax.psum_scatter(full, ("yy", "g"), scatter_dimension=2, tiled=True)
        summed = lax.psum_scatter(summed, "head", scatter_dimension=1, tiled=True).astype(F32)
        proj_part, qkv_part = summed[0], summed[1:]

    log_scale_grad = jnp.sum(vectors[2].reshape(heads_all, head_dim), axis=1)
    fc1_bias_grad = pick(vectors, 8 + z, 0)[: group * hidden]
    return (
        output,
        tokens_grad,
        ada_grad,
        ada_bias_grad,
        qkv_part,
        vectors[0],
        vectors[1],
        log_scale_grad,
        proj_part,
        vectors[3],
        up_part,
        fc1_bias_grad,
        down_part,
        vectors[4],
    )


def solution(mesh):
    head_size = mesh.shape["head"]
    dp_size = mesh.shape["dp"]
    inner = Mesh(
        mesh.devices.reshape(dp_size // head_size, head_size, head_size), ("yy", "g", "head")
    )
    dp = ("yy", "g")
    everything = ("yy", "g", "head")
    in_specs = (
        P(everything, None),
        P(everything, None),
        P(),
        P(),
        P(),
        P(),
        P(),
        P(),
        P(),
        P(),
        P(),
        P(None, "head"),
        P("head"),
        P("head", None),
        P(),
        P(),
        P(),
        P(dp, None),
        P(everything),
    )
    out_specs = (
        P(everything, None),
        P(everything, None),
        P(None, everything),
        P(everything),
        P(None, "head", dp),
        P(),
        P(),
        P(),
        P("head", dp),
        P(),
        P(dp, "head"),
        P("head"),
        P("head", dp),
        P(),
    )
    return jax.shard_map(
        shards, mesh=inner, in_specs=in_specs, out_specs=out_specs, check_vma=False
    )
```

```python
import functools

import jax
import jax.numpy as jnp
from jax import lax
from jax.experimental import pallas as pl
from jax.experimental.pallas import tpu as pltpu
from jax.sharding import Mesh, PartitionSpec as P

BF = jnp.bfloat16
F32 = jnp.float32
SMEM = pl.BlockSpec(memory_space=pltpu.SMEM)
VMEM = pl.BlockSpec(memory_space=pltpu.VMEM)
ANY = pl.BlockSpec(memory_space=pl.ANY)
HBM = "hbm"
LIMIT = 40
LIMITS = {"attend": 57, "attend_back": 57, "attend_back_end": 57, "feed": 50, "feed_weights": 57, "weights": 57, "qkv_weights": 57}
FLOPS, BYTES = 1_000_000_000, 3_000_000
TIMES = {
    "sort": 2, "first_norm": 2, "grad_mlp": 2, "attend": 26, "project": 5, "weights": 4, "feed": 12,
    "feed_weights": 12, "middle_back": 7, "proj_weights": 3, "output": 3, "attend_back": 16, "attend_back_end": 21, "add": 3,
    "qkv_weights": 8, "tokens_back": 5,
}
PLAIN = ((1,), (0,))
BY_ROW = ((1,), (1,))


def shape_of(shape, dtype):
    return jax.ShapeDtypeStruct(shape, dtype)


def dot(left, right, dims=PLAIN):
    return lax.dot_general(left, right, (dims, ((), ())), preferred_element_type=F32)


def call(name, kernel, operands, specs, outs, scratch=(), limit=LIMIT, out_specs=None):
    out_specs = out_specs or tuple(HBM if o.size >= 65536 else VMEM for o in outs)
    n_in, n_out, n_scratch = len(specs), len(outs), len(scratch)
    staged_in = [i for i, spec in enumerate(specs) if spec is HBM]
    staged_out = [i for i, spec in enumerate(out_specs) if spec is HBM]
    staged = [pltpu.VMEM(operands[i].shape, operands[i].dtype) for i in staged_in]
    staged += [pltpu.VMEM(outs[i].shape, outs[i].dtype) for i in staged_out]
    sems = [pltpu.SemaphoreType.DMA((len(staged),))] if staged else []

    def body(*refs):
        given, made = list(refs[:n_in]), list(refs[n_in : n_in + n_out])
        own = refs[n_in + n_out : n_in + n_out + n_scratch]
        held = refs[n_in + n_out + n_scratch :]
        copies = []
        for place, i in enumerate(staged_in):
            copies.append(pltpu.make_async_copy(given[i], held[place], held[-1].at[place]))
            copies[-1].start()
            given[i] = held[place]
        backs = []
        for place, i in enumerate(staged_out, len(staged_in)):
            backs.append(pltpu.make_async_copy(held[place], made[i], held[-1].at[place]))
            made[i] = held[place]
        for copy in copies:
            copy.wait()
        kernel(*given, *made, *own)
        for copy in backs:
            copy.start()
        for copy in backs:
            copy.wait()

    limit = LIMITS.get(name, limit)
    return pl.pallas_call(
        body,
        name=name,
        out_shape=tuple(outs),
        in_specs=[ANY if spec is HBM else spec for spec in specs],
        out_specs=tuple(ANY if spec is HBM else spec for spec in out_specs),
        scratch_shapes=list(scratch) + staged + sems,
        compiler_params=pltpu.CompilerParams(vmem_limit_bytes=limit * 1024 * 1024),
        cost_estimate=pl.CostEstimate(
            flops=TIMES.get(name, 1) * FLOPS, bytes_accessed=TIMES.get(name, 1) * BYTES, transcendentals=0
        ),
    )(*operands)


def row_norm(values):
    centre = values - jnp.mean(values, axis=-1, keepdims=True)
    inverse = lax.rsqrt(jnp.mean(centre * centre, axis=-1, keepdims=True) + 1e-06)
    return (centre * inverse, inverse)


def norm_back(gradient, normed, inverse):
    return inverse * (
        gradient
        - jnp.mean(gradient, axis=-1, keepdims=True)
        - normed * jnp.mean(gradient * normed, axis=-1, keepdims=True)
    )


def mod_rows(mod_ref, part, item, width):
    cols = slice(part * width, (part + 1) * width)
    rows = jnp.broadcast_to(mod_ref[0:1, cols], (item.shape[0], width))
    for index in range(1, mod_ref.shape[0]):
        rows = jnp.where(item == index, mod_ref[index : index + 1, cols], rows)
    return rows


def add_item_sums(sums_ref, part, item, values, count):
    width = values.shape[1]
    cols = slice(part * width, (part + 1) * width)
    for index in range(count):
        kept = jnp.where(item == index, values, 0.0)
        sums_ref[index : index + 1, cols] += jnp.sum(kept, axis=0, keepdims=True)


def same_head(width, head_dim):
    row = lax.broadcasted_iota(jnp.int32, (width, width), 0) // head_dim
    col = lax.broadcasted_iota(jnp.int32, (width, width), 1) // head_dim
    return (row == col).astype(BF)


def chunks(rows, size):
    return pl.loop(0, rows // size)


def at(index, size):
    return pl.ds(pl.multiple_of(index * size, size), size)


def first_norm_kernel(x_ref, mod_ref, item_ref, out_ref):
    rows, width = x_ref.shape

    @chunks(rows, 64)
    def _(i):
        r = at(i, 64)
        item = item_ref[r, :]
        normed, _ = row_norm(x_ref[r, :].astype(F32))
        scale, shift = mod_rows(mod_ref, 2, item, width), mod_rows(mod_ref, 4, item, width)
        out_ref[r, :] = (normed * (1.0 + scale) + shift).astype(BF)


def grad_mlp_kernel(up_ref, mod_ref, item_ref, out_ref, sum_ref):
    rows, width = up_ref.shape
    sum_ref[...] = jnp.zeros_like(sum_ref)

    @chunks(rows, 64)
    def _(i):
        r = at(i, 64)
        gamma = mod_rows(mod_ref, 1, item_ref[r, :], width)
        grad = (up_ref[r, :].astype(F32) * gamma).astype(BF)
        out_ref[r, :] = grad
        sum_ref[0:1, :] += jnp.sum(grad.astype(F32), axis=0, keepdims=True)


def load_columns(weight_ref, held, sems, offset_of, parts, sub):
    copies = []
    for t in range(3):
        for p in range(parts):
            copies.append(
                pltpu.make_async_copy(
                    weight_ref.at[t, :, pl.ds(pl.multiple_of(offset_of(p), sub), sub)],
                    held.at[:, pl.ds((t * parts + p) * sub, sub)],
                    sems.at[t * parts + p],
                )
            )
    for copy in copies:
        copy.start()
    return copies


def pick_heads(width, head_dim, first):
    row = lax.broadcasted_iota(jnp.int32, (width, 128), 0)
    col = lax.broadcasted_iota(jnp.int32, (width, 128), 1)
    return (row == (col - first) * head_dim).astype(BF)


def spread_heads(width, head_dim, first):
    row = lax.broadcasted_iota(jnp.int32, (128, width), 0)
    col = lax.broadcasted_iota(jnp.int32, (128, width), 1)
    return (row - first == col // head_dim).astype(BF)


def exact_dot(values, ones):
    high = values.astype(BF)
    low = (values - high.astype(F32)).astype(BF)
    return dot(high, ones) + dot(low, ones)


def attend_kernel(dims, *refs):
    group, segs, head_dim, parts, block = dims
    me_ref, first_ref, last_ref, lo_ref, hi_ref, temper_ref, qb_ref, vb_ref, w_ref = refs[:9]
    blocks = refs[9 : 9 + group]
    out_o, out_t_o, lse_ref, q_o, ql_o, k_o, v_o, inv_o = refs[9 + group : 17 + group]
    (held, block_s, q_ref, ql_ref, k_ref, v_ref, inv_ref, v_t, out_t_ref, out_s, acc, total, sems,
     in_sems, out_sems) = refs[17 + group :]
    pack_len, width = q_ref.shape
    rows = block_s.shape[1]
    seg, sub = rows // segs, width // parts
    pair, heads = 128 // head_dim, width // head_dim
    me = me_ref[0]
    loads = [
        pltpu.make_async_copy(blocks[k], block_s.at[k], in_sems.at[k]) for k in range(group)
    ]
    loads[0].start()
    copies = load_columns(w_ref, held, sems, lambda p: (p * group + me) * sub, parts, sub)
    for load in loads[1:]:
        load.start()
    same = same_head(width, head_dim)
    pick_q, pick_k = pick_heads(width, head_dim, 0), pick_heads(width, head_dim, heads)
    for copy in copies:
        copy.wait()
    for k in range(group):
        loads[k].wait()
        for y in range(segs):
            ranks = pl.ds(pl.multiple_of((y * group + (me ^ k)) * seg, 16), seg)
            made = dot(block_s[k, y * seg : (y + 1) * seg, :], held[...])
            query = made[:, :width] + qb_ref[...]
            key = made[:, width : 2 * width]
            inverse_q = lax.rsqrt(exact_dot(query * query, same) + 1e-06)
            query = query * inverse_q * temper_ref[...]
            rounded = query.astype(BF)
            q_ref[ranks, :] = rounded
            ql_ref[ranks, :] = (query - rounded.astype(F32)).astype(BF)
            inverse_k = lax.rsqrt(exact_dot(key * key, same) + 1e-06)
            k_ref[ranks, :] = (key * inverse_k).astype(BF)
            v_ref[ranks, :] = (made[:, 2 * width :] + vb_ref[...]).astype(BF)
            inv_ref[ranks, :] = exact_dot(inverse_q, pick_q) + exact_dot(inverse_k, pick_k)
    stores = []

    def store(source, target):
        stores.append(pltpu.make_async_copy(source, target, out_sems.at[len(stores)]))
        stores[-1].start()

    for source, target in (
        (q_ref, q_o), (ql_ref, ql_o), (k_ref, k_o), (v_ref, v_o), (inv_ref, inv_o)
    ):
        store(source, target)
    lanes = lax.broadcasted_iota(jnp.int32, (1, 128), 1) // head_dim
    v_t[...] = v_ref[...].T

    @pl.loop(0, pack_len // block)
    def _(q_block):
        q_rows = at(q_block, block)
        q_t = q_ref[q_rows, :].T
        low, high = lo_ref[:, q_rows], hi_ref[:, q_rows]
        acc[...] = jnp.zeros_like(acc)
        total[...] = jnp.zeros_like(total)

        @pl.loop(first_ref[q_block], last_ref[q_block])
        def _(k_block):
            k_rows = at(k_block, block)
            index = k_block * block + lax.broadcasted_iota(jnp.int32, (block, block), 0)
            seen = (index >= low) & (index < high)
            for h in range(heads):
                own = pl.ds(h * head_dim, head_dim)
                near = slice(h // pair * 128, (h // pair + 1) * 128)
                keys = k_ref[k_rows, near]
                scores = dot(jnp.where(lanes == h % pair, keys, jnp.zeros_like(keys)), q_t[near, :])
                raised = jnp.where(seen, jnp.exp(scores), 0.0)
                total[h : h + 1, :] += jnp.sum(raised, axis=0, keepdims=True)
                acc[own, :] += dot(v_t[own, k_rows], raised.astype(BF))

        for h in range(heads):
            own = pl.ds(h * head_dim, head_dim)
            acc[own, :] = acc[own, :] / total[h : h + 1, :]
            lse_ref[h : h + 1, q_rows] = jnp.log(total[h : h + 1, :])
        out_t_ref[:, q_rows] = acc[...]
        out_s[q_rows, :] = acc[...].T.astype(BF)

    for y in range(segs):
        for g in range(group):
            start = (y * group + g) * seg
            store(out_s.at[pl.ds(start, seg), :], out_o.at[g, pl.ds(y * seg, seg), :])
    store(out_t_ref, out_t_o)
    for copy in stores:
        copy.wait()


def attend_back_heads(dims, refs, scratch, outs):
    head_dim, block, near = dims
    first_ref, last_ref, lo_ref, hi_ref, lse_ref, q_ref, k_ref, v_ref, out_t_ref, g_s = refs
    k_t, dk_acc, dv_acc, acc, sums = scratch
    dq_ref, dk_ref, dv_ref = outs
    pack_len = q_ref.shape[0]
    pair = 128 // head_dim
    lanes = lax.broadcasted_iota(jnp.int32, (1, 128), 1) // head_dim
    k_t[...] = k_ref[...].T
    dk_acc[...] = jnp.zeros_like(dk_acc)
    dv_acc[...] = jnp.zeros_like(dv_acc)

    @pl.loop(0, pack_len // block)
    def _(q_block):
        q_rows = at(q_block, block)
        queries, grads = q_ref[q_rows, :], g_s[q_rows, :]
        q_t, g_t = queries.T, grads.T
        low, high = lo_ref[:, q_rows], hi_ref[:, q_rows]
        weighted = g_t.astype(F32) * out_t_ref[:, q_rows]
        for h in range(pair):
            sums[h : h + 1, :] = jnp.sum(
                weighted[h * head_dim : (h + 1) * head_dim, :], axis=0, keepdims=True
            )
        acc[...] = jnp.zeros_like(acc)

        @pl.loop(first_ref[q_block], last_ref[q_block])
        def _(k_block):
            k_rows = at(k_block, block)
            keys, values = k_ref[k_rows, :], v_ref[k_rows, :]
            index = k_block * block + lax.broadcasted_iota(jnp.int32, (block, block), 0)
            seen = (index >= low) & (index < high)
            for h in range(pair):
                own = pl.ds(h * head_dim, head_dim)
                row = near * pair + h
                mine = lanes == h
                scores = dot(jnp.where(mine, keys, jnp.zeros_like(keys)), q_t)
                probs = jnp.where(seen, jnp.exp(scores - lse_ref[row : row + 1, q_rows]), 0.0)
                grad_probs = dot(jnp.where(mine, values, jnp.zeros_like(values)), g_t)
                grad_scores = (probs * (grad_probs - sums[h : h + 1, :])).astype(BF)
                acc[own, :] += dot(k_t[own, k_rows], grad_scores)
                dk_acc[k_rows, :] += dot(
                    grad_scores, jnp.where(mine, queries, jnp.zeros_like(queries))
                )
                dv_acc[k_rows, :] += dot(
                    probs.astype(BF), jnp.where(mine, grads, jnp.zeros_like(grads))
                )

        dq_ref[q_rows, :] = acc[...].T.astype(BF)

    dk_ref[...] = dk_acc[...].astype(BF)
    dv_ref[...] = dv_acc[...].astype(BF)


def load_pair(dims, ins, held, sems):
    group, segs, near = dims
    in_ref, q_ref, k_ref, v_ref, out_t_ref = ins
    q_s, k_s, v_s, out_s, g_s = held
    cols = pl.ds(near * 128, 128)
    seg = in_ref.shape[1] // segs
    moves = [(q_ref.at[:, cols], q_s), (k_ref.at[:, cols], k_s), (v_ref.at[:, cols], v_s)]
    moves.append((out_t_ref.at[cols, :], out_s))
    for y in range(segs):
        for g in range(group):
            start = (y * group + g) * seg
            moves.append((in_ref.at[g, pl.ds(y * seg, seg), cols], g_s.at[pl.ds(start, seg), :]))
    copies = []
    for place, (source, target) in enumerate(moves):
        copies.append(pltpu.make_async_copy(source, target, sems.at[place]))
        copies[-1].start()
    return copies


def attend_back_kernel(dims, *refs):
    group, segs, head_dim, block, near = dims
    ranges, lse_ref, ins, outs = refs[:4], refs[4], refs[5:10], refs[10:13]
    held, scratch, made, sems, out_sems = refs[13:18], refs[18:23], refs[23:26], refs[26], refs[27]
    for copy in load_pair((group, segs, near), ins, held, sems):
        copy.wait()
    attend_back_heads((head_dim, block, near), (*ranges, lse_ref, *held), scratch, made)
    stores = [pltpu.make_async_copy(made[i], outs[i], out_sems.at[i]) for i in range(3)]
    for copy in stores:
        copy.start()
    for copy in stores:
        copy.wait()


def attend_back_end_kernel(dims, *refs):
    group, segs, head_dim, parts, block, pairs = dims
    me_ref, temper_ref, w_ref, inv_ref, ql_ref = refs[:5]
    ranges, lse_ref, ins = refs[5:9], refs[9], refs[10:15]
    earlier, refs = refs[15 : 12 + 3 * pairs], refs[12 + 3 * pairs :]
    sent, (dqkv_o, sums_ref), refs = refs[:group], refs[group : 2 + group], refs[2 + group :]
    held, scratch, made, refs = refs[:5], refs[5:10], refs[10:13], refs[13:]
    (w_s, inv_s, q_s, ql_s, k_s, dqkv_s, sent_s), (sems, w_sems, in_sems, out_sems) = refs[:7], refs[7:]
    pack_len, width = q_s.shape
    rows = sent_s.shape[1]
    seg, sub = rows // segs, width // parts
    heads = width // head_dim
    me = me_ref[0]
    loads = load_pair((group, segs, pairs - 1), ins, held, sems)
    last = pl.ds((pairs - 1) * 128, 128)
    copies = load_columns(w_ref, w_s, w_sems, lambda p: (p * group + me) * sub, parts, sub)
    moves = [(inv_ref, inv_s), (ins[1], q_s), (ql_ref, ql_s), (ins[2], k_s)]
    for p in range(pairs - 1):
        for which in range(3):
            cols = pl.ds(p * 128, 128)
            moves.append((earlier[3 * p + which], made[which].at[:, cols]))
    for place, (source, target) in enumerate(moves):
        copies.append(pltpu.make_async_copy(source, target, in_sems.at[place]))
        copies[-1].start()
    for load in loads:
        load.wait()
    attend_back_heads(
        (head_dim, block, pairs - 1),
        (*ranges, lse_ref, *held),
        scratch,
        tuple(ref.at[:, last] for ref in made),
    )
    same = same_head(width, head_dim)
    spread_q, spread_k = spread_heads(width, head_dim, 0), spread_heads(width, head_dim, heads)
    sums_ref[...] = jnp.zeros_like(sums_ref)
    for copy in copies:
        copy.wait()
    stores = []
    dq_s, dk_s, dv_s = made
    for k in reversed(range(group)):
        whole = slice(k * rows, (k + 1) * rows)
        for y in range(segs):
            ranks = pl.ds(pl.multiple_of((y * group + (me ^ k)) * seg, 16), seg)
            own = slice(k * rows + y * seg, k * rows + (y + 1) * seg)
            inverse = inv_s[ranks, :]
            query = q_s[ranks, :].astype(F32) + ql_s[ranks, :].astype(F32)
            unit = query / temper_ref[...]
            raw = dq_s[ranks, :].astype(F32)
            grad = raw * temper_ref[...]
            grad_query = exact_dot(inverse, spread_q) * (grad - unit * exact_dot(grad * unit, same))
            unit_k = k_s[ranks, :].astype(F32)
            grad = dk_s[ranks, :].astype(F32)
            grad_key = exact_dot(inverse, spread_k) * (
                grad - unit_k * exact_dot(grad * unit_k, same)
            )
            grad_query, grad_value = grad_query.astype(BF), dv_s[ranks, :]
            dqkv_s[own, :width] = grad_query
            dqkv_s[own, width : 2 * width] = grad_key.astype(BF)
            dqkv_s[own, 2 * width :] = grad_value
            for index, values in enumerate((grad_query, grad_value, raw * query)):
                sums_ref[index : index + 1, :] += jnp.sum(
                    values.astype(F32), axis=0, keepdims=True
                )
        sent_s[k] = dot(dqkv_s[whole, :], w_s[...], BY_ROW).astype(BF)
        own = pl.ds(k * rows, rows)
        for source, target in ((sent_s.at[k], sent[k]), (dqkv_s.at[own, :], dqkv_o.at[own, :])):
            stores.append(pltpu.make_async_copy(source, target, out_sems.at[len(stores)]))
            stores[-1].start()
    for copy in stores:
        copy.wait()


def project_kernel(
    parts, ret_ref, wp_ref, pb_ref, x_ref, mod_ref, item_ref, attn_ref, branch_ref, middle_ref, out_ref, made
):
    group, rows, width = ret_ref.shape
    model = x_ref.shape[1]
    sub = width // parts
    for g in range(group):
        for p in range(parts):
            start = (p * group + g) * sub
            attn_ref[:, start : start + sub] = ret_ref[g, :, p * sub : (p + 1) * sub]
    made[...] = dot(attn_ref[...], wp_ref[...]) + pb_ref[...].astype(F32)
    branch_ref[...] = made[...].astype(BF)

    @chunks(rows, 64)
    def _(i):
        r = at(i, 64)
        item = item_ref[r, :]
        middle = x_ref[r, :].astype(F32) + mod_rows(mod_ref, 0, item, model) * made[r, :]
        middle_ref[r, :] = middle
        normed, _ = row_norm(middle)
        scale, shift = mod_rows(mod_ref, 3, item, model), mod_rows(mod_ref, 5, item, model)
        out_ref[r, :] = (normed * (1.0 + scale) + shift).astype(BF)


def add_blocks(terms, outs):
    count = outs[0].shape[0]
    for j in range(terms[0].shape[0]):
        made = sum(term[j].astype(F32) for term in terms).astype(BF)
        outs[j // count][j % count] = made


def weights_kernel(fc1_ref, fc2_ref, w1_ref, w2_ref, sems):
    segs, head_size, _, hidden = fc1_ref.shape
    half = fc2_ref.shape[3]
    copies = []
    for y in range(segs):
        for z in range(head_size):
            own = pl.ds(z * hidden, hidden)
            rows = pl.ds(y * half, half)
            for source, target in (
                (fc1_ref.at[y, z, pl.ds(0, half), :], w1_ref.at[rows, own]),
                (fc2_ref.at[y, z], w2_ref.at[own, rows]),
            ):
                copies.append(pltpu.make_async_copy(source, target, sems.at[len(copies)]))
                copies[-1].start()
    for copy in copies:
        copy.wait()


def feed_kernel(count, *refs):
    w1, w2, b1_ref = refs[:3]
    ins, grads = refs[3 : 3 + count], refs[3 + count : 3 + 2 * count]
    rest = refs[3 + 2 * count :]
    back, outs = rest[:count], rest[count : 2 * count]
    act_ref, gh_ref, sum_ref = rest[2 * count : 2 * count + 3]
    in_s, grad_s, back_s, out_s, act_s, gh_s, pre, grad, in_sems, out_sems = rest[2 * count + 3 :]
    rows = ins[0].shape[0]
    loads, stores = [], []
    for k in range(count):
        pair = (
            pltpu.make_async_copy(ins[k], in_s.at[k], in_sems.at[2 * k]),
            pltpu.make_async_copy(grads[k], grad_s.at[k], in_sems.at[2 * k + 1]),
        )
        pair[0].start()
        pair[1].start()
        loads.append(pair)
    sum_ref[...] = jnp.zeros_like(sum_ref)

    def store(source, target, index):
        stores.append(pltpu.make_async_copy(source, target, out_sems.at[index]))
        stores[-1].start()

    def front(k):
        loads[k][0].wait()
        pre[k % 2] = dot(in_s[k], w1[...]) + b1_ref[...]
        loads[k][1].wait()
        grad[k % 2] = dot(grad_s[k], w2[...], BY_ROW)

    def middle(k):
        total = 0.0
        for start in range(0, rows, 32):
            r = slice(start, start + 32)
            value = pre[k % 2, r, :]
            square = value * value
            gate = jnp.tanh(value * (0.7978845608028654 + 0.035677408136300125 * square))
            half = 0.5 + 0.5 * gate
            act = value * half
            slope = half + act * (1.0 - gate) * (0.7978845608028654 + 0.10703222440890037 * square)
            back_grad = (slope * grad[k % 2, r, :]).astype(BF)
            act_s[k, r, :] = act.astype(BF)
            gh_s[k, r, :] = back_grad
            total = total + jnp.sum(back_grad.astype(F32), axis=0, keepdims=True)
        sum_ref[0:1, :] += total
        own = pl.ds(k * rows, rows)
        store(act_s.at[k], act_ref.at[own, :], 4 * k)
        store(gh_s.at[k], gh_ref.at[own, :], 4 * k + 1)

    def end(k):
        back_s[k] = dot(gh_s[k], w1[...], BY_ROW).astype(BF)
        store(back_s.at[k], back[k], 4 * k + 2)
        out_s[k] = dot(act_s[k], w2[...]).astype(BF)
        store(out_s.at[k], outs[k], 4 * k + 3)

    order = list(reversed(range(count)))
    front(order[0])
    for place, k in enumerate(order):
        if place + 1 < count:
            front(order[place + 1])
        middle(k)
        end(k)
    for started in stores:
        started.wait()


def turned(index, count):
    made = 0
    while count > 1:
        made, index, count = made * 2 + index % 2, index // 2, count // 2
    return made


def feed_weights_kernel(dims, *refs):
    count, group, split, halves, term_count = dims
    me_ref, acts, ghs = refs[0], refs[1 : 1 + halves], refs[1 + halves : 1 + 2 * halves]
    refs = refs[1 + 2 * halves :]
    ins, grads, refs = refs[:count], refs[count : 2 * count], refs[2 * count :]
    terms, refs = refs[:term_count], refs[term_count:]
    outs, sum_o, rest = refs[: 2 * split], refs[2 * split], refs[2 * split + 1 :]
    in_t, grad_t, act_s, gh_s, in_s, grad_s, term_s, sum_s, tile_s, in_sems, out_sems = rest
    rows, model = in_s.shape[1:]

    def load(source, target, index):
        copy = pltpu.make_async_copy(source, target, in_sems.at[index])
        copy.start()
        return copy

    part_rows = act_s.shape[0] // halves
    own = [pl.ds(k * part_rows, part_rows) for k in range(halves)]
    in_loads = [load(ins[k], in_s.at[k], k) for k in range(count)]
    index = count
    gh_loads = [load(ghs[k], gh_s.at[own[k], :], index + k) for k in range(halves)]
    index += halves
    grad_loads = [load(grads[k], grad_s.at[k], index + k) for k in range(count)]
    index += count
    act_loads = [load(acts[k], act_s.at[own[k], :], index + k) for k in range(halves)]
    index += halves
    term_loads = [load(terms[k], term_s.at[k], index + k) for k in range(term_count)]
    for k in range(count):
        in_loads[k].wait()
        in_t[:, k * rows : (k + 1) * rows] = in_s[k].T
    for copy in gh_loads:
        copy.wait()
    stores = []

    def store(source, target):
        stores.append(pltpu.make_async_copy(source, target, out_sems.at[len(stores)]))
        stores[-1].start()

    part = model // split
    fine = part // group
    _, _, head_size, _, _, hidden = tile_s.shape

    def tiles(y, which, left, right):
        start = pl.multiple_of((me_ref[1] ^ y) * part, part) if split > 1 else 0
        for j in range(head_size):
            z = me_ref[2] ^ turned(j, head_size)
            cols = slice(None)
            if split > 1:
                cols = pl.ds(pl.multiple_of(z * hidden, hidden), hidden)
            made = dot(left[pl.ds(start, part), :], right[:, cols]).astype(BF)
            for g in range(group):
                to = (me_ref[0] ^ g) if group > 1 else 0
                tile_s[which, y, j, to] = made[g * fine : (g + 1) * fine, :]
        store(tile_s.at[which, y], outs[which * split + y])

    for y in reversed(range(split)):
        tiles(y, 0, in_t, gh_s)
    for k in range(count):
        grad_loads[k].wait()
        grad_t[:, k * rows : (k + 1) * rows] = grad_s[k].T
    for copy in act_loads:
        copy.wait()
    for y in reversed(range(split)):
        tiles(y, 1, grad_t, act_s)
    for copy in term_loads:
        copy.wait()
    sum_s[...] = sum(term_s[k].astype(F32) for k in range(term_count)).astype(BF)
    store(sum_s, sum_o)
    for copy in stores:
        copy.wait()


def middle_back_kernel(
    dims, middle_ref, branch_ref, up_ref, mod_ref, item_ref, wp_ref, *refs
):
    parts, items, count = dims
    terms, (out_ref, gb_ref, gm_ref, sums_ref, col_ref, attn) = refs[:count], refs[count:]
    rows, model = middle_ref.shape
    group, _, width = out_ref.shape
    sub = width // parts
    sums_ref[...] = jnp.zeros_like(sums_ref)
    col_ref[...] = jnp.zeros_like(col_ref)

    @chunks(rows, 64)
    def _(i):
        r = at(i, 64)
        item = item_ref[r, :]
        grad_in = sum(term[r, :].astype(F32) for term in terms)
        normed, inverse = row_norm(middle_ref[r, :])
        scale = mod_rows(mod_ref, 3, item, model)
        grad_middle = up_ref[r, :].astype(F32) + norm_back(grad_in * (1.0 + scale), normed, inverse)
        gm_ref[r, :] = grad_middle
        grad_branch = (grad_middle * mod_rows(mod_ref, 0, item, model)).astype(BF)
        gb_ref[r, :] = grad_branch
        col_ref[0:1, :] += jnp.sum(grad_branch.astype(F32), axis=0, keepdims=True)
        add_item_sums(sums_ref, 0, item, grad_middle * branch_ref[r, :].astype(F32), items)
        add_item_sums(sums_ref, 1, item, grad_in * normed, items)
        add_item_sums(sums_ref, 2, item, grad_in, items)

    attn[...] = dot(gb_ref[...], wp_ref[...], BY_ROW).astype(BF)
    for g in range(group):
        for p in range(parts):
            start = (p * group + g) * sub
            out_ref[g, :, p * sub : (p + 1) * sub] = attn[:, start : start + sub]


def output_kernel(dims, middle_ref, up_ref, mod_ref, item_ref, bias_ref, *refs):
    items, count, proj_count, tile_count = dims
    terms, refs = refs[:count], refs[count:]
    projs, refs = refs[:proj_count], refs[proj_count:]
    tiles, (out_ref, sums_ref, proj_ref, kept_ref, sent_ref) = refs[:tile_count], refs[tile_count:]
    add_blocks(tiles, (kept_ref, sent_ref))
    proj_ref[...] = sum(proj[...].astype(F32) for proj in projs).astype(BF)
    rows, model = middle_ref.shape
    sums_ref[...] = jnp.zeros_like(sums_ref)

    @chunks(rows, 64)
    def _(i):
        r = at(i, 64)
        item = item_ref[r, :]
        made = sum(term[r, :].astype(F32) for term in terms) + bias_ref[...].astype(F32)
        gamma = mod_rows(mod_ref, 1, item, model)
        out_ref[r, :] = (middle_ref[r, :] + gamma * made).astype(BF)
        add_item_sums(sums_ref, 0, item, up_ref[r, :].astype(F32) * made, items)


def tokens_back_kernel(dims, x_ref, gm_ref, mod_ref, item_ref, *refs):
    items, count = dims
    terms, (out_ref, sums_ref) = refs[:count], refs[count:]
    rows, model = x_ref.shape
    sums_ref[...] = jnp.zeros_like(sums_ref)

    @chunks(rows, 64)
    def _(i):
        r = at(i, 64)
        item = item_ref[r, :]
        grad_in = sum(term[r, :].astype(F32) for term in terms)
        normed, inverse = row_norm(x_ref[r, :].astype(F32))
        scale = mod_rows(mod_ref, 2, item, model)
        out_ref[r, :] = (
            gm_ref[r, :] + norm_back(grad_in * (1.0 + scale), normed, inverse)
        ).astype(BF)
        add_item_sums(sums_ref, 0, item, grad_in * normed, items)
        add_item_sums(sums_ref, 1, item, grad_in, items)


def proj_weights_kernel(dims, me_ref, attn_ref, gb_ref, *refs):
    group, split = dims
    outs, (left_t, right) = refs[:group], refs[group:]
    left_t[...] = attn_ref[...].T
    chunk, head_size, tall, wide = outs[0].shape
    for k in range(group):
        for y in range(chunk):
            part = (me_ref[1] ^ y) if split else y
            start = pl.multiple_of((part * group + (me_ref[0] ^ k)) * wide, wide)
            right[:, y * wide : (y + 1) * wide] = gb_ref[:, pl.ds(start, wide)]
        for j in range(head_size):
            z = (me_ref[2] ^ turned(j, head_size)) if split else j
            made = dot(left_t[pl.ds(pl.multiple_of(z * tall, tall), tall), :], right[...])
            for y in range(chunk):
                outs[k][y, j] = made[:, y * wide : (y + 1) * wide].astype(BF)


def qkv_weights_kernel(dims, me_ref, dqkv_ref, *refs):
    count, chunk, split, proj_count = dims
    ins, refs = refs[:count], refs[count:]
    projs, refs = refs[:proj_count], refs[proj_count:]
    outs, (left_t, right) = refs[:chunk], refs[chunk:]
    rows = ins[0].shape[0]
    for k in range(count):
        left_t[:, k * rows : (k + 1) * rows] = ins[k][...].T
    head_size, _, tall, wide = outs[0].shape
    for y in reversed(range(chunk)):
        part = (me_ref[1] ^ y) if split else y
        for t in range(3):
            start = pl.multiple_of((t * chunk + part) * wide, wide)
            right[:, t * wide : (t + 1) * wide] = dqkv_ref[:, pl.ds(start, wide)]
        for j in range(head_size):
            z = (me_ref[2] ^ turned(j, head_size)) if split else j
            made = dot(left_t[pl.ds(pl.multiple_of(z * tall, tall), tall), :], right[...])
            outs[y][j, 0] = sum(proj[y, j].astype(F32) for proj in projs).astype(BF)
            for t in range(3):
                outs[y][j, 1 + t] = made[:, t * wide : (t + 1) * wide].astype(BF)


def sort_kernel(pack_len, dest_ref, tokens_ref, cot_ref, to_slot_ref, tokens_out, cot_out):
    rows = tokens_ref.shape[0]
    pack = dest_ref[...] // pack_len
    other = jnp.broadcast_to(pack, (8, rows)).astype(F32).T[:, 0:1].astype(jnp.int32)
    this = lax.broadcasted_iota(jnp.int32, (rows, rows), 1)
    that = lax.broadcasted_iota(jnp.int32, (rows, rows), 0)
    before = (other < pack) | ((other == pack) & (that < this))
    slot = jnp.sum(before.astype(jnp.int32), axis=0, keepdims=True)
    to_slot_ref[...] = (slot == that).astype(F32).astype(BF)
    tokens_out[...] = dot(to_slot_ref[...], tokens_ref[...]).astype(BF)
    cot_out[...] = dot(to_slot_ref[...], cot_ref[...]).astype(BF)


def item_blocks_kernel(dims, me_ref, middle_ref, output_ref, tokens_ref, out_ref, joined):
    group, segs, head_size, size = dims
    model = output_ref.shape[1]
    parts = (
        (middle_ref, 0), (output_ref, 0), (tokens_ref, 0),
        (middle_ref, 1), (tokens_ref, 1), (middle_ref, 2),
    )
    for part, (ref, start) in enumerate(parts):
        joined[:, part * model : (part + 1) * model] = ref[:, start * model : (start + 1) * model]
    place = me_ref[1] * head_size + me_ref[2]
    for g in range(group):
        for y in range(segs):
            for z in range(head_size):
                start = ((y * group + g) * head_size + z) * size
                block = place ^ (y * head_size + z)
                rows = pl.ds(pl.multiple_of(block * 8, 8), 8)
                out_ref[me_ref[0] ^ g, rows, 0:size] = joined[:, start : start + size]


def group_sums_kernel(count, bit, kept_ref, came_ref, vector_ref, own_ref, sent_ref, sum_ref):
    rows = kept_ref.shape[1]
    vectors = vector_ref[...] + came_ref[pl.ds(came_ref.shape[0] - 64, 64), :]
    sum_ref[...] = vectors
    last = count == 2
    place = 0
    for k in range(0, count, 2):
        made = kept_ref[k] + came_ref[pl.ds(k // 2 * rows, rows), :]
        if last:
            half = rows // 2
            own_ref[...] = made[:half]
            sent_ref[0:half, :] = made[half:]
        elif k // 2 % 2 == 0:
            own_ref[k // 2] = made
        else:
            own_ref[k // 2] = made
            sent_ref[place * rows : (place + 1) * rows, :] = made
            place += 1
    sent_ref[pl.ds(sent_ref.shape[0] - 64, 64), :] = vectors


def pack_sums_kernel(kept_ref, came_ref, vector_ref, own_ref, *refs):
    blocks, senders = own_ref.shape[0] * (2 if len(refs) == 2 else 1), kept_ref.shape[1]
    vectors = vector_ref[...] + came_ref[pl.ds(came_ref.shape[0] - 64, 64), :]
    refs[-1][...] = vectors
    for c in range(blocks):
        for t in range(2 * senders):
            if t < senders:
                value = kept_ref[c, t]
            else:
                value = came_ref[pl.ds((c * senders + t - senders) * 8, 8), :]
            if len(refs) == 1 or c < blocks // 2:
                own_ref[c, t] = value
            else:
                refs[0][pl.ds(((c - blocks // 2) * 2 * senders + t) * 8, 8), :] = value
    if len(refs) == 2:
        refs[0][pl.ds(refs[0].shape[0] - 64, 64), :] = vectors


def ada_kernel(me_ref, silu_ref, blocks_ref, grad_ref, bias_ref, held):
    head_size = me_ref[3]
    place = me_ref[1] * head_size + me_ref[2]
    for c in range(blocks_ref.shape[0]):
        sender = place ^ turned(c, blocks_ref.shape[0])
        held[pl.ds(pl.multiple_of(sender * 8, 8), 8), :] = blocks_ref[c]
    low = held[:, 0 : grad_ref.shape[1]].astype(BF)
    bias_ref[...] = jnp.broadcast_to(
        jnp.sum(low.astype(F32), axis=0, keepdims=True), bias_ref.shape
    )
    grad_ref[...] = lax.dot_general(
        silu_ref[...], low, (((0,), (0,)), ((), ())), preferred_element_type=F32
    )


def add_kernel(counts, *refs):
    terms, outs = refs[: sum(counts)], refs[sum(counts) :]
    for place, count in enumerate(counts):
        add_blocks(terms[:count], outs[2 * place : 2 * place + 2])
        terms = terms[count:]


def own_tiles_kernel(*refs):
    ups, downs, outs = refs[:2], refs[2:4], refs[4:]
    for i, out in enumerate(outs):
        for which, terms in enumerate((ups, downs)):
            out[which] = sum(term[0, i].astype(F32) for term in terms).astype(BF)


def place_kernel(group, me_ref, *refs):
    blocks, (up_ref, down_ref) = refs[:group], refs[group:]
    hidden = blocks[0].shape[2]
    for i in range(group):
        own = pl.ds(pl.multiple_of((me_ref[0] ^ i) * hidden, hidden), hidden)
        up_ref[:, own] = blocks[i][0].astype(F32)
        down_ref[own, :] = blocks[i][1].astype(F32).T


def vector_parts_kernel(dims, me_ref, qkv_ref, branch_ref, mlp_ref, *refs):
    group, parts, head_size = dims
    hidden_refs, (flat_ref, out_ref) = refs[:-2], refs[-2:]
    sub = qkv_ref.shape[1] // parts
    hidden = hidden_refs[0].shape[1] // head_size
    out_ref[...] = jnp.zeros_like(out_ref)
    for p in range(parts):
        own = pl.ds(pl.multiple_of((p * group + me_ref[0]) * sub, sub), sub)
        for row in range(3):
            out_ref[row : row + 1, own] = qkv_ref[row : row + 1, p * sub : (p + 1) * sub]
    out_ref[3:4, :] = branch_ref[0:1, :]
    out_ref[4:5, :] = mlp_ref[0:1, :]
    if hidden % 128 == 0:
        own = pl.ds(pl.multiple_of(me_ref[0] * hidden, hidden), hidden)
        for z in range(head_size):
            cols = slice(z * hidden, (z + 1) * hidden)
            out_ref[8 + z : 9 + z, own] = sum(ref[0:1, cols] for ref in hidden_refs)
    for c in range(out_ref.shape[1] // 256):
        flat_ref[c * 16 : (c + 1) * 16, :] = out_ref[:, c * 256 : (c + 1) * 256]


def to_packs(rows):
    return lax.all_to_all(rows, ("yy", "head"), split_axis=0, concat_axis=0, tiled=True)


def over_group(blocks):
    return lax.all_to_all(blocks, "g", split_axis=0, concat_axis=0, tiled=True)


def bits(count):
    steps = []
    while count > 1:
        count //= 2
        steps.append(count)
    return steps


def xor_swap(values, axis, step):
    size = lax.axis_size(axis)
    return lax.ppermute(values, axis, [(i, i ^ step) for i in range(size)])


def xor_gather(block, axis):
    blocks = {0: block}
    for step in bits(lax.axis_size(axis)):
        for k in list(blocks):
            blocks[k ^ step] = xor_swap(blocks[k], axis, step)
    return [blocks[k] for k in range(len(blocks))]


def xor_scatter(blocks, axis):
    terms = {k: [block] for k, block in enumerate(blocks)}
    for step in reversed(bits(lax.axis_size(axis))):
        for k in reversed([k for k in terms if k & step]):
            terms[k ^ step].append(xor_swap(add_low(*terms.pop(k)), axis, step))
    return terms[0]


def halves_over_head(values):
    count = lax.axis_size("head")
    step = count // values.shape[0]
    half = values.shape[0] // 2
    return values[:half], xor_swap(values[half:], "head", step)


def add_low(*terms):
    if len(terms) == 1:
        return terms[0]
    return sum(term.astype(F32) for term in terms).astype(terms[0].dtype)


def butterfly(values, axis):
    for step in bits(lax.axis_size(axis)):
        values = values + xor_swap(values, axis, step)
    return values


def pick(values, index, axis):
    return lax.dynamic_index_in_dim(values, index, axis, keepdims=False)


def xor_blocks(values, axis, dim):
    me = lax.axis_index(axis)
    return [pick(values, me ^ k, dim) for k in range(lax.axis_size(axis))]


def tie(*values):
    return lax.optimization_barrier(values)


def tie_groups(*groups):
    tied = list(tie(*[value for group in groups for value in group]))
    return [[tied.pop(0) for _ in group] for group in groups]


def shards(
    tokens,
    cotangent,
    class_table,
    ada_weight,
    ada_bias,
    qkv_weight,
    q_bias,
    v_bias,
    log_scale,
    proj_weight,
    proj_bias,
    fc1_weight,
    fc1_bias,
    fc2_weight,
    fc2_bias,
    item_lens,
    class_ids,
    section_ids,
    destination,
):
    segs = lax.axis_size("yy")
    group = lax.axis_size("g")
    head_size = lax.axis_size("head")
    yy, g, z = lax.axis_index("yy"), lax.axis_index("g"), lax.axis_index("head")
    me = jnp.stack([g, yy, z, jnp.int32(head_size)]).astype(jnp.int32)
    pack = yy * head_size + z
    rows, model = tokens.shape
    heads_all = log_scale.shape[0]
    head_dim = model // heads_all
    heads = heads_all // group
    width = model // group
    dp_size = segs * group
    pack_len = rows * head_size
    seg = rows // segs
    items = item_lens.shape[1]
    block = min(256, pack_len)
    col = model // dp_size
    parts = segs if col % 128 == 0 else 1
    sub = width // parts

    def own_cols(values):
        return pick(values.reshape(parts, group, sub), g, 1).reshape(1, width)

    rows_bf, rows_f32 = shape_of((rows, model), BF), shape_of((rows, model), F32)
    to_slot, sorted_tokens, sorted_cotangent = call(
        "sort",
        functools.partial(sort_kernel, pack_len),
        (destination[None, :], tokens, cotangent),
        (VMEM, HBM, HBM),
        (shape_of((rows, rows), BF), rows_bf, rows_bf),
    )
    inputs = to_packs(sorted_tokens)

    hidden = fc1_weight.shape[1] // group
    units = head_size * hidden
    half = model // segs
    fc1_own = lax.dynamic_slice(fc1_weight, (yy * half, g * hidden), (half, hidden))
    fc1_bias_own = lax.dynamic_slice(fc1_bias, (g * hidden,), (hidden,))
    fc2_own = lax.dynamic_slice(fc2_weight, (g * hidden, yy * half), (hidden, half))
    fc1_sent = jnp.concatenate(
        [fc1_own, jnp.broadcast_to(fc1_bias_own[None, :], (16, hidden))], axis=0
    )
    fc1_all = lax.all_gather(fc1_sent, ("yy", "head"), axis=0)
    fc1_all = fc1_all.reshape(segs, head_size, half + 16, hidden)
    fc2_all = lax.all_gather(fc2_own, ("yy", "head"), axis=0)
    fc2_all = fc2_all.reshape(segs, head_size, hidden, half)
    fc1_bias_here = fc1_all[0, :, half].reshape(1, units).astype(F32)
    tiled = hidden % 128 == 0
    if tiled:
        fc1_here, fc2_here = call(
            "weights",
            weights_kernel,
            (fc1_all, fc2_all),
            (ANY, ANY),
            (shape_of((model, units), BF), shape_of((units, model), BF)),
            [pltpu.SemaphoreType.DMA((2 * segs * head_size,))],
            out_specs=(VMEM, VMEM),
        )
    else:
        fc1_here = fc1_all[:, :, :half].transpose(0, 2, 1, 3).reshape(model, units)
        fc2_here = fc2_all.transpose(1, 2, 0, 3).reshape(units, model)

    lens_here = pick(item_lens, pack, 0)
    class_here = pick(class_ids, pack, 0)
    order_key = class_here * items + jnp.arange(items, dtype=jnp.int32)
    item_rank = jnp.sum(
        jnp.where(order_key[None, :] < order_key[:, None], lens_here[None, :], 0), axis=1
    )
    item_pos = jnp.cumsum(lens_here) - lens_here
    item_end = item_rank + lens_here

    def items_of(rank):
        return (rank[:, None] >= item_rank[None, :]) & (rank[:, None] < item_end[None, :])

    rank_all = jnp.arange(pack_len, dtype=jnp.int32)
    member = items_of(rank_all)

    def of_item(values):
        return jnp.sum(jnp.where(member, values[None, :], 0), axis=1)

    section_here = lax.ppermute(
        section_ids[0],
        ("g", "head"),
        [(a * head_size + b, b * head_size + a) for a in range(group) for b in range(head_size)],
    )
    position = rank_all - of_item(item_rank - item_pos)
    section_rank = jnp.sum(
        jnp.where(rank_all[None, :] == position[:, None], section_here[None, :], 0), axis=1
    )
    up_to = jnp.sum((section_here[None, :] <= section_rank[:, None]).astype(jnp.int32), axis=1)
    low = of_item(item_rank)
    high = jnp.minimum(up_to + of_item(item_rank - item_pos), of_item(item_end))
    first = low[::block] // block
    last = (high[block - 1 :: block] + block - 1) // block
    low, high = low[None, :], high[None, :]

    row_rank = (
        (jnp.arange(segs, dtype=jnp.int32)[:, None] * group + g) * seg
        + jnp.arange(seg, dtype=jnp.int32)[None, :]
    ).reshape(rows)
    row_item = jnp.sum(
        jnp.where(items_of(row_rank), jnp.arange(items, dtype=jnp.int32)[None, :], 0), axis=1
    )[:, None]

    class_rows = jnp.take(class_table, class_ids.reshape(-1), axis=0).astype(F32)
    silu_cond = jax.nn.silu(class_rows).astype(BF)
    silu_here = lax.dynamic_slice_in_dim(silu_cond, pack * items, items, 0)
    mod = jnp.dot(silu_here, ada_weight, preferred_element_type=F32) + ada_bias.astype(F32)

    (attn_in,) = call("first_norm",
        first_norm_kernel, (inputs, mod, row_item), (HBM, VMEM, VMEM), (shape_of((rows, model), BF),)
    )
    attn_blocks = xor_gather(attn_in, "g")
    per_part = sub // head_dim
    scale_here = pick(log_scale.reshape(parts, group, per_part), g, 1).reshape(heads)
    temper = jnp.repeat(jnp.exp(scale_here), head_dim)[None, :]
    wide = shape_of((pack_len, width), BF)
    tall = shape_of((width, pack_len), F32)
    sorted_cotangent, _ = tie(sorted_cotangent, inputs)
    upstream = to_packs(sorted_cotangent)
    def near_blocks(own):
        blocks = {0: own}
        for step in bits(group)[1:]:
            for k in list(blocks):
                blocks[k ^ step] = xor_swap(blocks[k], "g", step)
        return [blocks[k] for k in range(len(blocks))]

    near = group // 2
    held_bf = pltpu.VMEM((pack_len, width), BF)
    out_blocks, out_t, lse, queries, queries_low, keys, values, inverses = call(
        "attend",
        functools.partial(attend_kernel, (group, segs, head_dim, parts, block)),
        (me, first, last, low, high, temper, own_cols(q_bias).astype(F32),
         own_cols(v_bias).astype(F32), qkv_weight, *attn_blocks),
        (SMEM,) * 3 + (VMEM,) * 5 + (ANY,) * (1 + group),
        (shape_of((group, rows, width), BF), tall, shape_of((8, pack_len), F32), wide, wide, wide,
         wide, shape_of((pack_len, 128), F32)),
        [
            pltpu.VMEM((model, 3 * width), BF),
            pltpu.VMEM((group, rows, model), BF),
            held_bf,
            held_bf,
            held_bf,
            held_bf,
            pltpu.VMEM((pack_len, 128), F32),
            pltpu.VMEM((width, pack_len), BF),
            pltpu.VMEM((width, pack_len), F32),
            held_bf,
            pltpu.VMEM((width, block), F32),
            pltpu.VMEM((8, block), F32),
            pltpu.SemaphoreType.DMA((3 * parts,)),
            pltpu.SemaphoreType.DMA((group,)),
            pltpu.SemaphoreType.DMA((6 + segs * group,)),
        ],
        out_specs=(ANY, ANY, VMEM, ANY, ANY, ANY, ANY, ANY),
    )
    returned = over_group(out_blocks)
    upstream, _ = tie(upstream, out_blocks)
    grad_mlp, grad_mlp_sum = call(
        "grad_mlp",
        grad_mlp_kernel,
        (upstream, mod, row_item),
        (HBM, VMEM, VMEM),
        (rows_bf, shape_of((8, model), F32)),
    )
    grad_far = xor_swap(grad_mlp, "g", near)
    grad_blocks = near_blocks(grad_mlp)
    returned, grad_mlp_sum = tie(returned, grad_mlp_sum)
    attn_rows, branch, middle, mlp_in = call(
        "project",
        functools.partial(project_kernel, parts),
        (returned, proj_weight, proj_bias[None, :], inputs, mod, row_item),
        (HBM, HBM, VMEM, HBM, VMEM, VMEM),
        (rows_bf, rows_bf, rows_f32, rows_bf),
        [pltpu.VMEM((rows, model), F32)],
    )

    mlp_blocks = near_blocks(mlp_in)
    mlp_far = xor_swap(mlp_in, "g", near)
    grad_blocks += near_blocks(tie(grad_far, mlp_in)[0])
    back_parts, out_parts, acts, ghs, hidden_sums = [], [], [], [], []
    for start in (0, near):
        if start:
            mlp_blocks += near_blocks(tie(mlp_far, acts[0])[0])
        made = call(
            "feed",
            functools.partial(feed_kernel, near),
            (fc1_here, fc2_here, fc1_bias_here, *mlp_blocks[start : start + near],
             *grad_blocks[start : start + near]),
            (VMEM,) * 3 + (ANY,) * (2 * near),
            (rows_bf,) * (2 * near)
            + (shape_of((near * rows, units), BF),) * 2
            + (shape_of((8, units), F32),),
            [pltpu.VMEM((near, rows, model), BF)] * 4
            + [pltpu.VMEM((near, rows, units), BF)] * 2
            + [pltpu.VMEM((2, rows, units), F32)] * 2
            + [pltpu.SemaphoreType.DMA((2 * near,)), pltpu.SemaphoreType.DMA((4 * near,))],
            out_specs=(ANY,) * (2 * near + 2) + (VMEM,),
        )
        back_parts += made[:near]
        out_parts += made[near : 2 * near]
        acts.append(made[2 * near])
        ghs.append(made[2 * near + 1])
        hidden_sums.append(made[2 * near + 2])
    far_terms = {k: back_parts[k] for k in range(near, group)}
    for step in reversed(bits(group)[1:]):
        for k in reversed([k for k in far_terms if k & step]):
            came = xor_swap(far_terms.pop(k), "g", step)
            far_terms[k ^ step] = add_low(far_terms[k ^ step], came)
    far_sum = far_terms[near]
    back_parts = list(tie(*back_parts[:near], far_sum)[:near])
    in_terms = {k: [back_parts[k]] for k in range(near)}
    for step in reversed(bits(group)[1:]):
        for k in reversed([k for k in in_terms if k & step]):
            in_terms[k ^ step].append(xor_swap(add_low(*in_terms.pop(k)), "g", step))
    in_terms = in_terms[0] + [xor_swap(far_sum, "g", near)]
    acts[0], _ = tie(acts[0], far_sum)
    split = segs if tiled else 1

    def to_last(blocks):
        terms = {k: [block] for k, block in enumerate(blocks)}
        for step in reversed(bits(group)[1:]):
            for k in reversed([k for k in terms if k & step]):
                terms[k ^ step].append(xor_swap(add_low(*terms.pop(k)), "g", step))
        return terms[0], terms[near]

    out_terms, out_last = to_last(tie(*out_parts, far_sum)[:group])
    if tiled:
        fine = half // group
        tile_shape = (head_size, group, fine, hidden)
        feed_dims = (group, group, segs, 2, len(out_last))
    else:
        tile_shape = (1, 1, model, units)
        feed_dims = (group, 1, 1, 2, len(out_last))
    made = call(
        "feed_weights",
        functools.partial(feed_weights_kernel, feed_dims),
        (me, *acts, *ghs, *mlp_blocks, *grad_blocks, *out_last),
        (SMEM,) + (ANY,) * (4 + 2 * group + len(out_last)),
        (shape_of(tile_shape, BF),) * (2 * split) + (rows_bf,),
        [
            pltpu.VMEM((model, pack_len), BF),
            pltpu.VMEM((model, pack_len), BF),
            pltpu.VMEM((pack_len, units), BF),
            pltpu.VMEM((pack_len, units), BF),
            pltpu.VMEM((group, rows, model), BF),
            pltpu.VMEM((group, rows, model), BF),
            pltpu.VMEM((len(out_last), rows, model), BF),
            pltpu.VMEM((rows, model), BF),
            pltpu.VMEM((2, split, *tile_shape), BF),
            pltpu.SemaphoreType.DMA((4 + 2 * group + len(out_last),)),
            pltpu.SemaphoreType.DMA((2 * split + 1,)),
        ],
        out_specs=(ANY,) * (2 * split + 1),
    )
    up_parts, down_parts, out_sent = made[:split], made[split : 2 * split], made[2 * split]
    out_terms.append(xor_swap(out_sent, "g", near))
    if not tiled:
        fine = half // group
        order = jnp.array([turned(j, head_size) for j in range(head_size)]) ^ z
        near_g = jnp.arange(group) ^ g
        near_y = jnp.arange(segs) ^ yy

        def in_blocks(full):
            full = full.reshape(segs, group, fine, head_size, hidden).transpose(0, 3, 1, 2, 4)
            return list(full[near_y][:, order][:, :, near_g])

        up_parts, down_parts = in_blocks(up_parts[0]), in_blocks(down_parts[0])

    middle_in, _ = tie(middle, up_parts[0])
    outbound, grad_branch, grad_middle, middle_sums, branch_sum = call(
        "middle_back",
        functools.partial(middle_back_kernel, (parts, items, len(in_terms))),
        (middle_in, branch, upstream, mod, row_item, proj_weight, *in_terms),
        (HBM, HBM, HBM, VMEM, VMEM, HBM) + (HBM,) * len(in_terms),
        (shape_of((group, rows, width), BF), rows_bf, rows_f32, shape_of((8, 3 * model), F32),
         shape_of((8, model), F32)),
        [pltpu.VMEM((rows, model), BF)],
    )
    inbound = over_group(outbound)
    up_terms, down_terms = xor_scatter(up_parts, "yy"), xor_scatter(down_parts, "yy")
    made = call(
        "proj_weights",
        functools.partial(proj_weights_kernel, (group, parts == segs)),
        (me, attn_rows, grad_branch),
        (SMEM, HBM, HBM),
        (shape_of((parts, head_size, model // head_size, sub), BF),) * group,
        [pltpu.VMEM((model, rows), BF), pltpu.VMEM((rows, width), BF)],
    )
    proj_terms, proj_last = to_last(made)
    tied = tuple(out_terms) + tuple(proj_last) + tuple(up_terms)
    half_tiles = shape_of((head_size // 2, group, fine, hidden), BF)
    quarter_tiles = shape_of((head_size // 4, group, fine, hidden), BF)
    output_rows, output_sums, proj_sent, up_kept, up_sent = call(
        "output",
        functools.partial(
            output_kernel, (items, len(out_terms), len(proj_last), len(up_terms))
        ),
        (middle, upstream, mod, row_item, fc2_bias[None, :], *tied),
        (HBM, HBM, VMEM, VMEM, VMEM) + (HBM,) * len(tied),
        (rows_bf, shape_of((8, model), F32), shape_of(proj_last[0].shape, BF), half_tiles, half_tiles),
    )
    up_terms = (up_kept, xor_swap(up_sent, "head", 1))
    inbound, output_rows = tie(inbound, output_rows)
    output_back = to_packs(output_rows)
    proj_terms.append(xor_swap(proj_sent, "g", near))
    pairs = width // 128
    cols_bf, cols_f32 = pltpu.VMEM((pack_len, 128), BF), pltpu.VMEM((pack_len, 128), F32)
    pair_held = [cols_bf] * 3 + [pltpu.VMEM((128, pack_len), F32), cols_bf]
    pair_scratch = [pltpu.VMEM((128, pack_len), BF), cols_f32, cols_f32]
    pair_scratch += [pltpu.VMEM((128, block), F32), pltpu.VMEM((8, block), F32)]
    pair_sems = pltpu.SemaphoreType.DMA((4 + segs * group,))
    given = inbound
    earlier = []
    for near_pair in range(pairs - 1):
        earlier += call(
            "attend_back",
            functools.partial(attend_back_kernel, (group, segs, head_dim, block, near_pair)),
            (first, last, low, high, lse, given, queries, keys, values, out_t),
            (SMEM,) * 2 + (VMEM,) * 3 + (ANY,) * 5,
            (shape_of((pack_len, 128), BF),) * 3,
            pair_held + pair_scratch + [cols_bf] * 3 + [pair_sems, pltpu.SemaphoreType.DMA((3,))],
            out_specs=(ANY,) * 3,
        )
        if near_pair == 0:
            tied = tie(*down_terms, *up_terms, earlier[0])[:-1]
            down_kept, down_sent, up_kept, up_sent = call(
                "add",
                functools.partial(add_kernel, (len(down_terms), 2)),
                tied,
                (HBM,) * len(tied),
                (half_tiles, half_tiles, quarter_tiles, quarter_tiles),
            )
            down_terms = (down_kept, xor_swap(down_sent, "head", 1))
            up_terms = (up_kept, xor_swap(up_sent, "head", 2))
            given, _ = tie(given, up_sent)
    made = call(
        "attend_back_end",
        functools.partial(
            attend_back_end_kernel, (group, segs, head_dim, parts, block, pairs)
        ),
        (me, temper, qkv_weight, inverses, queries_low, first, last, low, high, lse, given, queries,
         keys, values, out_t, *earlier),
        (SMEM, VMEM, ANY, ANY, ANY, SMEM, SMEM, VMEM, VMEM, VMEM) + (ANY,) * (5 + len(earlier)),
        (rows_bf,) * group + (shape_of((pack_len, 3 * width), BF), shape_of((8, width), F32)),
        pair_held
        + pair_scratch
        + [held_bf] * 3
        + [
            pltpu.VMEM((model, 3 * width), BF),
            cols_f32,
            held_bf,
            held_bf,
            held_bf,
            pltpu.VMEM((pack_len, 3 * width), BF),
            pltpu.VMEM((group, rows, model), BF),
            pair_sems,
            pltpu.SemaphoreType.DMA((3 * parts,)),
            pltpu.SemaphoreType.DMA((4 + 3 * (pairs - 1),)),
            pltpu.SemaphoreType.DMA((2 * group,)),
        ],
        out_specs=(ANY,) * (group + 1) + (VMEM,),
    )
    made, down_terms, up_terms, proj_terms, (output_back,) = tie_groups(
        made, down_terms, up_terms, proj_terms, (output_back,)
    )
    grad_qkv, qkv_sums = made[group:]

    (vectors,) = call(
        "vector_parts",
        functools.partial(vector_parts_kernel, (group, parts, head_size)),
        (me, qkv_sums, branch_sum, grad_mlp_sum, *hidden_sums),
        (SMEM,) + (VMEM,) * (3 + len(hidden_sums)),
        (shape_of((64, 256), F32),),
        [pltpu.VMEM((16, model), F32)],
    )
    if not tiled:
        hidden_row = (hidden_sums[0] + hidden_sums[1])[0].reshape(head_size, hidden)
        hidden_row = lax.dynamic_update_slice(
            jnp.zeros((16, model), F32), hidden_row, (8, g * hidden)
        )
        vectors = vectors + hidden_row.reshape(16, 4, 256).transpose(1, 0, 2).reshape(64, 256)

    in_terms, last_terms = to_last(made[:group])
    if pairs == 1:
        down_terms = halves_over_head(add_low(*down_terms))
    down_kept, down_sent = call(
        "add", functools.partial(add_kernel, (2,)), down_terms, (HBM,) * 2, (quarter_tiles,) * 2
    )
    down_terms = (down_kept, xor_swap(down_sent, "head", 2))
    last_terms = tie(*last_terms, down_sent)[:-1]
    sent = add_low(*last_terms)
    in_terms.append(xor_swap(sent, "g", near))
    grad_qkv, _ = tie(grad_qkv, sent)
    qkv_parts = call(
        "qkv_weights",
        functools.partial(
            qkv_weights_kernel, (group, parts, parts == segs, len(proj_terms))
        ),
        (me, grad_qkv, *attn_blocks, *proj_terms),
        (SMEM,) + (HBM,) * (1 + group + len(proj_terms)),
        (shape_of((head_size, 4, model // head_size, sub), BF),) * parts,
        [pltpu.VMEM((model, pack_len), BF), pltpu.VMEM((pack_len, 3 * sub), BF)],
    )
    tied = tie(inputs, *down_terms, qkv_parts[0])
    inputs_back, down_terms = tied[0], tied[1:3]
    tokens_grad_rows, tokens_sums = call(
        "tokens_back",
        functools.partial(tokens_back_kernel, (items, len(in_terms))),
        (inputs_back, grad_middle, mod, row_item, *in_terms),
        (HBM, HBM, VMEM, VMEM) + (HBM,) * len(in_terms),
        (rows_bf, shape_of((8, 2 * model), F32)),
    )

    def to_data(values):
        return dot(to_slot, values, ((0,), (0,)))

    output = to_data(output_back).astype(BF)
    tokens_came = to_packs(tokens_grad_rows)

    ada_cols = 6 * model // (dp_size * head_size)
    packs = segs * head_size
    (kept,) = call(
        "item_blocks",
        functools.partial(item_blocks_kernel, (group, segs, head_size, ada_cols)),
        (me, middle_sums, output_sums, tokens_sums),
        (SMEM, VMEM, VMEM, VMEM),
        (shape_of((group, packs * 8, 256), F32),),
        [pltpu.VMEM((8, 6 * model), F32)],
        out_specs=(VMEM,),
    )
    sent = jnp.concatenate([kept[k] for k in range(1, group, 2)] + [vectors], axis=0)
    count = group
    for step in reversed(bits(group)):
        came = xor_swap(sent, "g", step)
        left = count // 2
        own = (left, packs * 8, 256) if left > 1 else (packs * 4, 256)
        rows_sent = (left // 2 * packs * 8 if left > 1 else packs * 4) + 64
        kept, sent, vectors = call(
            "group_sums",
            functools.partial(group_sums_kernel, count, step),
            (kept, came, vectors),
            (VMEM,) * 3,
            (shape_of(own, F32), shape_of((rows_sent, 256), F32), shape_of((64, 256), F32)),
            out_specs=(VMEM,) * 3,
        )
        count = left
    kept = kept.reshape(packs // 2, 1, 8, 256)
    tokens_sent = sent
    def over_head(terms):
        while terms[0].shape[0] > 1:
            terms = halves_over_head(add_low(*terms))
        return terms

    down_terms = tie(*down_terms, *up_terms, tokens_grad_rows)[:-1]
    down_terms, up_terms = down_terms[:2], down_terms[2:]
    tied = tuple(over_head(up_terms)) + tuple(over_head(down_terms))
    own_tiles = call(
        "own_tiles",
        own_tiles_kernel,
        tied,
        (HBM,) * 4,
        (shape_of((2, fine, hidden), BF),) * group,
    )
    both_all = [own_tiles[0]]
    for i in range(1, group):
        both_all.append(lax.ppermute(own_tiles[i], "g", [(k, k ^ i) for k in range(group)]))
    if parts == segs:
        terms = tie(*xor_scatter(qkv_parts, "yy"), tokens_sent)[:-1]
        terms = halves_over_head(add_low(*terms))
        terms, both_all, (tokens_came,) = tie_groups(terms, both_all, (tokens_came,))
        terms = over_head(terms)
        summed = sum(term[0].astype(F32) for term in terms)
        proj_part, qkv_part = summed[0], summed[1:]
    else:
        both = qkv_parts[0].transpose(1, 0, 2, 3).reshape(4, model, width)
        full = lax.dynamic_update_slice(
            jnp.zeros((4, model, model), BF), both, (0, 0, g * width)
        )
        summed = lax.psum_scatter(full, ("yy", "g"), scatter_dimension=2, tiled=True)
        summed = lax.psum_scatter(summed, "head", scatter_dimension=1, tiled=True).astype(F32)
        proj_part, qkv_part = summed[0], summed[1:]

    if tiled:
        up_part, down_part = call(
            "place",
            functools.partial(place_kernel, group),
            (me, *both_all),
            (SMEM,) + (HBM,) * group,
            (shape_of((fine, group * hidden), F32), shape_of((group * hidden, fine), F32)),
        )
    else:
        placed = jnp.stack(both_all)[jnp.arange(group) ^ g].astype(F32)
        up_part = placed[:, 0].transpose(1, 0, 2).reshape(fine, group * hidden)
        down_part = placed[:, 1].transpose(0, 2, 1).reshape(group * hidden, fine)


    sent, _ = tie(sent, tokens_came)
    tokens_grad = to_data(tokens_came)
    steps = [("yy", step) for step in bits(segs)] + [("head", step) for step in bits(head_size)]
    for place, (axis, step) in enumerate(steps):
        came = xor_swap(sent, axis, step)
        blocks, senders = kept.shape[0], kept.shape[1]
        end = place + 1 == len(steps)
        own = (blocks if end else blocks // 2, 2 * senders, 8, 256)
        outs = [shape_of(own, F32)]
        if not end:
            outs.append(shape_of((blocks // 2 * 2 * senders * 8 + 64, 256), F32))
        outs.append(shape_of((64, 256), F32))
        made = call(
            "pack_sums", pack_sums_kernel, (kept, came, vectors), (VMEM,) * 3, outs,
            out_specs=(VMEM,) * len(outs),
        )
        kept, vectors = made[0], made[-1]
        sent = made[1] if not end else None
    item_came = kept[0]
    vectors = vectors.reshape(4, 16, 256).transpose(1, 0, 2).reshape(16, model)
    silu_rows = jnp.pad(silu_cond.reshape(packs, items, model), ((0, 0), (0, 8 - items), (0, 0)))
    ada_grad, ada_bias_grad = call(
        "ada",
        ada_kernel,
        (me, silu_rows.reshape(packs * 8, model), item_came),
        (SMEM, VMEM, VMEM),
        (shape_of((model, ada_cols), F32), shape_of((8, ada_cols), F32)),
        [pltpu.VMEM((packs * 8, 256), F32)],
    )
    ada_bias_grad = ada_bias_grad[0]

    log_scale_grad = jnp.sum(vectors[2].reshape(heads_all, head_dim), axis=1)
    fc1_bias_grad = pick(vectors, 8 + z, 0)[: group * hidden]
    return (
        output,
        tokens_grad,
        ada_grad,
        ada_bias_grad,
        qkv_part,
        vectors[0],
        vectors[1],
        log_scale_grad,
        proj_part,
        vectors[3],
        up_part,
        fc1_bias_grad,
        down_part,
        vectors[4],
    )


def solution(mesh):
    head_size = mesh.shape["head"]
    dp_size = mesh.shape["dp"]
    inner = Mesh(
        mesh.devices.reshape(dp_size // head_size, head_size, head_size), ("yy", "g", "head")
    )
    dp = ("yy", "g")
    everything = ("yy", "g", "head")
    in_specs = (
        P(everything, None),
        P(everything, None),
        P(),
        P(),
        P(),
        P(),
        P(),
        P(),
        P(),
        P(),
        P(),
        P(None, "head"),
        P("head"),
        P("head", None),
        P(),
        P(),
        P(),
        P(dp, None),
        P(everything),
    )
    out_specs = (
        P(everything, None),
        P(everything, None),
        P(None, everything),
        P(everything),
        P(None, "head", dp),
        P(),
        P(),
        P(),
        P("head", dp),
        P(),
        P(dp, "head"),
        P("head"),
        P("head", dp),
        P(),
    )
    return jax.shard_map(
        shards, mesh=inner, in_specs=in_specs, out_specs=out_specs, check_vma=False
    )
```

```python
import functools

import jax
import jax.numpy as jnp
from jax import lax
from jax.experimental import pallas as pl
from jax.experimental.pallas import tpu as pltpu
from jax.sharding import Mesh, PartitionSpec as P

BF = jnp.bfloat16
F32 = jnp.float32
SMEM = pl.BlockSpec(memory_space=pltpu.SMEM)
VMEM = pl.BlockSpec(memory_space=pltpu.VMEM)
ANY = pl.BlockSpec(memory_space=pl.ANY)
HBM = "hbm"
LIMIT = 40
LIMITS = {"attend": 57, "attend_back": 57, "sort": 57, "middle_back": 50, "output": 50, "feed": 50, "feed_weights": 57, "weights": 57, "qkv_weights": 57}
FLOPS, BYTES = 1_000_000_000, 3_000_000
TIMES = {
    "sort": 2, "first_norm": 2, "grad_mlp": 2, "attend": 26, "project": 5, "weights": 4, "feed": 12,
    "feed_weights": 12, "middle_back": 7, "proj_weights": 3, "output": 3, "attend_back": 34, "add": 3,
    "qkv_weights": 8, "tokens_back": 5,
}
PLAIN = ((1,), (0,))
BY_ROW = ((1,), (1,))


def shape_of(shape, dtype):
    return jax.ShapeDtypeStruct(shape, dtype)


def dot(left, right, dims=PLAIN):
    return lax.dot_general(left, right, (dims, ((), ())), preferred_element_type=F32)


def call(name, kernel, operands, specs, outs, scratch=(), limit=LIMIT, out_specs=None):
    out_specs = out_specs or tuple(HBM if o.size >= 65536 else VMEM for o in outs)
    n_in, n_out, n_scratch = len(specs), len(outs), len(scratch)
    staged_in = [i for i, spec in enumerate(specs) if spec is HBM]
    staged_out = [i for i, spec in enumerate(out_specs) if spec is HBM]
    staged = [pltpu.VMEM(operands[i].shape, operands[i].dtype) for i in staged_in]
    staged += [pltpu.VMEM(outs[i].shape, outs[i].dtype) for i in staged_out]
    sems = [pltpu.SemaphoreType.DMA((len(staged),))] if staged else []

    def body(*refs):
        given, made = list(refs[:n_in]), list(refs[n_in : n_in + n_out])
        own = refs[n_in + n_out : n_in + n_out + n_scratch]
        held = refs[n_in + n_out + n_scratch :]
        copies = []
        for place, i in enumerate(staged_in):
            copies.append(pltpu.make_async_copy(given[i], held[place], held[-1].at[place]))
            copies[-1].start()
            given[i] = held[place]
        backs = []
        for place, i in enumerate(staged_out, len(staged_in)):
            backs.append(pltpu.make_async_copy(held[place], made[i], held[-1].at[place]))
            made[i] = held[place]
        for copy in copies:
            copy.wait()
        kernel(*given, *made, *own)
        for copy in backs:
            copy.start()
        for copy in backs:
            copy.wait()

    limit = LIMITS.get(name, limit)
    return pl.pallas_call(
        body,
        name=name,
        out_shape=tuple(outs),
        in_specs=[ANY if spec is HBM else spec for spec in specs],
        out_specs=tuple(ANY if spec is HBM else spec for spec in out_specs),
        scratch_shapes=list(scratch) + staged + sems,
        compiler_params=pltpu.CompilerParams(vmem_limit_bytes=limit * 1024 * 1024),
        cost_estimate=pl.CostEstimate(
            flops=TIMES.get(name, 1) * FLOPS, bytes_accessed=TIMES.get(name, 1) * BYTES, transcendentals=0
        ),
    )(*operands)


def row_norm(values):
    centre = values - jnp.mean(values, axis=-1, keepdims=True)
    inverse = lax.rsqrt(jnp.mean(centre * centre, axis=-1, keepdims=True) + 1e-06)
    return (centre * inverse, inverse)


def norm_back(gradient, normed, inverse):
    return inverse * (
        gradient
        - jnp.mean(gradient, axis=-1, keepdims=True)
        - normed * jnp.mean(gradient * normed, axis=-1, keepdims=True)
    )


def mod_rows(mod_ref, part, item, width):
    cols = slice(part * width, (part + 1) * width)
    rows = jnp.broadcast_to(mod_ref[0:1, cols], (item.shape[0], width))
    for index in range(1, mod_ref.shape[0]):
        rows = jnp.where(item == index, mod_ref[index : index + 1, cols], rows)
    return rows


def add_item_sums(sums_ref, part, item, values, count):
    width = values.shape[1]
    cols = slice(part * width, (part + 1) * width)
    for index in range(count):
        kept = jnp.where(item == index, values, 0.0)
        sums_ref[index : index + 1, cols] += jnp.sum(kept, axis=0, keepdims=True)


def same_head(width, head_dim):
    row = lax.broadcasted_iota(jnp.int32, (width, width), 0) // head_dim
    col = lax.broadcasted_iota(jnp.int32, (width, width), 1) // head_dim
    return (row == col).astype(BF)


def chunks(rows, size):
    return pl.loop(0, rows // size)


def at(index, size):
    return pl.ds(pl.multiple_of(index * size, size), size)


def first_norm_kernel(x_ref, mod_ref, item_ref, out_ref):
    rows, width = x_ref.shape

    @chunks(rows, 64)
    def _(i):
        r = at(i, 64)
        item = item_ref[r, :]
        normed, _ = row_norm(x_ref[r, :].astype(F32))
        scale, shift = mod_rows(mod_ref, 2, item, width), mod_rows(mod_ref, 4, item, width)
        out_ref[r, :] = (normed * (1.0 + scale) + shift).astype(BF)


def grad_mlp_kernel(up_ref, mod_ref, item_ref, out_ref, sum_ref):
    rows, width = up_ref.shape
    sum_ref[...] = jnp.zeros_like(sum_ref)

    @chunks(rows, 64)
    def _(i):
        r = at(i, 64)
        gamma = mod_rows(mod_ref, 1, item_ref[r, :], width)
        grad = (up_ref[r, :].astype(F32) * gamma).astype(BF)
        out_ref[r, :] = grad
        sum_ref[0:1, :] += jnp.sum(grad.astype(F32), axis=0, keepdims=True)


def load_columns(weight_ref, held, sems, offset_of, parts, sub):
    copies = []
    for t in range(3):
        for p in range(parts):
            copies.append(
                pltpu.make_async_copy(
                    weight_ref.at[t, :, pl.ds(pl.multiple_of(offset_of(p), sub), sub)],
                    held.at[:, pl.ds((t * parts + p) * sub, sub)],
                    sems.at[t * parts + p],
                )
            )
    for copy in copies:
        copy.start()
    return copies


def pick_heads(width, head_dim, first):
    row = lax.broadcasted_iota(jnp.int32, (width, 128), 0)
    col = lax.broadcasted_iota(jnp.int32, (width, 128), 1)
    return (row == (col - first) * head_dim).astype(BF)


def spread_heads(width, head_dim, first):
    row = lax.broadcasted_iota(jnp.int32, (128, width), 0)
    col = lax.broadcasted_iota(jnp.int32, (128, width), 1)
    return (row - first == col // head_dim).astype(BF)


def exact_dot(values, ones):
    high = values.astype(BF)
    low = (values - high.astype(F32)).astype(BF)
    return dot(high, ones) + dot(low, ones)


def own_lanes(values, mine):
    return jnp.where(mine, values, jnp.zeros_like(values))


def attend_kernel(dims, *refs):
    group, segs, head_dim, parts, block = dims
    me_ref, first_ref, last_ref, lo_ref, hi_ref, temper_ref, qb_ref, vb_ref, w_ref = refs[:9]
    blocks = refs[9 : 9 + group]
    out_o, out_t_o, lse_ref, q_o, ql_o, k_o, v_o, inv_o = refs[9 + group : 17 + group]
    (held, block_s, q_ref, ql_ref, k_ref, v_ref, inv_ref, v_t, out_t_ref, out_s, acc, total, sems,
     in_sems, out_sems) = refs[17 + group :]
    pack_len, width = q_ref.shape
    rows = block_s.shape[1]
    seg, sub = rows // segs, width // parts
    pair, heads = 128 // head_dim, width // head_dim
    me = me_ref[0]
    loads = [
        pltpu.make_async_copy(blocks[k], block_s.at[k], in_sems.at[k]) for k in range(group)
    ]
    loads[0].start()
    copies = load_columns(w_ref, held, sems, lambda p: (p * group + me) * sub, parts, sub)
    for load in loads[1:]:
        load.start()
    same = same_head(width, head_dim)
    pick_q, pick_k = pick_heads(width, head_dim, 0), pick_heads(width, head_dim, heads)
    for copy in copies:
        copy.wait()
    for k in range(group):
        loads[k].wait()
        for y in range(segs):
            ranks = pl.ds(pl.multiple_of((y * group + (me ^ k)) * seg, 16), seg)
            made = dot(block_s[k, y * seg : (y + 1) * seg, :], held[...])
            query = made[:, :width] + qb_ref[...]
            key = made[:, width : 2 * width]
            inverse_q = lax.rsqrt(exact_dot(query * query, same) + 1e-06)
            query = query * inverse_q * temper_ref[...]
            rounded = query.astype(BF)
            q_ref[ranks, :] = rounded
            ql_ref[ranks, :] = (query - rounded.astype(F32)).astype(BF)
            inverse_k = lax.rsqrt(exact_dot(key * key, same) + 1e-06)
            k_ref[ranks, :] = (key * inverse_k).astype(BF)
            v_ref[ranks, :] = (made[:, 2 * width :] + vb_ref[...]).astype(BF)
            inv_ref[ranks, :] = exact_dot(inverse_q, pick_q) + exact_dot(inverse_k, pick_k)
    stores = []

    def store(source, target):
        stores.append(pltpu.make_async_copy(source, target, out_sems.at[len(stores)]))
        stores[-1].start()

    for source, target in (
        (q_ref, q_o), (ql_ref, ql_o), (k_ref, k_o), (v_ref, v_o), (inv_ref, inv_o)
    ):
        store(source, target)
    lanes = lax.broadcasted_iota(jnp.int32, (1, 128), 1) // head_dim
    v_t[...] = v_ref[...].T

    @pl.loop(0, pack_len // block)
    def _(q_block):
        q_rows = at(q_block, block)
        q_t = q_ref[q_rows, :].T
        low, high = lo_ref[:, q_rows], hi_ref[:, q_rows]
        acc[...] = jnp.zeros_like(acc)
        total[...] = jnp.zeros_like(total)

        @pl.loop(first_ref[q_block], last_ref[q_block])
        def _(k_block):
            k_rows = at(k_block, block)
            index = k_block * block + lax.broadcasted_iota(jnp.int32, (block, block), 0)
            seen = (index >= low) & (index < high)
            scores = []
            for h in range(heads):
                near = slice(h // pair * 128, (h // pair + 1) * 128)
                scores.append(dot(own_lanes(k_ref[k_rows, near], lanes == h % pair), q_t[near, :]))
            raised = [jnp.where(seen, jnp.exp(values), 0.0) for values in scores]
            for h in range(heads):
                own = pl.ds(h * head_dim, head_dim)
                total[h : h + 1, :] += jnp.sum(raised[h], axis=0, keepdims=True)
                acc[own, :] += dot(v_t[own, k_rows], raised[h].astype(BF))

        for h in range(heads):
            own = pl.ds(h * head_dim, head_dim)
            acc[own, :] = acc[own, :] / total[h : h + 1, :]
            lse_ref[h : h + 1, q_rows] = jnp.log(total[h : h + 1, :])
        out_t_ref[:, q_rows] = acc[...]
        out_s[q_rows, :] = acc[...].T.astype(BF)

    for y in range(segs):
        for g in range(group):
            start = (y * group + g) * seg
            store(out_s.at[pl.ds(start, seg), :], out_o.at[g, pl.ds(y * seg, seg), :])
    store(out_t_ref, out_t_o)
    for copy in stores:
        copy.wait()


def attend_back_blocks(dims, refs, scratch, outs):
    head_dim, block = dims
    first_ref, last_ref, lo_ref, hi_ref, lse_ref, q_ref, k_ref, v_ref, out_t_ref, g_s = refs
    k_t, dk_acc, dv_acc, acc, sums = scratch
    dq_ref, dk_ref, dv_ref = outs
    pack_len, width = q_ref.shape
    pair, heads = 128 // head_dim, width // head_dim
    lanes = lax.broadcasted_iota(jnp.int32, (1, 128), 1) // head_dim
    cols = [slice(p * 128, (p + 1) * 128) for p in range(width // 128)]
    k_t[...] = k_ref[...].T
    dk_acc[...] = jnp.zeros_like(dk_acc)
    dv_acc[...] = jnp.zeros_like(dv_acc)

    @pl.loop(0, pack_len // block)
    def _(q_block):
        q_rows = at(q_block, block)
        queries, grads = q_ref[q_rows, :], g_s[q_rows, :]
        q_t, g_t = queries.T, grads.T
        low, high = lo_ref[:, q_rows], hi_ref[:, q_rows]
        weighted = g_t.astype(F32) * out_t_ref[:, q_rows]
        for h in range(heads):
            sums[h : h + 1, :] = jnp.sum(
                weighted[h * head_dim : (h + 1) * head_dim, :], axis=0, keepdims=True
            )
        acc[...] = jnp.zeros_like(acc)

        @pl.loop(first_ref[q_block], last_ref[q_block])
        def _(k_block):
            k_rows = at(k_block, block)
            index = k_block * block + lax.broadcasted_iota(jnp.int32, (block, block), 0)
            seen = (index >= low) & (index < high)
            scores, grad_probs, probs, grad_scores = [], [], [], []
            for h in range(heads):
                near, mine = cols[h // pair], lanes == h % pair
                scores.append(dot(own_lanes(k_ref[k_rows, near], mine), q_t[near, :]))
                grad_probs.append(dot(own_lanes(v_ref[k_rows, near], mine), g_t[near, :]))
            for h in range(heads):
                made = jnp.where(seen, jnp.exp(scores[h] - lse_ref[h : h + 1, q_rows]), 0.0)
                probs.append(made.astype(BF))
                grad_scores.append((made * (grad_probs[h] - sums[h : h + 1, :])).astype(BF))
            for h in range(heads):
                own = pl.ds(h * head_dim, head_dim)
                acc[own, :] += dot(k_t[own, k_rows], grad_scores[h])
            for p, near in enumerate(cols):
                grad_k = grad_v = 0.0
                for h in range(p * pair, (p + 1) * pair):
                    mine = lanes == h % pair
                    grad_k += dot(grad_scores[h], own_lanes(queries[:, near], mine))
                    grad_v += dot(probs[h], own_lanes(grads[:, near], mine))
                dk_acc[k_rows, near] += grad_k
                dv_acc[k_rows, near] += grad_v

        dq_ref[q_rows, :] = acc[...].T.astype(BF)

    dk_ref[...] = dk_acc[...].astype(BF)
    dv_ref[...] = dv_acc[...].astype(BF)


def attend_back_kernel(dims, *refs):
    group, segs, head_dim, parts, block = dims
    me_ref, temper_ref, w_ref, inv_ref, ql_ref = refs[:5]
    ranges, lse_ref, ins = refs[5:9], refs[9], refs[10:15]
    sent, (dqkv_o, sums_ref), refs = refs[15 : 15 + group], refs[15 + group : 17 + group], refs[17 + group :]
    (q_s, k_s, v_s, out_s, g_s), scratch, made, refs = refs[:5], refs[5:10], refs[10:13], refs[13:]
    (w_s, inv_s, ql_s, dqkv_s, sent_s), (sems, w_sems, out_sems) = refs[:5], refs[5:]
    pack_len, width = q_s.shape
    rows = sent_s.shape[1]
    seg, sub = rows // segs, width // parts
    heads = width // head_dim
    me = me_ref[0]
    moves = [(ins[1], q_s), (ins[2], k_s), (ins[3], v_s), (ins[4], out_s)]
    for y in range(segs):
        for g in range(group):
            to = pl.ds((y * group + g) * seg, seg)
            moves.append((ins[0].at[g, pl.ds(y * seg, seg), :], g_s.at[to, :]))
    moves += [(inv_ref, inv_s), (ql_ref, ql_s)]
    loads = []
    for place, (source, target) in enumerate(moves):
        loads.append(pltpu.make_async_copy(source, target, sems.at[place]))
        loads[-1].start()
    copies = load_columns(w_ref, w_s, w_sems, lambda p: (p * group + me) * sub, parts, sub)
    copies += loads[-2:]
    for load in loads[:-2]:
        load.wait()
    attend_back_blocks(
        (head_dim, block), (*ranges, lse_ref, q_s, k_s, v_s, out_s, g_s), scratch, made
    )
    same = same_head(width, head_dim)
    spread_q, spread_k = spread_heads(width, head_dim, 0), spread_heads(width, head_dim, heads)
    sums_ref[...] = jnp.zeros_like(sums_ref)
    for copy in copies:
        copy.wait()
    stores = []
    dq_s, dk_s, dv_s = made
    for k in reversed(range(group)):
        whole = slice(k * rows, (k + 1) * rows)
        for y in range(segs):
            ranks = pl.ds(pl.multiple_of((y * group + (me ^ k)) * seg, 16), seg)
            own = slice(k * rows + y * seg, k * rows + (y + 1) * seg)
            inverse = inv_s[ranks, :]
            query = q_s[ranks, :].astype(F32) + ql_s[ranks, :].astype(F32)
            unit = query / temper_ref[...]
            raw = dq_s[ranks, :].astype(F32)
            grad = raw * temper_ref[...]
            grad_query = exact_dot(inverse, spread_q) * (grad - unit * exact_dot(grad * unit, same))
            unit_k = k_s[ranks, :].astype(F32)
            grad = dk_s[ranks, :].astype(F32)
            grad_key = exact_dot(inverse, spread_k) * (
                grad - unit_k * exact_dot(grad * unit_k, same)
            )
            grad_query, grad_value = grad_query.astype(BF), dv_s[ranks, :]
            dqkv_s[own, :width] = grad_query
            dqkv_s[own, width : 2 * width] = grad_key.astype(BF)
            dqkv_s[own, 2 * width :] = grad_value
            for index, values in enumerate((grad_query, grad_value, raw * query)):
                sums_ref[index : index + 1, :] += jnp.sum(
                    values.astype(F32), axis=0, keepdims=True
                )
        sent_s[k] = dot(dqkv_s[whole, :], w_s[...], BY_ROW).astype(BF)
        own = pl.ds(k * rows, rows)
        for source, target in ((sent_s.at[k], sent[k]), (dqkv_s.at[own, :], dqkv_o.at[own, :])):
            stores.append(pltpu.make_async_copy(source, target, out_sems.at[len(stores)]))
            stores[-1].start()
    for copy in stores:
        copy.wait()


def project_kernel(
    parts, ret_ref, wp_ref, pb_ref, x_ref, mod_ref, item_ref, attn_ref, branch_ref, middle_ref, out_ref, made
):
    group, rows, width = ret_ref.shape
    model = x_ref.shape[1]
    sub = width // parts
    for g in range(group):
        for p in range(parts):
            start = (p * group + g) * sub
            attn_ref[:, start : start + sub] = ret_ref[g, :, p * sub : (p + 1) * sub]
    made[...] = dot(attn_ref[...], wp_ref[...]) + pb_ref[...].astype(F32)
    branch_ref[...] = made[...].astype(BF)

    @chunks(rows, 64)
    def _(i):
        r = at(i, 64)
        item = item_ref[r, :]
        middle = x_ref[r, :].astype(F32) + mod_rows(mod_ref, 0, item, model) * made[r, :]
        middle_ref[r, :] = middle
        normed, _ = row_norm(middle)
        scale, shift = mod_rows(mod_ref, 3, item, model), mod_rows(mod_ref, 5, item, model)
        out_ref[r, :] = (normed * (1.0 + scale) + shift).astype(BF)


def add_blocks(terms, outs):
    count = outs[0].shape[0]
    for j in range(terms[0].shape[0]):
        made = sum(term[j].astype(F32) for term in terms).astype(BF)
        outs[j // count][j % count] = made


def weights_kernel(fc1_ref, fc2_ref, w1_ref, w2_ref, sems):
    segs, head_size, _, hidden = fc1_ref.shape
    half = fc2_ref.shape[3]
    copies = []
    for y in range(segs):
        for z in range(head_size):
            own = pl.ds(z * hidden, hidden)
            rows = pl.ds(y * half, half)
            for source, target in (
                (fc1_ref.at[y, z, pl.ds(0, half), :], w1_ref.at[rows, own]),
                (fc2_ref.at[y, z], w2_ref.at[own, rows]),
            ):
                copies.append(pltpu.make_async_copy(source, target, sems.at[len(copies)]))
                copies[-1].start()
    for copy in copies:
        copy.wait()


def feed_kernel(count, *refs):
    w1, w2, b1_ref = refs[:3]
    ins, grads = refs[3 : 3 + count], refs[3 + count : 3 + 2 * count]
    rest = refs[3 + 2 * count :]
    back, outs = rest[:count], rest[count : 2 * count]
    act_ref, gh_ref, sum_ref = rest[2 * count : 2 * count + 3]
    in_s, grad_s, back_s, out_s, act_s, gh_s, pre, grad, in_sems, out_sems = rest[2 * count + 3 :]
    rows = ins[0].shape[0]
    loads, stores = [], []
    for k in range(count):
        pair = (
            pltpu.make_async_copy(ins[k], in_s.at[k], in_sems.at[2 * k]),
            pltpu.make_async_copy(grads[k], grad_s.at[k], in_sems.at[2 * k + 1]),
        )
        pair[0].start()
        pair[1].start()
        loads.append(pair)
    sum_ref[...] = jnp.zeros_like(sum_ref)

    def store(source, target, index):
        stores.append(pltpu.make_async_copy(source, target, out_sems.at[index]))
        stores[-1].start()

    def front(k):
        loads[k][0].wait()
        pre[k % 2] = dot(in_s[k], w1[...]) + b1_ref[...]
        loads[k][1].wait()
        grad[k % 2] = dot(grad_s[k], w2[...], BY_ROW)

    def middle(k):
        total = 0.0
        for start in range(0, rows, 32):
            r = slice(start, start + 32)
            value = pre[k % 2, r, :]
            square = value * value
            gate = jnp.tanh(value * (0.7978845608028654 + 0.035677408136300125 * square))
            half = 0.5 + 0.5 * gate
            act = value * half
            slope = half + act * (1.0 - gate) * (0.7978845608028654 + 0.10703222440890037 * square)
            back_grad = (slope * grad[k % 2, r, :]).astype(BF)
            act_s[k, r, :] = act.astype(BF)
            gh_s[k, r, :] = back_grad
            total = total + jnp.sum(back_grad.astype(F32), axis=0, keepdims=True)
        sum_ref[0:1, :] += total
        own = pl.ds(k * rows, rows)
        store(act_s.at[k], act_ref.at[own, :], 4 * k)
        store(gh_s.at[k], gh_ref.at[own, :], 4 * k + 1)

    def end(k):
        back_s[k] = dot(gh_s[k], w1[...], BY_ROW).astype(BF)
        store(back_s.at[k], back[k], 4 * k + 2)
        out_s[k] = dot(act_s[k], w2[...]).astype(BF)
        store(out_s.at[k], outs[k], 4 * k + 3)

    order = list(reversed(range(count)))
    front(order[0])
    for place, k in enumerate(order):
        if place + 1 < count:
            front(order[place + 1])
        middle(k)
        end(k)
    for started in stores:
        started.wait()


def turned(index, count):
    made = 0
    while count > 1:
        made, index, count = made * 2 + index % 2, index // 2, count // 2
    return made


def feed_weights_kernel(dims, *refs):
    count, group, split, halves, term_count = dims
    me_ref, acts, ghs = refs[0], refs[1 : 1 + halves], refs[1 + halves : 1 + 2 * halves]
    refs = refs[1 + 2 * halves :]
    ins, grads, refs = refs[:count], refs[count : 2 * count], refs[2 * count :]
    terms, refs = refs[:term_count], refs[term_count:]
    outs, sum_o, rest = refs[: 2 * split], refs[2 * split], refs[2 * split + 1 :]
    in_t, grad_t, act_s, gh_s, in_s, grad_s, term_s, sum_s, tile_s, in_sems, out_sems = rest
    rows, model = in_s.shape[1:]

    def load(source, target, index):
        copy = pltpu.make_async_copy(source, target, in_sems.at[index])
        copy.start()
        return copy

    part_rows = act_s.shape[0] // halves
    own = [pl.ds(k * part_rows, part_rows) for k in range(halves)]
    in_loads = [load(ins[k], in_s.at[k], k) for k in range(count)]
    index = count
    gh_loads = [load(ghs[k], gh_s.at[own[k], :], index + k) for k in range(halves)]
    index += halves
    grad_loads = [load(grads[k], grad_s.at[k], index + k) for k in range(count)]
    index += count
    act_loads = [load(acts[k], act_s.at[own[k], :], index + k) for k in range(halves)]
    index += halves
    term_loads = [load(terms[k], term_s.at[k], index + k) for k in range(term_count)]
    for k in range(count):
        in_loads[k].wait()
        in_t[:, k * rows : (k + 1) * rows] = in_s[k].T
    for copy in gh_loads:
        copy.wait()
    stores = []

    def store(source, target):
        stores.append(pltpu.make_async_copy(source, target, out_sems.at[len(stores)]))
        stores[-1].start()

    part = model // split
    fine = part // group
    _, _, head_size, _, _, hidden = tile_s.shape

    def tiles(y, which, left, right):
        start = pl.multiple_of((me_ref[1] ^ y) * part, part) if split > 1 else 0
        for j in range(head_size):
            z = me_ref[2] ^ turned(j, head_size)
            cols = slice(None)
            if split > 1:
                cols = pl.ds(pl.multiple_of(z * hidden, hidden), hidden)
            made = dot(left[pl.ds(start, part), :], right[:, cols]).astype(BF)
            for g in range(group):
                to = (me_ref[0] ^ g) if group > 1 else 0
                tile_s[which, y, j, to] = made[g * fine : (g + 1) * fine, :]
        store(tile_s.at[which, y], outs[which * split + y])

    for y in reversed(range(split)):
        tiles(y, 0, in_t, gh_s)
    for k in range(count):
        grad_loads[k].wait()
        grad_t[:, k * rows : (k + 1) * rows] = grad_s[k].T
    for copy in act_loads:
        copy.wait()
    for y in reversed(range(split)):
        tiles(y, 1, grad_t, act_s)
    for copy in term_loads:
        copy.wait()
    sum_s[...] = sum(term_s[k].astype(F32) for k in range(term_count)).astype(BF)
    store(sum_s, sum_o)
    for copy in stores:
        copy.wait()


def middle_back_kernel(
    dims, middle_ref, branch_ref, up_ref, mod_ref, item_ref, wp_ref, *refs
):
    parts, items, count, chunk = dims
    me_ref, attn_rows_ref = refs[0], refs[1]
    terms, refs = refs[2 : 2 + count], refs[2 + count :]
    out_ref, gb_ref, gm_ref, sums_ref, col_ref = refs[:5]
    proj_refs, (attn, left_t, right) = refs[5:-3], refs[-3:]
    rows, model = middle_ref.shape
    group, _, width = out_ref.shape
    sub = width // parts
    sums_ref[...] = jnp.zeros_like(sums_ref)
    col_ref[...] = jnp.zeros_like(col_ref)

    @chunks(rows, 64)
    def _(i):
        r = at(i, 64)
        item = item_ref[r, :]
        grad_in = sum(term[r, :].astype(F32) for term in terms)
        normed, inverse = row_norm(middle_ref[r, :])
        scale = mod_rows(mod_ref, 3, item, model)
        grad_middle = up_ref[r, :].astype(F32) + norm_back(grad_in * (1.0 + scale), normed, inverse)
        gm_ref[r, :] = grad_middle
        grad_branch = (grad_middle * mod_rows(mod_ref, 0, item, model)).astype(BF)
        gb_ref[r, :] = grad_branch
        col_ref[0:1, :] += jnp.sum(grad_branch.astype(F32), axis=0, keepdims=True)
        add_item_sums(sums_ref, 0, item, grad_middle * branch_ref[r, :].astype(F32), items)
        add_item_sums(sums_ref, 1, item, grad_in * normed, items)
        add_item_sums(sums_ref, 2, item, grad_in, items)

    attn[...] = dot(gb_ref[...], wp_ref[...], BY_ROW).astype(BF)
    for g in range(group):
        for p in range(parts):
            start = (p * group + g) * sub
            out_ref[g, :, p * sub : (p + 1) * sub] = attn[:, start : start + sub]
    proj_weights_kernel(
        (group, chunk), me_ref, attn_rows_ref, gb_ref, *proj_refs, left_t, right
    )


def output_kernel(dims, middle_ref, up_ref, mod_ref, item_ref, bias_ref, *refs):
    items, count, proj_count, tile_count = dims
    terms, refs = refs[:count], refs[count:]
    projs, refs = refs[:proj_count], refs[proj_count:]
    tiles, (out_ref, sums_ref, proj_ref, kept_ref, sent_ref) = refs[:tile_count], refs[tile_count:]
    add_blocks(tiles, (kept_ref, sent_ref))
    proj_ref[...] = sum(proj[...].astype(F32) for proj in projs).astype(BF)
    rows, model = middle_ref.shape
    sums_ref[...] = jnp.zeros_like(sums_ref)

    @chunks(rows, 64)
    def _(i):
        r = at(i, 64)
        item = item_ref[r, :]
        made = sum(term[r, :].astype(F32) for term in terms) + bias_ref[...].astype(F32)
        gamma = mod_rows(mod_ref, 1, item, model)
        out_ref[r, :] = (middle_ref[r, :] + gamma * made).astype(BF)
        add_item_sums(sums_ref, 0, item, up_ref[r, :].astype(F32) * made, items)


def tokens_back_kernel(dims, x_ref, gm_ref, mod_ref, item_ref, *refs):
    items, count = dims
    terms, (out_ref, sums_ref) = refs[:count], refs[count:]
    rows, model = x_ref.shape
    sums_ref[...] = jnp.zeros_like(sums_ref)

    @chunks(rows, 64)
    def _(i):
        r = at(i, 64)
        item = item_ref[r, :]
        grad_in = sum(term[r, :].astype(F32) for term in terms)
        normed, inverse = row_norm(x_ref[r, :].astype(F32))
        scale = mod_rows(mod_ref, 2, item, model)
        out_ref[r, :] = (
            gm_ref[r, :] + norm_back(grad_in * (1.0 + scale), normed, inverse)
        ).astype(BF)
        add_item_sums(sums_ref, 0, item, grad_in * normed, items)
        add_item_sums(sums_ref, 1, item, grad_in, items)


def proj_weights_kernel(dims, me_ref, attn_ref, gb_ref, *refs):
    group, split = dims
    outs, (left_t, right) = refs[:group], refs[group:]
    left_t[...] = attn_ref[...].T
    chunk, head_size, tall, wide = outs[0].shape
    for k in range(group):
        for y in range(chunk):
            part = (me_ref[1] ^ y) if split else y
            start = pl.multiple_of((part * group + (me_ref[0] ^ k)) * wide, wide)
            right[:, y * wide : (y + 1) * wide] = gb_ref[:, pl.ds(start, wide)]
        for j in range(head_size):
            z = (me_ref[2] ^ turned(j, head_size)) if split else j
            made = dot(left_t[pl.ds(pl.multiple_of(z * tall, tall), tall), :], right[...])
            for y in range(chunk):
                outs[k][y, j] = made[:, y * wide : (y + 1) * wide].astype(BF)


def qkv_weights_kernel(dims, me_ref, dqkv_ref, *refs):
    count, chunk, split, proj_count = dims
    ins, refs = refs[:count], refs[count:]
    projs, refs = refs[:proj_count], refs[proj_count:]
    outs, (left_t, right) = refs[:chunk], refs[chunk:]
    rows = ins[0].shape[0]
    for k in range(count):
        left_t[:, k * rows : (k + 1) * rows] = ins[k][...].T
    head_size, _, tall, wide = outs[0].shape
    for y in reversed(range(chunk)):
        part = (me_ref[1] ^ y) if split else y
        for t in range(3):
            start = pl.multiple_of((t * chunk + part) * wide, wide)
            right[:, t * wide : (t + 1) * wide] = dqkv_ref[:, pl.ds(start, wide)]
        for j in range(head_size):
            z = (me_ref[2] ^ turned(j, head_size)) if split else j
            made = dot(left_t[pl.ds(pl.multiple_of(z * tall, tall), tall), :], right[...])
            outs[y][j, 0] = sum(proj[y, j].astype(F32) for proj in projs).astype(BF)
            for t in range(3):
                outs[y][j, 1 + t] = made[:, t * wide : (t + 1) * wide].astype(BF)


def sort_kernel(pack_len, dest_ref, tokens_ref, cot_ref, to_slot_ref, tokens_out, cot_out):
    rows = tokens_ref.shape[0]
    pack = dest_ref[...] // pack_len
    other = jnp.broadcast_to(pack, (8, rows)).astype(F32).T[:, 0:1].astype(jnp.int32)
    this = lax.broadcasted_iota(jnp.int32, (rows, rows), 1)
    that = lax.broadcasted_iota(jnp.int32, (rows, rows), 0)
    before = (other < pack) | ((other == pack) & (that < this))
    slot = jnp.sum(before.astype(jnp.int32), axis=0, keepdims=True)
    to_slot_ref[...] = (slot == that).astype(F32).astype(BF)
    tokens_out[...] = dot(to_slot_ref[...], tokens_ref[...]).astype(BF)
    cot_out[...] = dot(to_slot_ref[...], cot_ref[...]).astype(BF)


def item_blocks_kernel(dims, me_ref, middle_ref, output_ref, tokens_ref, out_ref, joined):
    group, segs, head_size, size = dims
    model = output_ref.shape[1]
    parts = (
        (middle_ref, 0), (output_ref, 0), (tokens_ref, 0),
        (middle_ref, 1), (tokens_ref, 1), (middle_ref, 2),
    )
    for part, (ref, start) in enumerate(parts):
        joined[:, part * model : (part + 1) * model] = ref[:, start * model : (start + 1) * model]
    for g in range(group):
        for y in range(segs):
            for z in range(head_size):
                start = ((y * group + g) * head_size + z) * size
                near = me_ref[2] ^ z
                turn, count = jnp.int32(0), head_size
                while count > 1:
                    turn, near, count = turn * 2 + near % 2, near // 2, count // 2
                block = (me_ref[1] ^ y) * head_size + turn
                rows = pl.ds(pl.multiple_of(block * 8, 8), 8)
                out_ref[me_ref[0] ^ g, rows, 0:size] = joined[:, start : start + size]


def group_sums_kernel(count, bit, kept_ref, came_ref, vector_ref, own_ref, sent_ref, sum_ref):
    rows = kept_ref.shape[1]
    vectors = vector_ref[...] + came_ref[pl.ds(came_ref.shape[0] - 64, 64), :]
    sum_ref[...] = vectors
    last = count == 2
    place = 0
    for k in range(0, count, 2):
        made = kept_ref[k] + came_ref[pl.ds(k // 2 * rows, rows), :]
        if last:
            half = rows // 2
            own_ref[...] = made[:half]
            sent_ref[0:half, :] = made[half:]
        elif k // 2 % 2 == 0:
            own_ref[k // 2] = made
        else:
            own_ref[k // 2] = made
            sent_ref[place * rows : (place + 1) * rows, :] = made
            place += 1
    sent_ref[pl.ds(sent_ref.shape[0] - 64, 64), :] = vectors


def pack_sums_kernel(kept_ref, came_ref, vector_ref, own_ref, *refs):
    blocks, senders = own_ref.shape[0] * (2 if len(refs) == 2 else 1), kept_ref.shape[1]
    vectors = vector_ref[...] + came_ref[pl.ds(came_ref.shape[0] - 64, 64), :]
    refs[-1][...] = vectors
    for c in range(blocks):
        for t in range(2 * senders):
            if t < senders:
                value = kept_ref[c, t]
            else:
                value = came_ref[pl.ds((c * senders + t - senders) * 8, 8), :]
            if len(refs) == 1 or c < blocks // 2:
                own_ref[c, t] = value
            else:
                refs[0][pl.ds(((c - blocks // 2) * 2 * senders + t) * 8, 8), :] = value
    if len(refs) == 2:
        refs[0][pl.ds(refs[0].shape[0] - 64, 64), :] = vectors


def ada_kernel(segs, me_ref, silu_ref, blocks_ref, grad_ref, bias_ref, held):
    for c in range(blocks_ref.shape[0]):
        sender = (me_ref[1] ^ turned(c % segs, segs)) * me_ref[3] + (me_ref[2] ^ c // segs)
        held[pl.ds(pl.multiple_of(sender * 8, 8), 8), :] = blocks_ref[c]
    low = held[:, 0 : grad_ref.shape[1]].astype(BF)
    bias_ref[...] = jnp.broadcast_to(
        jnp.sum(low.astype(F32), axis=0, keepdims=True), bias_ref.shape
    )
    grad_ref[...] = lax.dot_general(
        silu_ref[...], low, (((0,), (0,)), ((), ())), preferred_element_type=F32
    )


def add_kernel(counts, *refs):
    terms, outs = refs[: sum(counts)], refs[sum(counts) :]
    for place, count in enumerate(counts):
        add_blocks(terms[:count], outs[2 * place : 2 * place + 2])
        terms = terms[count:]


def own_tiles_kernel(*refs):
    ups, downs, outs = refs[:2], refs[2:4], refs[4:]
    for i, out in enumerate(outs):
        for which, terms in enumerate((ups, downs)):
            out[which] = sum(term[0, i].astype(F32) for term in terms).astype(BF)


def place_kernel(group, me_ref, *refs):
    blocks, (up_ref, down_ref) = refs[:group], refs[group:]
    hidden = blocks[0].shape[2]
    for i in range(group):
        own = pl.ds(pl.multiple_of((me_ref[0] ^ i) * hidden, hidden), hidden)
        up_ref[:, own] = blocks[i][0].astype(F32)
        down_ref[own, :] = blocks[i][1].astype(F32).T


def vector_parts_kernel(dims, me_ref, qkv_ref, branch_ref, mlp_ref, *refs):
    group, parts, head_size = dims
    hidden_refs, (flat_ref, out_ref) = refs[:-2], refs[-2:]
    sub = qkv_ref.shape[1] // parts
    hidden = hidden_refs[0].shape[1] // head_size
    out_ref[...] = jnp.zeros_like(out_ref)
    for p in range(parts):
        own = pl.ds(pl.multiple_of((p * group + me_ref[0]) * sub, sub), sub)
        for row in range(3):
            out_ref[row : row + 1, own] = qkv_ref[row : row + 1, p * sub : (p + 1) * sub]
    out_ref[3:4, :] = branch_ref[0:1, :]
    out_ref[4:5, :] = mlp_ref[0:1, :]
    if hidden % 128 == 0:
        own = pl.ds(pl.multiple_of(me_ref[0] * hidden, hidden), hidden)
        for z in range(head_size):
            cols = slice(z * hidden, (z + 1) * hidden)
            out_ref[8 + z : 9 + z, own] = sum(ref[0:1, cols] for ref in hidden_refs)
    for c in range(out_ref.shape[1] // 256):
        flat_ref[c * 16 : (c + 1) * 16, :] = out_ref[:, c * 256 : (c + 1) * 256]


def to_packs(rows):
    return lax.all_to_all(rows, ("yy", "head"), split_axis=0, concat_axis=0, tiled=True)


def over_group(blocks):
    return lax.all_to_all(blocks, "g", split_axis=0, concat_axis=0, tiled=True)


def bits(count):
    steps = []
    while count > 1:
        count //= 2
        steps.append(count)
    return steps


def xor_swap(values, axis, step):
    size = lax.axis_size(axis)
    return lax.ppermute(values, axis, [(i, i ^ step) for i in range(size)])


def xor_gather(block, axis):
    blocks = {0: block}
    for step in bits(lax.axis_size(axis)):
        for k in list(blocks):
            blocks[k ^ step] = xor_swap(blocks[k], axis, step)
    return [blocks[k] for k in range(len(blocks))]


def xor_scatter(blocks, axis):
    terms = {k: [block] for k, block in enumerate(blocks)}
    for step in reversed(bits(lax.axis_size(axis))):
        for k in reversed([k for k in terms if k & step]):
            terms[k ^ step].append(xor_swap(add_low(*terms.pop(k)), axis, step))
    return terms[0]


def halves_over_head(values):
    count = lax.axis_size("head")
    step = count // values.shape[0]
    half = values.shape[0] // 2
    return values[:half], xor_swap(values[half:], "head", step)


def add_low(*terms):
    if len(terms) == 1:
        return terms[0]
    return sum(term.astype(F32) for term in terms).astype(terms[0].dtype)


def butterfly(values, axis):
    for step in bits(lax.axis_size(axis)):
        values = values + xor_swap(values, axis, step)
    return values


def pick(values, index, axis):
    return lax.dynamic_index_in_dim(values, index, axis, keepdims=False)


def xor_blocks(values, axis, dim):
    me = lax.axis_index(axis)
    return [pick(values, me ^ k, dim) for k in range(lax.axis_size(axis))]


def tie(*values):
    return lax.optimization_barrier(values)


def tie_groups(*groups):
    tied = list(tie(*[value for group in groups for value in group]))
    return [[tied.pop(0) for _ in group] for group in groups]


def shards(
    tokens,
    cotangent,
    class_table,
    ada_weight,
    ada_bias,
    qkv_weight,
    q_bias,
    v_bias,
    log_scale,
    proj_weight,
    proj_bias,
    fc1_weight,
    fc1_bias,
    fc2_weight,
    fc2_bias,
    item_lens,
    class_ids,
    section_ids,
    destination,
):
    segs = lax.axis_size("yy")
    group = lax.axis_size("g")
    head_size = lax.axis_size("head")
    yy, g, z = lax.axis_index("yy"), lax.axis_index("g"), lax.axis_index("head")
    me = jnp.stack([g, yy, z, jnp.int32(head_size)]).astype(jnp.int32)
    pack = yy * head_size + z
    rows, model = tokens.shape
    heads_all = log_scale.shape[0]
    head_dim = model // heads_all
    heads = heads_all // group
    width = model // group
    dp_size = segs * group
    pack_len = rows * head_size
    seg = rows // segs
    items = item_lens.shape[1]
    block = min(256, pack_len)
    col = model // dp_size
    parts = segs if col % 128 == 0 else 1
    sub = width // parts

    def own_cols(values):
        return pick(values.reshape(parts, group, sub), g, 1).reshape(1, width)

    rows_bf, rows_f32 = shape_of((rows, model), BF), shape_of((rows, model), F32)
    to_slot, sorted_tokens, sorted_cotangent = call(
        "sort",
        functools.partial(sort_kernel, pack_len),
        (destination[None, :], tokens, cotangent),
        (VMEM, HBM, HBM),
        (shape_of((rows, rows), BF), rows_bf, rows_bf),
    )
    inputs = to_packs(sorted_tokens)

    hidden = fc1_weight.shape[1] // group
    units = head_size * hidden
    half = model // segs
    fc1_own = lax.dynamic_slice(fc1_weight, (yy * half, g * hidden), (half, hidden))
    fc1_bias_own = lax.dynamic_slice(fc1_bias, (g * hidden,), (hidden,))
    fc2_own = lax.dynamic_slice(fc2_weight, (g * hidden, yy * half), (hidden, half))
    fc1_sent = jnp.concatenate(
        [fc1_own, jnp.broadcast_to(fc1_bias_own[None, :], (16, hidden))], axis=0
    )
    fc1_all = lax.all_gather(fc1_sent, ("yy", "head"), axis=0)
    fc1_all = fc1_all.reshape(segs, head_size, half + 16, hidden)
    fc2_all = lax.all_gather(fc2_own, ("yy", "head"), axis=0)
    fc2_all = fc2_all.reshape(segs, head_size, hidden, half)
    fc1_bias_here = fc1_all[0, :, half].reshape(1, units).astype(F32)
    tiled = hidden % 128 == 0
    if tiled:
        fc1_here, fc2_here = call(
            "weights",
            weights_kernel,
            (fc1_all, fc2_all),
            (ANY, ANY),
            (shape_of((model, units), BF), shape_of((units, model), BF)),
            [pltpu.SemaphoreType.DMA((2 * segs * head_size,))],
            out_specs=(VMEM, VMEM),
        )
    else:
        fc1_here = fc1_all[:, :, :half].transpose(0, 2, 1, 3).reshape(model, units)
        fc2_here = fc2_all.transpose(1, 2, 0, 3).reshape(units, model)

    lens_here = pick(item_lens, pack, 0)
    class_here = pick(class_ids, pack, 0)
    order_key = class_here * items + jnp.arange(items, dtype=jnp.int32)
    item_rank = jnp.sum(
        jnp.where(order_key[None, :] < order_key[:, None], lens_here[None, :], 0), axis=1
    )
    item_pos = jnp.cumsum(lens_here) - lens_here
    item_end = item_rank + lens_here

    def items_of(rank):
        return (rank[:, None] >= item_rank[None, :]) & (rank[:, None] < item_end[None, :])

    rank_all = jnp.arange(pack_len, dtype=jnp.int32)
    member = items_of(rank_all)

    def of_item(values):
        return jnp.sum(jnp.where(member, values[None, :], 0), axis=1)

    section_here = lax.ppermute(
        section_ids[0],
        ("g", "head"),
        [(a * head_size + b, b * head_size + a) for a in range(group) for b in range(head_size)],
    )
    position = rank_all - of_item(item_rank - item_pos)
    section_rank = jnp.sum(
        jnp.where(rank_all[None, :] == position[:, None], section_here[None, :], 0), axis=1
    )
    up_to = jnp.sum((section_here[None, :] <= section_rank[:, None]).astype(jnp.int32), axis=1)
    low = of_item(item_rank)
    high = jnp.minimum(up_to + of_item(item_rank - item_pos), of_item(item_end))
    first = low[::block] // block
    last = (high[block - 1 :: block] + block - 1) // block
    low, high = low[None, :], high[None, :]

    row_rank = (
        (jnp.arange(segs, dtype=jnp.int32)[:, None] * group + g) * seg
        + jnp.arange(seg, dtype=jnp.int32)[None, :]
    ).reshape(rows)
    row_item = jnp.sum(
        jnp.where(items_of(row_rank), jnp.arange(items, dtype=jnp.int32)[None, :], 0), axis=1
    )[:, None]

    class_rows = jnp.take(class_table, class_ids.reshape(-1), axis=0).astype(F32)
    silu_cond = jax.nn.silu(class_rows).astype(BF)
    silu_here = lax.dynamic_slice_in_dim(silu_cond, pack * items, items, 0)
    mod = jnp.dot(silu_here, ada_weight, preferred_element_type=F32) + ada_bias.astype(F32)

    inputs, first, last, low, high = tie(inputs, first, last, low, high)
    (attn_in,) = call(
        "first_norm",
        first_norm_kernel, (inputs, mod, row_item), (HBM, VMEM, VMEM), (shape_of((rows, model), BF),)
    )
    attn_blocks = xor_gather(attn_in, "g")
    per_part = sub // head_dim
    scale_here = pick(log_scale.reshape(parts, group, per_part), g, 1).reshape(heads)
    temper = jnp.repeat(jnp.exp(scale_here), head_dim)[None, :]
    wide = shape_of((pack_len, width), BF)
    tall = shape_of((width, pack_len), F32)
    sorted_cotangent, _ = tie(sorted_cotangent, inputs)
    upstream = to_packs(sorted_cotangent)
    def near_blocks(own):
        blocks = {0: own}
        for step in bits(group)[1:]:
            for k in list(blocks):
                blocks[k ^ step] = xor_swap(blocks[k], "g", step)
        return [blocks[k] for k in range(len(blocks))]

    near = group // 2
    held_bf = pltpu.VMEM((pack_len, width), BF)
    out_blocks, out_t, lse, queries, queries_low, keys, values, inverses = call(
        "attend",
        functools.partial(attend_kernel, (group, segs, head_dim, parts, block)),
        (me, first, last, low, high, temper, own_cols(q_bias).astype(F32),
         own_cols(v_bias).astype(F32), qkv_weight, *attn_blocks),
        (SMEM,) * 3 + (VMEM,) * 5 + (ANY,) * (1 + group),
        (shape_of((group, rows, width), BF), tall, shape_of((8, pack_len), F32), wide, wide, wide,
         wide, shape_of((pack_len, 128), F32)),
        [
            pltpu.VMEM((model, 3 * width), BF),
            pltpu.VMEM((group, rows, model), BF),
            held_bf,
            held_bf,
            held_bf,
            held_bf,
            pltpu.VMEM((pack_len, 128), F32),
            pltpu.VMEM((width, pack_len), BF),
            pltpu.VMEM((width, pack_len), F32),
            held_bf,
            pltpu.VMEM((width, block), F32),
            pltpu.VMEM((8, block), F32),
            pltpu.SemaphoreType.DMA((3 * parts,)),
            pltpu.SemaphoreType.DMA((group,)),
            pltpu.SemaphoreType.DMA((6 + segs * group,)),
        ],
        out_specs=(ANY, ANY, VMEM, ANY, ANY, ANY, ANY, ANY),
    )
    returned = over_group(out_blocks)
    upstream, _ = tie(upstream, out_blocks)
    grad_mlp, grad_mlp_sum = call(
        "grad_mlp",
        grad_mlp_kernel,
        (upstream, mod, row_item),
        (HBM, VMEM, VMEM),
        (rows_bf, shape_of((8, model), F32)),
    )
    grad_far = xor_swap(grad_mlp, "g", near)
    grad_blocks = near_blocks(grad_mlp)
    returned, grad_mlp_sum = tie(returned, grad_mlp_sum)
    attn_rows, branch, middle, mlp_in = call(
        "project",
        functools.partial(project_kernel, parts),
        (returned, proj_weight, proj_bias[None, :], inputs, mod, row_item),
        (HBM, HBM, VMEM, HBM, VMEM, VMEM),
        (rows_bf, rows_bf, rows_f32, rows_bf),
        [pltpu.VMEM((rows, model), F32)],
    )

    mlp_blocks = near_blocks(mlp_in)
    mlp_far = xor_swap(mlp_in, "g", near)
    grad_blocks += near_blocks(tie(grad_far, mlp_in, fc1_here)[0])
    back_parts, out_parts, acts, ghs, hidden_sums = [], [], [], [], []
    for start in (0, near):
        if start:
            mlp_blocks += near_blocks(tie(mlp_far, acts[0])[0])
        made = call(
            "feed",
            functools.partial(feed_kernel, near),
            (fc1_here, fc2_here, fc1_bias_here, *mlp_blocks[start : start + near],
             *grad_blocks[start : start + near]),
            (VMEM,) * 3 + (ANY,) * (2 * near),
            (rows_bf,) * (2 * near)
            + (shape_of((near * rows, units), BF),) * 2
            + (shape_of((8, units), F32),),
            [pltpu.VMEM((near, rows, model), BF)] * 4
            + [pltpu.VMEM((near, rows, units), BF)] * 2
            + [pltpu.VMEM((2, rows, units), F32)] * 2
            + [pltpu.SemaphoreType.DMA((2 * near,)), pltpu.SemaphoreType.DMA((4 * near,))],
            out_specs=(ANY,) * (2 * near + 2) + (VMEM,),
        )
        back_parts += made[:near]
        out_parts += made[near : 2 * near]
        acts.append(made[2 * near])
        ghs.append(made[2 * near + 1])
        hidden_sums.append(made[2 * near + 2])
    far_terms = {k: back_parts[k] for k in range(near, group)}
    for step in reversed(bits(group)[1:]):
        for k in reversed([k for k in far_terms if k & step]):
            came = xor_swap(far_terms.pop(k), "g", step)
            far_terms[k ^ step] = add_low(far_terms[k ^ step], came)
    far_sum = far_terms[near]
    back_parts = list(tie(*back_parts[:near], far_sum)[:near])
    in_terms = {k: [back_parts[k]] for k in range(near)}
    for step in reversed(bits(group)[1:]):
        for k in reversed([k for k in in_terms if k & step]):
            in_terms[k ^ step].append(xor_swap(add_low(*in_terms.pop(k)), "g", step))
    in_terms = in_terms[0] + [xor_swap(far_sum, "g", near)]
    acts[0], _ = tie(acts[0], far_sum)
    split = segs if tiled else 1

    def to_last(blocks):
        terms = {k: [block] for k, block in enumerate(blocks)}
        for step in reversed(bits(group)[1:]):
            for k in reversed([k for k in terms if k & step]):
                terms[k ^ step].append(xor_swap(add_low(*terms.pop(k)), "g", step))
        return terms[0], terms[near]

    out_terms, out_last = to_last(tie(*out_parts, far_sum)[:group])
    if tiled:
        fine = half // group
        tile_shape = (head_size, group, fine, hidden)
        feed_dims = (group, group, segs, 2, len(out_last))
    else:
        tile_shape = (1, 1, model, units)
        feed_dims = (group, 1, 1, 2, len(out_last))
    made = call(
        "feed_weights",
        functools.partial(feed_weights_kernel, feed_dims),
        (me, *acts, *ghs, *mlp_blocks, *grad_blocks, *out_last),
        (SMEM,) + (ANY,) * (4 + 2 * group + len(out_last)),
        (shape_of(tile_shape, BF),) * (2 * split) + (rows_bf,),
        [
            pltpu.VMEM((model, pack_len), BF),
            pltpu.VMEM((model, pack_len), BF),
            pltpu.VMEM((pack_len, units), BF),
            pltpu.VMEM((pack_len, units), BF),
            pltpu.VMEM((group, rows, model), BF),
            pltpu.VMEM((group, rows, model), BF),
            pltpu.VMEM((len(out_last), rows, model), BF),
            pltpu.VMEM((rows, model), BF),
            pltpu.VMEM((2, split, *tile_shape), BF),
            pltpu.SemaphoreType.DMA((4 + 2 * group + len(out_last),)),
            pltpu.SemaphoreType.DMA((2 * split + 1,)),
        ],
        out_specs=(ANY,) * (2 * split + 1),
    )
    up_parts, down_parts, out_sent = made[:split], made[split : 2 * split], made[2 * split]
    out_terms.append(xor_swap(out_sent, "g", near))
    if not tiled:
        fine = half // group
        order = jnp.array([turned(j, head_size) for j in range(head_size)]) ^ z
        near_g = jnp.arange(group) ^ g
        near_y = jnp.arange(segs) ^ yy

        def in_blocks(full):
            full = full.reshape(segs, group, fine, head_size, hidden).transpose(0, 3, 1, 2, 4)
            return list(full[near_y][:, order][:, :, near_g])

        up_parts, down_parts = in_blocks(up_parts[0]), in_blocks(down_parts[0])

    middle_in, _ = tie(middle, up_parts[0])
    outbound, _, grad_middle, middle_sums, branch_sum, *proj_parts = call(
        "middle_back",
        functools.partial(
            middle_back_kernel, (parts, items, len(in_terms), parts == segs)
        ),
        (middle_in, branch, upstream, mod, row_item, proj_weight, me, attn_rows, *in_terms),
        (HBM, HBM, HBM, VMEM, VMEM, HBM, SMEM) + (HBM,) * (1 + len(in_terms)),
        (shape_of((group, rows, width), BF), rows_bf, rows_f32, shape_of((8, 3 * model), F32),
         shape_of((8, model), F32))
        + (shape_of((parts, head_size, model // head_size, sub), BF),) * group,
        [
            pltpu.VMEM((rows, model), BF),
            pltpu.VMEM((model, rows), BF),
            pltpu.VMEM((rows, width), BF),
        ],
    )
    inbound = over_group(outbound)
    up_terms, down_terms = xor_scatter(up_parts, "yy"), xor_scatter(down_parts, "yy")
    proj_terms, proj_last = to_last(proj_parts)
    tied = tuple(out_terms) + tuple(proj_last) + tuple(up_terms)
    half_tiles = shape_of((head_size // 2, group, fine, hidden), BF)
    quarter_tiles = shape_of((head_size // 4, group, fine, hidden), BF)
    output_rows, output_sums, proj_sent, up_kept, up_sent = call(
        "output",
        functools.partial(
            output_kernel, (items, len(out_terms), len(proj_last), len(up_terms))
        ),
        (middle, upstream, mod, row_item, fc2_bias[None, :], *tied),
        (HBM, HBM, VMEM, VMEM, VMEM) + (HBM,) * len(tied),
        (rows_bf, shape_of((8, model), F32), shape_of(proj_last[0].shape, BF), half_tiles, half_tiles),
    )
    up_terms = (up_kept, xor_swap(up_sent, "head", 1))
    inbound, output_rows = tie(inbound, output_rows)
    output_back = to_packs(output_rows)
    proj_terms.append(xor_swap(proj_sent, "g", near))
    cols_f32 = pltpu.VMEM((pack_len, 128), F32)
    held_f32 = pltpu.VMEM((pack_len, width), F32)
    made = call(
        "attend_back",
        functools.partial(attend_back_kernel, (group, segs, head_dim, parts, block)),
        (me, temper, qkv_weight, inverses, queries_low, first, last, low, high, lse, inbound, queries,
         keys, values, out_t),
        (SMEM, VMEM, ANY, ANY, ANY, SMEM, SMEM, VMEM, VMEM, VMEM) + (ANY,) * 5,
        (rows_bf,) * group + (shape_of((pack_len, 3 * width), BF), shape_of((8, width), F32)),
        [
            held_bf,
            held_bf,
            held_bf,
            pltpu.VMEM((width, pack_len), F32),
            held_bf,
            pltpu.VMEM((width, pack_len), BF),
            held_f32,
            held_f32,
            pltpu.VMEM((width, block), F32),
            pltpu.VMEM((8, block), F32),
            held_bf,
            held_bf,
            held_bf,
            pltpu.VMEM((model, 3 * width), BF),
            cols_f32,
            held_bf,
            pltpu.VMEM((pack_len, 3 * width), BF),
            pltpu.VMEM((group, rows, model), BF),
            pltpu.SemaphoreType.DMA((6 + segs * group,)),
            pltpu.SemaphoreType.DMA((3 * parts,)),
            pltpu.SemaphoreType.DMA((2 * group,)),
        ],
        out_specs=(ANY,) * (group + 1) + (VMEM,),
    )
    made, down_terms, up_terms, proj_terms, (output_back,) = tie_groups(
        made, down_terms, up_terms, proj_terms, (output_back,)
    )
    grad_qkv, qkv_sums = made[group:]

    (vectors,) = call(
        "vector_parts",
        functools.partial(vector_parts_kernel, (group, parts, head_size)),
        (me, qkv_sums, branch_sum, grad_mlp_sum, *hidden_sums),
        (SMEM,) + (VMEM,) * (3 + len(hidden_sums)),
        (shape_of((64, 256), F32),),
        [pltpu.VMEM((16, model), F32)],
    )
    if not tiled:
        hidden_row = (hidden_sums[0] + hidden_sums[1])[0].reshape(head_size, hidden)
        hidden_row = lax.dynamic_update_slice(
            jnp.zeros((16, model), F32), hidden_row, (8, g * hidden)
        )
        vectors = vectors + hidden_row.reshape(16, 4, 256).transpose(1, 0, 2).reshape(64, 256)

    in_terms, last_terms = to_last(made[:group])
    sent = add_low(*last_terms)
    in_terms.append(xor_swap(sent, "g", near))
    tied = tie(*down_terms, *up_terms, sent)[:-1]
    down_kept, down_sent, up_kept, up_sent = call(
        "add",
        functools.partial(add_kernel, (len(down_terms), 2)),
        tied,
        (HBM,) * len(tied),
        (half_tiles, half_tiles, quarter_tiles, quarter_tiles),
    )
    down_terms = (down_kept, xor_swap(down_sent, "head", 1))
    up_terms = (up_kept, xor_swap(up_sent, "head", 2))
    grad_qkv, _ = tie(grad_qkv, down_sent)
    qkv_parts = call(
        "qkv_weights",
        functools.partial(
            qkv_weights_kernel, (group, parts, parts == segs, len(proj_terms))
        ),
        (me, grad_qkv, *attn_blocks, *proj_terms),
        (SMEM,) + (HBM,) * (1 + group + len(proj_terms)),
        (shape_of((head_size, 4, model // head_size, sub), BF),) * parts,
        [pltpu.VMEM((model, pack_len), BF), pltpu.VMEM((pack_len, 3 * sub), BF)],
    )
    down_terms, up_terms, _ = tie_groups(down_terms, up_terms, qkv_parts)
    down_kept, down_sent = call(
        "add", functools.partial(add_kernel, (2,)), down_terms, (HBM,) * 2, (quarter_tiles,) * 2
    )
    down_terms = (down_kept, xor_swap(down_sent, "head", 2))
    inputs_back, _ = tie(inputs, down_sent)
    tokens_grad_rows, tokens_sums = call(
        "tokens_back",
        functools.partial(tokens_back_kernel, (items, len(in_terms))),
        (inputs_back, grad_middle, mod, row_item, *in_terms),
        (HBM, HBM, VMEM, VMEM) + (HBM,) * len(in_terms),
        (rows_bf, shape_of((8, 2 * model), F32)),
    )

    tokens_grad_rows, *down_terms = tie(tokens_grad_rows, *down_terms)

    def to_data(values):
        return dot(to_slot, values, ((0,), (0,)))

    output = to_data(output_back).astype(BF)
    tokens_came = to_packs(tokens_grad_rows)

    ada_cols = 6 * model // (dp_size * head_size)
    packs = segs * head_size
    (kept,) = call(
        "item_blocks",
        functools.partial(item_blocks_kernel, (group, segs, head_size, ada_cols)),
        (me, middle_sums, output_sums, tokens_sums),
        (SMEM, VMEM, VMEM, VMEM),
        (shape_of((group, packs * 8, 256), F32),),
        [pltpu.VMEM((8, 6 * model), F32)],
        out_specs=(VMEM,),
    )
    sent = jnp.concatenate([kept[k] for k in range(1, group, 2)] + [vectors], axis=0)
    count = group
    for step in reversed(bits(group)):
        came = xor_swap(sent, "g", step)
        left = count // 2
        own = (left, packs * 8, 256) if left > 1 else (packs * 4, 256)
        rows_sent = (left // 2 * packs * 8 if left > 1 else packs * 4) + 64
        kept, sent, vectors = call(
            "group_sums",
            functools.partial(group_sums_kernel, count, step),
            (kept, came, vectors),
            (VMEM,) * 3,
            (shape_of(own, F32), shape_of((rows_sent, 256), F32), shape_of((64, 256), F32)),
            out_specs=(VMEM,) * 3,
        )
        count = left
    kept = kept.reshape(packs // 2, 1, 8, 256)
    tokens_sent = sent
    def over_head(terms):
        while terms[0].shape[0] > 1:
            terms = halves_over_head(add_low(*terms))
        return terms

    down_terms = tie(*down_terms, *up_terms, tokens_grad_rows)[:-1]
    down_terms, up_terms = down_terms[:2], down_terms[2:]
    tied = tuple(over_head(up_terms)) + tuple(over_head(down_terms))
    own_tiles = call(
        "own_tiles",
        own_tiles_kernel,
        tied,
        (HBM,) * 4,
        (shape_of((2, fine, hidden), BF),) * group,
    )
    both_all = [own_tiles[0]]
    for i in range(1, group):
        both_all.append(lax.ppermute(own_tiles[i], "g", [(k, k ^ i) for k in range(group)]))
    if parts == segs:
        terms = tie(*xor_scatter(qkv_parts, "yy"), tokens_sent)[:-1]
        terms = halves_over_head(add_low(*terms))
        terms, both_all, (tokens_came,) = tie_groups(terms, both_all, (tokens_came,))
        terms = over_head(terms)
        summed = sum(term[0].astype(F32) for term in terms)
        proj_part, qkv_part = summed[0], summed[1:]
    else:
        both = qkv_parts[0].transpose(1, 0, 2, 3).reshape(4, model, width)
        full = lax.dynamic_update_slice(
            jnp.zeros((4, model, model), BF), both, (0, 0, g * width)
        )
        summed = lax.psum_scatter(full, ("yy", "g"), scatter_dimension=2, tiled=True)
        summed = lax.psum_scatter(summed, "head", scatter_dimension=1, tiled=True).astype(F32)
        proj_part, qkv_part = summed[0], summed[1:]

    if tiled:
        up_part, down_part = call(
            "place",
            functools.partial(place_kernel, group),
            (me, *both_all),
            (SMEM,) + (HBM,) * group,
            (shape_of((fine, group * hidden), F32), shape_of((group * hidden, fine), F32)),
        )
    else:
        placed = jnp.stack(both_all)[jnp.arange(group) ^ g].astype(F32)
        up_part = placed[:, 0].transpose(1, 0, 2).reshape(fine, group * hidden)
        down_part = placed[:, 1].transpose(0, 2, 1).reshape(group * hidden, fine)


    sent, _ = tie(sent, tokens_came)
    tokens_grad = to_data(tokens_came)
    steps = [("yy", step) for step in bits(segs)] + [("head", step) for step in reversed(bits(head_size))]
    for place, (axis, step) in enumerate(steps):
        came = xor_swap(sent, axis, step)
        blocks, senders = kept.shape[0], kept.shape[1]
        end = place + 1 == len(steps)
        own = (blocks if end else blocks // 2, 2 * senders, 8, 256)
        outs = [shape_of(own, F32)]
        if not end:
            outs.append(shape_of((blocks // 2 * 2 * senders * 8 + 64, 256), F32))
        outs.append(shape_of((64, 256), F32))
        made = call(
            "pack_sums", pack_sums_kernel, (kept, came, vectors), (VMEM,) * 3, outs,
            out_specs=(VMEM,) * len(outs),
        )
        kept, vectors = made[0], made[-1]
        sent = made[1] if not end else None
    item_came = kept[0]
    vectors = vectors.reshape(4, 16, 256).transpose(1, 0, 2).reshape(16, model)
    silu_rows = jnp.pad(silu_cond.reshape(packs, items, model), ((0, 0), (0, 8 - items), (0, 0)))
    ada_grad, ada_bias_grad = call(
        "ada",
        functools.partial(ada_kernel, segs),
        (me, silu_rows.reshape(packs * 8, model), item_came),
        (SMEM, VMEM, VMEM),
        (shape_of((model, ada_cols), F32), shape_of((8, ada_cols), F32)),
        [pltpu.VMEM((packs * 8, 256), F32)],
    )
    ada_bias_grad = ada_bias_grad[0]

    log_scale_grad = jnp.sum(vectors[2].reshape(heads_all, head_dim), axis=1)
    fc1_bias_grad = pick(vectors, 8 + z, 0)[: group * hidden]
    return (
        output,
        tokens_grad,
        ada_grad,
        ada_bias_grad,
        qkv_part,
        vectors[0],
        vectors[1],
        log_scale_grad,
        proj_part,
        vectors[3],
        up_part,
        fc1_bias_grad,
        down_part,
        vectors[4],
    )


def solution(mesh):
    head_size = mesh.shape["head"]
    dp_size = mesh.shape["dp"]
    inner = Mesh(
        mesh.devices.reshape(dp_size // head_size, head_size, head_size), ("yy", "g", "head")
    )
    dp = ("yy", "g")
    everything = ("yy", "g", "head")
    in_specs = (
        P(everything, None),
        P(everything, None),
        P(),
        P(),
        P(),
        P(),
        P(),
        P(),
        P(),
        P(),
        P(),
        P(None, "head"),
        P("head"),
        P("head", None),
        P(),
        P(),
        P(),
        P(dp, None),
        P(everything),
    )
    out_specs = (
        P(everything, None),
        P(everything, None),
        P(None, everything),
        P(everything),
        P(None, "head", dp),
        P(),
        P(),
        P(),
        P("head", dp),
        P(),
        P(dp, "head"),
        P("head"),
        P("head", dp),
        P(),
    )
    return jax.shard_map(
        shards, mesh=inner, in_specs=in_specs, out_specs=out_specs, check_vma=False
    )
```

```python
import functools

import jax
import jax.numpy as jnp
from jax import lax
from jax.experimental import pallas as pl
from jax.experimental.pallas import tpu as pltpu
from jax.sharding import Mesh, PartitionSpec as P

BF = jnp.bfloat16
F32 = jnp.float32
SMEM = pl.BlockSpec(memory_space=pltpu.SMEM)
VMEM = pl.BlockSpec(memory_space=pltpu.VMEM)
ANY = pl.BlockSpec(memory_space=pl.ANY)
HBM = "hbm"
LIMIT = 40
LIMITS = {"attend": 57, "attend_back": 57, "sort": 57, "middle_back": 50, "output": 50, "feed": 50, "feed_weights": 57, "weights": 57, "qkv_weights": 57}
FLOPS, BYTES = 1_000_000_000, 3_000_000
TIMES = {
    "sort": 2, "first_norm": 2, "grad_mlp": 2, "attend": 26, "project": 0, "weights": 4, "feed": 12,
    "feed_weights": 12, "middle_back": 7, "proj_weights": 3, "output": 3, "attend_back": 34, "add": 3,
    "qkv_weights": 8, "tokens_back": 5,
}
PLAIN = ((1,), (0,))
BY_ROW = ((1,), (1,))


def shape_of(shape, dtype):
    return jax.ShapeDtypeStruct(shape, dtype)


def dot(left, right, dims=PLAIN):
    return lax.dot_general(left, right, (dims, ((), ())), preferred_element_type=F32)


def call(name, kernel, operands, specs, outs, scratch=(), limit=LIMIT, out_specs=None):
    out_specs = out_specs or tuple(HBM if o.size >= 65536 else VMEM for o in outs)
    n_in, n_out, n_scratch = len(specs), len(outs), len(scratch)
    staged_in = [i for i, spec in enumerate(specs) if spec is HBM]
    staged_out = [i for i, spec in enumerate(out_specs) if spec is HBM]
    staged = [pltpu.VMEM(operands[i].shape, operands[i].dtype) for i in staged_in]
    staged += [pltpu.VMEM(outs[i].shape, outs[i].dtype) for i in staged_out]
    sems = [pltpu.SemaphoreType.DMA((len(staged),))] if staged else []

    def body(*refs):
        given, made = list(refs[:n_in]), list(refs[n_in : n_in + n_out])
        own = refs[n_in + n_out : n_in + n_out + n_scratch]
        held = refs[n_in + n_out + n_scratch :]
        copies = []
        for place, i in enumerate(staged_in):
            copies.append(pltpu.make_async_copy(given[i], held[place], held[-1].at[place]))
            copies[-1].start()
            given[i] = held[place]
        backs = []
        for place, i in enumerate(staged_out, len(staged_in)):
            backs.append(pltpu.make_async_copy(held[place], made[i], held[-1].at[place]))
            made[i] = held[place]
        for copy in copies:
            copy.wait()
        kernel(*given, *made, *own)
        for copy in backs:
            copy.start()
        for copy in backs:
            copy.wait()

    limit = LIMITS.get(name, limit)
    return pl.pallas_call(
        body,
        name=name,
        out_shape=tuple(outs),
        in_specs=[ANY if spec is HBM else spec for spec in specs],
        out_specs=tuple(ANY if spec is HBM else spec for spec in out_specs),
        scratch_shapes=list(scratch) + staged + sems,
        compiler_params=pltpu.CompilerParams(vmem_limit_bytes=limit * 1024 * 1024),
        cost_estimate=pl.CostEstimate(
            flops=TIMES.get(name, 1) * FLOPS + 1, bytes_accessed=TIMES.get(name, 1) * BYTES + 1, transcendentals=0
        ),
    )(*operands)


def row_norm(values):
    centre = values - jnp.mean(values, axis=-1, keepdims=True)
    inverse = lax.rsqrt(jnp.mean(centre * centre, axis=-1, keepdims=True) + 1e-06)
    return (centre * inverse, inverse)


def norm_back(gradient, normed, inverse):
    return inverse * (
        gradient
        - jnp.mean(gradient, axis=-1, keepdims=True)
        - normed * jnp.mean(gradient * normed, axis=-1, keepdims=True)
    )


def mod_rows(mod_ref, part, item, width):
    cols = slice(part * width, (part + 1) * width)
    rows = jnp.broadcast_to(mod_ref[0:1, cols], (item.shape[0], width))
    for index in range(1, mod_ref.shape[0]):
        rows = jnp.where(item == index, mod_ref[index : index + 1, cols], rows)
    return rows


def add_item_sums(sums_ref, part, item, values, count):
    width = values.shape[1]
    cols = slice(part * width, (part + 1) * width)
    for index in range(count):
        kept = jnp.where(item == index, values, 0.0)
        sums_ref[index : index + 1, cols] += jnp.sum(kept, axis=0, keepdims=True)


def same_head(width, head_dim):
    row = lax.broadcasted_iota(jnp.int32, (width, width), 0) // head_dim
    col = lax.broadcasted_iota(jnp.int32, (width, width), 1) // head_dim
    return (row == col).astype(BF)


def chunks(rows, size):
    return pl.loop(0, rows // size)


def at(index, size):
    return pl.ds(pl.multiple_of(index * size, size), size)


def first_norm_kernel(x_ref, mod_ref, item_ref, out_ref):
    rows, width = x_ref.shape

    @chunks(rows, 64)
    def _(i):
        r = at(i, 64)
        item = item_ref[r, :]
        normed, _ = row_norm(x_ref[r, :].astype(F32))
        scale, shift = mod_rows(mod_ref, 2, item, width), mod_rows(mod_ref, 4, item, width)
        out_ref[r, :] = (normed * (1.0 + scale) + shift).astype(BF)


def grad_mlp_kernel(up_ref, mod_ref, item_ref, out_ref, sum_ref):
    rows, width = up_ref.shape
    sum_ref[...] = jnp.zeros_like(sum_ref)

    @chunks(rows, 64)
    def _(i):
        r = at(i, 64)
        gamma = mod_rows(mod_ref, 1, item_ref[r, :], width)
        grad = (up_ref[r, :].astype(F32) * gamma).astype(BF)
        out_ref[r, :] = grad
        sum_ref[0:1, :] += jnp.sum(grad.astype(F32), axis=0, keepdims=True)


def load_columns(weight_ref, held, sems, offset_of, parts, sub):
    copies = []
    for t in range(3):
        for p in range(parts):
            copies.append(
                pltpu.make_async_copy(
                    weight_ref.at[t, :, pl.ds(pl.multiple_of(offset_of(p), sub), sub)],
                    held.at[:, pl.ds((t * parts + p) * sub, sub)],
                    sems.at[t * parts + p],
                )
            )
    for copy in copies:
        copy.start()
    return copies


def pick_heads(width, head_dim, first):
    row = lax.broadcasted_iota(jnp.int32, (width, 128), 0)
    col = lax.broadcasted_iota(jnp.int32, (width, 128), 1)
    return (row == (col - first) * head_dim).astype(BF)


def spread_heads(width, head_dim, first):
    row = lax.broadcasted_iota(jnp.int32, (128, width), 0)
    col = lax.broadcasted_iota(jnp.int32, (128, width), 1)
    return (row - first == col // head_dim).astype(BF)


def exact_dot(values, ones):
    high = values.astype(BF)
    low = (values - high.astype(F32)).astype(BF)
    return dot(high, ones) + dot(low, ones)


def own_lanes(values, mine):
    return jnp.where(mine, values, jnp.zeros_like(values))


def attend_kernel(dims, *refs):
    group, segs, head_dim, parts, block = dims
    me_ref, first_ref, last_ref, lo_ref, hi_ref, temper_ref, qb_ref, vb_ref, w_ref = refs[:9]
    blocks = refs[9 : 9 + group]
    out_o, out_t_o, lse_ref, q_o, ql_o, k_o, v_o, inv_o = refs[9 + group : 17 + group]
    (held, block_s, q_ref, ql_ref, k_ref, v_ref, inv_ref, v_t, out_t_ref, out_s, acc, total, sems,
     in_sems, out_sems) = refs[17 + group :]
    pack_len, width = q_ref.shape
    rows = block_s.shape[1]
    seg, sub = rows // segs, width // parts
    pair, heads = 128 // head_dim, width // head_dim
    me = me_ref[0]
    loads = [
        pltpu.make_async_copy(blocks[k], block_s.at[k], in_sems.at[k]) for k in range(group)
    ]
    loads[0].start()
    copies = load_columns(w_ref, held, sems, lambda p: (p * group + me) * sub, parts, sub)
    for load in loads[1:]:
        load.start()
    same = same_head(width, head_dim)
    pick_q, pick_k = pick_heads(width, head_dim, 0), pick_heads(width, head_dim, heads)
    for copy in copies:
        copy.wait()
    for k in range(group):
        loads[k].wait()
        for y in range(segs):
            ranks = pl.ds(pl.multiple_of((y * group + (me ^ k)) * seg, 16), seg)
            made = dot(block_s[k, y * seg : (y + 1) * seg, :], held[...])
            query = made[:, :width] + qb_ref[...]
            key = made[:, width : 2 * width]
            inverse_q = lax.rsqrt(exact_dot(query * query, same) + 1e-06)
            query = query * inverse_q * temper_ref[...]
            rounded = query.astype(BF)
            q_ref[ranks, :] = rounded
            ql_ref[ranks, :] = (query - rounded.astype(F32)).astype(BF)
            inverse_k = lax.rsqrt(exact_dot(key * key, same) + 1e-06)
            k_ref[ranks, :] = (key * inverse_k).astype(BF)
            v_ref[ranks, :] = (made[:, 2 * width :] + vb_ref[...]).astype(BF)
            inv_ref[ranks, :] = exact_dot(inverse_q, pick_q) + exact_dot(inverse_k, pick_k)
    stores = []

    def store(source, target):
        stores.append(pltpu.make_async_copy(source, target, out_sems.at[len(stores)]))
        stores[-1].start()

    for source, target in (
        (q_ref, q_o), (ql_ref, ql_o), (k_ref, k_o), (v_ref, v_o), (inv_ref, inv_o)
    ):
        store(source, target)
    lanes = lax.broadcasted_iota(jnp.int32, (1, 128), 1) // head_dim
    v_t[...] = v_ref[...].T

    @pl.loop(0, pack_len // block)
    def _(q_block):
        q_rows = at(q_block, block)
        q_t = q_ref[q_rows, :].T
        low, high = lo_ref[:, q_rows], hi_ref[:, q_rows]
        acc[...] = jnp.zeros_like(acc)
        total[...] = jnp.zeros_like(total)

        @pl.loop(first_ref[q_block], last_ref[q_block])
        def _(k_block):
            k_rows = at(k_block, block)
            index = k_block * block + lax.broadcasted_iota(jnp.int32, (block, block), 0)
            seen = (index >= low) & (index < high)
            scores = []
            for h in range(heads):
                near = slice(h // pair * 128, (h // pair + 1) * 128)
                scores.append(dot(own_lanes(k_ref[k_rows, near], lanes == h % pair), q_t[near, :]))
            raised = [jnp.where(seen, jnp.exp(values), 0.0) for values in scores]
            for h in range(heads):
                own = pl.ds(h * head_dim, head_dim)
                total[h : h + 1, :] += jnp.sum(raised[h], axis=0, keepdims=True)
                acc[own, :] += dot(v_t[own, k_rows], raised[h].astype(BF))

        for h in range(heads):
            own = pl.ds(h * head_dim, head_dim)
            acc[own, :] = acc[own, :] / total[h : h + 1, :]
            lse_ref[h : h + 1, q_rows] = jnp.log(total[h : h + 1, :])
        out_t_ref[:, q_rows] = acc[...]
        out_s[q_rows, :] = acc[...].T.astype(BF)

    for y in range(segs):
        for g in range(group):
            start = (y * group + g) * seg
            store(out_s.at[pl.ds(start, seg), :], out_o.at[g, pl.ds(y * seg, seg), :])
    store(out_t_ref, out_t_o)
    for copy in stores:
        copy.wait()


def attend_back_blocks(dims, refs, scratch, outs):
    head_dim, block = dims
    first_ref, last_ref, lo_ref, hi_ref, lse_ref, q_ref, k_ref, v_ref, out_t_ref, g_s = refs
    k_t, dk_acc, dv_acc, acc, sums = scratch
    dq_ref, dk_ref, dv_ref = outs
    pack_len, width = q_ref.shape
    pair, heads = 128 // head_dim, width // head_dim
    lanes = lax.broadcasted_iota(jnp.int32, (1, 128), 1) // head_dim
    cols = [slice(p * 128, (p + 1) * 128) for p in range(width // 128)]
    k_t[...] = k_ref[...].T
    dk_acc[...] = jnp.zeros_like(dk_acc)
    dv_acc[...] = jnp.zeros_like(dv_acc)

    @pl.loop(0, pack_len // block)
    def _(q_block):
        q_rows = at(q_block, block)
        queries, grads = q_ref[q_rows, :], g_s[q_rows, :]
        q_t, g_t = queries.T, grads.T
        low, high = lo_ref[:, q_rows], hi_ref[:, q_rows]
        weighted = g_t.astype(F32) * out_t_ref[:, q_rows]
        for h in range(heads):
            sums[h : h + 1, :] = jnp.sum(
                weighted[h * head_dim : (h + 1) * head_dim, :], axis=0, keepdims=True
            )
        acc[...] = jnp.zeros_like(acc)

        @pl.loop(first_ref[q_block], last_ref[q_block])
        def _(k_block):
            k_rows = at(k_block, block)
            index = k_block * block + lax.broadcasted_iota(jnp.int32, (block, block), 0)
            seen = (index >= low) & (index < high)
            scores, grad_probs, probs, grad_scores = [], [], [], []
            for h in range(heads):
                near, mine = cols[h // pair], lanes == h % pair
                scores.append(dot(own_lanes(k_ref[k_rows, near], mine), q_t[near, :]))
                grad_probs.append(dot(own_lanes(v_ref[k_rows, near], mine), g_t[near, :]))
            for h in range(heads):
                made = jnp.where(seen, jnp.exp(scores[h] - lse_ref[h : h + 1, q_rows]), 0.0)
                probs.append(made.astype(BF))
                grad_scores.append((made * (grad_probs[h] - sums[h : h + 1, :])).astype(BF))
            for h in range(heads):
                own = pl.ds(h * head_dim, head_dim)
                acc[own, :] += dot(k_t[own, k_rows], grad_scores[h])
            for p, near in enumerate(cols):
                grad_k = grad_v = 0.0
                for h in range(p * pair, (p + 1) * pair):
                    mine = lanes == h % pair
                    grad_k += dot(grad_scores[h], own_lanes(queries[:, near], mine))
                    grad_v += dot(probs[h], own_lanes(grads[:, near], mine))
                dk_acc[k_rows, near] += grad_k
                dv_acc[k_rows, near] += grad_v

        dq_ref[q_rows, :] = acc[...].T.astype(BF)

    dk_ref[...] = dk_acc[...].astype(BF)
    dv_ref[...] = dv_acc[...].astype(BF)


def attend_back_kernel(dims, *refs):
    group, segs, head_dim, parts, block = dims
    me_ref, temper_ref, w_ref, inv_ref, ql_ref = refs[:5]
    ranges, lse_ref, ins = refs[5:9], refs[9], refs[10:15]
    sent, (dqkv_o, sums_ref), refs = refs[15 : 15 + group], refs[15 + group : 17 + group], refs[17 + group :]
    (q_s, k_s, v_s, out_s, g_s), scratch, made, refs = refs[:5], refs[5:10], refs[10:13], refs[13:]
    (w_s, inv_s, ql_s, dqkv_s, sent_s), (sems, w_sems, out_sems) = refs[:5], refs[5:]
    pack_len, width = q_s.shape
    rows = sent_s.shape[1]
    seg, sub = rows // segs, width // parts
    heads = width // head_dim
    me = me_ref[0]
    moves = [(ins[1], q_s), (ins[2], k_s), (ins[3], v_s), (ins[4], out_s)]
    for y in range(segs):
        for g in range(group):
            to = pl.ds((y * group + g) * seg, seg)
            moves.append((ins[0].at[g, pl.ds(y * seg, seg), :], g_s.at[to, :]))
    moves += [(inv_ref, inv_s), (ql_ref, ql_s)]
    loads = []
    for place, (source, target) in enumerate(moves):
        loads.append(pltpu.make_async_copy(source, target, sems.at[place]))
        loads[-1].start()
    copies = load_columns(w_ref, w_s, w_sems, lambda p: (p * group + me) * sub, parts, sub)
    copies += loads[-2:]
    for load in loads[:-2]:
        load.wait()
    attend_back_blocks(
        (head_dim, block), (*ranges, lse_ref, q_s, k_s, v_s, out_s, g_s), scratch, made
    )
    same = same_head(width, head_dim)
    spread_q, spread_k = spread_heads(width, head_dim, 0), spread_heads(width, head_dim, heads)
    sums_ref[...] = jnp.zeros_like(sums_ref)
    for copy in copies:
        copy.wait()
    stores = []
    dq_s, dk_s, dv_s = made
    for k in reversed(range(group)):
        whole = slice(k * rows, (k + 1) * rows)
        for y in range(segs):
            ranks = pl.ds(pl.multiple_of((y * group + (me ^ k)) * seg, 16), seg)
            own = slice(k * rows + y * seg, k * rows + (y + 1) * seg)
            inverse = inv_s[ranks, :]
            query = q_s[ranks, :].astype(F32) + ql_s[ranks, :].astype(F32)
            unit = query / temper_ref[...]
            raw = dq_s[ranks, :].astype(F32)
            grad = raw * temper_ref[...]
            grad_query = exact_dot(inverse, spread_q) * (grad - unit * exact_dot(grad * unit, same))
            unit_k = k_s[ranks, :].astype(F32)
            grad = dk_s[ranks, :].astype(F32)
            grad_key = exact_dot(inverse, spread_k) * (
                grad - unit_k * exact_dot(grad * unit_k, same)
            )
            grad_query, grad_value = grad_query.astype(BF), dv_s[ranks, :]
            dqkv_s[own, :width] = grad_query
            dqkv_s[own, width : 2 * width] = grad_key.astype(BF)
            dqkv_s[own, 2 * width :] = grad_value
            for index, values in enumerate((grad_query, grad_value, raw * query)):
                sums_ref[index : index + 1, :] += jnp.sum(
                    values.astype(F32), axis=0, keepdims=True
                )
        sent_s[k] = dot(dqkv_s[whole, :], w_s[...], BY_ROW).astype(BF)
        own = pl.ds(k * rows, rows)
        for source, target in ((sent_s.at[k], sent[k]), (dqkv_s.at[own, :], dqkv_o.at[own, :])):
            stores.append(pltpu.make_async_copy(source, target, out_sems.at[len(stores)]))
            stores[-1].start()
    for copy in stores:
        copy.wait()


def project_kernel(
    parts, ret_ref, wp_ref, pb_ref, x_ref, mod_ref, item_ref, attn_ref, branch_ref, middle_ref, out_ref, made
):
    group, rows, width = ret_ref.shape
    model = x_ref.shape[1]
    sub = width // parts
    for g in range(group):
        for p in range(parts):
            start = (p * group + g) * sub
            attn_ref[:, start : start + sub] = ret_ref[g, :, p * sub : (p + 1) * sub]
    made[...] = dot(attn_ref[...], wp_ref[...]) + pb_ref[...].astype(F32)
    branch_ref[...] = made[...].astype(BF)

    @chunks(rows, 64)
    def _(i):
        r = at(i, 64)
        item = item_ref[r, :]
        middle = x_ref[r, :].astype(F32) + mod_rows(mod_ref, 0, item, model) * made[r, :]
        middle_ref[r, :] = middle
        normed, _ = row_norm(middle)
        scale, shift = mod_rows(mod_ref, 3, item, model), mod_rows(mod_ref, 5, item, model)
        out_ref[r, :] = (normed * (1.0 + scale) + shift).astype(BF)


def add_blocks(terms, outs):
    count = outs[0].shape[0]
    for j in range(terms[0].shape[0]):
        made = sum(term[j].astype(F32) for term in terms).astype(BF)
        outs[j // count][j % count] = made


def weights_kernel(dims, me_ref, *refs):
    segs, head_size = dims
    count = segs * head_size
    tiles, pairs, (w1_ref, w2_ref, bias_ref, bias_s, sems) = refs[:count], refs[count : 2 * count], refs[2 * count :]
    hidden, half = pairs[0].shape
    copies = []

    def copy(source, target):
        copies.append(pltpu.make_async_copy(source, target, sems.at[len(copies)]))
        copies[-1].start()

    for k in range(count):
        own = pl.ds(pl.multiple_of((me_ref[2] ^ (k % head_size)) * hidden, hidden), hidden)
        part = pl.ds(pl.multiple_of((me_ref[1] ^ (k // head_size)) * half, half), half)
        copy(tiles[k].at[pl.ds(0, half), :], w1_ref.at[part, own])
        copy(pairs[k], w2_ref.at[own, part])
        if k < head_size:
            copy(tiles[k].at[pl.ds(half, 16), :], bias_s.at[:, own])
    for started in copies:
        started.wait()
    bias_ref[...] = bias_s[0:1, :].astype(F32)


def feed_kernel(count, *refs):
    w1, w2, b1_ref = refs[:3]
    ins, grads = refs[3 : 3 + count], refs[3 + count : 3 + 2 * count]
    rest = refs[3 + 2 * count :]
    back, outs = rest[:count], rest[count : 2 * count]
    act_ref, gh_ref, sum_ref = rest[2 * count : 2 * count + 3]
    in_s, grad_s, back_s, out_s, act_s, gh_s, pre, grad, in_sems, out_sems = rest[2 * count + 3 :]
    rows = ins[0].shape[0]
    loads, stores = [], []
    for k in range(count):
        pair = (
            pltpu.make_async_copy(ins[k], in_s.at[k], in_sems.at[2 * k]),
            pltpu.make_async_copy(grads[k], grad_s.at[k], in_sems.at[2 * k + 1]),
        )
        pair[0].start()
        pair[1].start()
        loads.append(pair)
    sum_ref[...] = jnp.zeros_like(sum_ref)

    def store(source, target, index):
        stores.append(pltpu.make_async_copy(source, target, out_sems.at[index]))
        stores[-1].start()

    def front(k):
        loads[k][0].wait()
        pre[k % 2] = dot(in_s[k], w1[...]) + b1_ref[...]
        loads[k][1].wait()
        grad[k % 2] = dot(grad_s[k], w2[...], BY_ROW)

    def middle(k):
        total = 0.0
        for start in range(0, rows, 32):
            r = slice(start, start + 32)
            value = pre[k % 2, r, :]
            square = value * value
            gate = jnp.tanh(value * (0.7978845608028654 + 0.035677408136300125 * square))
            half = 0.5 + 0.5 * gate
            act = value * half
            slope = half + act * (1.0 - gate) * (0.7978845608028654 + 0.10703222440890037 * square)
            back_grad = (slope * grad[k % 2, r, :]).astype(BF)
            act_s[k, r, :] = act.astype(BF)
            gh_s[k, r, :] = back_grad
            total = total + jnp.sum(back_grad.astype(F32), axis=0, keepdims=True)
        sum_ref[0:1, :] += total
        own = pl.ds(k * rows, rows)
        store(act_s.at[k], act_ref.at[own, :], 4 * k)
        store(gh_s.at[k], gh_ref.at[own, :], 4 * k + 1)

    def end(k):
        back_s[k] = dot(gh_s[k], w1[...], BY_ROW).astype(BF)
        store(back_s.at[k], back[k], 4 * k + 2)
        out_s[k] = dot(act_s[k], w2[...]).astype(BF)
        store(out_s.at[k], outs[k], 4 * k + 3)

    order = list(reversed(range(count)))
    front(order[0])
    for place, k in enumerate(order):
        if place + 1 < count:
            front(order[place + 1])
        middle(k)
        end(k)
    for started in stores:
        started.wait()


def turned(index, count):
    made = 0
    while count > 1:
        made, index, count = made * 2 + index % 2, index // 2, count // 2
    return made


def feed_weights_kernel(dims, *refs):
    count, group, split, halves, term_count = dims
    me_ref, acts, ghs = refs[0], refs[1 : 1 + halves], refs[1 + halves : 1 + 2 * halves]
    refs = refs[1 + 2 * halves :]
    ins, grads, refs = refs[:count], refs[count : 2 * count], refs[2 * count :]
    terms, refs = refs[:term_count], refs[term_count:]
    outs, sum_o, rest = refs[: 2 * split], refs[2 * split], refs[2 * split + 1 :]
    in_t, grad_t, act_s, gh_s, in_s, grad_s, term_s, sum_s, tile_s, in_sems, out_sems = rest
    rows, model = in_s.shape[1:]

    def load(source, target, index):
        copy = pltpu.make_async_copy(source, target, in_sems.at[index])
        copy.start()
        return copy

    part_rows = act_s.shape[0] // halves
    own = [pl.ds(k * part_rows, part_rows) for k in range(halves)]
    in_loads = [load(ins[k], in_s.at[k], k) for k in range(count)]
    index = count
    gh_loads = [load(ghs[k], gh_s.at[own[k], :], index + k) for k in range(halves)]
    index += halves
    grad_loads = [load(grads[k], grad_s.at[k], index + k) for k in range(count)]
    index += count
    act_loads = [load(acts[k], act_s.at[own[k], :], index + k) for k in range(halves)]
    index += halves
    term_loads = [load(terms[k], term_s.at[k], index + k) for k in range(term_count)]
    for k in range(count):
        in_loads[k].wait()
        in_t[:, k * rows : (k + 1) * rows] = in_s[k].T
    for copy in gh_loads:
        copy.wait()
    stores = []

    def store(source, target):
        stores.append(pltpu.make_async_copy(source, target, out_sems.at[len(stores)]))
        stores[-1].start()

    part = model // split
    fine = part // group
    _, _, head_size, _, _, hidden = tile_s.shape

    def tiles(y, which, left, right):
        start = pl.multiple_of((me_ref[1] ^ y) * part, part) if split > 1 else 0
        for j in range(head_size):
            z = me_ref[2] ^ turned(j, head_size)
            cols = slice(None)
            if split > 1:
                cols = pl.ds(pl.multiple_of(z * hidden, hidden), hidden)
            made = dot(left[pl.ds(start, part), :], right[:, cols]).astype(BF)
            for g in range(group):
                to = (me_ref[0] ^ g) if group > 1 else 0
                tile_s[which, y, j, to] = made[g * fine : (g + 1) * fine, :]
        store(tile_s.at[which, y], outs[which * split + y])

    for y in reversed(range(split)):
        tiles(y, 0, in_t, gh_s)
    for k in range(count):
        grad_loads[k].wait()
        grad_t[:, k * rows : (k + 1) * rows] = grad_s[k].T
    for copy in act_loads:
        copy.wait()
    for y in reversed(range(split)):
        tiles(y, 1, grad_t, act_s)
    for copy in term_loads:
        copy.wait()
    sum_s[...] = sum(term_s[k].astype(F32) for k in range(term_count)).astype(BF)
    store(sum_s, sum_o)
    for copy in stores:
        copy.wait()


def middle_back_kernel(
    dims, middle_ref, branch_ref, up_ref, mod_ref, item_ref, wp_ref, *refs
):
    parts, items, count, chunk = dims
    me_ref, attn_rows_ref = refs[0], refs[1]
    terms, refs = refs[2 : 2 + count], refs[2 + count :]
    out_ref, gb_ref, gm_ref, sums_ref, col_ref = refs[:5]
    proj_refs, (attn, left_t, right) = refs[5:-3], refs[-3:]
    rows, model = middle_ref.shape
    group, _, width = out_ref.shape
    sub = width // parts
    sums_ref[...] = jnp.zeros_like(sums_ref)
    col_ref[...] = jnp.zeros_like(col_ref)

    @chunks(rows, 64)
    def _(i):
        r = at(i, 64)
        item = item_ref[r, :]
        grad_in = sum(term[r, :].astype(F32) for term in terms)
        normed, inverse = row_norm(middle_ref[r, :])
        scale = mod_rows(mod_ref, 3, item, model)
        grad_middle = up_ref[r, :].astype(F32) + norm_back(grad_in * (1.0 + scale), normed, inverse)
        gm_ref[r, :] = grad_middle
        grad_branch = (grad_middle * mod_rows(mod_ref, 0, item, model)).astype(BF)
        gb_ref[r, :] = grad_branch
        col_ref[0:1, :] += jnp.sum(grad_branch.astype(F32), axis=0, keepdims=True)
        add_item_sums(sums_ref, 0, item, grad_middle * branch_ref[r, :].astype(F32), items)
        add_item_sums(sums_ref, 1, item, grad_in * normed, items)
        add_item_sums(sums_ref, 2, item, grad_in, items)

    attn[...] = dot(gb_ref[...], wp_ref[...], BY_ROW).astype(BF)
    for g in range(group):
        for p in range(parts):
            start = (p * group + g) * sub
            out_ref[g, :, p * sub : (p + 1) * sub] = attn[:, start : start + sub]
    proj_weights_kernel(
        (group, chunk), me_ref, attn_rows_ref, gb_ref, *proj_refs, left_t, right
    )


def output_kernel(dims, middle_ref, up_ref, mod_ref, item_ref, bias_ref, *refs):
    items, count, proj_count, tile_count = dims
    terms, refs = refs[:count], refs[count:]
    projs, refs = refs[:proj_count], refs[proj_count:]
    tiles, (out_ref, sums_ref, proj_ref, kept_ref, sent_ref) = refs[:tile_count], refs[tile_count:]
    add_blocks(tiles, (kept_ref, sent_ref))
    proj_ref[...] = sum(proj[...].astype(F32) for proj in projs).astype(BF)
    rows, model = middle_ref.shape
    sums_ref[...] = jnp.zeros_like(sums_ref)

    @chunks(rows, 64)
    def _(i):
        r = at(i, 64)
        item = item_ref[r, :]
        made = sum(term[r, :].astype(F32) for term in terms) + bias_ref[...].astype(F32)
        gamma = mod_rows(mod_ref, 1, item, model)
        out_ref[r, :] = (middle_ref[r, :] + gamma * made).astype(BF)
        add_item_sums(sums_ref, 0, item, up_ref[r, :].astype(F32) * made, items)


def tokens_back_kernel(dims, x_ref, gm_ref, mod_ref, item_ref, *refs):
    items, count = dims
    terms, (out_ref, sums_ref) = refs[:count], refs[count:]
    rows, model = x_ref.shape
    sums_ref[...] = jnp.zeros_like(sums_ref)

    @chunks(rows, 64)
    def _(i):
        r = at(i, 64)
        item = item_ref[r, :]
        grad_in = sum(term[r, :].astype(F32) for term in terms)
        normed, inverse = row_norm(x_ref[r, :].astype(F32))
        scale = mod_rows(mod_ref, 2, item, model)
        out_ref[r, :] = (
            gm_ref[r, :] + norm_back(grad_in * (1.0 + scale), normed, inverse)
        ).astype(BF)
        add_item_sums(sums_ref, 0, item, grad_in * normed, items)
        add_item_sums(sums_ref, 1, item, grad_in, items)


def proj_weights_kernel(dims, me_ref, attn_ref, gb_ref, *refs):
    group, split = dims
    outs, (left_t, right) = refs[:group], refs[group:]
    left_t[...] = attn_ref[...].T
    chunk, head_size, tall, wide = outs[0].shape
    for k in range(group):
        for y in range(chunk):
            part = (me_ref[1] ^ y) if split else y
            start = pl.multiple_of((part * group + (me_ref[0] ^ k)) * wide, wide)
            right[:, y * wide : (y + 1) * wide] = gb_ref[:, pl.ds(start, wide)]
        for j in range(head_size):
            z = (me_ref[2] ^ turned(j, head_size)) if split else j
            made = dot(left_t[pl.ds(pl.multiple_of(z * tall, tall), tall), :], right[...])
            for y in range(chunk):
                outs[k][y, j] = made[:, y * wide : (y + 1) * wide].astype(BF)


def qkv_weights_kernel(dims, me_ref, dqkv_ref, *refs):
    count, chunk, split, proj_count = dims
    ins, refs = refs[:count], refs[count:]
    projs, refs = refs[:proj_count], refs[proj_count:]
    outs, (left_t, right) = refs[:chunk], refs[chunk:]
    rows = ins[0].shape[0]
    for k in range(count):
        left_t[:, k * rows : (k + 1) * rows] = ins[k][...].T
    head_size, _, tall, wide = outs[0].shape
    for y in reversed(range(chunk)):
        part = (me_ref[1] ^ y) if split else y
        for t in range(3):
            start = pl.multiple_of((t * chunk + part) * wide, wide)
            right[:, t * wide : (t + 1) * wide] = dqkv_ref[:, pl.ds(start, wide)]
        for j in range(head_size):
            z = (me_ref[2] ^ turned(j, head_size)) if split else j
            made = dot(left_t[pl.ds(pl.multiple_of(z * tall, tall), tall), :], right[...])
            outs[y][j, 0] = sum(proj[y, j].astype(F32) for proj in projs).astype(BF)
            for t in range(3):
                outs[y][j, 1 + t] = made[:, t * wide : (t + 1) * wide].astype(BF)


def sort_kernel(pack_len, dest_ref, tokens_ref, cot_ref, to_slot_ref, tokens_out, cot_out):
    rows = tokens_ref.shape[0]
    pack = dest_ref[...] // pack_len
    other = jnp.broadcast_to(pack, (8, rows)).astype(F32).T[:, 0:1].astype(jnp.int32)
    this = lax.broadcasted_iota(jnp.int32, (rows, rows), 1)
    that = lax.broadcasted_iota(jnp.int32, (rows, rows), 0)
    before = (other < pack) | ((other == pack) & (that < this))
    slot = jnp.sum(before.astype(jnp.int32), axis=0, keepdims=True)
    to_slot_ref[...] = (slot == that).astype(F32).astype(BF)
    tokens_out[...] = dot(to_slot_ref[...], tokens_ref[...]).astype(BF)
    cot_out[...] = dot(to_slot_ref[...], cot_ref[...]).astype(BF)


def item_blocks_kernel(dims, me_ref, middle_ref, output_ref, tokens_ref, out_ref, joined):
    group, segs, head_size, size = dims
    model = output_ref.shape[1]
    parts = (
        (middle_ref, 0), (output_ref, 0), (tokens_ref, 0),
        (middle_ref, 1), (tokens_ref, 1), (middle_ref, 2),
    )
    for part, (ref, start) in enumerate(parts):
        joined[:, part * model : (part + 1) * model] = ref[:, start * model : (start + 1) * model]
    for g in range(group):
        for y in range(segs):
            for z in range(head_size):
                start = ((y * group + g) * head_size + z) * size
                near = me_ref[2] ^ z
                turn, count = jnp.int32(0), head_size
                while count > 1:
                    turn, near, count = turn * 2 + near % 2, near // 2, count // 2
                block = (me_ref[1] ^ y) * head_size + turn
                rows = pl.ds(pl.multiple_of(block * 8, 8), 8)
                out_ref[me_ref[0] ^ g, rows, 0:size] = joined[:, start : start + size]


def group_sums_kernel(count, bit, kept_ref, came_ref, vector_ref, own_ref, sent_ref, sum_ref):
    rows = kept_ref.shape[1]
    vectors = vector_ref[...] + came_ref[pl.ds(came_ref.shape[0] - 64, 64), :]
    sum_ref[...] = vectors
    last = count == 2
    place = 0
    for k in range(0, count, 2):
        made = kept_ref[k] + came_ref[pl.ds(k // 2 * rows, rows), :]
        if last:
            half = rows // 2
            own_ref[...] = made[:half]
            sent_ref[0:half, :] = made[half:]
        elif k // 2 % 2 == 0:
            own_ref[k // 2] = made
        else:
            own_ref[k // 2] = made
            sent_ref[place * rows : (place + 1) * rows, :] = made
            place += 1
    sent_ref[pl.ds(sent_ref.shape[0] - 64, 64), :] = vectors


def pack_sums_kernel(kept_ref, came_ref, vector_ref, own_ref, *refs):
    blocks, senders = own_ref.shape[0] * (2 if len(refs) == 2 else 1), kept_ref.shape[1]
    vectors = vector_ref[...] + came_ref[pl.ds(came_ref.shape[0] - 64, 64), :]
    refs[-1][...] = vectors
    for c in range(blocks):
        for t in range(2 * senders):
            if t < senders:
                value = kept_ref[c, t]
            else:
                value = came_ref[pl.ds((c * senders + t - senders) * 8, 8), :]
            if len(refs) == 1 or c < blocks // 2:
                own_ref[c, t] = value
            else:
                refs[0][pl.ds(((c - blocks // 2) * 2 * senders + t) * 8, 8), :] = value
    if len(refs) == 2:
        refs[0][pl.ds(refs[0].shape[0] - 64, 64), :] = vectors


def ada_kernel(segs, me_ref, silu_ref, blocks_ref, grad_ref, bias_ref, held):
    for c in range(blocks_ref.shape[0]):
        sender = (me_ref[1] ^ turned(c % segs, segs)) * me_ref[3] + (me_ref[2] ^ c // segs)
        held[pl.ds(pl.multiple_of(sender * 8, 8), 8), :] = blocks_ref[c]
    low = held[:, 0 : grad_ref.shape[1]].astype(BF)
    bias_ref[...] = jnp.broadcast_to(
        jnp.sum(low.astype(F32), axis=0, keepdims=True), bias_ref.shape
    )
    grad_ref[...] = lax.dot_general(
        silu_ref[...], low, (((0,), (0,)), ((), ())), preferred_element_type=F32
    )


def add_kernel(counts, *refs):
    terms, outs = refs[: sum(counts)], refs[sum(counts) :]
    for place, count in enumerate(counts):
        add_blocks(terms[:count], outs[2 * place : 2 * place + 2])
        terms = terms[count:]


def own_tiles_kernel(*refs):
    ups, downs, outs = refs[:2], refs[2:4], refs[4:]
    for i, out in enumerate(outs):
        for which, terms in enumerate((ups, downs)):
            out[which] = sum(term[0, i].astype(F32) for term in terms).astype(BF)


def place_kernel(group, me_ref, *refs):
    blocks, (up_ref, down_ref) = refs[:group], refs[group:]
    hidden = blocks[0].shape[2]
    for i in range(group):
        own = pl.ds(pl.multiple_of((me_ref[0] ^ i) * hidden, hidden), hidden)
        up_ref[:, own] = blocks[i][0].astype(F32)
        down_ref[own, :] = blocks[i][1].astype(F32).T


def vector_parts_kernel(dims, me_ref, qkv_ref, branch_ref, mlp_ref, *refs):
    group, parts, head_size = dims
    hidden_refs, (flat_ref, out_ref) = refs[:-2], refs[-2:]
    sub = qkv_ref.shape[1] // parts
    hidden = hidden_refs[0].shape[1] // head_size
    out_ref[...] = jnp.zeros_like(out_ref)
    for p in range(parts):
        own = pl.ds(pl.multiple_of((p * group + me_ref[0]) * sub, sub), sub)
        for row in range(3):
            out_ref[row : row + 1, own] = qkv_ref[row : row + 1, p * sub : (p + 1) * sub]
    out_ref[3:4, :] = branch_ref[0:1, :]
    out_ref[4:5, :] = mlp_ref[0:1, :]
    if hidden % 128 == 0:
        own = pl.ds(pl.multiple_of(me_ref[0] * hidden, hidden), hidden)
        for z in range(head_size):
            cols = slice(z * hidden, (z + 1) * hidden)
            out_ref[8 + z : 9 + z, own] = sum(ref[0:1, cols] for ref in hidden_refs)
    for c in range(out_ref.shape[1] // 256):
        flat_ref[c * 16 : (c + 1) * 16, :] = out_ref[:, c * 256 : (c + 1) * 256]


def to_packs(rows):
    return lax.all_to_all(rows, ("yy", "head"), split_axis=0, concat_axis=0, tiled=True)


def over_group(blocks):
    return lax.all_to_all(blocks, "g", split_axis=0, concat_axis=0, tiled=True)


def bits(count):
    steps = []
    while count > 1:
        count //= 2
        steps.append(count)
    return steps


def xor_swap(values, axis, step):
    size = lax.axis_size(axis)
    return lax.ppermute(values, axis, [(i, i ^ step) for i in range(size)])


def xor_gather(block, axis):
    blocks = {0: block}
    for step in bits(lax.axis_size(axis)):
        for k in list(blocks):
            blocks[k ^ step] = xor_swap(blocks[k], axis, step)
    return [blocks[k] for k in range(len(blocks))]


def xor_scatter(blocks, axis):
    terms = {k: [block] for k, block in enumerate(blocks)}
    for step in reversed(bits(lax.axis_size(axis))):
        for k in reversed([k for k in terms if k & step]):
            terms[k ^ step].append(xor_swap(add_low(*terms.pop(k)), axis, step))
    return terms[0]


def halves_over_head(values):
    count = lax.axis_size("head")
    step = count // values.shape[0]
    half = values.shape[0] // 2
    return values[:half], xor_swap(values[half:], "head", step)


def add_low(*terms):
    if len(terms) == 1:
        return terms[0]
    return sum(term.astype(F32) for term in terms).astype(terms[0].dtype)


def butterfly(values, axis):
    for step in bits(lax.axis_size(axis)):
        values = values + xor_swap(values, axis, step)
    return values


def pick(values, index, axis):
    return lax.dynamic_index_in_dim(values, index, axis, keepdims=False)


def xor_blocks(values, axis, dim):
    me = lax.axis_index(axis)
    return [pick(values, me ^ k, dim) for k in range(lax.axis_size(axis))]


def tie(*values):
    return lax.optimization_barrier(values)


def tie_groups(*groups):
    tied = list(tie(*[value for group in groups for value in group]))
    return [[tied.pop(0) for _ in group] for group in groups]


def spread_steps(depth, segs, head_size):
    steps = []
    for k in range(segs * head_size):
        if bin(k).count("1") == depth:
            y, z = k // head_size, k % head_size
            step = y & -y if y else z & -z
            steps.append((k, k - step * head_size if y else k - step, "yy" if y else "head", step))
    return sorted(steps, key=lambda made: made[2])


def shards(
    tokens,
    cotangent,
    class_table,
    ada_weight,
    ada_bias,
    qkv_weight,
    q_bias,
    v_bias,
    log_scale,
    proj_weight,
    proj_bias,
    fc1_weight,
    fc1_bias,
    fc2_weight,
    fc2_bias,
    item_lens,
    class_ids,
    section_ids,
    destination,
):
    segs = lax.axis_size("yy")
    group = lax.axis_size("g")
    head_size = lax.axis_size("head")
    yy, g, z = lax.axis_index("yy"), lax.axis_index("g"), lax.axis_index("head")
    me = jnp.stack([g, yy, z, jnp.int32(head_size)]).astype(jnp.int32)
    pack = yy * head_size + z
    rows, model = tokens.shape
    heads_all = log_scale.shape[0]
    head_dim = model // heads_all
    heads = heads_all // group
    width = model // group
    dp_size = segs * group
    pack_len = rows * head_size
    seg = rows // segs
    items = item_lens.shape[1]
    block = min(256, pack_len)
    col = model // dp_size
    parts = segs if col % 128 == 0 else 1
    sub = width // parts

    def own_cols(values):
        return pick(values.reshape(parts, group, sub), g, 1).reshape(1, width)

    rows_bf, rows_f32 = shape_of((rows, model), BF), shape_of((rows, model), F32)
    to_slot, sorted_tokens, sorted_cotangent = call(
        "sort",
        functools.partial(sort_kernel, pack_len),
        (destination[None, :], tokens, cotangent),
        (VMEM, HBM, HBM),
        (shape_of((rows, rows), BF), rows_bf, rows_bf),
    )
    inputs = to_packs(sorted_tokens)

    hidden = fc1_weight.shape[1] // group
    units = head_size * hidden
    half = model // segs
    fc1_own = lax.dynamic_slice(fc1_weight, (yy * half, g * hidden), (half, hidden))
    fc1_bias_own = lax.dynamic_slice(fc1_bias, (g * hidden,), (hidden,))
    fc2_own = lax.dynamic_slice(fc2_weight, (g * hidden, yy * half), (hidden, half))
    fc1_own = jnp.concatenate(
        [fc1_own, jnp.broadcast_to(fc1_bias_own[None, :], (16, hidden))], axis=0
    )
    tiled = hidden % 128 == 0
    tile_count = segs * head_size

    fc1_tiles, fc2_tiles = {0: fc1_own}, {0: fc2_own}

    def next_hop(tiles, depth):
        for k, source, axis, step in spread_steps(depth, segs, head_size):
            tiles[k] = xor_swap(tiles[source], axis, step)

    def with_tiles(values):
        first, second = sorted(fc1_tiles), sorted(fc2_tiles)
        values, held, held_too = tie_groups(
            values, [fc1_tiles[k] for k in first], [fc2_tiles[k] for k in second]
        )
        fc1_tiles.update(zip(first, held))
        fc2_tiles.update(zip(second, held_too))
        return values

    lens_here = pick(item_lens, pack, 0)
    class_here = pick(class_ids, pack, 0)
    order_key = class_here * items + jnp.arange(items, dtype=jnp.int32)
    item_rank = jnp.sum(
        jnp.where(order_key[None, :] < order_key[:, None], lens_here[None, :], 0), axis=1
    )
    item_pos = jnp.cumsum(lens_here) - lens_here
    item_end = item_rank + lens_here

    def items_of(rank):
        return (rank[:, None] >= item_rank[None, :]) & (rank[:, None] < item_end[None, :])

    rank_all = jnp.arange(pack_len, dtype=jnp.int32)
    member = items_of(rank_all)

    def of_item(values):
        return jnp.sum(jnp.where(member, values[None, :], 0), axis=1)

    section_here = lax.ppermute(
        section_ids[0],
        ("g", "head"),
        [(a * head_size + b, b * head_size + a) for a in range(group) for b in range(head_size)],
    )
    position = rank_all - of_item(item_rank - item_pos)
    section_rank = jnp.sum(
        jnp.where(rank_all[None, :] == position[:, None], section_here[None, :], 0), axis=1
    )
    up_to = jnp.sum((section_here[None, :] <= section_rank[:, None]).astype(jnp.int32), axis=1)
    low = of_item(item_rank)
    high = jnp.minimum(up_to + of_item(item_rank - item_pos), of_item(item_end))
    first = low[::block] // block
    last = (high[block - 1 :: block] + block - 1) // block
    low, high = low[None, :], high[None, :]

    row_rank = (
        (jnp.arange(segs, dtype=jnp.int32)[:, None] * group + g) * seg
        + jnp.arange(seg, dtype=jnp.int32)[None, :]
    ).reshape(rows)
    row_item = jnp.sum(
        jnp.where(items_of(row_rank), jnp.arange(items, dtype=jnp.int32)[None, :], 0), axis=1
    )[:, None]

    class_rows = jnp.take(class_table, class_ids.reshape(-1), axis=0).astype(F32)
    silu_cond = jax.nn.silu(class_rows).astype(BF)
    silu_here = lax.dynamic_slice_in_dim(silu_cond, pack * items, items, 0)
    mod = jnp.dot(silu_here, ada_weight, preferred_element_type=F32) + ada_bias.astype(F32)

    inputs, first, last, low, high = tie(inputs, first, last, low, high)
    (attn_in,) = call(
        "first_norm",
        first_norm_kernel, (inputs, mod, row_item), (HBM, VMEM, VMEM), (shape_of((rows, model), BF),)
    )
    def near_blocks(own):
        blocks = {0: own}
        for step in bits(group)[1:]:
            for k in list(blocks):
                blocks[k ^ step] = xor_swap(blocks[k], "g", step)
        return [blocks[k] for k in range(len(blocks))]

    near = group // 2

    (attn_in,) = with_tiles([attn_in])
    next_hop(fc1_tiles, 1)
    attn_blocks = near_blocks(attn_in)
    (attn_far,) = with_tiles([xor_swap(attn_in, "g", near)])
    next_hop(fc1_tiles, 2)
    next_hop(fc2_tiles, 1)
    attn_blocks += near_blocks(attn_far)
    per_part = sub // head_dim
    scale_here = pick(log_scale.reshape(parts, group, per_part), g, 1).reshape(heads)
    temper = jnp.repeat(jnp.exp(scale_here), head_dim)[None, :]
    wide = shape_of((pack_len, width), BF)
    tall = shape_of((width, pack_len), F32)
    sorted_cotangent, _ = tie(sorted_cotangent, inputs)
    upstream = to_packs(sorted_cotangent)
    held_bf = pltpu.VMEM((pack_len, width), BF)
    out_blocks, out_t, lse, queries, queries_low, keys, values, inverses = call(
        "attend",
        functools.partial(attend_kernel, (group, segs, head_dim, parts, block)),
        (me, first, last, low, high, temper, own_cols(q_bias).astype(F32),
         own_cols(v_bias).astype(F32), qkv_weight, *attn_blocks),
        (SMEM,) * 3 + (VMEM,) * 5 + (ANY,) * (1 + group),
        (shape_of((group, rows, width), BF), tall, shape_of((8, pack_len), F32), wide, wide, wide,
         wide, shape_of((pack_len, 128), F32)),
        [
            pltpu.VMEM((model, 3 * width), BF),
            pltpu.VMEM((group, rows, model), BF),
            held_bf,
            held_bf,
            held_bf,
            held_bf,
            pltpu.VMEM((pack_len, 128), F32),
            pltpu.VMEM((width, pack_len), BF),
            pltpu.VMEM((width, pack_len), F32),
            held_bf,
            pltpu.VMEM((width, block), F32),
            pltpu.VMEM((8, block), F32),
            pltpu.SemaphoreType.DMA((3 * parts,)),
            pltpu.SemaphoreType.DMA((group,)),
            pltpu.SemaphoreType.DMA((6 + segs * group,)),
        ],
        out_specs=(ANY, ANY, VMEM, ANY, ANY, ANY, ANY, ANY),
    )
    (out_blocks,) = with_tiles([out_blocks])
    next_hop(fc1_tiles, 3)
    next_hop(fc2_tiles, 2)
    returned = over_group(out_blocks)
    upstream, _ = tie(upstream, out_blocks)
    grad_mlp, grad_mlp_sum = call(
        "grad_mlp",
        grad_mlp_kernel,
        (upstream, mod, row_item),
        (HBM, VMEM, VMEM),
        (rows_bf, shape_of((8, model), F32)),
    )
    grad_far = xor_swap(grad_mlp, "g", near)
    grad_blocks = near_blocks(grad_mlp)
    attn_rows, branch, middle, mlp_in = call(
        "project",
        functools.partial(project_kernel, parts),
        (returned, proj_weight, proj_bias[None, :], inputs, mod, row_item),
        (HBM, HBM, VMEM, HBM, VMEM, VMEM),
        (rows_bf, rows_bf, rows_f32, rows_bf),
        [pltpu.VMEM((rows, model), F32)],
    )

    (middle,) = with_tiles([middle])
    for depth in range(4, tile_count.bit_length()):
        next_hop(fc1_tiles, depth)
    for depth in range(3, tile_count.bit_length()):
        next_hop(fc2_tiles, depth)
    if tiled:
        fc1_here, fc2_here, fc1_bias_here = call(
            "weights",
            functools.partial(weights_kernel, (segs, head_size)),
            (me, *[fc1_tiles[k] for k in range(tile_count)], *[fc2_tiles[k] for k in range(tile_count)]),
            (SMEM,) + (ANY,) * (2 * tile_count),
            (shape_of((model, units), BF), shape_of((units, model), BF), shape_of((1, units), F32)),
            [
                pltpu.VMEM((16, units), BF),
                pltpu.SemaphoreType.DMA((2 * tile_count + head_size,)),
            ],
            out_specs=(VMEM,) * 3,
        )
    else:
        def placed(tiles):
            held = jnp.stack([tiles[k] for k in range(tile_count)])
            held = held.reshape(segs, head_size, *held.shape[1:])
            return held[jnp.arange(segs) ^ yy][:, jnp.arange(head_size) ^ z]

        fc1_all, fc2_all = placed(fc1_tiles), placed(fc2_tiles)
        fc1_here = fc1_all[:, :, :half].transpose(0, 2, 1, 3).reshape(model, units)
        fc1_bias_here = fc1_all[0, :, half].reshape(1, units).astype(F32)
        fc2_here = fc2_all.transpose(1, 2, 0, 3).reshape(units, model)

    mlp_blocks = near_blocks(mlp_in)
    mlp_far = xor_swap(mlp_in, "g", near)
    grad_blocks += near_blocks(tie(grad_far, mlp_in, fc1_here)[0])
    back_parts, out_parts, acts, ghs, hidden_sums = [], [], [], [], []
    for start in (0, near):
        if start:
            mlp_blocks += near_blocks(tie(mlp_far, acts[0])[0])
        made = call(
            "feed",
            functools.partial(feed_kernel, near),
            (fc1_here, fc2_here, fc1_bias_here, *mlp_blocks[start : start + near],
             *grad_blocks[start : start + near]),
            (VMEM,) * 3 + (ANY,) * (2 * near),
            (rows_bf,) * (2 * near)
            + (shape_of((near * rows, units), BF),) * 2
            + (shape_of((8, units), F32),),
            [pltpu.VMEM((near, rows, model), BF)] * 4
            + [pltpu.VMEM((near, rows, units), BF)] * 2
            + [pltpu.VMEM((2, rows, units), F32)] * 2
            + [pltpu.SemaphoreType.DMA((2 * near,)), pltpu.SemaphoreType.DMA((4 * near,))],
            out_specs=(ANY,) * (2 * near + 2) + (VMEM,),
        )
        back_parts += made[:near]
        out_parts += made[near : 2 * near]
        acts.append(made[2 * near])
        ghs.append(made[2 * near + 1])
        hidden_sums.append(made[2 * near + 2])
    far_terms = {k: back_parts[k] for k in range(near, group)}
    for step in reversed(bits(group)[1:]):
        for k in reversed([k for k in far_terms if k & step]):
            came = xor_swap(far_terms.pop(k), "g", step)
            far_terms[k ^ step] = add_low(far_terms[k ^ step], came)
    far_sum = far_terms[near]
    back_parts = list(tie(*back_parts[:near], far_sum)[:near])
    in_terms = {k: [back_parts[k]] for k in range(near)}
    for step in reversed(bits(group)[1:]):
        for k in reversed([k for k in in_terms if k & step]):
            in_terms[k ^ step].append(xor_swap(add_low(*in_terms.pop(k)), "g", step))
    in_terms = in_terms[0] + [xor_swap(far_sum, "g", near)]
    acts[0], _ = tie(acts[0], far_sum)
    split = segs if tiled else 1

    def to_last(blocks):
        terms = {k: [block] for k, block in enumerate(blocks)}
        for step in reversed(bits(group)[1:]):
            for k in reversed([k for k in terms if k & step]):
                terms[k ^ step].append(xor_swap(add_low(*terms.pop(k)), "g", step))
        return terms[0], terms[near]

    out_terms, out_last = to_last(tie(*out_parts, far_sum)[:group])
    if tiled:
        fine = half // group
        tile_shape = (head_size, group, fine, hidden)
        feed_dims = (group, group, segs, 2, len(out_last))
    else:
        tile_shape = (1, 1, model, units)
        feed_dims = (group, 1, 1, 2, len(out_last))
    made = call(
        "feed_weights",
        functools.partial(feed_weights_kernel, feed_dims),
        (me, *acts, *ghs, *mlp_blocks, *grad_blocks, *out_last),
        (SMEM,) + (ANY,) * (4 + 2 * group + len(out_last)),
        (shape_of(tile_shape, BF),) * (2 * split) + (rows_bf,),
        [
            pltpu.VMEM((model, pack_len), BF),
            pltpu.VMEM((model, pack_len), BF),
            pltpu.VMEM((pack_len, units), BF),
            pltpu.VMEM((pack_len, units), BF),
            pltpu.VMEM((group, rows, model), BF),
            pltpu.VMEM((group, rows, model), BF),
            pltpu.VMEM((len(out_last), rows, model), BF),
            pltpu.VMEM((rows, model), BF),
            pltpu.VMEM((2, split, *tile_shape), BF),
            pltpu.SemaphoreType.DMA((4 + 2 * group + len(out_last),)),
            pltpu.SemaphoreType.DMA((2 * split + 1,)),
        ],
        out_specs=(ANY,) * (2 * split + 1),
    )
    up_parts, down_parts, out_sent = made[:split], made[split : 2 * split], made[2 * split]
    out_terms.append(xor_swap(out_sent, "g", near))
    if not tiled:
        fine = half // group
        order = jnp.array([turned(j, head_size) for j in range(head_size)]) ^ z
        near_g = jnp.arange(group) ^ g
        near_y = jnp.arange(segs) ^ yy

        def in_blocks(full):
            full = full.reshape(segs, group, fine, head_size, hidden).transpose(0, 3, 1, 2, 4)
            return list(full[near_y][:, order][:, :, near_g])

        up_parts, down_parts = in_blocks(up_parts[0]), in_blocks(down_parts[0])

    middle_in, _ = tie(middle, up_parts[0])
    outbound, _, grad_middle, middle_sums, branch_sum, *proj_parts = call(
        "middle_back",
        functools.partial(
            middle_back_kernel, (parts, items, len(in_terms), parts == segs)
        ),
        (middle_in, branch, upstream, mod, row_item, proj_weight, me, attn_rows, *in_terms),
        (HBM, HBM, HBM, VMEM, VMEM, HBM, SMEM) + (HBM,) * (1 + len(in_terms)),
        (shape_of((group, rows, width), BF), rows_bf, rows_f32, shape_of((8, 3 * model), F32),
         shape_of((8, model), F32))
        + (shape_of((parts, head_size, model // head_size, sub), BF),) * group,
        [
            pltpu.VMEM((rows, model), BF),
            pltpu.VMEM((model, rows), BF),
            pltpu.VMEM((rows, width), BF),
        ],
    )
    inbound = over_group(outbound)
    up_terms, down_terms = xor_scatter(up_parts, "yy"), xor_scatter(down_parts, "yy")
    proj_terms, proj_last = to_last(proj_parts)
    tied = tuple(out_terms) + tuple(proj_last) + tuple(up_terms)
    half_tiles = shape_of((head_size // 2, group, fine, hidden), BF)
    quarter_tiles = shape_of((head_size // 4, group, fine, hidden), BF)
    output_rows, output_sums, proj_sent, up_kept, up_sent = call(
        "output",
        functools.partial(
            output_kernel, (items, len(out_terms), len(proj_last), len(up_terms))
        ),
        (middle, upstream, mod, row_item, fc2_bias[None, :], *tied),
        (HBM, HBM, VMEM, VMEM, VMEM) + (HBM,) * len(tied),
        (rows_bf, shape_of((8, model), F32), shape_of(proj_last[0].shape, BF), half_tiles, half_tiles),
    )
    up_terms = (up_kept, xor_swap(up_sent, "head", 1))
    inbound, output_rows = tie(inbound, output_rows)
    output_back = to_packs(output_rows)
    proj_terms.append(xor_swap(proj_sent, "g", near))
    cols_f32 = pltpu.VMEM((pack_len, 128), F32)
    held_f32 = pltpu.VMEM((pack_len, width), F32)
    made = call(
        "attend_back",
        functools.partial(attend_back_kernel, (group, segs, head_dim, parts, block)),
        (me, temper, qkv_weight, inverses, queries_low, first, last, low, high, lse, inbound, queries,
         keys, values, out_t),
        (SMEM, VMEM, ANY, ANY, ANY, SMEM, SMEM, VMEM, VMEM, VMEM) + (ANY,) * 5,
        (rows_bf,) * group + (shape_of((pack_len, 3 * width), BF), shape_of((8, width), F32)),
        [
            held_bf,
            held_bf,
            held_bf,
            pltpu.VMEM((width, pack_len), F32),
            held_bf,
            pltpu.VMEM((width, pack_len), BF),
            held_f32,
            held_f32,
            pltpu.VMEM((width, block), F32),
            pltpu.VMEM((8, block), F32),
            held_bf,
            held_bf,
            held_bf,
            pltpu.VMEM((model, 3 * width), BF),
            cols_f32,
            held_bf,
            pltpu.VMEM((pack_len, 3 * width), BF),
            pltpu.VMEM((group, rows, model), BF),
            pltpu.SemaphoreType.DMA((6 + segs * group,)),
            pltpu.SemaphoreType.DMA((3 * parts,)),
            pltpu.SemaphoreType.DMA((2 * group,)),
        ],
        out_specs=(ANY,) * (group + 1) + (VMEM,),
    )
    made, down_terms, up_terms, proj_terms, (output_back,) = tie_groups(
        made, down_terms, up_terms, proj_terms, (output_back,)
    )
    grad_qkv, qkv_sums = made[group:]

    (vectors,) = call(
        "vector_parts",
        functools.partial(vector_parts_kernel, (group, parts, head_size)),
        (me, qkv_sums, branch_sum, grad_mlp_sum, *hidden_sums),
        (SMEM,) + (VMEM,) * (3 + len(hidden_sums)),
        (shape_of((64, 256), F32),),
        [pltpu.VMEM((16, model), F32)],
    )
    if not tiled:
        hidden_row = (hidden_sums[0] + hidden_sums[1])[0].reshape(head_size, hidden)
        hidden_row = lax.dynamic_update_slice(
            jnp.zeros((16, model), F32), hidden_row, (8, g * hidden)
        )
        vectors = vectors + hidden_row.reshape(16, 4, 256).transpose(1, 0, 2).reshape(64, 256)

    in_terms, last_terms = to_last(made[:group])
    sent = add_low(*last_terms)
    in_terms.append(xor_swap(sent, "g", near))
    tied = tie(*down_terms, *up_terms, sent)[:-1]
    down_kept, down_sent, up_kept, up_sent = call(
        "add",
        functools.partial(add_kernel, (len(down_terms), 2)),
        tied,
        (HBM,) * len(tied),
        (half_tiles, half_tiles, quarter_tiles, quarter_tiles),
    )
    down_terms = (down_kept, xor_swap(down_sent, "head", 1))
    up_terms = (up_kept, xor_swap(up_sent, "head", 2))
    grad_qkv, _ = tie(grad_qkv, down_sent)
    qkv_parts = call(
        "qkv_weights",
        functools.partial(
            qkv_weights_kernel, (group, parts, parts == segs, len(proj_terms))
        ),
        (me, grad_qkv, *attn_blocks, *proj_terms),
        (SMEM,) + (HBM,) * (1 + group + len(proj_terms)),
        (shape_of((head_size, 4, model // head_size, sub), BF),) * parts,
        [pltpu.VMEM((model, pack_len), BF), pltpu.VMEM((pack_len, 3 * sub), BF)],
    )
    down_terms, up_terms, _ = tie_groups(down_terms, up_terms, qkv_parts)
    down_kept, down_sent = call(
        "add", functools.partial(add_kernel, (2,)), down_terms, (HBM,) * 2, (quarter_tiles,) * 2
    )
    down_terms = (down_kept, xor_swap(down_sent, "head", 2))
    inputs_back, _ = tie(inputs, down_sent)
    tokens_grad_rows, tokens_sums = call(
        "tokens_back",
        functools.partial(tokens_back_kernel, (items, len(in_terms))),
        (inputs_back, grad_middle, mod, row_item, *in_terms),
        (HBM, HBM, VMEM, VMEM) + (HBM,) * len(in_terms),
        (rows_bf, shape_of((8, 2 * model), F32)),
    )

    tokens_grad_rows, *down_terms = tie(tokens_grad_rows, *down_terms)

    def to_data(values):
        return dot(to_slot, values, ((0,), (0,)))

    output = to_data(output_back).astype(BF)
    tokens_came = to_packs(tokens_grad_rows)

    ada_cols = 6 * model // (dp_size * head_size)
    packs = segs * head_size
    (kept,) = call(
        "item_blocks",
        functools.partial(item_blocks_kernel, (group, segs, head_size, ada_cols)),
        (me, middle_sums, output_sums, tokens_sums),
        (SMEM, VMEM, VMEM, VMEM),
        (shape_of((group, packs * 8, 256), F32),),
        [pltpu.VMEM((8, 6 * model), F32)],
        out_specs=(VMEM,),
    )
    sent = jnp.concatenate([kept[k] for k in range(1, group, 2)] + [vectors], axis=0)
    count = group
    for step in reversed(bits(group)):
        came = xor_swap(sent, "g", step)
        left = count // 2
        own = (left, packs * 8, 256) if left > 1 else (packs * 4, 256)
        rows_sent = (left // 2 * packs * 8 if left > 1 else packs * 4) + 64
        kept, sent, vectors = call(
            "group_sums",
            functools.partial(group_sums_kernel, count, step),
            (kept, came, vectors),
            (VMEM,) * 3,
            (shape_of(own, F32), shape_of((rows_sent, 256), F32), shape_of((64, 256), F32)),
            out_specs=(VMEM,) * 3,
        )
        count = left
    kept = kept.reshape(packs // 2, 1, 8, 256)
    tokens_sent = sent
    def over_head(terms):
        while terms[0].shape[0] > 1:
            terms = halves_over_head(add_low(*terms))
        return terms

    down_terms = tie(*down_terms, *up_terms, tokens_grad_rows)[:-1]
    down_terms, up_terms = down_terms[:2], down_terms[2:]
    tied = tuple(over_head(up_terms)) + tuple(over_head(down_terms))
    own_tiles = call(
        "own_tiles",
        own_tiles_kernel,
        tied,
        (HBM,) * 4,
        (shape_of((2, fine, hidden), BF),) * group,
    )
    both_all = [own_tiles[0]]
    for i in range(1, group):
        both_all.append(lax.ppermute(own_tiles[i], "g", [(k, k ^ i) for k in range(group)]))
    if parts == segs:
        terms = tie(*xor_scatter(qkv_parts, "yy"), tokens_sent)[:-1]
        terms = halves_over_head(add_low(*terms))
        terms, both_all, (tokens_came,) = tie_groups(terms, both_all, (tokens_came,))
        terms = over_head(terms)
        summed = sum(term[0].astype(F32) for term in terms)
        proj_part, qkv_part = summed[0], summed[1:]
    else:
        both = qkv_parts[0].transpose(1, 0, 2, 3).reshape(4, model, width)
        full = lax.dynamic_update_slice(
            jnp.zeros((4, model, model), BF), both, (0, 0, g * width)
        )
        summed = lax.psum_scatter(full, ("yy", "g"), scatter_dimension=2, tiled=True)
        summed = lax.psum_scatter(summed, "head", scatter_dimension=1, tiled=True).astype(F32)
        proj_part, qkv_part = summed[0], summed[1:]

    if tiled:
        up_part, down_part = call(
            "place",
            functools.partial(place_kernel, group),
            (me, *both_all),
            (SMEM,) + (HBM,) * group,
            (shape_of((fine, group * hidden), F32), shape_of((group * hidden, fine), F32)),
        )
    else:
        placed = jnp.stack(both_all)[jnp.arange(group) ^ g].astype(F32)
        up_part = placed[:, 0].transpose(1, 0, 2).reshape(fine, group * hidden)
        down_part = placed[:, 1].transpose(0, 2, 1).reshape(group * hidden, fine)


    sent, _ = tie(sent, tokens_came)
    tokens_grad = to_data(tokens_came)
    steps = [("yy", step) for step in bits(segs)] + [("head", step) for step in reversed(bits(head_size))]
    for place, (axis, step) in enumerate(steps):
        came = xor_swap(sent, axis, step)
        blocks, senders = kept.shape[0], kept.shape[1]
        end = place + 1 == len(steps)
        own = (blocks if end else blocks // 2, 2 * senders, 8, 256)
        outs = [shape_of(own, F32)]
        if not end:
            outs.append(shape_of((blocks // 2 * 2 * senders * 8 + 64, 256), F32))
        outs.append(shape_of((64, 256), F32))
        made = call(
            "pack_sums", pack_sums_kernel, (kept, came, vectors), (VMEM,) * 3, outs,
            out_specs=(VMEM,) * len(outs),
        )
        kept, vectors = made[0], made[-1]
        sent = made[1] if not end else None
    item_came = kept[0]
    vectors = vectors.reshape(4, 16, 256).transpose(1, 0, 2).reshape(16, model)
    silu_rows = jnp.pad(silu_cond.reshape(packs, items, model), ((0, 0), (0, 8 - items), (0, 0)))
    ada_grad, ada_bias_grad = call(
        "ada",
        functools.partial(ada_kernel, segs),
        (me, silu_rows.reshape(packs * 8, model), item_came),
        (SMEM, VMEM, VMEM),
        (shape_of((model, ada_cols), F32), shape_of((8, ada_cols), F32)),
        [pltpu.VMEM((packs * 8, 256), F32)],
    )
    ada_bias_grad = ada_bias_grad[0]

    log_scale_grad = jnp.sum(vectors[2].reshape(heads_all, head_dim), axis=1)
    fc1_bias_grad = pick(vectors, 8 + z, 0)[: group * hidden]
    return (
        output,
        tokens_grad,
        ada_grad,
        ada_bias_grad,
        qkv_part,
        vectors[0],
        vectors[1],
        log_scale_grad,
        proj_part,
        vectors[3],
        up_part,
        fc1_bias_grad,
        down_part,
        vectors[4],
    )


def solution(mesh):
    head_size = mesh.shape["head"]
    dp_size = mesh.shape["dp"]
    inner = Mesh(
        mesh.devices.reshape(dp_size // head_size, head_size, head_size), ("yy", "g", "head")
    )
    dp = ("yy", "g")
    everything = ("yy", "g", "head")
    in_specs = (
        P(everything, None),
        P(everything, None),
        P(),
        P(),
        P(),
        P(),
        P(),
        P(),
        P(),
        P(),
        P(),
        P(None, "head"),
        P("head"),
        P("head", None),
        P(),
        P(),
        P(),
        P(dp, None),
        P(everything),
    )
    out_specs = (
        P(everything, None),
        P(everything, None),
        P(None, everything),
        P(everything),
        P(None, "head", dp),
        P(),
        P(),
        P(),
        P("head", dp),
        P(),
        P(dp, "head"),
        P("head"),
        P("head", dp),
        P(),
    )
    return jax.shard_map(
        shards, mesh=inner, in_specs=in_specs, out_specs=out_specs, check_vma=False
    )
```

```python
import functools

import jax
import jax.numpy as jnp
from jax import lax
from jax.experimental import pallas as pl
from jax.experimental.pallas import tpu as pltpu
from jax.sharding import Mesh, PartitionSpec as P

BF = jnp.bfloat16
F32 = jnp.float32
SMEM = pl.BlockSpec(memory_space=pltpu.SMEM)
VMEM = pl.BlockSpec(memory_space=pltpu.VMEM)
ANY = pl.BlockSpec(memory_space=pl.ANY)
HBM = "hbm"
LIMIT = 40
LIMITS = {"attend": 57, "attend_back": 57, "sort": 57, "middle_back": 50, "output": 50, "feed": 50, "feed_weights": 57, "weights": 57, "qkv_weights": 57}
FLOPS, BYTES = 1_000_000_000, 3_000_000
TIMES = {
    "sort": 2, "first_norm": 2, "grad_mlp": 2, "attend": 26, "project": 0, "weights": 4, "feed": 12,
    "feed_weights": 12, "middle_back": 7, "proj_weights": 3, "output": 3, "attend_back": 34, "add": 3,
    "qkv_weights": 8, "tokens_back": 5,
}
PLAIN = ((1,), (0,))
BY_ROW = ((1,), (1,))


def shape_of(shape, dtype):
    return jax.ShapeDtypeStruct(shape, dtype)


def dot(left, right, dims=PLAIN):
    return lax.dot_general(left, right, (dims, ((), ())), preferred_element_type=F32)


def call(name, kernel, operands, specs, outs, scratch=(), limit=LIMIT, out_specs=None, late=None):
    out_specs = out_specs or tuple(HBM if o.size >= 65536 else VMEM for o in outs)
    n_in, n_out, n_scratch = len(specs), len(outs), len(scratch)
    staged_in = [i for i, spec in enumerate(specs) if spec is HBM]
    staged_out = [i for i, spec in enumerate(out_specs) if spec is HBM]
    staged = [pltpu.VMEM(operands[i].shape, operands[i].dtype) for i in staged_in]
    staged += [pltpu.VMEM(outs[i].shape, outs[i].dtype) for i in staged_out]
    sems = [pltpu.SemaphoreType.DMA((len(staged),))] if staged else []

    def body(*refs):
        given, made = list(refs[:n_in]), list(refs[n_in : n_in + n_out])
        own = refs[n_in + n_out : n_in + n_out + n_scratch]
        held = refs[n_in + n_out + n_scratch :]
        copies = []
        for place, i in enumerate(staged_in):
            copies.append(pltpu.make_async_copy(given[i], held[place], held[-1].at[place]))
            copies[-1].start()
            given[i] = held[place]
        backs = []
        for place, i in enumerate(staged_out, len(staged_in)):
            backs.append(pltpu.make_async_copy(held[place], made[i], held[-1].at[place]))
            made[i] = held[place]
        last = [copy for copy, i in zip(copies, staged_in) if i in (late or ())]
        for copy, i in zip(copies, staged_in):
            if i not in (late or ()):
                copy.wait()
        sent = []

        def wait_late():
            for copy in last:
                copy.wait()

        def send(i):
            backs[staged_out.index(i)].start()
            sent.append(staged_out.index(i))

        if late:
            kernel(*given, *made, *own, wait_late=wait_late, send=send)
        else:
            kernel(*given, *made, *own)
        for place, copy in enumerate(backs):
            if place not in sent:
                copy.start()
        for copy in backs:
            copy.wait()

    limit = LIMITS.get(name, limit)
    return pl.pallas_call(
        body,
        name=name,
        out_shape=tuple(outs),
        in_specs=[ANY if spec is HBM else spec for spec in specs],
        out_specs=tuple(ANY if spec is HBM else spec for spec in out_specs),
        scratch_shapes=list(scratch) + staged + sems,
        compiler_params=pltpu.CompilerParams(vmem_limit_bytes=limit * 1024 * 1024),
        cost_estimate=pl.CostEstimate(
            flops=TIMES.get(name, 1) * FLOPS + 1, bytes_accessed=TIMES.get(name, 1) * BYTES + 1, transcendentals=0
        ),
    )(*operands)


def row_norm(values):
    centre = values - jnp.mean(values, axis=-1, keepdims=True)
    inverse = lax.rsqrt(jnp.mean(centre * centre, axis=-1, keepdims=True) + 1e-06)
    return (centre * inverse, inverse)


def norm_back(gradient, normed, inverse):
    return inverse * (
        gradient
        - jnp.mean(gradient, axis=-1, keepdims=True)
        - normed * jnp.mean(gradient * normed, axis=-1, keepdims=True)
    )


def mod_rows(mod_ref, part, item, width):
    cols = slice(part * width, (part + 1) * width)
    rows = jnp.broadcast_to(mod_ref[0:1, cols], (item.shape[0], width))
    for index in range(1, mod_ref.shape[0]):
        rows = jnp.where(item == index, mod_ref[index : index + 1, cols], rows)
    return rows


def add_item_sums(sums_ref, part, item, values, count):
    width = values.shape[1]
    cols = slice(part * width, (part + 1) * width)
    for index in range(count):
        kept = jnp.where(item == index, values, 0.0)
        sums_ref[index : index + 1, cols] += jnp.sum(kept, axis=0, keepdims=True)


def same_head(width, head_dim):
    row = lax.broadcasted_iota(jnp.int32, (width, width), 0) // head_dim
    col = lax.broadcasted_iota(jnp.int32, (width, width), 1) // head_dim
    return (row == col).astype(BF)


def chunks(rows, size):
    return pl.loop(0, rows // size)


def at(index, size):
    return pl.ds(pl.multiple_of(index * size, size), size)


def first_norm_kernel(x_ref, mod_ref, item_ref, out_ref):
    rows, width = x_ref.shape

    @chunks(rows, 64)
    def _(i):
        r = at(i, 64)
        item = item_ref[r, :]
        normed, _ = row_norm(x_ref[r, :].astype(F32))
        scale, shift = mod_rows(mod_ref, 2, item, width), mod_rows(mod_ref, 4, item, width)
        out_ref[r, :] = (normed * (1.0 + scale) + shift).astype(BF)


def grad_mlp_kernel(up_ref, mod_ref, item_ref, out_ref, sum_ref):
    rows, width = up_ref.shape
    sum_ref[...] = jnp.zeros_like(sum_ref)

    @chunks(rows, 64)
    def _(i):
        r = at(i, 64)
        gamma = mod_rows(mod_ref, 1, item_ref[r, :], width)
        grad = (up_ref[r, :].astype(F32) * gamma).astype(BF)
        out_ref[r, :] = grad
        sum_ref[0:1, :] += jnp.sum(grad.astype(F32), axis=0, keepdims=True)


def load_columns(weight_ref, held, sems, offset_of, parts, sub):
    copies = []
    for t in range(3):
        for p in range(parts):
            copies.append(
                pltpu.make_async_copy(
                    weight_ref.at[t, :, pl.ds(pl.multiple_of(offset_of(p), sub), sub)],
                    held.at[:, pl.ds((t * parts + p) * sub, sub)],
                    sems.at[t * parts + p],
                )
            )
    for copy in copies:
        copy.start()
    return copies


def pick_heads(width, head_dim, first):
    row = lax.broadcasted_iota(jnp.int32, (width, 128), 0)
    col = lax.broadcasted_iota(jnp.int32, (width, 128), 1)
    return (row == (col - first) * head_dim).astype(BF)


def spread_heads(width, head_dim, first):
    row = lax.broadcasted_iota(jnp.int32, (128, width), 0)
    col = lax.broadcasted_iota(jnp.int32, (128, width), 1)
    return (row - first == col // head_dim).astype(BF)


def exact_dot(values, ones):
    high = values.astype(BF)
    low = (values - high.astype(F32)).astype(BF)
    return dot(high, ones) + dot(low, ones)


def own_lanes(values, mine):
    return jnp.where(mine, values, jnp.zeros_like(values))


def attend_kernel(dims, *refs):
    group, segs, head_dim, parts, block = dims
    me_ref, first_ref, last_ref, lo_ref, hi_ref, temper_ref, qb_ref, vb_ref, w_ref = refs[:9]
    blocks = refs[9 : 9 + group]
    out_o, out_t_o, lse_ref, q_o, ql_o, k_o, v_o, inv_o = refs[9 + group : 17 + group]
    (held, block_s, q_ref, ql_ref, k_ref, v_ref, inv_ref, v_t, out_t_ref, out_s, acc, total, sems,
     in_sems, out_sems) = refs[17 + group :]
    pack_len, width = q_ref.shape
    rows = block_s.shape[1]
    seg, sub = rows // segs, width // parts
    pair, heads = 128 // head_dim, width // head_dim
    me = me_ref[0]
    loads = [
        pltpu.make_async_copy(blocks[k], block_s.at[k], in_sems.at[k]) for k in range(group)
    ]
    loads[0].start()
    copies = load_columns(w_ref, held, sems, lambda p: (p * group + me) * sub, parts, sub)
    for load in loads[1:]:
        load.start()
    same = same_head(width, head_dim)
    pick_q, pick_k = pick_heads(width, head_dim, 0), pick_heads(width, head_dim, heads)
    for copy in copies:
        copy.wait()
    for k in range(group):
        loads[k].wait()
        for y in range(segs):
            ranks = pl.ds(pl.multiple_of((y * group + (me ^ k)) * seg, 16), seg)
            made = dot(block_s[k, y * seg : (y + 1) * seg, :], held[...])
            query = made[:, :width] + qb_ref[...]
            key = made[:, width : 2 * width]
            inverse_q = lax.rsqrt(exact_dot(query * query, same) + 1e-06)
            query = query * inverse_q * temper_ref[...]
            rounded = query.astype(BF)
            q_ref[ranks, :] = rounded
            ql_ref[ranks, :] = (query - rounded.astype(F32)).astype(BF)
            inverse_k = lax.rsqrt(exact_dot(key * key, same) + 1e-06)
            k_ref[ranks, :] = (key * inverse_k).astype(BF)
            v_ref[ranks, :] = (made[:, 2 * width :] + vb_ref[...]).astype(BF)
            inv_ref[ranks, :] = exact_dot(inverse_q, pick_q) + exact_dot(inverse_k, pick_k)
    stores = []

    def store(source, target):
        stores.append(pltpu.make_async_copy(source, target, out_sems.at[len(stores)]))
        stores[-1].start()

    for source, target in (
        (q_ref, q_o), (ql_ref, ql_o), (k_ref, k_o), (v_ref, v_o), (inv_ref, inv_o)
    ):
        store(source, target)
    lanes = lax.broadcasted_iota(jnp.int32, (1, 128), 1) // head_dim
    v_t[...] = v_ref[...].T

    @pl.loop(0, pack_len // block)
    def _(q_block):
        q_rows = at(q_block, block)
        q_t = q_ref[q_rows, :].T
        low, high = lo_ref[:, q_rows], hi_ref[:, q_rows]
        acc[...] = jnp.zeros_like(acc)
        total[...] = jnp.zeros_like(total)

        @pl.loop(first_ref[q_block], last_ref[q_block])
        def _(k_block):
            k_rows = at(k_block, block)
            index = k_block * block + lax.broadcasted_iota(jnp.int32, (block, block), 0)
            seen = (index >= low) & (index < high)
            scores = []
            for h in range(heads):
                near = slice(h // pair * 128, (h // pair + 1) * 128)
                scores.append(dot(own_lanes(k_ref[k_rows, near], lanes == h % pair), q_t[near, :]))
            raised = [jnp.where(seen, jnp.exp(values), 0.0) for values in scores]
            for h in range(heads):
                own = pl.ds(h * head_dim, head_dim)
                total[h : h + 1, :] += jnp.sum(raised[h], axis=0, keepdims=True)
                acc[own, :] += dot(v_t[own, k_rows], raised[h].astype(BF))

        for h in range(heads):
            own = pl.ds(h * head_dim, head_dim)
            acc[own, :] = acc[own, :] / total[h : h + 1, :]
            lse_ref[h : h + 1, q_rows] = jnp.log(total[h : h + 1, :])
        out_t_ref[:, q_rows] = acc[...]
        out_s[q_rows, :] = acc[...].T.astype(BF)

    for y in range(segs):
        for g in range(group):
            start = (y * group + g) * seg
            store(out_s.at[pl.ds(start, seg), :], out_o.at[g, pl.ds(y * seg, seg), :])
    store(out_t_ref, out_t_o)
    for copy in stores:
        copy.wait()


def attend_back_blocks(dims, refs, scratch, outs):
    head_dim, block = dims
    first_ref, last_ref, lo_ref, hi_ref, lse_ref, q_ref, k_ref, v_ref, out_t_ref, g_s = refs
    k_t, dk_acc, dv_acc, acc, sums = scratch
    dq_ref, dk_ref, dv_ref = outs
    pack_len, width = q_ref.shape
    pair, heads = 128 // head_dim, width // head_dim
    lanes = lax.broadcasted_iota(jnp.int32, (1, 128), 1) // head_dim
    cols = [slice(p * 128, (p + 1) * 128) for p in range(width // 128)]
    k_t[...] = k_ref[...].T
    dk_acc[...] = jnp.zeros_like(dk_acc)
    dv_acc[...] = jnp.zeros_like(dv_acc)

    @pl.loop(0, pack_len // block)
    def _(q_block):
        q_rows = at(q_block, block)
        queries, grads = q_ref[q_rows, :], g_s[q_rows, :]
        q_t, g_t = queries.T, grads.T
        low, high = lo_ref[:, q_rows], hi_ref[:, q_rows]
        weighted = g_t.astype(F32) * out_t_ref[:, q_rows]
        for h in range(heads):
            sums[h : h + 1, :] = jnp.sum(
                weighted[h * head_dim : (h + 1) * head_dim, :], axis=0, keepdims=True
            )
        acc[...] = jnp.zeros_like(acc)

        @pl.loop(first_ref[q_block], last_ref[q_block])
        def _(k_block):
            k_rows = at(k_block, block)
            index = k_block * block + lax.broadcasted_iota(jnp.int32, (block, block), 0)
            seen = (index >= low) & (index < high)
            scores, grad_probs, probs, grad_scores = [], [], [], []
            for h in range(heads):
                near, mine = cols[h // pair], lanes == h % pair
                scores.append(dot(own_lanes(k_ref[k_rows, near], mine), q_t[near, :]))
                grad_probs.append(dot(own_lanes(v_ref[k_rows, near], mine), g_t[near, :]))
            for h in range(heads):
                made = jnp.where(seen, jnp.exp(scores[h] - lse_ref[h : h + 1, q_rows]), 0.0)
                probs.append(made.astype(BF))
                grad_scores.append((made * (grad_probs[h] - sums[h : h + 1, :])).astype(BF))
            for h in range(heads):
                own = pl.ds(h * head_dim, head_dim)
                acc[own, :] += dot(k_t[own, k_rows], grad_scores[h])
            for p, near in enumerate(cols):
                grad_k = grad_v = 0.0
                for h in range(p * pair, (p + 1) * pair):
                    mine = lanes == h % pair
                    grad_k += dot(grad_scores[h], own_lanes(queries[:, near], mine))
                    grad_v += dot(probs[h], own_lanes(grads[:, near], mine))
                dk_acc[k_rows, near] += grad_k
                dv_acc[k_rows, near] += grad_v

        dq_ref[q_rows, :] = acc[...].T.astype(BF)

    dk_ref[...] = dk_acc[...].astype(BF)
    dv_ref[...] = dv_acc[...].astype(BF)


def attend_back_kernel(dims, *refs):
    group, segs, head_dim, parts, block = dims
    me_ref, temper_ref, w_ref, inv_ref, ql_ref = refs[:5]
    ranges, lse_ref, ins = refs[5:9], refs[9], refs[10:15]
    sent, (dqkv_o, sums_ref), refs = refs[15 : 15 + group], refs[15 + group : 17 + group], refs[17 + group :]
    (q_s, k_s, v_s, out_s, g_s), scratch, made, refs = refs[:5], refs[5:10], refs[10:13], refs[13:]
    (w_s, inv_s, ql_s, dqkv_s, sent_s), (sems, w_sems, out_sems) = refs[:5], refs[5:]
    pack_len, width = q_s.shape
    rows = sent_s.shape[1]
    seg, sub = rows // segs, width // parts
    heads = width // head_dim
    me = me_ref[0]
    moves = [(ins[1], q_s), (ins[2], k_s), (ins[3], v_s), (ins[4], out_s)]
    for y in range(segs):
        for g in range(group):
            to = pl.ds((y * group + g) * seg, seg)
            moves.append((ins[0].at[g, pl.ds(y * seg, seg), :], g_s.at[to, :]))
    moves += [(inv_ref, inv_s), (ql_ref, ql_s)]
    loads = []
    for place, (source, target) in enumerate(moves):
        loads.append(pltpu.make_async_copy(source, target, sems.at[place]))
        loads[-1].start()
    copies = load_columns(w_ref, w_s, w_sems, lambda p: (p * group + me) * sub, parts, sub)
    copies += loads[-2:]
    for load in loads[:-2]:
        load.wait()
    attend_back_blocks(
        (head_dim, block), (*ranges, lse_ref, q_s, k_s, v_s, out_s, g_s), scratch, made
    )
    same = same_head(width, head_dim)
    spread_q, spread_k = spread_heads(width, head_dim, 0), spread_heads(width, head_dim, heads)
    sums_ref[...] = jnp.zeros_like(sums_ref)
    for copy in copies:
        copy.wait()
    stores = []
    dq_s, dk_s, dv_s = made
    for k in reversed(range(group)):
        whole = slice(k * rows, (k + 1) * rows)
        for y in range(segs):
            ranks = pl.ds(pl.multiple_of((y * group + (me ^ k)) * seg, 16), seg)
            own = slice(k * rows + y * seg, k * rows + (y + 1) * seg)
            inverse = inv_s[ranks, :]
            query = q_s[ranks, :].astype(F32) + ql_s[ranks, :].astype(F32)
            unit = query / temper_ref[...]
            raw = dq_s[ranks, :].astype(F32)
            grad = raw * temper_ref[...]
            grad_query = exact_dot(inverse, spread_q) * (grad - unit * exact_dot(grad * unit, same))
            unit_k = k_s[ranks, :].astype(F32)
            grad = dk_s[ranks, :].astype(F32)
            grad_key = exact_dot(inverse, spread_k) * (
                grad - unit_k * exact_dot(grad * unit_k, same)
            )
            grad_query, grad_value = grad_query.astype(BF), dv_s[ranks, :]
            dqkv_s[own, :width] = grad_query
            dqkv_s[own, width : 2 * width] = grad_key.astype(BF)
            dqkv_s[own, 2 * width :] = grad_value
            for index, values in enumerate((grad_query, grad_value, raw * query)):
                sums_ref[index : index + 1, :] += jnp.sum(
                    values.astype(F32), axis=0, keepdims=True
                )
        sent_s[k] = dot(dqkv_s[whole, :], w_s[...], BY_ROW).astype(BF)
        own = pl.ds(k * rows, rows)
        for source, target in ((sent_s.at[k], sent[k]), (dqkv_s.at[own, :], dqkv_o.at[own, :])):
            stores.append(pltpu.make_async_copy(source, target, out_sems.at[len(stores)]))
            stores[-1].start()
    for copy in stores:
        copy.wait()


def project_kernel(
    parts, ret_ref, wp_ref, pb_ref, x_ref, mod_ref, item_ref, attn_ref, branch_ref, middle_ref, out_ref, made
):
    group, rows, width = ret_ref.shape
    model = x_ref.shape[1]
    sub = width // parts
    for g in range(group):
        for p in range(parts):
            start = (p * group + g) * sub
            attn_ref[:, start : start + sub] = ret_ref[g, :, p * sub : (p + 1) * sub]
    made[...] = dot(attn_ref[...], wp_ref[...]) + pb_ref[...].astype(F32)
    branch_ref[...] = made[...].astype(BF)

    @chunks(rows, 64)
    def _(i):
        r = at(i, 64)
        item = item_ref[r, :]
        middle = x_ref[r, :].astype(F32) + mod_rows(mod_ref, 0, item, model) * made[r, :]
        middle_ref[r, :] = middle
        normed, _ = row_norm(middle)
        scale, shift = mod_rows(mod_ref, 3, item, model), mod_rows(mod_ref, 5, item, model)
        out_ref[r, :] = (normed * (1.0 + scale) + shift).astype(BF)


def add_blocks(terms, outs):
    count = outs[0].shape[0]
    for j in range(terms[0].shape[0]):
        made = sum(term[j].astype(F32) for term in terms).astype(BF)
        outs[j // count][j % count] = made


def weights_kernel(dims, me_ref, *refs):
    segs, head_size = dims
    count = segs * head_size
    tiles, pairs, (w1_ref, w2_ref, bias_ref, bias_s, sems) = refs[:count], refs[count : 2 * count], refs[2 * count :]
    hidden, half = pairs[0].shape
    copies = []

    def copy(source, target):
        copies.append(pltpu.make_async_copy(source, target, sems.at[len(copies)]))
        copies[-1].start()

    for k in range(count):
        own = pl.ds(pl.multiple_of((me_ref[2] ^ (k % head_size)) * hidden, hidden), hidden)
        part = pl.ds(pl.multiple_of((me_ref[1] ^ (k // head_size)) * half, half), half)
        copy(tiles[k].at[pl.ds(0, half), :], w1_ref.at[part, own])
        copy(pairs[k], w2_ref.at[own, part])
        if k < head_size:
            copy(tiles[k].at[pl.ds(half, 16), :], bias_s.at[:, own])
    for started in copies:
        started.wait()
    bias_ref[...] = bias_s[0:1, :].astype(F32)


def feed_kernel(count, *refs):
    w1, w2, b1_ref = refs[:3]
    ins, grads = refs[3 : 3 + count], refs[3 + count : 3 + 2 * count]
    rest = refs[3 + 2 * count :]
    back, outs = rest[:count], rest[count : 2 * count]
    act_ref, gh_ref, sum_ref = rest[2 * count : 2 * count + 3]
    in_s, grad_s, back_s, out_s, act_s, gh_s, pre, grad, in_sems, out_sems = rest[2 * count + 3 :]
    rows = ins[0].shape[0]
    loads, stores = [], []
    for k in range(count):
        pair = (
            pltpu.make_async_copy(ins[k], in_s.at[k], in_sems.at[2 * k]),
            pltpu.make_async_copy(grads[k], grad_s.at[k], in_sems.at[2 * k + 1]),
        )
        pair[0].start()
        pair[1].start()
        loads.append(pair)
    sum_ref[...] = jnp.zeros_like(sum_ref)

    def store(source, target, index):
        stores.append(pltpu.make_async_copy(source, target, out_sems.at[index]))
        stores[-1].start()

    def front(k):
        loads[k][0].wait()
        pre[k % 2] = dot(in_s[k], w1[...]) + b1_ref[...]
        loads[k][1].wait()
        grad[k % 2] = dot(grad_s[k], w2[...], BY_ROW)

    def middle(k):
        total = 0.0
        for start in range(0, rows, 32):
            r = slice(start, start + 32)
            value = pre[k % 2, r, :]
            square = value * value
            gate = jnp.tanh(value * (0.7978845608028654 + 0.035677408136300125 * square))
            half = 0.5 + 0.5 * gate
            act = value * half
            slope = half + act * (1.0 - gate) * (0.7978845608028654 + 0.10703222440890037 * square)
            back_grad = (slope * grad[k % 2, r, :]).astype(BF)
            act_s[k, r, :] = act.astype(BF)
            gh_s[k, r, :] = back_grad
            total = total + jnp.sum(back_grad.astype(F32), axis=0, keepdims=True)
        sum_ref[0:1, :] += total
        own = pl.ds(k * rows, rows)
        store(act_s.at[k], act_ref.at[own, :], 4 * k)
        store(gh_s.at[k], gh_ref.at[own, :], 4 * k + 1)

    def end(k):
        back_s[k] = dot(gh_s[k], w1[...], BY_ROW).astype(BF)
        store(back_s.at[k], back[k], 4 * k + 2)
        out_s[k] = dot(act_s[k], w2[...]).astype(BF)
        store(out_s.at[k], outs[k], 4 * k + 3)

    order = list(reversed(range(count)))
    front(order[0])
    for place, k in enumerate(order):
        if place + 1 < count:
            front(order[place + 1])
        middle(k)
        end(k)
    for started in stores:
        started.wait()


def turned(index, count):
    made = 0
    while count > 1:
        made, index, count = made * 2 + index % 2, index // 2, count // 2
    return made


def feed_weights_kernel(dims, *refs):
    count, group, split, halves, term_count = dims
    me_ref, acts, ghs = refs[0], refs[1 : 1 + halves], refs[1 + halves : 1 + 2 * halves]
    refs = refs[1 + 2 * halves :]
    ins, grads, refs = refs[:count], refs[count : 2 * count], refs[2 * count :]
    terms, refs = refs[:term_count], refs[term_count:]
    outs, sum_o, rest = refs[: 2 * split], refs[2 * split], refs[2 * split + 1 :]
    in_t, grad_t, act_s, gh_s, in_s, grad_s, term_s, sum_s, tile_s, in_sems, out_sems = rest
    rows, model = in_s.shape[1:]

    def load(source, target, index):
        copy = pltpu.make_async_copy(source, target, in_sems.at[index])
        copy.start()
        return copy

    part_rows = act_s.shape[0] // halves
    own = [pl.ds(k * part_rows, part_rows) for k in range(halves)]
    in_loads = [load(ins[k], in_s.at[k], k) for k in range(count)]
    index = count
    gh_loads = [load(ghs[k], gh_s.at[own[k], :], index + k) for k in range(halves)]
    index += halves
    grad_loads = [load(grads[k], grad_s.at[k], index + k) for k in range(count)]
    index += count
    act_loads = [load(acts[k], act_s.at[own[k], :], index + k) for k in range(halves)]
    index += halves
    term_loads = [load(terms[k], term_s.at[k], index + k) for k in range(term_count)]
    for k in range(count):
        in_loads[k].wait()
        in_t[:, k * rows : (k + 1) * rows] = in_s[k].T
    for copy in gh_loads:
        copy.wait()
    stores = []

    def store(source, target):
        stores.append(pltpu.make_async_copy(source, target, out_sems.at[len(stores)]))
        stores[-1].start()

    part = model // split
    fine = part // group
    _, _, head_size, _, _, hidden = tile_s.shape

    def tiles(y, which, left, right):
        start = pl.multiple_of((me_ref[1] ^ y) * part, part) if split > 1 else 0
        for j in range(head_size):
            z = me_ref[2] ^ turned(j, head_size)
            cols = slice(None)
            if split > 1:
                cols = pl.ds(pl.multiple_of(z * hidden, hidden), hidden)
            made = dot(left[pl.ds(start, part), :], right[:, cols]).astype(BF)
            for g in range(group):
                to = (me_ref[0] ^ g) if group > 1 else 0
                tile_s[which, y, j, to] = made[g * fine : (g + 1) * fine, :]
        store(tile_s.at[which, y], outs[which * split + y])

    for y in reversed(range(split)):
        tiles(y, 0, in_t, gh_s)
    for k in range(count):
        grad_loads[k].wait()
        grad_t[:, k * rows : (k + 1) * rows] = grad_s[k].T
    for copy in act_loads:
        copy.wait()
    for y in reversed(range(split)):
        tiles(y, 1, grad_t, act_s)
    for copy in term_loads:
        copy.wait()
    sum_s[...] = sum(term_s[k].astype(F32) for k in range(term_count)).astype(BF)
    store(sum_s, sum_o)
    for copy in stores:
        copy.wait()


def middle_back_kernel(
    dims, middle_ref, branch_ref, up_ref, mod_ref, item_ref, wp_ref, *refs, wait_late, send
):
    parts, items, count, chunk = dims
    me_ref, attn_rows_ref = refs[0], refs[1]
    terms, refs = refs[2 : 2 + count], refs[2 + count :]
    out_ref, gb_ref, gm_ref, sums_ref, col_ref = refs[:5]
    proj_refs, (attn, left_t, right) = refs[5:-3], refs[-3:]
    rows, model = middle_ref.shape
    group, _, width = out_ref.shape
    sub = width // parts
    sums_ref[...] = jnp.zeros_like(sums_ref)
    col_ref[...] = jnp.zeros_like(col_ref)

    @chunks(rows, 64)
    def _(i):
        r = at(i, 64)
        item = item_ref[r, :]
        grad_in = sum(term[r, :].astype(F32) for term in terms)
        normed, inverse = row_norm(middle_ref[r, :])
        scale = mod_rows(mod_ref, 3, item, model)
        grad_middle = up_ref[r, :].astype(F32) + norm_back(grad_in * (1.0 + scale), normed, inverse)
        gm_ref[r, :] = grad_middle
        grad_branch = (grad_middle * mod_rows(mod_ref, 0, item, model)).astype(BF)
        gb_ref[r, :] = grad_branch
        col_ref[0:1, :] += jnp.sum(grad_branch.astype(F32), axis=0, keepdims=True)
        add_item_sums(sums_ref, 0, item, grad_middle * branch_ref[r, :].astype(F32), items)
        add_item_sums(sums_ref, 1, item, grad_in * normed, items)
        add_item_sums(sums_ref, 2, item, grad_in, items)

    send(1)
    send(2)
    wait_late()
    attn[...] = dot(gb_ref[...], wp_ref[...], BY_ROW).astype(BF)
    for g in range(group):
        for p in range(parts):
            start = (p * group + g) * sub
            out_ref[g, :, p * sub : (p + 1) * sub] = attn[:, start : start + sub]
    send(0)
    proj_weights_kernel(
        (group, chunk), me_ref, attn_rows_ref, gb_ref, *proj_refs, left_t, right
    )


def output_kernel(dims, middle_ref, up_ref, mod_ref, item_ref, bias_ref, *refs):
    items, count, proj_count = dims
    terms, refs = refs[:count], refs[count:]
    projs, (out_ref, sums_ref, proj_ref) = refs[:proj_count], refs[proj_count:]
    proj_ref[...] = sum(proj[...].astype(F32) for proj in projs).astype(BF)
    rows, model = middle_ref.shape
    sums_ref[...] = jnp.zeros_like(sums_ref)

    @chunks(rows, 64)
    def _(i):
        r = at(i, 64)
        item = item_ref[r, :]
        made = sum(term[r, :].astype(F32) for term in terms) + bias_ref[...].astype(F32)
        gamma = mod_rows(mod_ref, 1, item, model)
        out_ref[r, :] = (middle_ref[r, :] + gamma * made).astype(BF)
        add_item_sums(sums_ref, 0, item, up_ref[r, :].astype(F32) * made, items)


def tokens_back_kernel(dims, x_ref, gm_ref, mod_ref, item_ref, *refs):
    items, count = dims
    terms, (out_ref, sums_ref) = refs[:count], refs[count:]
    rows, model = x_ref.shape
    sums_ref[...] = jnp.zeros_like(sums_ref)

    @chunks(rows, 64)
    def _(i):
        r = at(i, 64)
        item = item_ref[r, :]
        grad_in = sum(term[r, :].astype(F32) for term in terms)
        normed, inverse = row_norm(x_ref[r, :].astype(F32))
        scale = mod_rows(mod_ref, 2, item, model)
        out_ref[r, :] = (
            gm_ref[r, :] + norm_back(grad_in * (1.0 + scale), normed, inverse)
        ).astype(BF)
        add_item_sums(sums_ref, 0, item, grad_in * normed, items)
        add_item_sums(sums_ref, 1, item, grad_in, items)


def proj_weights_kernel(dims, me_ref, attn_ref, gb_ref, *refs):
    group, split = dims
    outs, (left_t, right) = refs[:group], refs[group:]
    left_t[...] = attn_ref[...].T
    chunk, head_size, tall, wide = outs[0].shape
    for k in range(group):
        for y in range(chunk):
            part = (me_ref[1] ^ y) if split else y
            start = pl.multiple_of((part * group + (me_ref[0] ^ k)) * wide, wide)
            right[:, y * wide : (y + 1) * wide] = gb_ref[:, pl.ds(start, wide)]
        for j in range(head_size):
            z = (me_ref[2] ^ turned(j, head_size)) if split else j
            made = dot(left_t[pl.ds(pl.multiple_of(z * tall, tall), tall), :], right[...])
            for y in range(chunk):
                outs[k][y, j] = made[:, y * wide : (y + 1) * wide].astype(BF)


def qkv_weights_kernel(dims, me_ref, dqkv_ref, *refs):
    count, chunk, split, proj_count = dims
    ins, refs = refs[:count], refs[count:]
    projs, refs = refs[:proj_count], refs[proj_count:]
    outs, (left_t, right) = refs[:chunk], refs[chunk:]
    rows = ins[0].shape[0]
    for k in range(count):
        left_t[:, k * rows : (k + 1) * rows] = ins[k][...].T
    head_size, _, tall, wide = outs[0].shape
    for y in reversed(range(chunk)):
        part = (me_ref[1] ^ y) if split else y
        for t in range(3):
            start = pl.multiple_of((t * chunk + part) * wide, wide)
            right[:, t * wide : (t + 1) * wide] = dqkv_ref[:, pl.ds(start, wide)]
        for j in range(head_size):
            z = (me_ref[2] ^ turned(j, head_size)) if split else j
            made = dot(left_t[pl.ds(pl.multiple_of(z * tall, tall), tall), :], right[...])
            outs[y][j, 0] = sum(proj[y, j].astype(F32) for proj in projs).astype(BF)
            for t in range(3):
                outs[y][j, 1 + t] = made[:, t * wide : (t + 1) * wide].astype(BF)


def sort_kernel(pack_len, dest_ref, tokens_ref, cot_ref, to_slot_ref, tokens_out, cot_out):
    rows = tokens_ref.shape[0]
    pack = dest_ref[...] // pack_len
    other = jnp.broadcast_to(pack, (8, rows)).astype(F32).T[:, 0:1].astype(jnp.int32)
    this = lax.broadcasted_iota(jnp.int32, (rows, rows), 1)
    that = lax.broadcasted_iota(jnp.int32, (rows, rows), 0)
    before = (other < pack) | ((other == pack) & (that < this))
    slot = jnp.sum(before.astype(jnp.int32), axis=0, keepdims=True)
    to_slot_ref[...] = (slot == that).astype(F32).astype(BF)
    tokens_out[...] = dot(to_slot_ref[...], tokens_ref[...]).astype(BF)
    cot_out[...] = dot(to_slot_ref[...], cot_ref[...]).astype(BF)


def item_blocks_kernel(dims, me_ref, middle_ref, output_ref, tokens_ref, out_ref, joined):
    group, segs, head_size, size = dims
    model = output_ref.shape[1]
    parts = (
        (middle_ref, 0), (output_ref, 0), (tokens_ref, 0),
        (middle_ref, 1), (tokens_ref, 1), (middle_ref, 2),
    )
    for part, (ref, start) in enumerate(parts):
        joined[:, part * model : (part + 1) * model] = ref[:, start * model : (start + 1) * model]
    for g in range(group):
        for y in range(segs):
            for z in range(head_size):
                start = ((y * group + g) * head_size + z) * size
                near = me_ref[2] ^ z
                turn, count = jnp.int32(0), head_size
                while count > 1:
                    turn, near, count = turn * 2 + near % 2, near // 2, count // 2
                block = (me_ref[1] ^ y) * head_size + turn
                rows = pl.ds(pl.multiple_of(block * 8, 8), 8)
                out_ref[me_ref[0] ^ g, rows, 0:size] = joined[:, start : start + size]


def group_sums_kernel(count, bit, kept_ref, came_ref, vector_ref, own_ref, sent_ref, sum_ref):
    rows = kept_ref.shape[1]
    vectors = vector_ref[...] + came_ref[pl.ds(came_ref.shape[0] - 64, 64), :]
    sum_ref[...] = vectors
    last = count == 2
    place = 0
    for k in range(0, count, 2):
        made = kept_ref[k] + came_ref[pl.ds(k // 2 * rows, rows), :]
        if last:
            half = rows // 2
            own_ref[...] = made[:half]
            sent_ref[0:half, :] = made[half:]
        elif k // 2 % 2 == 0:
            own_ref[k // 2] = made
        else:
            own_ref[k // 2] = made
            sent_ref[place * rows : (place + 1) * rows, :] = made
            place += 1
    sent_ref[pl.ds(sent_ref.shape[0] - 64, 64), :] = vectors


def pack_sums_kernel(kept_ref, came_ref, vector_ref, own_ref, *refs):
    blocks, senders = own_ref.shape[0] * (2 if len(refs) == 2 else 1), kept_ref.shape[1]
    vectors = vector_ref[...] + came_ref[pl.ds(came_ref.shape[0] - 64, 64), :]
    refs[-1][...] = vectors
    for c in range(blocks):
        for t in range(2 * senders):
            if t < senders:
                value = kept_ref[c, t]
            else:
                value = came_ref[pl.ds((c * senders + t - senders) * 8, 8), :]
            if len(refs) == 1 or c < blocks // 2:
                own_ref[c, t] = value
            else:
                refs[0][pl.ds(((c - blocks // 2) * 2 * senders + t) * 8, 8), :] = value
    if len(refs) == 2:
        refs[0][pl.ds(refs[0].shape[0] - 64, 64), :] = vectors


def ada_kernel(segs, me_ref, silu_ref, blocks_ref, grad_ref, bias_ref, held):
    for c in range(blocks_ref.shape[0]):
        sender = (me_ref[1] ^ turned(c % segs, segs)) * me_ref[3] + (me_ref[2] ^ c // segs)
        held[pl.ds(pl.multiple_of(sender * 8, 8), 8), :] = blocks_ref[c]
    low = held[:, 0 : grad_ref.shape[1]].astype(BF)
    bias_ref[...] = jnp.broadcast_to(
        jnp.sum(low.astype(F32), axis=0, keepdims=True), bias_ref.shape
    )
    grad_ref[...] = lax.dot_general(
        silu_ref[...], low, (((0,), (0,)), ((), ())), preferred_element_type=F32
    )


def add_kernel(counts, *refs):
    terms, outs = refs[: sum(counts)], refs[sum(counts) :]
    for place, count in enumerate(counts):
        add_blocks(terms[:count], outs[2 * place : 2 * place + 2])
        terms = terms[count:]


def own_tiles_kernel(*refs):
    ups, downs, outs = refs[:2], refs[2:4], refs[4:]
    for i, out in enumerate(outs):
        for which, terms in enumerate((ups, downs)):
            out[which] = sum(term[0, i].astype(F32) for term in terms).astype(BF)


def place_kernel(group, me_ref, *refs):
    blocks, (up_ref, down_ref) = refs[:group], refs[group:]
    hidden = blocks[0].shape[2]
    for i in range(group):
        own = pl.ds(pl.multiple_of((me_ref[0] ^ i) * hidden, hidden), hidden)
        up_ref[:, own] = blocks[i][0].astype(F32)
        down_ref[own, :] = blocks[i][1].astype(F32).T


def vector_parts_kernel(dims, me_ref, qkv_ref, branch_ref, mlp_ref, *refs):
    group, parts, head_size = dims
    hidden_refs, (flat_ref, out_ref) = refs[:-2], refs[-2:]
    sub = qkv_ref.shape[1] // parts
    hidden = hidden_refs[0].shape[1] // head_size
    out_ref[...] = jnp.zeros_like(out_ref)
    for p in range(parts):
        own = pl.ds(pl.multiple_of((p * group + me_ref[0]) * sub, sub), sub)
        for row in range(3):
            out_ref[row : row + 1, own] = qkv_ref[row : row + 1, p * sub : (p + 1) * sub]
    out_ref[3:4, :] = branch_ref[0:1, :]
    out_ref[4:5, :] = mlp_ref[0:1, :]
    if hidden % 128 == 0:
        own = pl.ds(pl.multiple_of(me_ref[0] * hidden, hidden), hidden)
        for z in range(head_size):
            cols = slice(z * hidden, (z + 1) * hidden)
            out_ref[8 + z : 9 + z, own] = sum(ref[0:1, cols] for ref in hidden_refs)
    for c in range(out_ref.shape[1] // 256):
        flat_ref[c * 16 : (c + 1) * 16, :] = out_ref[:, c * 256 : (c + 1) * 256]


def to_packs(rows):
    return lax.all_to_all(rows, ("yy", "head"), split_axis=0, concat_axis=0, tiled=True)


def over_group(blocks):
    return lax.all_to_all(blocks, "g", split_axis=0, concat_axis=0, tiled=True)


def bits(count):
    steps = []
    while count > 1:
        count //= 2
        steps.append(count)
    return steps


def xor_swap(values, axis, step):
    size = lax.axis_size(axis)
    return lax.ppermute(values, axis, [(i, i ^ step) for i in range(size)])


def xor_gather(block, axis):
    blocks = {0: block}
    for step in bits(lax.axis_size(axis)):
        for k in list(blocks):
            blocks[k ^ step] = xor_swap(blocks[k], axis, step)
    return [blocks[k] for k in range(len(blocks))]


def xor_scatter(blocks, axis):
    terms = {k: [block] for k, block in enumerate(blocks)}
    for step in reversed(bits(lax.axis_size(axis))):
        for k in reversed([k for k in terms if k & step]):
            terms[k ^ step].append(xor_swap(add_low(*terms.pop(k)), axis, step))
    return terms[0]


def halves_over_head(values):
    count = lax.axis_size("head")
    step = count // values.shape[0]
    half = values.shape[0] // 2
    return values[:half], xor_swap(values[half:], "head", step)


def add_low(*terms):
    if len(terms) == 1:
        return terms[0]
    return sum(term.astype(F32) for term in terms).astype(terms[0].dtype)


def butterfly(values, axis):
    for step in bits(lax.axis_size(axis)):
        values = values + xor_swap(values, axis, step)
    return values


def pick(values, index, axis):
    return lax.dynamic_index_in_dim(values, index, axis, keepdims=False)


def xor_blocks(values, axis, dim):
    me = lax.axis_index(axis)
    return [pick(values, me ^ k, dim) for k in range(lax.axis_size(axis))]


def tie(*values):
    return lax.optimization_barrier(values)


def tie_groups(*groups):
    tied = list(tie(*[value for group in groups for value in group]))
    return [[tied.pop(0) for _ in group] for group in groups]


def spread_steps(depth, segs, head_size):
    steps = []
    for k in range(segs * head_size):
        if bin(k).count("1") == depth:
            y, z = k // head_size, k % head_size
            step = y & -y if y else z & -z
            steps.append((k, k - step * head_size if y else k - step, "yy" if y else "head", step))
    return sorted(steps, key=lambda made: made[2])


def shards(
    tokens,
    cotangent,
    class_table,
    ada_weight,
    ada_bias,
    qkv_weight,
    q_bias,
    v_bias,
    log_scale,
    proj_weight,
    proj_bias,
    fc1_weight,
    fc1_bias,
    fc2_weight,
    fc2_bias,
    item_lens,
    class_ids,
    section_ids,
    destination,
):
    segs = lax.axis_size("yy")
    group = lax.axis_size("g")
    head_size = lax.axis_size("head")
    yy, g, z = lax.axis_index("yy"), lax.axis_index("g"), lax.axis_index("head")
    me = jnp.stack([g, yy, z, jnp.int32(head_size)]).astype(jnp.int32)
    pack = yy * head_size + z
    rows, model = tokens.shape
    heads_all = log_scale.shape[0]
    head_dim = model // heads_all
    heads = heads_all // group
    width = model // group
    dp_size = segs * group
    pack_len = rows * head_size
    seg = rows // segs
    items = item_lens.shape[1]
    block = min(256, pack_len)
    col = model // dp_size
    parts = segs if col % 128 == 0 else 1
    sub = width // parts

    def own_cols(values):
        return pick(values.reshape(parts, group, sub), g, 1).reshape(1, width)

    rows_bf, rows_f32 = shape_of((rows, model), BF), shape_of((rows, model), F32)
    to_slot, sorted_tokens, sorted_cotangent = call(
        "sort",
        functools.partial(sort_kernel, pack_len),
        (destination[None, :], tokens, cotangent),
        (VMEM, HBM, HBM),
        (shape_of((rows, rows), BF), rows_bf, rows_bf),
    )
    inputs = to_packs(sorted_tokens)

    hidden = fc1_weight.shape[1] // group
    units = head_size * hidden
    half = model // segs
    fc1_own = lax.dynamic_slice(fc1_weight, (yy * half, g * hidden), (half, hidden))
    fc1_bias_own = lax.dynamic_slice(fc1_bias, (g * hidden,), (hidden,))
    fc2_own = lax.dynamic_slice(fc2_weight, (g * hidden, yy * half), (hidden, half))
    fc1_own = jnp.concatenate(
        [fc1_own, jnp.broadcast_to(fc1_bias_own[None, :], (16, hidden))], axis=0
    )
    tiled = hidden % 128 == 0
    tile_count = segs * head_size

    fc1_tiles, fc2_tiles = {0: fc1_own}, {0: fc2_own}

    def next_hop(tiles, depth):
        for k, source, axis, step in spread_steps(depth, segs, head_size):
            tiles[k] = xor_swap(tiles[source], axis, step)

    def with_tiles(values):
        first, second = sorted(fc1_tiles), sorted(fc2_tiles)
        values, held, held_too = tie_groups(
            values, [fc1_tiles[k] for k in first], [fc2_tiles[k] for k in second]
        )
        fc1_tiles.update(zip(first, held))
        fc2_tiles.update(zip(second, held_too))
        return values

    lens_here = pick(item_lens, pack, 0)
    class_here = pick(class_ids, pack, 0)
    order_key = class_here * items + jnp.arange(items, dtype=jnp.int32)
    item_rank = jnp.sum(
        jnp.where(order_key[None, :] < order_key[:, None], lens_here[None, :], 0), axis=1
    )
    item_pos = jnp.cumsum(lens_here) - lens_here
    item_end = item_rank + lens_here

    def items_of(rank):
        return (rank[:, None] >= item_rank[None, :]) & (rank[:, None] < item_end[None, :])

    rank_all = jnp.arange(pack_len, dtype=jnp.int32)
    member = items_of(rank_all)

    def of_item(values):
        return jnp.sum(jnp.where(member, values[None, :], 0), axis=1)

    section_here = lax.ppermute(
        section_ids[0],
        ("g", "head"),
        [(a * head_size + b, b * head_size + a) for a in range(group) for b in range(head_size)],
    )
    position = rank_all - of_item(item_rank - item_pos)
    section_rank = jnp.sum(
        jnp.where(rank_all[None, :] == position[:, None], section_here[None, :], 0), axis=1
    )
    up_to = jnp.sum((section_here[None, :] <= section_rank[:, None]).astype(jnp.int32), axis=1)
    low = of_item(item_rank)
    high = jnp.minimum(up_to + of_item(item_rank - item_pos), of_item(item_end))
    first = low[::block] // block
    last = (high[block - 1 :: block] + block - 1) // block
    low, high = low[None, :], high[None, :]

    row_rank = (
        (jnp.arange(segs, dtype=jnp.int32)[:, None] * group + g) * seg
        + jnp.arange(seg, dtype=jnp.int32)[None, :]
    ).reshape(rows)
    row_item = jnp.sum(
        jnp.where(items_of(row_rank), jnp.arange(items, dtype=jnp.int32)[None, :], 0), axis=1
    )[:, None]

    class_rows = jnp.take(class_table, class_ids.reshape(-1), axis=0).astype(F32)
    silu_cond = jax.nn.silu(class_rows).astype(BF)
    silu_here = lax.dynamic_slice_in_dim(silu_cond, pack * items, items, 0)
    mod = jnp.dot(silu_here, ada_weight, preferred_element_type=F32) + ada_bias.astype(F32)

    inputs, first, last, low, high = tie(inputs, first, last, low, high)
    (attn_in,) = call(
        "first_norm",
        first_norm_kernel, (inputs, mod, row_item), (HBM, VMEM, VMEM), (shape_of((rows, model), BF),)
    )
    def near_blocks(own):
        blocks = {0: own}
        for step in bits(group)[1:]:
            for k in list(blocks):
                blocks[k ^ step] = xor_swap(blocks[k], "g", step)
        return [blocks[k] for k in range(len(blocks))]

    near = group // 2

    (attn_in,) = with_tiles([attn_in])
    next_hop(fc1_tiles, 1)
    attn_blocks = near_blocks(attn_in)
    (attn_far,) = with_tiles([xor_swap(attn_in, "g", near)])
    next_hop(fc1_tiles, 2)
    next_hop(fc2_tiles, 1)
    attn_blocks += near_blocks(attn_far)
    per_part = sub // head_dim
    scale_here = pick(log_scale.reshape(parts, group, per_part), g, 1).reshape(heads)
    temper = jnp.repeat(jnp.exp(scale_here), head_dim)[None, :]
    wide = shape_of((pack_len, width), BF)
    tall = shape_of((width, pack_len), F32)
    sorted_cotangent, _ = tie(sorted_cotangent, inputs)
    upstream = to_packs(sorted_cotangent)
    held_bf = pltpu.VMEM((pack_len, width), BF)
    out_blocks, out_t, lse, queries, queries_low, keys, values, inverses = call(
        "attend",
        functools.partial(attend_kernel, (group, segs, head_dim, parts, block)),
        (me, first, last, low, high, temper, own_cols(q_bias).astype(F32),
         own_cols(v_bias).astype(F32), qkv_weight, *attn_blocks),
        (SMEM,) * 3 + (VMEM,) * 5 + (ANY,) * (1 + group),
        (shape_of((group, rows, width), BF), tall, shape_of((8, pack_len), F32), wide, wide, wide,
         wide, shape_of((pack_len, 128), F32)),
        [
            pltpu.VMEM((model, 3 * width), BF),
            pltpu.VMEM((group, rows, model), BF),
            held_bf,
            held_bf,
            held_bf,
            held_bf,
            pltpu.VMEM((pack_len, 128), F32),
            pltpu.VMEM((width, pack_len), BF),
            pltpu.VMEM((width, pack_len), F32),
            held_bf,
            pltpu.VMEM((width, block), F32),
            pltpu.VMEM((8, block), F32),
            pltpu.SemaphoreType.DMA((3 * parts,)),
            pltpu.SemaphoreType.DMA((group,)),
            pltpu.SemaphoreType.DMA((6 + segs * group,)),
        ],
        out_specs=(ANY, ANY, VMEM, ANY, ANY, ANY, ANY, ANY),
    )
    (out_blocks,) = with_tiles([out_blocks])
    next_hop(fc1_tiles, 3)
    next_hop(fc2_tiles, 2)
    returned = over_group(out_blocks)
    upstream, _ = tie(upstream, out_blocks)
    grad_mlp, grad_mlp_sum = call(
        "grad_mlp",
        grad_mlp_kernel,
        (upstream, mod, row_item),
        (HBM, VMEM, VMEM),
        (rows_bf, shape_of((8, model), F32)),
    )
    grad_far = xor_swap(grad_mlp, "g", near)
    grad_blocks = near_blocks(grad_mlp)
    attn_rows, branch, middle, mlp_in = call(
        "project",
        functools.partial(project_kernel, parts),
        (returned, proj_weight, proj_bias[None, :], inputs, mod, row_item),
        (HBM, HBM, VMEM, HBM, VMEM, VMEM),
        (rows_bf, rows_bf, rows_f32, rows_bf),
        [pltpu.VMEM((rows, model), F32)],
    )

    (middle,) = with_tiles([middle])
    for depth in range(4, tile_count.bit_length()):
        next_hop(fc1_tiles, depth)
    for depth in range(3, tile_count.bit_length()):
        next_hop(fc2_tiles, depth)
    if tiled:
        fc1_here, fc2_here, fc1_bias_here = call(
            "weights",
            functools.partial(weights_kernel, (segs, head_size)),
            (me, *[fc1_tiles[k] for k in range(tile_count)], *[fc2_tiles[k] for k in range(tile_count)]),
            (SMEM,) + (ANY,) * (2 * tile_count),
            (shape_of((model, units), BF), shape_of((units, model), BF), shape_of((1, units), F32)),
            [
                pltpu.VMEM((16, units), BF),
                pltpu.SemaphoreType.DMA((2 * tile_count + head_size,)),
            ],
            out_specs=(VMEM,) * 3,
        )
    else:
        def placed(tiles):
            held = jnp.stack([tiles[k] for k in range(tile_count)])
            held = held.reshape(segs, head_size, *held.shape[1:])
            return held[jnp.arange(segs) ^ yy][:, jnp.arange(head_size) ^ z]

        fc1_all, fc2_all = placed(fc1_tiles), placed(fc2_tiles)
        fc1_here = fc1_all[:, :, :half].transpose(0, 2, 1, 3).reshape(model, units)
        fc1_bias_here = fc1_all[0, :, half].reshape(1, units).astype(F32)
        fc2_here = fc2_all.transpose(1, 2, 0, 3).reshape(units, model)

    mlp_blocks = near_blocks(mlp_in)
    mlp_far = xor_swap(mlp_in, "g", near)
    grad_blocks += near_blocks(tie(grad_far, mlp_in, fc1_here)[0])
    back_parts, out_parts, acts, ghs, hidden_sums = [], [], [], [], []
    for start in (0, near):
        if start:
            mlp_blocks += near_blocks(tie(mlp_far, acts[0])[0])
        made = call(
            "feed",
            functools.partial(feed_kernel, near),
            (fc1_here, fc2_here, fc1_bias_here, *mlp_blocks[start : start + near],
             *grad_blocks[start : start + near]),
            (VMEM,) * 3 + (ANY,) * (2 * near),
            (rows_bf,) * (2 * near)
            + (shape_of((near * rows, units), BF),) * 2
            + (shape_of((8, units), F32),),
            [pltpu.VMEM((near, rows, model), BF)] * 4
            + [pltpu.VMEM((near, rows, units), BF)] * 2
            + [pltpu.VMEM((2, rows, units), F32)] * 2
            + [pltpu.SemaphoreType.DMA((2 * near,)), pltpu.SemaphoreType.DMA((4 * near,))],
            out_specs=(ANY,) * (2 * near + 2) + (VMEM,),
        )
        back_parts += made[:near]
        out_parts += made[near : 2 * near]
        acts.append(made[2 * near])
        ghs.append(made[2 * near + 1])
        hidden_sums.append(made[2 * near + 2])
    far_terms = {k: back_parts[k] for k in range(near, group)}
    for step in reversed(bits(group)[1:]):
        for k in reversed([k for k in far_terms if k & step]):
            came = xor_swap(far_terms.pop(k), "g", step)
            far_terms[k ^ step] = add_low(far_terms[k ^ step], came)
    far_sum = far_terms[near]
    back_parts = list(tie(*back_parts[:near], far_sum)[:near])
    in_terms = {k: [back_parts[k]] for k in range(near)}
    for step in reversed(bits(group)[1:]):
        for k in reversed([k for k in in_terms if k & step]):
            in_terms[k ^ step].append(xor_swap(add_low(*in_terms.pop(k)), "g", step))
    in_terms = in_terms[0] + [xor_swap(far_sum, "g", near)]
    acts[0], _ = tie(acts[0], far_sum)
    split = segs if tiled else 1

    def to_last(blocks):
        terms = {k: [block] for k, block in enumerate(blocks)}
        for step in reversed(bits(group)[1:]):
            for k in reversed([k for k in terms if k & step]):
                terms[k ^ step].append(xor_swap(add_low(*terms.pop(k)), "g", step))
        return terms[0], terms[near]

    out_terms, out_last = to_last(tie(*out_parts, far_sum)[:group])
    if tiled:
        fine = half // group
        tile_shape = (head_size, group, fine, hidden)
        feed_dims = (group, group, segs, 2, len(out_last))
    else:
        tile_shape = (1, 1, model, units)
        feed_dims = (group, 1, 1, 2, len(out_last))
    made = call(
        "feed_weights",
        functools.partial(feed_weights_kernel, feed_dims),
        (me, *acts, *ghs, *mlp_blocks, *grad_blocks, *out_last),
        (SMEM,) + (ANY,) * (4 + 2 * group + len(out_last)),
        (shape_of(tile_shape, BF),) * (2 * split) + (rows_bf,),
        [
            pltpu.VMEM((model, pack_len), BF),
            pltpu.VMEM((model, pack_len), BF),
            pltpu.VMEM((pack_len, units), BF),
            pltpu.VMEM((pack_len, units), BF),
            pltpu.VMEM((group, rows, model), BF),
            pltpu.VMEM((group, rows, model), BF),
            pltpu.VMEM((len(out_last), rows, model), BF),
            pltpu.VMEM((rows, model), BF),
            pltpu.VMEM((2, split, *tile_shape), BF),
            pltpu.SemaphoreType.DMA((4 + 2 * group + len(out_last),)),
            pltpu.SemaphoreType.DMA((2 * split + 1,)),
        ],
        out_specs=(ANY,) * (2 * split + 1),
    )
    up_parts, down_parts, out_sent = made[:split], made[split : 2 * split], made[2 * split]
    out_terms.append(xor_swap(out_sent, "g", near))
    if not tiled:
        fine = half // group
        order = jnp.array([turned(j, head_size) for j in range(head_size)]) ^ z
        near_g = jnp.arange(group) ^ g
        near_y = jnp.arange(segs) ^ yy

        def in_blocks(full):
            full = full.reshape(segs, group, fine, head_size, hidden).transpose(0, 3, 1, 2, 4)
            return list(full[near_y][:, order][:, :, near_g])

        up_parts, down_parts = in_blocks(up_parts[0]), in_blocks(down_parts[0])

    middle_in, _ = tie(middle, up_parts[0])
    outbound, _, grad_middle, middle_sums, branch_sum, *proj_parts = call(
        "middle_back",
        functools.partial(
            middle_back_kernel, (parts, items, len(in_terms), parts == segs)
        ),
        (middle_in, branch, upstream, mod, row_item, proj_weight, me, attn_rows, *in_terms),
        (HBM, HBM, HBM, VMEM, VMEM, HBM, SMEM) + (HBM,) * (1 + len(in_terms)),
        (shape_of((group, rows, width), BF), rows_bf, rows_f32, shape_of((8, 3 * model), F32),
         shape_of((8, model), F32))
        + (shape_of((parts, head_size, model // head_size, sub), BF),) * group,
        [
            pltpu.VMEM((rows, model), BF),
            pltpu.VMEM((model, rows), BF),
            pltpu.VMEM((rows, width), BF),
        ],
        late=(5, 7),
    )
    inbound = over_group(outbound)
    up_terms, down_terms = xor_scatter(up_parts, "yy"), xor_scatter(down_parts, "yy")
    proj_terms, proj_last = to_last(proj_parts)
    tied = tuple(out_terms) + tuple(proj_last)
    half_tiles = shape_of((head_size // 2, group, fine, hidden), BF)
    quarter_tiles = shape_of((head_size // 4, group, fine, hidden), BF)
    output_rows, output_sums, proj_sent = call(
        "output",
        functools.partial(output_kernel, (items, len(out_terms), len(proj_last))),
        (middle, upstream, mod, row_item, fc2_bias[None, :], *tied),
        (HBM, HBM, VMEM, VMEM, VMEM) + (HBM,) * len(tied),
        (rows_bf, shape_of((8, model), F32), shape_of(proj_last[0].shape, BF)),
    )
    up_terms = tie(*up_terms, output_rows)[:-1]
    up_kept, up_sent = call(
        "add",
        functools.partial(add_kernel, (len(up_terms),)),
        up_terms,
        (HBM,) * len(up_terms),
        (half_tiles, half_tiles),
    )
    up_terms = (up_kept, xor_swap(up_sent, "head", 1))
    inbound, output_rows, _ = tie(inbound, output_rows, up_sent)
    output_back = to_packs(output_rows)
    proj_terms.append(xor_swap(proj_sent, "g", near))
    cols_f32 = pltpu.VMEM((pack_len, 128), F32)
    held_f32 = pltpu.VMEM((pack_len, width), F32)
    made = call(
        "attend_back",
        functools.partial(attend_back_kernel, (group, segs, head_dim, parts, block)),
        (me, temper, qkv_weight, inverses, queries_low, first, last, low, high, lse, inbound, queries,
         keys, values, out_t),
        (SMEM, VMEM, ANY, ANY, ANY, SMEM, SMEM, VMEM, VMEM, VMEM) + (ANY,) * 5,
        (rows_bf,) * group + (shape_of((pack_len, 3 * width), BF), shape_of((8, width), F32)),
        [
            held_bf,
            held_bf,
            held_bf,
            pltpu.VMEM((width, pack_len), F32),
            held_bf,
            pltpu.VMEM((width, pack_len), BF),
            held_f32,
            held_f32,
            pltpu.VMEM((width, block), F32),
            pltpu.VMEM((8, block), F32),
            held_bf,
            held_bf,
            held_bf,
            pltpu.VMEM((model, 3 * width), BF),
            cols_f32,
            held_bf,
            pltpu.VMEM((pack_len, 3 * width), BF),
            pltpu.VMEM((group, rows, model), BF),
            pltpu.SemaphoreType.DMA((6 + segs * group,)),
            pltpu.SemaphoreType.DMA((3 * parts,)),
            pltpu.SemaphoreType.DMA((2 * group,)),
        ],
        out_specs=(ANY,) * (group + 1) + (VMEM,),
    )
    made, down_terms, up_terms, proj_terms, (output_back,) = tie_groups(
        made, down_terms, up_terms, proj_terms, (output_back,)
    )
    grad_qkv, qkv_sums = made[group:]

    (vectors,) = call(
        "vector_parts",
        functools.partial(vector_parts_kernel, (group, parts, head_size)),
        (me, qkv_sums, branch_sum, grad_mlp_sum, *hidden_sums),
        (SMEM,) + (VMEM,) * (3 + len(hidden_sums)),
        (shape_of((64, 256), F32),),
        [pltpu.VMEM((16, model), F32)],
    )
    if not tiled:
        hidden_row = (hidden_sums[0] + hidden_sums[1])[0].reshape(head_size, hidden)
        hidden_row = lax.dynamic_update_slice(
            jnp.zeros((16, model), F32), hidden_row, (8, g * hidden)
        )
        vectors = vectors + hidden_row.reshape(16, 4, 256).transpose(1, 0, 2).reshape(64, 256)

    in_terms, last_terms = to_last(made[:group])
    sent = add_low(*last_terms)
    in_terms.append(xor_swap(sent, "g", near))
    tied = tie(*down_terms, *up_terms, sent)[:-1]
    down_kept, down_sent, up_kept, up_sent = call(
        "add",
        functools.partial(add_kernel, (len(down_terms), 2)),
        tied,
        (HBM,) * len(tied),
        (half_tiles, half_tiles, quarter_tiles, quarter_tiles),
    )
    down_terms = (down_kept, xor_swap(down_sent, "head", 1))
    up_terms = (up_kept, xor_swap(up_sent, "head", 2))
    grad_qkv, _ = tie(grad_qkv, down_sent)
    qkv_parts = call(
        "qkv_weights",
        functools.partial(
            qkv_weights_kernel, (group, parts, parts == segs, len(proj_terms))
        ),
        (me, grad_qkv, *attn_blocks, *proj_terms),
        (SMEM,) + (HBM,) * (1 + group + len(proj_terms)),
        (shape_of((head_size, 4, model // head_size, sub), BF),) * parts,
        [pltpu.VMEM((model, pack_len), BF), pltpu.VMEM((pack_len, 3 * sub), BF)],
    )
    down_terms, up_terms, _ = tie_groups(down_terms, up_terms, qkv_parts)
    down_kept, down_sent = call(
        "add", functools.partial(add_kernel, (2,)), down_terms, (HBM,) * 2, (quarter_tiles,) * 2
    )
    down_terms = (down_kept, xor_swap(down_sent, "head", 2))
    inputs_back, _ = tie(inputs, down_sent)
    tokens_grad_rows, tokens_sums = call(
        "tokens_back",
        functools.partial(tokens_back_kernel, (items, len(in_terms))),
        (inputs_back, grad_middle, mod, row_item, *in_terms),
        (HBM, HBM, VMEM, VMEM) + (HBM,) * len(in_terms),
        (rows_bf, shape_of((8, 2 * model), F32)),
    )

    tokens_grad_rows, *down_terms = tie(tokens_grad_rows, *down_terms)

    def to_data(values):
        return dot(to_slot, values, ((0,), (0,)))

    output = to_data(output_back).astype(BF)
    tokens_came = to_packs(tokens_grad_rows)

    ada_cols = 6 * model // (dp_size * head_size)
    packs = segs * head_size
    (kept,) = call(
        "item_blocks",
        functools.partial(item_blocks_kernel, (group, segs, head_size, ada_cols)),
        (me, middle_sums, output_sums, tokens_sums),
        (SMEM, VMEM, VMEM, VMEM),
        (shape_of((group, packs * 8, 256), F32),),
        [pltpu.VMEM((8, 6 * model), F32)],
        out_specs=(VMEM,),
    )
    sent = jnp.concatenate([kept[k] for k in range(1, group, 2)] + [vectors], axis=0)
    count = group
    for step in reversed(bits(group)):
        came = xor_swap(sent, "g", step)
        left = count // 2
        own = (left, packs * 8, 256) if left > 1 else (packs * 4, 256)
        rows_sent = (left // 2 * packs * 8 if left > 1 else packs * 4) + 64
        kept, sent, vectors = call(
            "group_sums",
            functools.partial(group_sums_kernel, count, step),
            (kept, came, vectors),
            (VMEM,) * 3,
            (shape_of(own, F32), shape_of((rows_sent, 256), F32), shape_of((64, 256), F32)),
            out_specs=(VMEM,) * 3,
        )
        count = left
    kept = kept.reshape(packs // 2, 1, 8, 256)
    tokens_sent = sent
    def over_head(terms):
        while terms[0].shape[0] > 1:
            terms = halves_over_head(add_low(*terms))
        return terms

    down_terms = tie(*down_terms, *up_terms, tokens_grad_rows)[:-1]
    down_terms, up_terms = down_terms[:2], down_terms[2:]
    tied = tuple(over_head(up_terms)) + tuple(over_head(down_terms))
    own_tiles = call(
        "own_tiles",
        own_tiles_kernel,
        tied,
        (HBM,) * 4,
        (shape_of((2, fine, hidden), BF),) * group,
    )
    both_all = [own_tiles[0]]
    for i in range(1, group):
        both_all.append(lax.ppermute(own_tiles[i], "g", [(k, k ^ i) for k in range(group)]))
    if parts == segs:
        terms = tie(*xor_scatter(qkv_parts, "yy"), tokens_sent)[:-1]
        terms = halves_over_head(add_low(*terms))
        terms, both_all, (tokens_came,) = tie_groups(terms, both_all, (tokens_came,))
        terms = over_head(terms)
        summed = sum(term[0].astype(F32) for term in terms)
        proj_part, qkv_part = summed[0], summed[1:]
    else:
        both = qkv_parts[0].transpose(1, 0, 2, 3).reshape(4, model, width)
        full = lax.dynamic_update_slice(
            jnp.zeros((4, model, model), BF), both, (0, 0, g * width)
        )
        summed = lax.psum_scatter(full, ("yy", "g"), scatter_dimension=2, tiled=True)
        summed = lax.psum_scatter(summed, "head", scatter_dimension=1, tiled=True).astype(F32)
        proj_part, qkv_part = summed[0], summed[1:]

    if tiled:
        up_part, down_part = call(
            "place",
            functools.partial(place_kernel, group),
            (me, *both_all),
            (SMEM,) + (HBM,) * group,
            (shape_of((fine, group * hidden), F32), shape_of((group * hidden, fine), F32)),
        )
    else:
        placed = jnp.stack(both_all)[jnp.arange(group) ^ g].astype(F32)
        up_part = placed[:, 0].transpose(1, 0, 2).reshape(fine, group * hidden)
        down_part = placed[:, 1].transpose(0, 2, 1).reshape(group * hidden, fine)


    sent, _ = tie(sent, tokens_came)
    tokens_grad = to_data(tokens_came)
    steps = [("yy", step) for step in bits(segs)] + [("head", step) for step in reversed(bits(head_size))]
    for place, (axis, step) in enumerate(steps):
        came = xor_swap(sent, axis, step)
        blocks, senders = kept.shape[0], kept.shape[1]
        end = place + 1 == len(steps)
        own = (blocks if end else blocks // 2, 2 * senders, 8, 256)
        outs = [shape_of(own, F32)]
        if not end:
            outs.append(shape_of((blocks // 2 * 2 * senders * 8 + 64, 256), F32))
        outs.append(shape_of((64, 256), F32))
        made = call(
            "pack_sums", pack_sums_kernel, (kept, came, vectors), (VMEM,) * 3, outs,
            out_specs=(VMEM,) * len(outs),
        )
        kept, vectors = made[0], made[-1]
        sent = made[1] if not end else None
    item_came = kept[0]
    vectors = vectors.reshape(4, 16, 256).transpose(1, 0, 2).reshape(16, model)
    silu_rows = jnp.pad(silu_cond.reshape(packs, items, model), ((0, 0), (0, 8 - items), (0, 0)))
    ada_grad, ada_bias_grad = call(
        "ada",
        functools.partial(ada_kernel, segs),
        (me, silu_rows.reshape(packs * 8, model), item_came),
        (SMEM, VMEM, VMEM),
        (shape_of((model, ada_cols), F32), shape_of((8, ada_cols), F32)),
        [pltpu.VMEM((packs * 8, 256), F32)],
    )
    ada_bias_grad = ada_bias_grad[0]

    log_scale_grad = jnp.sum(vectors[2].reshape(heads_all, head_dim), axis=1)
    fc1_bias_grad = pick(vectors, 8 + z, 0)[: group * hidden]
    return (
        output,
        tokens_grad,
        ada_grad,
        ada_bias_grad,
        qkv_part,
        vectors[0],
        vectors[1],
        log_scale_grad,
        proj_part,
        vectors[3],
        up_part,
        fc1_bias_grad,
        down_part,
        vectors[4],
    )


def solution(mesh):
    head_size = mesh.shape["head"]
    dp_size = mesh.shape["dp"]
    inner = Mesh(
        mesh.devices.reshape(dp_size // head_size, head_size, head_size), ("yy", "g", "head")
    )
    dp = ("yy", "g")
    everything = ("yy", "g", "head")
    in_specs = (
        P(everything, None),
        P(everything, None),
        P(),
        P(),
        P(),
        P(),
        P(),
        P(),
        P(),
        P(),
        P(),
        P(None, "head"),
        P("head"),
        P("head", None),
        P(),
        P(),
        P(),
        P(dp, None),
        P(everything),
    )
    out_specs = (
        P(everything, None),
        P(everything, None),
        P(None, everything),
        P(everything),
        P(None, "head", dp),
        P(),
        P(),
        P(),
        P("head", dp),
        P(),
        P(dp, "head"),
        P("head"),
        P("head", dp),
        P(),
    )
    return jax.shard_map(
        shards, mesh=inner, in_specs=in_specs, out_specs=out_specs, check_vma=False
    )
```
